32 devices in a mesh: section: 2 (over core), ctx: 4 (over y, x), tp: 4 (over z).
Axes of the slice: x: 2, y: 2, z: 4, core: 2. Of those that a mesh axis runs over, the one named last changes fastest.
Arguments:
- inputs: bfloat16 [2, 4096, 1024], P(None, ('ctx', 'tp')), may hold values from -6 to 6
- cotangent: bfloat16 [2, 4096, 1024], P(None, ('ctx', 'tp')), may hold values from -6 to 6
- lengths: int32 [2, 4], replicated, may hold values from 1 to 3074, 4096 in all within a row
- gain1: bfloat16 [2, 1024], P('section'), may hold values from 0.5 to 1.5
- wqkv: bfloat16 [2, 3, 16, 64, 1024], P('section', None, 'tp'), may hold values from -0.1875 to 0.1875
- wo: bfloat16 [2, 1024, 1024], P('section', 'tp'), may hold values from -0.75 to 0.75
- gain2: bfloat16 [2, 1024], P('section'), may hold values from 0.5 to 1.5
- wgu: bfloat16 [2, 2, 2816, 1024], P('section', None, 'tp'), may hold values from -0.1875 to 0.1875
- wd: bfloat16 [2, 2816, 1024], P('section', 'tp'), may hold values from -0.109375 to 0.109375
Outputs:
- acts: bfloat16 [2, 2, 4096, 1024], P('section', None, ('ctx', 'tp'))
- input_grads: float32 [2, 2, 4096, 1024], P('section', None, ('ctx', 'tp'))
- grad_gain1: float32 [2, 1024], P('section')
- grad_wqkv: float32 [2, 3, 16, 64, 1024], P('section', None, 'tp')
- grad_wo: float32 [2, 1024, 1024], P('section', 'tp')
- grad_gain2: float32 [2, 1024], P('section')
- grad_wgu: float32 [2, 2, 2816, 1024], P('section', None, 'tp')
- grad_wd: float32 [2, 2816, 1024], P('section', 'tp')
The draws below stay inside these ranges and needn't reach their ends.
Inputs may be any that keep to these rules, and one draw needn't show every extreme that they name: In each micro-batch the 4 lengths sum to 4096 and the longest is exactly 3074.
All inputs are finite; a program needn't handle non-finite values.
Results may differ from the reference program's by a relative error of at most 0.03.
Values may be sent and summed in bfloat16 or wider, within the bound.
No kernel may reach another device: no remote copies, remote signals or barrier semaphores. Data moves between devices by JAX's collectives and lax.ppermute only.
A program may use at most 256 MiB of HBM per device.

```python
import math
import jax
import jax.numpy as jnp
import numpy as np
from jax import lax

D = 1024
HEADS = 16
HD = 64
FF = 2816
MICRO = 2
NSEQ = 4
TOK_MB = 4096
LONGEST = 3074


def block_scale(key, dims, cuts, smallest, high):
    factor_of, own = 1.0, jax.random.fold_in(key, 6)
    for axis_at, blocks in cuts:
        steps = jnp.exp(jax.random.uniform(jax.random.fold_in(own, axis_at), (blocks,), jnp.float32, smallest / len(cuts), high / len(cuts)))
        factor_of = factor_of * jnp.repeat(steps, dims[axis_at] // blocks).reshape([-1 if axis == axis_at else 1 for axis in range(len(dims))])
    return factor_of


def split_up(number_of, total, limit, slope):
    loads = [(1 << 20) // math.isqrt(grade ** slope) + 1 for grade in range(2, number_of + 1)]
    surplus, counts = total - limit - (number_of - 1), [1] * (number_of - 1)
    while surplus > 0:
        candidates = [i for i in range(number_of - 1) if counts[i] < limit]
        pool, left = sum([loads[i] for i in candidates]), surplus
        for i in candidates:
            addition = min(limit - counts[i], max(1, left * loads[i] // pool), surplus)
            counts[i] = counts[i] + addition
            surplus = surplus - addition
    return np.array([limit] + counts)


def ragged(rng, amount, total, most, lean):
    if amount == 2:
        one = jax.random.randint(rng, (), max(1, total - most), min(most, total - 1) + 1)
        return jnp.stack([one, total - one])
    sizes = jnp.asarray(split_up(amount, total, most, lean), jnp.int32)
    twos = (amount - 1) // 2
    giver, taker = sizes[1:1 + 2 * twos:2], sizes[2:2 + 2 * twos:2]
    slack = jnp.minimum(giver - 1, most - taker)
    moved = jax.random.randint(jax.random.fold_in(rng, 1), (twos,), 0, 1 << 20) % (slack + 1)
    sizes = sizes.at[1:1 + 2 * twos:2].set(giver - moved).at[2:2 + 2 * twos:2].set(taker + moved)
    return sizes[jax.random.permutation(jax.random.fold_in(rng, 2), amount)]


def bell_draw(stream_key, extent, deviation, reach, cuts=(), kind=jnp.bfloat16):
    entries = jax.random.normal(stream_key, extent, jnp.float32) * deviation
    if len(cuts) > 0:
        entries = block_scale(stream_key, extent, cuts, -0.22, 0.18) * entries
    return jnp.clip(entries, min=-reach, max=reach).astype(kind)


def setup_inputs(seed: int = 0) -> dict:
    splits = jax.random.split(jax.random.key(seed), 10)
    return {
        "inputs": bell_draw(splits[0], (MICRO, TOK_MB, D), 1.0, 6.0, ((1, 16),)),
        "cotangent": bell_draw(splits[1], (MICRO, TOK_MB, D), 1.0, 6.0, ((1, 16),)),
        "lengths": jax.vmap(lambda own: ragged(own, NSEQ, TOK_MB, LONGEST, 2))(jax.random.split(splits[2], MICRO)).reshape((MICRO, NSEQ)).astype(jnp.int32),
        "gain1": jnp.clip(1.0 + 0.1 * jax.random.normal(splits[3], (2, D), jnp.float32), 0.5, 1.5).astype(jnp.bfloat16),
        "wqkv": bell_draw(splits[4], (2, 3, HEADS, HD, D), D ** -0.5, 0.1875, ((0, 2), (2, 4))),
        "wo": bell_draw(splits[5], (2, HEADS * HD, D), (HEADS * HD // 16) ** -0.5, 0.75, ((0, 2), (1, 4))),
        "gain2": jnp.clip(1.0 + 0.1 * jax.random.normal(splits[6], (2, D), jnp.float32), 0.5, 1.5).astype(jnp.bfloat16),
        "wgu": bell_draw(splits[7], (2, 2, FF, D), D ** -0.5, 0.1875, ((0, 2), (2, 4))),
        "wd": bell_draw(splits[8], (2, FF, D), FF ** -0.5, 0.109375, ((0, 2), (1, 4))),
    }


@jax.custom_vjp
def low(v):
    return lax.optimization_barrier(v.astype(jnp.bfloat16)).astype(jnp.float32)

@jax.custom_vjp
def low_back(v):
    return v

def low_keep(v):
    return (low(v), None)

def low_pass(kept, grad):
    return (grad,)

def back_keep(v):
    return (v, None)

def back_low(kept, grad):
    return (low(grad),)
low.defvjp(low_keep, low_pass)
low_back.defvjp(back_keep, back_low)
EPSILON = 1e-06

def matmul(left, right):
    return jnp.dot(left, right, precision=lax.Precision.HIGHEST)

def token_bounds(seq_lengths):
    token_index = jnp.arange(TOK_MB, dtype=jnp.int32)
    doc_ends = jnp.cumsum(seq_lengths).astype(jnp.int32)
    before = (doc_ends[None, :] <= token_index[:, None]).astype(jnp.int32)
    doc_start = lax.optimization_barrier(jnp.sum(before * seq_lengths[None, :], axis=1)).astype(jnp.int32)
    return (token_index, doc_start)

def rope_parts(position):
    half_width = HD // 2
    frequency = jnp.exp(-jnp.log(10000.0) * jnp.arange(half_width, dtype=jnp.float32) / half_width)
    angles = position.astype(jnp.float32)[:, None] * frequency[None, :]
    return (jnp.cos(angles), jnp.sin(angles))

def rotate(vectors, cosine, sine_part):
    half_width = HD // 2
    leading_half = vectors[..., :half_width]
    trailing_half = vectors[..., half_width:]
    cosine = cosine[:, None, :]
    sine_part = sine_part[:, None, :]
    return jnp.concatenate([leading_half * cosine - trailing_half * sine_part, trailing_half * cosine + leading_half * sine_part], axis=-1)

def decoder_layer(row_block, first_values, value_mix, gain_first, w_qkv, w_out, gain_second, w_gateup, w_down, token_index, doc_start):
    row_count = row_block.shape[0]
    head_width = HEADS * HD
    scale_first = lax.rsqrt(lax.optimization_barrier(jnp.mean(row_block * row_block, axis=-1, keepdims=True)) + EPSILON)
    normed = low(row_block * scale_first * gain_first)
    projected = low_back(matmul(normed, w_qkv.reshape(3 * head_width, D).T))
    cosine, sine_part = rope_parts(token_index - doc_start)
    query_heads = low(rotate(projected[:, :head_width].reshape(row_count, HEADS, HD), cosine, sine_part))
    key_heads = low(rotate(projected[:, head_width:2 * head_width].reshape(row_count, HEADS, HD), cosine, sine_part))
    values = projected[:, 2 * head_width:]
    if first_values is None:
        mixed = low(values)
    else:
        mixed = low((1.0 - value_mix) * values + value_mix * first_values)
    allowed = (token_index[None, :] >= doc_start[:, None]) & (token_index[None, :] <= token_index[:, None])
    scale = HD ** (-0.5)

    def one_head(head_parts):
        query_head, key_head, value_head = head_parts
        scores = low_back(matmul(query_head, key_head.T) * scale)
        masked = jnp.where(allowed, scores, -1e+30)
        running_top = lax.optimization_barrier(jnp.max(masked, axis=-1, keepdims=True))
        exp_scores = jnp.where(allowed, jnp.exp(masked - running_top), 0.0)
        soft_weights = low(exp_scores / lax.optimization_barrier(jnp.sum(exp_scores, axis=-1, keepdims=True)))
        return matmul(soft_weights, value_head)
    heads_out = lax.map(jax.checkpoint(one_head), (query_heads.transpose(1, 0, 2), key_heads.transpose(1, 0, 2), mixed.reshape(row_count, HEADS, HD).transpose(1, 0, 2)))
    attended = low_back(low(heads_out.transpose(1, 0, 2).reshape(row_count, head_width)))
    hidden = row_block + low_back(matmul(attended, w_out))
    scale_second = lax.rsqrt(lax.optimization_barrier(jnp.mean(hidden * hidden, axis=-1, keepdims=True)) + EPSILON)
    normed_second = low(hidden * scale_second * gain_second)
    gate_up = low_back(matmul(normed_second, w_gateup.reshape(2 * FF, D).T))
    activated = low(jax.nn.silu(gate_up[:, :FF]) * gate_up[:, FF:])
    layer_out = low(hidden + low_back(matmul(activated, w_down)))
    return (layer_out, mixed)

def reference(inputs, cotangent, lengths, gain1, wqkv, wo, gain2, wgu, wd):
    weights = tuple((weight.astype(jnp.float32) for weight in (gain1, wqkv, wo, gain2, wgu, wd)))
    rows_in = inputs.astype(jnp.float32)
    probe_rows = jnp.zeros_like(rows_in)

    def forward(rows_all, extra_all, gain_one, w_qkv, w_out, gain_two, w_gateup, w_down):

        def one_batch(batch_parts):
            row_block, extra_rows, seq_lengths = batch_parts
            token_index, doc_start = token_bounds(seq_lengths)
            first_out, first_values = decoder_layer(row_block, None, 0.0, gain_one[0], w_qkv[0], w_out[0], gain_two[0], w_gateup[0], w_down[0], token_index, doc_start)
            passed = low_back(first_out + extra_rows)
            second_out, unused = decoder_layer(passed, low_back(first_values), 0.5, gain_one[1], w_qkv[1], w_out[1], gain_two[1], w_gateup[1], w_down[1], token_index, doc_start)
            return (first_out, second_out)
        return lax.map(one_batch, (rows_all, extra_all, lengths))
    (first_all, second_all), pullback = jax.vjp(forward, rows_in, probe_rows, *weights)
    grads = pullback((jnp.zeros_like(first_all), cotangent.astype(jnp.float32)))
    acts = jnp.stack([first_all, second_all]).astype(jnp.bfloat16)
    input_grads = jnp.stack([grads[0], grads[1]])
    return (acts, input_grads, grads[2], grads[3], grads[4], grads[5], grads[6], grads[7])
```

```python
import functools

import jax
import jax.numpy as jnp
from jax import lax
from jax.experimental import pallas as pl
from jax.experimental.pallas import tpu as pltpu
from jax.sharding import PartitionSpec as P

HD = 64
EPSILON = 1e-06
MASKED = -1e30
ALL_AXES = ("section", "ctx", "tp")
VMEM_LIMIT = 40 * 1024 * 1024


def shifted(block, axis, distance):
    devices = range(lax.axis_size(axis))
    route = [(i - distance, i) for i in devices if i - distance in devices]
    return lax.ppermute(block, axis, route)


def rope_parts(position):
    half_width = HD // 2
    frequency = jnp.exp(-jnp.log(10000.0) * jnp.arange(half_width, dtype=jnp.float32) / half_width)
    angles = position.astype(jnp.float32)[:, None] * frequency[None, :]
    return (jnp.cos(angles), jnp.sin(angles))


def rotate(vectors, cosine, sine_part):
    half_width = HD // 2
    leading_half = vectors[..., :half_width]
    trailing_half = vectors[..., half_width:]
    cosine = cosine[:, None, :]
    sine_part = sine_part[:, None, :]
    return jnp.concatenate(
        [
            leading_half * cosine - trailing_half * sine_part,
            trailing_half * cosine + leading_half * sine_part,
        ],
        axis=-1,
    )


def rotate_back(vectors, cosine, sine_part):
    half_width = HD // 2
    leading_half = vectors[..., :half_width]
    trailing_half = vectors[..., half_width:]
    cosine = cosine[:, None, :]
    sine_part = sine_part[:, None, :]
    return jnp.concatenate(
        [
            leading_half * cosine + trailing_half * sine_part,
            trailing_half * cosine - leading_half * sine_part,
        ],
        axis=-1,
    )


def inner_rows(left, right):
    return lax.dot_general(
        left, right, (((0,), (0,)), ((), ())), preferred_element_type=jnp.float32
    )


def outer_cols(left, right):
    return lax.dot_general(
        left, right, (((1,), (1,)), ((), ())), preferred_element_type=jnp.float32
    )


def spread(row_block):
    return lax.all_gather(row_block, "tp", axis=0, tiled=True)


def collect(partial_value):
    return lax.psum_scatter(
        partial_value.astype(jnp.bfloat16), "tp", scatter_dimension=0, tiled=True
    ).astype(jnp.float32)


def fetch_keys(key_value):
    return lax.all_gather(key_value, "ctx", axis=0, tiled=True)


def query_bounds(seq_lengths, block_first, row_count):
    token_index = block_first + jnp.arange(row_count, dtype=jnp.int32)
    doc_ends = jnp.cumsum(seq_lengths)
    before = (doc_ends[None, :] <= token_index[:, None]).astype(jnp.int32)
    doc_start = jnp.sum(before * seq_lengths[None, :], axis=1)
    return (token_index, doc_start)


def block_scores(query_heads, pair_block, block_first, token_index, doc_start, head_width):
    row_count = pair_block.shape[0]
    key_heads = pair_block[:, :head_width].reshape(row_count, head_width // HD, HD)
    value_heads = pair_block[:, head_width:].reshape(row_count, head_width // HD, HD)
    scores = jnp.einsum(
        "qhd,khd->hqk", query_heads, key_heads, preferred_element_type=jnp.float32
    ) * HD ** (-0.5)
    key_index = block_first + jnp.arange(row_count, dtype=jnp.int32)
    allowed = (key_index[None, :] >= doc_start[:, None]) & (
        key_index[None, :] <= token_index[:, None]
    )
    return (scores, allowed[None], key_heads, value_heads)


def split_blocks(pairs_all, row_count):
    blocks = pairs_all.reshape(-1, row_count, pairs_all.shape[1])
    block_starts = jnp.arange(blocks.shape[0], dtype=jnp.int32) * row_count
    return (blocks, block_starts)


def attend(query_heads, pairs_all, token_index, doc_start, head_width):
    row_count = query_heads.shape[0]
    head_count = head_width // HD
    blocks, block_starts = split_blocks(pairs_all, row_count)
    last_query = token_index[row_count - 1]
    first_query = doc_start[0]

    def rowmax_live(carried, block_parts):
        running_top, running_sum = carried
        scores, allowed, unused_keys, unused_values = block_scores(
            query_heads, block_parts[0], block_parts[1], token_index, doc_start, head_width
        )
        masked = jnp.where(allowed, scores, -1e30)
        new_top = jnp.maximum(running_top, jnp.max(masked, axis=-1))
        running_sum = running_sum * jnp.exp(running_top - new_top) + jnp.sum(
            jnp.where(allowed, jnp.exp(masked - new_top[..., None]), 0.0), axis=-1
        )
        return (new_top, running_sum)

    def rowmax_step(carried, block_parts):
        live = (block_parts[1] <= last_query) & (block_parts[1] + row_count > first_query)
        return (
            lax.cond(live, lambda held: rowmax_live(held, block_parts), lambda held: held, carried),
            None,
        )

    initial = (
        jnp.full((head_count, row_count), -1e30, jnp.float32),
        jnp.zeros((head_count, row_count), jnp.float32),
    )
    (running_top, running_sum), unused = lax.scan(rowmax_step, initial, (blocks, block_starts))
    log_total = running_top + jnp.log(running_sum)

    def output_live(accumulated, block_parts):
        scores, allowed, unused_keys, value_heads = block_scores(
            query_heads, block_parts[0], block_parts[1], token_index, doc_start, head_width
        )
        soft_weights = jnp.where(allowed, jnp.exp(scores - log_total[..., None]), 0.0).astype(
            jnp.bfloat16
        )
        return accumulated + jnp.einsum(
            "hqk,khd->qhd", soft_weights, value_heads, preferred_element_type=jnp.float32
        )

    def output_step(accumulated, block_parts):
        live = (block_parts[1] <= last_query) & (block_parts[1] + row_count > first_query)
        return (
            lax.cond(
                live, lambda held: output_live(held, block_parts), lambda held: held, accumulated
            ),
            None,
        )

    accumulated, unused = lax.scan(
        output_step, jnp.zeros((row_count, head_count, HD), jnp.float32), (blocks, block_starts)
    )
    return (accumulated, log_total)


def attend_back(
    query_heads, pairs_all, token_index, doc_start, head_width, log_total, accumulated, grad_heads
):
    row_count = query_heads.shape[0]
    head_count = head_width // HD
    blocks, block_starts = split_blocks(pairs_all, row_count)
    last_query = token_index[row_count - 1]
    first_query = doc_start[0]
    rowdot = jnp.sum(grad_heads.astype(jnp.float32) * accumulated, axis=-1).T

    def grad_live(grad_acc, block_parts):
        scores, allowed, key_heads, value_heads = block_scores(
            query_heads, block_parts[0], block_parts[1], token_index, doc_start, head_width
        )
        soft_weights = jnp.where(allowed, jnp.exp(scores - log_total[..., None]), 0.0)
        grad_soft = jnp.einsum(
            "qhd,khd->hqk", grad_heads, value_heads, preferred_element_type=jnp.float32
        )
        grad_scores = (soft_weights * (grad_soft - rowdot[..., None])).astype(jnp.bfloat16)
        grad_acc = grad_acc + jnp.einsum(
            "hqk,khd->qhd", grad_scores, key_heads, preferred_element_type=jnp.float32
        )
        grad_keys = jnp.einsum(
            "hqk,qhd->khd", grad_scores, query_heads, preferred_element_type=jnp.float32
        ) * HD ** (-0.5)
        grad_values = jnp.einsum(
            "hqk,qhd->khd",
            soft_weights.astype(jnp.bfloat16),
            grad_heads,
            preferred_element_type=jnp.float32,
        )
        return (grad_acc, (grad_keys, grad_values))

    def grad_skip(grad_acc):
        empty = jnp.zeros((row_count, head_count, HD), jnp.float32)
        return (grad_acc, (empty, empty))

    def grad_step(grad_acc, block_parts):
        live = (block_parts[1] <= last_query) & (block_parts[1] + row_count > first_query)
        return lax.cond(live, lambda held: grad_live(held, block_parts), grad_skip, grad_acc)

    grad_query, (grad_keys, grad_values) = lax.scan(
        grad_step, jnp.zeros((row_count, head_count, HD), jnp.float32), (blocks, block_starts)
    )
    grad_query = grad_query * HD ** (-0.5)
    grad_pairs = jnp.concatenate(
        [grad_keys.reshape(-1, head_width), grad_values.reshape(-1, head_width)], axis=1
    )
    return (grad_query, grad_pairs)


def norm_back(whole_rows, scale_rows, gain, grad_normed, grad_rest):
    unit_rows = whole_rows * scale_rows
    scaled = grad_normed * gain.astype(jnp.float32)
    grad_gain = jnp.sum(grad_normed * unit_rows, axis=0)
    grad_whole = grad_rest + scale_rows * (
        scaled - unit_rows * jnp.mean(scaled * unit_rows, axis=-1, keepdims=True)
    )
    return (grad_gain, grad_whole)


def layer_forward(row_block, first_values, value_mix, weights, seq_lengths):
    gain_first, w_qkv, w_out, gain_second, w_gateup, w_down = weights
    head_count = w_qkv.shape[1]
    head_width = head_count * HD
    model_width = row_block.shape[1]
    whole_rows = row_block.astype(jnp.float32)
    scale_first = lax.rsqrt(jnp.mean(whole_rows * whole_rows, axis=-1, keepdims=True) + EPSILON)
    normed = (whole_rows * scale_first * gain_first.astype(jnp.float32)).astype(jnp.bfloat16)
    normed_all = spread(normed)
    row_count = normed_all.shape[0]
    projected = outer_cols(normed_all, w_qkv.reshape(3 * head_width, model_width))
    token_index, doc_start = query_bounds(seq_lengths, lax.axis_index("ctx") * row_count, row_count)
    cosine, sine_part = rope_parts(token_index - doc_start)
    query_heads = rotate(
        projected[:, :head_width].reshape(row_count, head_count, HD), cosine, sine_part
    ).astype(jnp.bfloat16)
    key_heads = rotate(
        projected[:, head_width : 2 * head_width].reshape(row_count, head_count, HD),
        cosine,
        sine_part,
    ).astype(jnp.bfloat16)
    mixed = (
        (1.0 - value_mix) * projected[:, 2 * head_width :]
        + value_mix * first_values.astype(jnp.float32)
    ).astype(jnp.bfloat16)
    key_value = jnp.concatenate([key_heads.reshape(row_count, head_width), mixed], axis=1)
    pairs_all = fetch_keys(key_value)
    accumulated, log_total = attend(query_heads, pairs_all, token_index, doc_start, head_width)
    attended = accumulated.reshape(row_count, head_width).astype(jnp.bfloat16)
    hidden = whole_rows + collect(jnp.dot(attended, w_out, preferred_element_type=jnp.float32))
    scale_second = lax.rsqrt(jnp.mean(hidden * hidden, axis=-1, keepdims=True) + EPSILON)
    normed_second = (hidden * scale_second * gain_second.astype(jnp.float32)).astype(jnp.bfloat16)
    ffn_rows = spread(normed_second)
    gate_up = outer_cols(ffn_rows, w_gateup.reshape(-1, model_width))
    unit_count = gate_up.shape[1] // 2
    gate_part = gate_up[:, :unit_count]
    up_part = gate_up[:, unit_count:]
    activated = (jax.nn.silu(gate_part) * up_part).astype(jnp.bfloat16)
    down_part = jnp.dot(activated, w_down, preferred_element_type=jnp.float32)
    branch_out = collect(down_part)
    layer_out = (hidden + branch_out).astype(jnp.bfloat16)
    saved = (
        whole_rows,
        scale_first,
        normed_all,
        query_heads,
        pairs_all,
        token_index,
        doc_start,
        cosine,
        sine_part,
        log_total,
        accumulated,
        attended,
        hidden,
        scale_second,
        ffn_rows,
        gate_part,
        up_part,
        activated,
    )
    return (layer_out, mixed, pairs_all, saved)


def layer_backward(grad_rows, extra_values, value_mix, weights, saved):
    gain_first, w_qkv, w_out, gain_second, w_gateup, w_down = weights
    (
        whole_rows,
        scale_first,
        normed_all,
        query_heads,
        pairs_all,
        token_index,
        doc_start,
        cosine,
        sine_part,
        log_total,
        accumulated,
        attended,
        hidden,
        scale_second,
        ffn_rows,
        gate_part,
        up_part,
        activated,
    ) = saved
    model_width = whole_rows.shape[1]
    head_count = w_qkv.shape[1]
    head_width = head_count * HD
    row_count = normed_all.shape[0]
    grad_hidden = grad_rows.astype(jnp.float32)
    grad_down = spread(grad_rows)
    grad_wd = inner_rows(activated, grad_down)
    grad_act = outer_cols(grad_down, w_down)
    sigmoid_gate = jax.nn.sigmoid(gate_part)
    grad_gate = grad_act * up_part * sigmoid_gate * (1.0 + gate_part * (1.0 - sigmoid_gate))
    grad_up = grad_act * gate_part * sigmoid_gate
    grad_gate_up = jnp.concatenate([grad_gate, grad_up], axis=1).astype(jnp.bfloat16)
    grad_wgu = inner_rows(grad_gate_up, ffn_rows).reshape(w_gateup.shape)
    back_second = jnp.dot(
        grad_gate_up, w_gateup.reshape(-1, model_width), preferred_element_type=jnp.float32
    )
    grad_normed_second = collect(back_second)
    grad_gain2, grad_hidden = norm_back(
        hidden, scale_second, gain_second, grad_normed_second, grad_hidden
    )
    grad_branch_all = spread(grad_hidden.astype(jnp.bfloat16))
    grad_wo = inner_rows(attended, grad_branch_all)
    grad_heads = (
        outer_cols(grad_branch_all, w_out).astype(jnp.bfloat16).reshape(row_count, head_count, HD)
    )
    grad_query, grad_pairs_all = attend_back(
        query_heads,
        pairs_all,
        token_index,
        doc_start,
        head_width,
        log_total,
        accumulated,
        grad_heads,
    )
    grad_pairs = lax.psum_scatter(
        grad_pairs_all.astype(jnp.bfloat16), "ctx", scatter_dimension=0, tiled=True
    ).astype(jnp.float32)
    grad_mixed = grad_pairs[:, head_width:] + extra_values.astype(jnp.float32)
    grad_keys = rotate_back(
        grad_pairs[:, :head_width].reshape(row_count, head_count, HD), cosine, sine_part
    )
    grad_query = rotate_back(grad_query, cosine, sine_part)
    grad_projected = jnp.concatenate(
        [
            grad_query.reshape(row_count, head_width),
            grad_keys.reshape(row_count, head_width),
            (1.0 - value_mix) * grad_mixed,
        ],
        axis=1,
    ).astype(jnp.bfloat16)
    send_values = (value_mix * grad_mixed).astype(jnp.bfloat16)
    grad_wqkv = inner_rows(grad_projected, normed_all).reshape(w_qkv.shape)
    grad_normed = collect(
        jnp.dot(
            grad_projected,
            w_qkv.reshape(3 * head_width, model_width),
            preferred_element_type=jnp.float32,
        )
    )
    grad_gain1, grad_whole = norm_back(
        whole_rows, scale_first, gain_first, grad_normed, grad_hidden
    )
    return (
        grad_whole,
        send_values,
        (grad_gain1, grad_wqkv, grad_wo, grad_gain2, grad_wgu, grad_wd),
    )


def general_body(inputs, cotangent, lengths, gain1, wqkv, wo, gain2, wgu, wd):
    section_index = lax.axis_index("section")
    leading = section_index == 0
    value_mix = jnp.where(leading, 0.0, 0.5).astype(jnp.float32)
    micro_count = inputs.shape[0]
    local_rows = inputs.shape[1]
    model_width = inputs.shape[2]
    head_width = wqkv.shape[2] * HD
    row_count = local_rows * lax.axis_size("tp")
    gateup_use, down_use = (wgu[0], wd[0])
    weights = (gain1[0], wqkv[0], wo[0], gain2[0], gateup_use, down_use)
    recv_rows = jnp.zeros((local_rows, model_width), jnp.bfloat16)
    recv_values = jnp.zeros((row_count, head_width), jnp.bfloat16)
    states = []
    outputs = []
    for turn_index in range(micro_count + 1):
        own_rows = inputs[min(turn_index, micro_count - 1)]
        row_block = jnp.where(leading, own_rows, recv_rows)
        seq_lengths = jnp.where(
            leading, lengths[min(turn_index, micro_count - 1)], lengths[max(turn_index - 1, 0)]
        )
        layer_out, mixed, pairs_all, unused = layer_forward(
            row_block, recv_values, value_mix, weights, seq_lengths
        )
        kept_pairs = None
        states.append((row_block, recv_values, seq_lengths, kept_pairs))
        outputs.append(layer_out)
        if turn_index < micro_count:
            recv_rows, recv_values = shifted((layer_out, mixed), "section", 1)
    grad_rows_in = jnp.zeros((local_rows, model_width), jnp.bfloat16)
    grad_values_in = jnp.zeros((row_count, head_width), jnp.bfloat16)
    totals = None
    turn_grads = []
    for turn_index in range(micro_count + 1):
        row_block, first_values, seq_lengths, kept_pairs = states[micro_count - turn_index]
        if turn_index < micro_count:
            fed_grad = cotangent[micro_count - 1 - turn_index]
        else:
            fed_grad = jnp.zeros_like(cotangent[0])
        grad_out = jnp.where(leading, grad_rows_in, fed_grad)
        unused_out, unused_mixed, unused_pairs, saved = layer_forward(
            row_block, first_values, value_mix, weights, seq_lengths
        )
        grad_whole, send_values, grads = layer_backward(
            grad_out, grad_values_in, value_mix, weights, saved
        )
        totals = grads if totals is None else jax.tree.map(jnp.add, totals, grads)
        sent_rows = grad_whole.astype(jnp.bfloat16)
        turn_grads.append(jnp.where(leading, grad_whole, sent_rows.astype(jnp.float32)))
        if turn_index < micro_count:
            grad_rows_in, grad_values_in = shifted((sent_rows, send_values), "section", -1)
    grad_gain1, grad_wqkv, grad_wo, grad_gain2, grad_wgu, grad_wd = totals
    grad_wqkv, grad_wo, grad_wgu, grad_wd = (
        lax.psum(grad_wqkv.astype(jnp.bfloat16), "ctx").astype(jnp.float32),
        lax.psum(grad_wo.astype(jnp.bfloat16), "ctx").astype(jnp.float32),
        lax.psum(grad_wgu.astype(jnp.bfloat16), "ctx").astype(jnp.float32),
        lax.psum(grad_wd.astype(jnp.bfloat16), "ctx").astype(jnp.float32),
    )
    grad_gain1, grad_gain2 = lax.psum((grad_gain1, grad_gain2), ("ctx", "tp"))
    acts = jnp.stack(
        [
            jnp.where(leading, outputs[batch_index], outputs[batch_index + 1])
            for batch_index in range(micro_count)
        ]
    )[None]
    input_grads = jnp.stack(
        [
            jnp.where(
                leading,
                turn_grads[micro_count - batch_index],
                turn_grads[micro_count - 1 - batch_index],
            )
            for batch_index in range(micro_count)
        ]
    )[None]
    return (
        acts,
        input_grads,
        grad_gain1[None],
        grad_wqkv[None],
        grad_wo[None],
        grad_gain2[None],
        grad_wgu[None],
        grad_wd[None],
    )


def device_groups(mesh_sizes, key, order):
    sections, contexts, parts = mesh_sizes
    groups = {}
    for section in range(sections):
        for ctx in range(contexts):
            for tp in range(parts):
                place = (section, ctx, tp)
                number = (section * contexts + ctx) * parts + tp
                groups.setdefault(key(*place), []).append((order(*place), number))
    return [[number for _, number in sorted(members)] for _, members in sorted(groups.items())]


def exchange(value, groups):
    return lax.all_to_all(
        value, ALL_AXES, split_axis=0, concat_axis=0, tiled=True, axis_index_groups=groups
    )


def document_bounds(ends_ref, first, index):
    start = jnp.zeros_like(index)
    for entry in range(ends_ref.shape[0]):
        end = ends_ref[entry]
        start = jnp.where(index >= end, end, start)
    return start


def scalar_start(ends_ref, index):
    start = jnp.int32(0)
    for entry in range(ends_ref.shape[0]):
        start = jnp.where(index >= ends_ref[entry], ends_ref[entry], start)
    return start


def scalar_end(ends_ref, index):
    end = ends_ref[ends_ref.shape[0] - 1]
    for entry in range(ends_ref.shape[0] - 2, -1, -1):
        end = jnp.where(index < ends_ref[entry], ends_ref[entry], end)
    return end


def dot(left, right, left_dim, right_dim):
    return lax.dot_general(
        left, right, (((left_dim,), (right_dim,)), ((), ())), preferred_element_type=jnp.float32
    )


def attention_forward_kernel(ends_ref, qkv_ref, out_ref, lse_ref, keys_ref):
    block = pl.program_id(0)
    blocks, _, width = qkv_ref.shape

    @pl.when(block == 0)
    def _():
        def turn(j, carry):
            keys_ref[j] = qkv_ref[j, HD : 2 * HD, :].T
            return carry

        lax.fori_loop(0, blocks, turn, 0)

    query = qkv_ref[block, 0:HD, :]
    first = block * width
    query_index = first + lax.broadcasted_iota(jnp.int32, (1, width), 1)
    start = document_bounds(ends_ref, first, query_index)
    low = scalar_start(ends_ref, first) // width
    high_start = scalar_start(ends_ref, first + width - 1)
    middle = jnp.clip((high_start + width - 1) // width, low, block)

    def step(j, carry, masked):
        top, total, acc = carry
        scores = dot(keys_ref[j], query, 1, 0)
        if masked:
            key_index = j * width + lax.broadcasted_iota(jnp.int32, (width, 1), 0)
            allowed = (key_index >= start) & (key_index <= query_index)
            scores = jnp.where(allowed, scores, MASKED)
        new_top = jnp.maximum(top, jnp.max(scores, axis=0, keepdims=True))
        shrink = jnp.exp(top - new_top)
        weights = jnp.exp(scores - new_top)
        total = total * shrink + jnp.sum(weights, axis=0, keepdims=True)
        values = qkv_ref[j, 2 * HD : 3 * HD, :]
        acc = acc * shrink + dot(values, weights.astype(jnp.bfloat16), 1, 0)
        return new_top, total, acc

    carry = (
        jnp.full((1, width), MASKED, jnp.float32),
        jnp.zeros((1, width), jnp.float32),
        jnp.zeros((HD, width), jnp.float32),
    )
    carry = lax.fori_loop(low, middle, functools.partial(step, masked=True), carry)
    carry = lax.fori_loop(middle, block, functools.partial(step, masked=False), carry)
    top, total, acc = step(block, carry, True)
    out_ref[0] = (acc / total).astype(jnp.bfloat16)
    lse_ref[0] = top + jnp.log(total)


def attention_forward(ends, qkv):
    blocks, _, width = qkv.shape
    pairs = blocks * (blocks + 1) // 2 * width * width
    return pl.pallas_call(
        attention_forward_kernel,
        grid_spec=pltpu.PrefetchScalarGridSpec(
            num_scalar_prefetch=1,
            grid=(blocks,),
            in_specs=[pl.BlockSpec(qkv.shape, lambda i, ends_ref: (0, 0, 0))],
            out_specs=[
                pl.BlockSpec((1, HD, width), lambda i, ends_ref: (i, 0, 0)),
                pl.BlockSpec((1, 1, width), lambda i, ends_ref: (i, 0, 0)),
            ],
            scratch_shapes=[pltpu.VMEM((blocks, width, HD), jnp.bfloat16)],
        ),
        out_shape=[
            jax.ShapeDtypeStruct((blocks, HD, width), jnp.bfloat16),
            jax.ShapeDtypeStruct((blocks, 1, width), jnp.float32),
        ],
        compiler_params=pltpu.CompilerParams(vmem_limit_bytes=VMEM_LIMIT),
        cost_estimate=pl.CostEstimate(
            flops=4 * HD * pairs, bytes_accessed=2 * qkv.size, transcendentals=pairs
        ),
        name="attention_forward",
    )(ends, qkv)


def attention_backward_kernel(
    ends_ref, qkv_ref, out_ref, grad_ref, lse_ref, result_ref, query_grad_ref, delta_ref
):
    block = pl.program_id(0)
    blocks, _, width = qkv_ref.shape

    @pl.when(block == 0)
    def _():
        def turn(i, carry):
            delta_ref[i] = jnp.sum(
                grad_ref[i].astype(jnp.float32) * out_ref[i].astype(jnp.float32),
                axis=0,
                keepdims=True,
            )
            query_grad_ref[i] = jnp.zeros((HD, width), jnp.float32)
            return carry

        lax.fori_loop(0, blocks, turn, 0)

    first = block * width
    keys_t = qkv_ref[block, HD : 2 * HD, :]
    keys = keys_t.T
    values = qkv_ref[block, 2 * HD : 3 * HD, :].T
    key_index = first + lax.broadcasted_iota(jnp.int32, (width, 1), 0)
    near_end = scalar_end(ends_ref, first)
    far_end = scalar_end(ends_ref, first + width - 1)
    stop = (far_end - 1) // width + 1
    middle = jnp.clip(near_end // width, block + 1, stop)

    def step(i, carry, masked):
        key_grad, value_grad = carry
        query = qkv_ref[i, 0:HD, :]
        grad = grad_ref[i]
        weights = jnp.exp(dot(keys, query, 1, 0) - lse_ref[i])
        if masked:
            query_index = i * width + lax.broadcasted_iota(jnp.int32, (1, width), 1)
            start = document_bounds(ends_ref, first, query_index)
            allowed = (key_index >= start) & (key_index <= query_index)
            weights = jnp.where(allowed, weights, 0.0)
        grad_weights = dot(values, grad, 1, 0)
        grad_scores = (weights * (grad_weights - delta_ref[i])).astype(jnp.bfloat16)
        value_grad = value_grad + dot(grad, weights.astype(jnp.bfloat16), 1, 1)
        key_grad = key_grad + dot(query, grad_scores, 1, 1)
        query_grad_ref[i] += dot(keys_t, grad_scores, 1, 0)
        return key_grad, value_grad

    empty = jnp.zeros((HD, width), jnp.float32)
    carry = step(block, (empty, empty), True)
    carry = lax.fori_loop(block + 1, middle, functools.partial(step, masked=False), carry)
    key_grad, value_grad = lax.fori_loop(middle, stop, functools.partial(step, masked=True), carry)
    result_ref[0, 0:HD] = (query_grad_ref[block] * HD ** (-0.5)).astype(jnp.bfloat16)
    result_ref[0, HD : 2 * HD] = key_grad.astype(jnp.bfloat16)
    result_ref[0, 2 * HD : 3 * HD] = value_grad.astype(jnp.bfloat16)


def attention_backward(ends, qkv, out, grad, lse):
    blocks, _, width = qkv.shape
    pairs = blocks * (blocks + 1) // 2 * width * width

    def whole(value):
        return pl.BlockSpec(value.shape, lambda i, ends_ref: (0, 0, 0))

    return pl.pallas_call(
        attention_backward_kernel,
        grid_spec=pltpu.PrefetchScalarGridSpec(
            num_scalar_prefetch=1,
            grid=(blocks,),
            in_specs=[whole(qkv), whole(out), whole(grad), whole(lse)],
            out_specs=pl.BlockSpec((1, 3 * HD, width), lambda i, ends_ref: (i, 0, 0)),
            scratch_shapes=[
                pltpu.VMEM((blocks, HD, width), jnp.float32),
                pltpu.VMEM((blocks, 1, width), jnp.float32),
            ],
        ),
        out_shape=jax.ShapeDtypeStruct(qkv.shape, jnp.bfloat16),
        compiler_params=pltpu.CompilerParams(vmem_limit_bytes=VMEM_LIMIT),
        cost_estimate=pl.CostEstimate(
            flops=10 * HD * pairs, bytes_accessed=6 * qkv.size, transcendentals=pairs
        ),
        name="attention_backward",
    )(ends, qkv, out, grad, lse)


def rope_pairs(pair_block, cosine, sine_part):
    half_width = HD // 2
    leading_half = pair_block[:, :half_width]
    trailing_half = pair_block[:, half_width:]
    return jnp.concatenate(
        [
            leading_half * cosine - trailing_half * sine_part,
            trailing_half * cosine + leading_half * sine_part,
        ],
        axis=1,
    )


def split_body(mesh_sizes, inputs, cotangent, lengths, gain1, wqkv, wo, gain2, wgu, wd):
    sections, contexts, parts = mesh_sizes
    half_parts = parts // 2
    section = lax.axis_index("section")
    ctx = lax.axis_index("ctx")
    tp = lax.axis_index("tp")
    leading = section == 0
    batch = tp // half_parts
    model_width = inputs.shape[2]
    rows = inputs.shape[1]
    heads = wqkv.shape[2] * parts
    units = wd.shape[1] // contexts
    number = lambda s, c, t: (s * contexts + c) * parts + t
    places = [
        (s, c, t) for s in range(sections) for c in range(contexts) for t in range(parts)
    ]
    everyone = [[number(*place) for place in places]]
    token_of = lambda s, c, t: c * parts + t % half_parts + half_parts * s
    batch_groups = device_groups(mesh_sizes, lambda s, c, t: t // half_parts, token_of)
    side_groups = device_groups(mesh_sizes, lambda s, c, t: c % 2, lambda s, c, t: (s, c, t))
    side_out_groups = device_groups(mesh_sizes, lambda s, c, t: c % 2, lambda s, c, t: (c, t, s))
    all_out_groups = device_groups(mesh_sizes, lambda s, c, t: 0, lambda s, c, t: (c, t, s))

    crossing = [
        (number(s, c, t), number(s, c, (t + half_parts) % parts))
        for s, c, t in places
        if t // half_parts == s
    ]

    def to_batch(value):
        mine = lax.dynamic_index_in_dim(value, batch, 0, keepdims=False)
        other = lax.dynamic_index_in_dim(value, 1 - batch, 0, keepdims=False)
        moved = lax.ppermute(other, ALL_AXES, crossing)
        return jnp.where(section == batch, mine, moved)

    def to_home(value, layer):
        stay = [
            (number(s, c, t), number(layer, c, t)) for s, c, t in places if t // half_parts == s
        ]
        cross = [
            (number(s, c, t), number(layer, c, (t + half_parts) % parts))
            for s, c, t in places
            if t // half_parts != s
        ]
        return (lax.ppermute(value, ALL_AXES, stay), lax.ppermute(value, ALL_AXES, cross))

    def at_home(first_pair, second_pair):
        near = jnp.where(leading, first_pair[0], second_pair[0])
        far = jnp.where(leading, first_pair[1], second_pair[1])
        upper = batch == 0
        return jnp.stack([jnp.where(upper, near, far), jnp.where(upper, far, near)])[None]

    def swap_side(value):
        return lax.ppermute(value, "ctx", [(c, c ^ 1) for c in range(contexts)])

    def swap_section(value):
        return lax.ppermute(value, "section", [(0, 1), (1, 0)])

    def gather(value, groups):
        return lax.all_gather(value, ALL_AXES, axis=0, tiled=True, axis_index_groups=groups)

    def own_part(value, axis, size):
        return lax.dynamic_slice_in_dim(value, ctx * size, size, axis)

    rows_in = to_batch(inputs)
    grad_in = to_batch(cotangent)

    head_part = own_part(wqkv[0], 1, heads // (parts * contexts)).reshape(-1, model_width)
    out_part = own_part(wo[0], 0, HD)
    gate_piece = own_part(wgu[0, 0], 0, units)
    up_piece = own_part(wgu[0, 1], 0, units)
    down_piece = own_part(wd[0], 0, units)
    w_heads = gather(head_part, everyone).reshape(2, -1, model_width)
    w_outs = gather(out_part, everyone).reshape(2, -1, model_width)
    w_gates = gather(gate_piece, side_groups).reshape(2, -1, model_width)
    w_ups = gather(up_piece, side_groups).reshape(2, -1, model_width)
    w_downs = gather(down_piece, side_groups).reshape(2, -1, model_width)
    gains = jnp.concatenate([gain1, gain2], axis=0).astype(jnp.float32)
    other_gains = swap_section(gains)
    gain_sets = (jnp.where(leading, gains, other_gains), jnp.where(leading, other_gains, gains))

    seq_lengths = lax.dynamic_index_in_dim(lengths, batch, 0, keepdims=False)
    ends = jnp.cumsum(seq_lengths).astype(jnp.int32)
    token_index = (ctx * parts + tp % half_parts + half_parts * section) * rows + jnp.arange(
        rows, dtype=jnp.int32
    )
    before = (ends[None, :] <= token_index[:, None]).astype(jnp.int32)
    position = token_index - jnp.sum(before * seq_lengths[None, :], axis=1)
    half_width = HD // 2
    frequency = jnp.exp(
        -jnp.log(10000.0) * jnp.arange(half_width, dtype=jnp.float32) / half_width
    )
    angles = position.astype(jnp.float32)[None, :] * frequency[:, None]
    cosine, sine_part = jnp.cos(angles), jnp.sin(angles)

    def low(value):
        return value.astype(jnp.bfloat16)

    def layer_forward(whole_rows, first_values, layer):
        gain_first, gain_second = gain_sets[layer][0], gain_sets[layer][1]
        scale_first = lax.rsqrt(jnp.mean(whole_rows * whole_rows, axis=-1, keepdims=True) + EPSILON)
        normed = low(whole_rows * scale_first * gain_first)
        projected = dot(w_heads[layer], normed, 1, 1).reshape(heads, 3, HD, rows)
        query = rope_pairs(projected[:, 0], cosine, sine_part) * HD ** (-0.5)
        key = rope_pairs(projected[:, 1], cosine, sine_part)
        value = projected[:, 2]
        if first_values is not None:
            value = 0.5 * value + 0.5 * first_values.astype(jnp.float32)
        mixed = low(value)
        qkv = exchange(jnp.concatenate([low(query), low(key), mixed], axis=1), batch_groups)
        out, lse = attention_forward(ends, qkv)
        attended = exchange(out, batch_groups).reshape(heads * HD, rows)
        hidden = whole_rows + dot(attended, w_outs[layer], 0, 0)
        scale_second = lax.rsqrt(jnp.mean(hidden * hidden, axis=-1, keepdims=True) + EPSILON)
        normed_second = low(hidden * scale_second * gain_second)
        ffn_rows = (normed_second, swap_side(normed_second))
        gates = [dot(part, w_gates[layer], 1, 1) for part in ffn_rows]
        ups = [dot(part, w_ups[layer], 1, 1) for part in ffn_rows]
        activated = [low(jax.nn.silu(gate) * up) for gate, up in zip(gates, ups)]
        far_down = swap_side(low(dot(activated[1], w_downs[layer], 1, 0)))
        layer_out = low(
            hidden + (dot(activated[0], w_downs[layer], 1, 0) + far_down.astype(jnp.float32))
        )
        saved = (
            whole_rows, scale_first, normed, qkv, out, lse, attended, hidden, scale_second,
            ffn_rows, gates, ups, activated,
        )
        return layer_out, mixed, saved

    def norm_back(whole_rows, scale_rows, gain, grad_normed, grad_rest):
        unit_rows = whole_rows * scale_rows
        scaled = grad_normed * gain
        grad_gain = jnp.sum(grad_normed * unit_rows, axis=0)
        grad_whole = grad_rest + scale_rows * (
            scaled - unit_rows * jnp.mean(scaled * unit_rows, axis=-1, keepdims=True)
        )
        return grad_gain, grad_whole

    def reduce_weight(partial_sum, groups):
        mine = lax.psum_scatter(
            low(partial_sum), ALL_AXES, scatter_dimension=0, tiled=True, axis_index_groups=groups
        )
        return lax.all_gather(mine, "ctx", axis=0, tiled=False)

    def layer_backward(grad_rows, extra_values, saved, layer):
        (
            whole_rows, scale_first, normed, qkv, out, lse, attended, hidden, scale_second,
            ffn_rows, gates, ups, activated,
        ) = saved
        gain_first, gain_second = gain_sets[layer][0], gain_sets[layer][1]
        grad_down = low(grad_rows)
        grad_downs = (grad_down, swap_side(grad_down))
        grad_gates, grad_ups = [], []
        for part, gate, up in zip(grad_downs, gates, ups):
            grad_act = dot(part, w_downs[layer], 1, 1)
            sigmoid_gate = jax.nn.sigmoid(gate)
            grad_gates.append(
                low(grad_act * up * sigmoid_gate * (1.0 + gate * (1.0 - sigmoid_gate)))
            )
            grad_ups.append(low(grad_act * gate * sigmoid_gate))
        back = [
            dot(grad_gate, w_gates[layer], 1, 0) + dot(grad_up, w_ups[layer], 1, 0)
            for grad_gate, grad_up in zip(grad_gates, grad_ups)
        ]
        far_back = swap_side(low(back[1]))
        grad_gain2, grad_hidden = norm_back(
            hidden, scale_second, gain_second, back[0] + far_back.astype(jnp.float32),
            grad_rows.astype(jnp.float32),
        )
        grad_branch = low(grad_hidden)
        grad_heads = low(dot(w_outs[layer], grad_branch, 1, 1)).reshape(heads, HD, rows)
        grad_heads = exchange(grad_heads, batch_groups)
        join = lambda pair: jnp.concatenate(pair, axis=0)
        all_rows, all_down = join(ffn_rows), join(grad_downs)
        grad_wd = reduce_weight(dot(join(activated), all_down, 0, 0), side_out_groups)
        grad_wgate = reduce_weight(dot(join(grad_gates), all_rows, 0, 0), side_out_groups)
        grad_wup = reduce_weight(dot(join(grad_ups), all_rows, 0, 0), side_out_groups)
        grad_wo = reduce_weight(dot(attended, grad_branch, 1, 0), all_out_groups)
        grad_qkv = attention_backward(ends, qkv, out, grad_heads, lse)
        grad_qkv = exchange(grad_qkv, batch_groups).reshape(heads, 3, HD, rows)
        grad_query = rope_pairs(grad_qkv[:, 0].astype(jnp.float32), cosine, -sine_part)
        grad_key = rope_pairs(grad_qkv[:, 1].astype(jnp.float32), cosine, -sine_part)
        grad_value = grad_qkv[:, 2].astype(jnp.float32)
        send_values = None
        if extra_values is None:
            grad_value = 0.5 * grad_value
            send_values = low(grad_value)
        else:
            grad_value = grad_value + extra_values.astype(jnp.float32)
        grad_projected = jnp.concatenate(
            [low(grad_query), low(grad_key), low(grad_value)], axis=1
        ).reshape(3 * heads * HD, rows)
        grad_normed = dot(grad_projected, w_heads[layer], 0, 0)
        grad_wqkv = reduce_weight(dot(grad_projected, normed, 1, 0), all_out_groups)
        grad_gain1, grad_whole = norm_back(
            whole_rows, scale_first, gain_first, grad_normed, grad_hidden
        )
        return grad_whole, send_values, (grad_gain1, grad_gain2), (
            grad_wqkv, grad_wo, grad_wgate, grad_wup, grad_wd,
        )

    first_out, first_values, first_saved = layer_forward(rows_in.astype(jnp.float32), None, 0)
    first_home = to_home(first_out, 0)
    second_out, _, second_saved = layer_forward(first_out.astype(jnp.float32), first_values, 1)
    second_home = to_home(second_out, 1)
    second_grad, send_values, second_gains, second_grads = layer_backward(
        grad_in, None, second_saved, 1
    )
    second_grad = low(second_grad)
    second_grad_home = to_home(second_grad, 1)
    first_grad, _, first_gains, first_grads = layer_backward(
        second_grad, send_values, first_saved, 0
    )
    first_grad_home = to_home(low(first_grad), 0)

    gain_total = lax.psum(
        jnp.stack([first_gains[0], first_gains[1], second_gains[0], second_gains[1]]), ALL_AXES
    )
    gain_total = jnp.where(leading, gain_total[:2], gain_total[2:])

    def finish(first_half, second_half):
        mine = jnp.where(leading, first_half, second_half)
        moved = swap_section(jnp.where(leading, second_half, first_half))
        lower = jnp.where(leading, mine, moved)
        upper = jnp.where(leading, moved, mine)
        return jnp.concatenate([lower, upper], axis=1).astype(jnp.float32)

    grad_wqkv, grad_wo, grad_wgate, grad_wup, grad_wd = [
        finish(first, second) for first, second in zip(first_grads, second_grads)
    ]
    grad_wqkv = grad_wqkv.reshape(contexts, 3, HD, model_width).transpose(1, 0, 2, 3)
    return (
        at_home(first_home, second_home),
        at_home(first_grad_home, second_grad_home).astype(jnp.float32),
        gain_total[0:1],
        grad_wqkv[None],
        grad_wo.reshape(wo.shape),
        gain_total[1:2],
        jnp.stack([grad_wgate.reshape(wd.shape[1:]), grad_wup.reshape(wd.shape[1:])])[None],
        grad_wd.reshape(wd.shape),
    )


def body(mesh_sizes, *arguments):
    inputs, _, _, _, wqkv = arguments[:5]
    sections, contexts, parts = mesh_sizes
    own_heads, own_units = wqkv.shape[2], arguments[7].shape[2]
    fits = (
        sections == 2
        and inputs.shape[0] == 2
        and contexts % 2 == 0
        and parts % 2 == 0
        and own_heads == contexts
        and own_units % (16 * contexts) == 0
        and inputs.shape[1] % 128 == 0
    )
    if fits:
        return split_body(mesh_sizes, *arguments)
    return general_body(*arguments)


def solution(mesh):
    placed = (
        P(None, ("ctx", "tp"), None),
        P(None, ("ctx", "tp"), None),
        P(),
        P("section", None),
        P("section", None, "tp", None, None),
        P("section", "tp", None),
        P("section", None),
        P("section", None, "tp", None),
        P("section", "tp", None),
    )
    mesh_sizes = tuple(mesh.shape[axis] for axis in ALL_AXES)
    return jax.shard_map(
        functools.partial(body, mesh_sizes),
        mesh=mesh,
        in_specs=placed,
        out_specs=(
            P("section", None, ("ctx", "tp"), None),
            P("section", None, ("ctx", "tp"), None),
            P("section", None),
            P("section", None, "tp", None, None),
            P("section", "tp", None),
            P("section", None),
            P("section", None, "tp", None),
            P("section", "tp", None),
        ),
        check_vma=False,
    )
```

```python
import functools

import jax
import jax.numpy as jnp
from jax import lax
from jax.experimental import pallas as pl
from jax.experimental.pallas import tpu as pltpu
from jax.sharding import PartitionSpec as P

HD = 64
EPSILON = 1e-06
MASKED = -1e30
ALL_AXES = ("section", "ctx", "tp")
CHUNK = 2
LIGHT = pl.CostEstimate(flops=1, bytes_accessed=1, transcendentals=0)
VMEM_LIMIT = 40 * 1024 * 1024


def shifted(block, axis, distance):
    devices = range(lax.axis_size(axis))
    route = [(i - distance, i) for i in devices if i - distance in devices]
    return lax.ppermute(block, axis, route)


def rope_parts(position):
    half_width = HD // 2
    frequency = jnp.exp(-jnp.log(10000.0) * jnp.arange(half_width, dtype=jnp.float32) / half_width)
    angles = position.astype(jnp.float32)[:, None] * frequency[None, :]
    return (jnp.cos(angles), jnp.sin(angles))


def rotate(vectors, cosine, sine_part):
    half_width = HD // 2
    leading_half = vectors[..., :half_width]
    trailing_half = vectors[..., half_width:]
    cosine = cosine[:, None, :]
    sine_part = sine_part[:, None, :]
    return jnp.concatenate(
        [
            leading_half * cosine - trailing_half * sine_part,
            trailing_half * cosine + leading_half * sine_part,
        ],
        axis=-1,
    )


def rotate_back(vectors, cosine, sine_part):
    half_width = HD // 2
    leading_half = vectors[..., :half_width]
    trailing_half = vectors[..., half_width:]
    cosine = cosine[:, None, :]
    sine_part = sine_part[:, None, :]
    return jnp.concatenate(
        [
            leading_half * cosine + trailing_half * sine_part,
            trailing_half * cosine - leading_half * sine_part,
        ],
        axis=-1,
    )


def inner_rows(left, right):
    return lax.dot_general(
        left, right, (((0,), (0,)), ((), ())), preferred_element_type=jnp.float32
    )


def outer_cols(left, right):
    return lax.dot_general(
        left, right, (((1,), (1,)), ((), ())), preferred_element_type=jnp.float32
    )


def spread(row_block):
    return lax.all_gather(row_block, "tp", axis=0, tiled=True)


def collect(partial_value):
    return lax.psum_scatter(
        partial_value.astype(jnp.bfloat16), "tp", scatter_dimension=0, tiled=True
    ).astype(jnp.float32)


def fetch_keys(key_value):
    return lax.all_gather(key_value, "ctx", axis=0, tiled=True)


def query_bounds(seq_lengths, block_first, row_count):
    token_index = block_first + jnp.arange(row_count, dtype=jnp.int32)
    doc_ends = jnp.cumsum(seq_lengths)
    before = (doc_ends[None, :] <= token_index[:, None]).astype(jnp.int32)
    doc_start = jnp.sum(before * seq_lengths[None, :], axis=1)
    return (token_index, doc_start)


def block_scores(query_heads, pair_block, block_first, token_index, doc_start, head_width):
    row_count = pair_block.shape[0]
    key_heads = pair_block[:, :head_width].reshape(row_count, head_width // HD, HD)
    value_heads = pair_block[:, head_width:].reshape(row_count, head_width // HD, HD)
    scores = jnp.einsum(
        "qhd,khd->hqk", query_heads, key_heads, preferred_element_type=jnp.float32
    ) * HD ** (-0.5)
    key_index = block_first + jnp.arange(row_count, dtype=jnp.int32)
    allowed = (key_index[None, :] >= doc_start[:, None]) & (
        key_index[None, :] <= token_index[:, None]
    )
    return (scores, allowed[None], key_heads, value_heads)


def split_blocks(pairs_all, row_count):
    blocks = pairs_all.reshape(-1, row_count, pairs_all.shape[1])
    block_starts = jnp.arange(blocks.shape[0], dtype=jnp.int32) * row_count
    return (blocks, block_starts)


def attend(query_heads, pairs_all, token_index, doc_start, head_width):
    row_count = query_heads.shape[0]
    head_count = head_width // HD
    blocks, block_starts = split_blocks(pairs_all, row_count)
    last_query = token_index[row_count - 1]
    first_query = doc_start[0]

    def rowmax_live(carried, block_parts):
        running_top, running_sum = carried
        scores, allowed, unused_keys, unused_values = block_scores(
            query_heads, block_parts[0], block_parts[1], token_index, doc_start, head_width
        )
        masked = jnp.where(allowed, scores, -1e30)
        new_top = jnp.maximum(running_top, jnp.max(masked, axis=-1))
        running_sum = running_sum * jnp.exp(running_top - new_top) + jnp.sum(
            jnp.where(allowed, jnp.exp(masked - new_top[..., None]), 0.0), axis=-1
        )
        return (new_top, running_sum)

    def rowmax_step(carried, block_parts):
        live = (block_parts[1] <= last_query) & (block_parts[1] + row_count > first_query)
        return (
            lax.cond(live, lambda held: rowmax_live(held, block_parts), lambda held: held, carried),
            None,
        )

    initial = (
        jnp.full((head_count, row_count), -1e30, jnp.float32),
        jnp.zeros((head_count, row_count), jnp.float32),
    )
    (running_top, running_sum), unused = lax.scan(rowmax_step, initial, (blocks, block_starts))
    log_total = running_top + jnp.log(running_sum)

    def output_live(accumulated, block_parts):
        scores, allowed, unused_keys, value_heads = block_scores(
            query_heads, block_parts[0], block_parts[1], token_index, doc_start, head_width
        )
        soft_weights = jnp.where(allowed, jnp.exp(scores - log_total[..., None]), 0.0).astype(
            jnp.bfloat16
        )
        return accumulated + jnp.einsum(
            "hqk,khd->qhd", soft_weights, value_heads, preferred_element_type=jnp.float32
        )

    def output_step(accumulated, block_parts):
        live = (block_parts[1] <= last_query) & (block_parts[1] + row_count > first_query)
        return (
            lax.cond(
                live, lambda held: output_live(held, block_parts), lambda held: held, accumulated
            ),
            None,
        )

    accumulated, unused = lax.scan(
        output_step, jnp.zeros((row_count, head_count, HD), jnp.float32), (blocks, block_starts)
    )
    return (accumulated, log_total)


def attend_back(
    query_heads, pairs_all, token_index, doc_start, head_width, log_total, accumulated, grad_heads
):
    row_count = query_heads.shape[0]
    head_count = head_width // HD
    blocks, block_starts = split_blocks(pairs_all, row_count)
    last_query = token_index[row_count - 1]
    first_query = doc_start[0]
    rowdot = jnp.sum(grad_heads.astype(jnp.float32) * accumulated, axis=-1).T

    def grad_live(grad_acc, block_parts):
        scores, allowed, key_heads, value_heads = block_scores(
            query_heads, block_parts[0], block_parts[1], token_index, doc_start, head_width
        )
        soft_weights = jnp.where(allowed, jnp.exp(scores - log_total[..., None]), 0.0)
        grad_soft = jnp.einsum(
            "qhd,khd->hqk", grad_heads, value_heads, preferred_element_type=jnp.float32
        )
        grad_scores = (soft_weights * (grad_soft - rowdot[..., None])).astype(jnp.bfloat16)
        grad_acc = grad_acc + jnp.einsum(
            "hqk,khd->qhd", grad_scores, key_heads, preferred_element_type=jnp.float32
        )
        grad_keys = jnp.einsum(
            "hqk,qhd->khd", grad_scores, query_heads, preferred_element_type=jnp.float32
        ) * HD ** (-0.5)
        grad_values = jnp.einsum(
            "hqk,qhd->khd",
            soft_weights.astype(jnp.bfloat16),
            grad_heads,
            preferred_element_type=jnp.float32,
        )
        return (grad_acc, (grad_keys, grad_values))

    def grad_skip(grad_acc):
        empty = jnp.zeros((row_count, head_count, HD), jnp.float32)
        return (grad_acc, (empty, empty))

    def grad_step(grad_acc, block_parts):
        live = (block_parts[1] <= last_query) & (block_parts[1] + row_count > first_query)
        return lax.cond(live, lambda held: grad_live(held, block_parts), grad_skip, grad_acc)

    grad_query, (grad_keys, grad_values) = lax.scan(
        grad_step, jnp.zeros((row_count, head_count, HD), jnp.float32), (blocks, block_starts)
    )
    grad_query = grad_query * HD ** (-0.5)
    grad_pairs = jnp.concatenate(
        [grad_keys.reshape(-1, head_width), grad_values.reshape(-1, head_width)], axis=1
    )
    return (grad_query, grad_pairs)


def norm_back(whole_rows, scale_rows, gain, grad_normed, grad_rest):
    unit_rows = whole_rows * scale_rows
    scaled = grad_normed * gain.astype(jnp.float32)
    grad_gain = jnp.sum(grad_normed * unit_rows, axis=0)
    grad_whole = grad_rest + scale_rows * (
        scaled - unit_rows * jnp.mean(scaled * unit_rows, axis=-1, keepdims=True)
    )
    return (grad_gain, grad_whole)


def layer_forward(row_block, first_values, value_mix, weights, seq_lengths):
    gain_first, w_qkv, w_out, gain_second, w_gateup, w_down = weights
    head_count = w_qkv.shape[1]
    head_width = head_count * HD
    model_width = row_block.shape[1]
    whole_rows = row_block.astype(jnp.float32)
    scale_first = lax.rsqrt(jnp.mean(whole_rows * whole_rows, axis=-1, keepdims=True) + EPSILON)
    normed = (whole_rows * scale_first * gain_first.astype(jnp.float32)).astype(jnp.bfloat16)
    normed_all = spread(normed)
    row_count = normed_all.shape[0]
    projected = outer_cols(normed_all, w_qkv.reshape(3 * head_width, model_width))
    token_index, doc_start = query_bounds(seq_lengths, lax.axis_index("ctx") * row_count, row_count)
    cosine, sine_part = rope_parts(token_index - doc_start)
    query_heads = rotate(
        projected[:, :head_width].reshape(row_count, head_count, HD), cosine, sine_part
    ).astype(jnp.bfloat16)
    key_heads = rotate(
        projected[:, head_width : 2 * head_width].reshape(row_count, head_count, HD),
        cosine,
        sine_part,
    ).astype(jnp.bfloat16)
    mixed = (
        (1.0 - value_mix) * projected[:, 2 * head_width :]
        + value_mix * first_values.astype(jnp.float32)
    ).astype(jnp.bfloat16)
    key_value = jnp.concatenate([key_heads.reshape(row_count, head_width), mixed], axis=1)
    pairs_all = fetch_keys(key_value)
    accumulated, log_total = attend(query_heads, pairs_all, token_index, doc_start, head_width)
    attended = accumulated.reshape(row_count, head_width).astype(jnp.bfloat16)
    hidden = whole_rows + collect(jnp.dot(attended, w_out, preferred_element_type=jnp.float32))
    scale_second = lax.rsqrt(jnp.mean(hidden * hidden, axis=-1, keepdims=True) + EPSILON)
    normed_second = (hidden * scale_second * gain_second.astype(jnp.float32)).astype(jnp.bfloat16)
    ffn_rows = spread(normed_second)
    gate_up = outer_cols(ffn_rows, w_gateup.reshape(-1, model_width))
    unit_count = gate_up.shape[1] // 2
    gate_part = gate_up[:, :unit_count]
    up_part = gate_up[:, unit_count:]
    activated = (jax.nn.silu(gate_part) * up_part).astype(jnp.bfloat16)
    down_part = jnp.dot(activated, w_down, preferred_element_type=jnp.float32)
    branch_out = collect(down_part)
    layer_out = (hidden + branch_out).astype(jnp.bfloat16)
    saved = (
        whole_rows,
        scale_first,
        normed_all,
        query_heads,
        pairs_all,
        token_index,
        doc_start,
        cosine,
        sine_part,
        log_total,
        accumulated,
        attended,
        hidden,
        scale_second,
        ffn_rows,
        gate_part,
        up_part,
        activated,
    )
    return (layer_out, mixed, pairs_all, saved)


def layer_backward(grad_rows, extra_values, value_mix, weights, saved):
    gain_first, w_qkv, w_out, gain_second, w_gateup, w_down = weights
    (
        whole_rows,
        scale_first,
        normed_all,
        query_heads,
        pairs_all,
        token_index,
        doc_start,
        cosine,
        sine_part,
        log_total,
        accumulated,
        attended,
        hidden,
        scale_second,
        ffn_rows,
        gate_part,
        up_part,
        activated,
    ) = saved
    model_width = whole_rows.shape[1]
    head_count = w_qkv.shape[1]
    head_width = head_count * HD
    row_count = normed_all.shape[0]
    grad_hidden = grad_rows.astype(jnp.float32)
    grad_down = spread(grad_rows)
    grad_wd = inner_rows(activated, grad_down)
    grad_act = outer_cols(grad_down, w_down)
    sigmoid_gate = jax.nn.sigmoid(gate_part)
    grad_gate = grad_act * up_part * sigmoid_gate * (1.0 + gate_part * (1.0 - sigmoid_gate))
    grad_up = grad_act * gate_part * sigmoid_gate
    grad_gate_up = jnp.concatenate([grad_gate, grad_up], axis=1).astype(jnp.bfloat16)
    grad_wgu = inner_rows(grad_gate_up, ffn_rows).reshape(w_gateup.shape)
    back_second = jnp.dot(
        grad_gate_up, w_gateup.reshape(-1, model_width), preferred_element_type=jnp.float32
    )
    grad_normed_second = collect(back_second)
    grad_gain2, grad_hidden = norm_back(
        hidden, scale_second, gain_second, grad_normed_second, grad_hidden
    )
    grad_branch_all = spread(grad_hidden.astype(jnp.bfloat16))
    grad_wo = inner_rows(attended, grad_branch_all)
    grad_heads = (
        outer_cols(grad_branch_all, w_out).astype(jnp.bfloat16).reshape(row_count, head_count, HD)
    )
    grad_query, grad_pairs_all = attend_back(
        query_heads,
        pairs_all,
        token_index,
        doc_start,
        head_width,
        log_total,
        accumulated,
        grad_heads,
    )
    grad_pairs = lax.psum_scatter(
        grad_pairs_all.astype(jnp.bfloat16), "ctx", scatter_dimension=0, tiled=True
    ).astype(jnp.float32)
    grad_mixed = grad_pairs[:, head_width:] + extra_values.astype(jnp.float32)
    grad_keys = rotate_back(
        grad_pairs[:, :head_width].reshape(row_count, head_count, HD), cosine, sine_part
    )
    grad_query = rotate_back(grad_query, cosine, sine_part)
    grad_projected = jnp.concatenate(
        [
            grad_query.reshape(row_count, head_width),
            grad_keys.reshape(row_count, head_width),
            (1.0 - value_mix) * grad_mixed,
        ],
        axis=1,
    ).astype(jnp.bfloat16)
    send_values = (value_mix * grad_mixed).astype(jnp.bfloat16)
    grad_wqkv = inner_rows(grad_projected, normed_all).reshape(w_qkv.shape)
    grad_normed = collect(
        jnp.dot(
            grad_projected,
            w_qkv.reshape(3 * head_width, model_width),
            preferred_element_type=jnp.float32,
        )
    )
    grad_gain1, grad_whole = norm_back(
        whole_rows, scale_first, gain_first, grad_normed, grad_hidden
    )
    return (
        grad_whole,
        send_values,
        (grad_gain1, grad_wqkv, grad_wo, grad_gain2, grad_wgu, grad_wd),
    )


def general_body(inputs, cotangent, lengths, gain1, wqkv, wo, gain2, wgu, wd):
    section_index = lax.axis_index("section")
    leading = section_index == 0
    value_mix = jnp.where(leading, 0.0, 0.5).astype(jnp.float32)
    micro_count = inputs.shape[0]
    local_rows = inputs.shape[1]
    model_width = inputs.shape[2]
    head_width = wqkv.shape[2] * HD
    row_count = local_rows * lax.axis_size("tp")
    gateup_use, down_use = (wgu[0], wd[0])
    weights = (gain1[0], wqkv[0], wo[0], gain2[0], gateup_use, down_use)
    recv_rows = jnp.zeros((local_rows, model_width), jnp.bfloat16)
    recv_values = jnp.zeros((row_count, head_width), jnp.bfloat16)
    states = []
    outputs = []
    for turn_index in range(micro_count + 1):
        own_rows = inputs[min(turn_index, micro_count - 1)]
        row_block = jnp.where(leading, own_rows, recv_rows)
        seq_lengths = jnp.where(
            leading, lengths[min(turn_index, micro_count - 1)], lengths[max(turn_index - 1, 0)]
        )
        layer_out, mixed, pairs_all, unused = layer_forward(
            row_block, recv_values, value_mix, weights, seq_lengths
        )
        kept_pairs = None
        states.append((row_block, recv_values, seq_lengths, kept_pairs))
        outputs.append(layer_out)
        if turn_index < micro_count:
            recv_rows, recv_values = shifted((layer_out, mixed), "section", 1)
    grad_rows_in = jnp.zeros((local_rows, model_width), jnp.bfloat16)
    grad_values_in = jnp.zeros((row_count, head_width), jnp.bfloat16)
    totals = None
    turn_grads = []
    for turn_index in range(micro_count + 1):
        row_block, first_values, seq_lengths, kept_pairs = states[micro_count - turn_index]
        if turn_index < micro_count:
            fed_grad = cotangent[micro_count - 1 - turn_index]
        else:
            fed_grad = jnp.zeros_like(cotangent[0])
        grad_out = jnp.where(leading, grad_rows_in, fed_grad)
        unused_out, unused_mixed, unused_pairs, saved = layer_forward(
            row_block, first_values, value_mix, weights, seq_lengths
        )
        grad_whole, send_values, grads = layer_backward(
            grad_out, grad_values_in, value_mix, weights, saved
        )
        totals = grads if totals is None else jax.tree.map(jnp.add, totals, grads)
        sent_rows = grad_whole.astype(jnp.bfloat16)
        turn_grads.append(jnp.where(leading, grad_whole, sent_rows.astype(jnp.float32)))
        if turn_index < micro_count:
            grad_rows_in, grad_values_in = shifted((sent_rows, send_values), "section", -1)
    grad_gain1, grad_wqkv, grad_wo, grad_gain2, grad_wgu, grad_wd = totals
    grad_wqkv, grad_wo, grad_wgu, grad_wd = (
        lax.psum(grad_wqkv.astype(jnp.bfloat16), "ctx").astype(jnp.float32),
        lax.psum(grad_wo.astype(jnp.bfloat16), "ctx").astype(jnp.float32),
        lax.psum(grad_wgu.astype(jnp.bfloat16), "ctx").astype(jnp.float32),
        lax.psum(grad_wd.astype(jnp.bfloat16), "ctx").astype(jnp.float32),
    )
    grad_gain1, grad_gain2 = lax.psum((grad_gain1, grad_gain2), ("ctx", "tp"))
    acts = jnp.stack(
        [
            jnp.where(leading, outputs[batch_index], outputs[batch_index + 1])
            for batch_index in range(micro_count)
        ]
    )[None]
    input_grads = jnp.stack(
        [
            jnp.where(
                leading,
                turn_grads[micro_count - batch_index],
                turn_grads[micro_count - 1 - batch_index],
            )
            for batch_index in range(micro_count)
        ]
    )[None]
    return (
        acts,
        input_grads,
        grad_gain1[None],
        grad_wqkv[None],
        grad_wo[None],
        grad_gain2[None],
        grad_wgu[None],
        grad_wd[None],
    )


def device_groups(mesh_sizes, key, order):
    sections, contexts, parts = mesh_sizes
    groups = {}
    for section in range(sections):
        for ctx in range(contexts):
            for tp in range(parts):
                place = (section, ctx, tp)
                number = (section * contexts + ctx) * parts + tp
                groups.setdefault(key(*place), []).append((order(*place), number))
    return [[number for _, number in sorted(members)] for _, members in sorted(groups.items())]


def exchange(value, groups):
    return lax.all_to_all(
        value, ALL_AXES, split_axis=0, concat_axis=0, tiled=True, axis_index_groups=groups
    )


def document_bounds(ends_ref, index):
    start = jnp.zeros_like(index)
    for entry in range(ends_ref.shape[0]):
        end = ends_ref[entry]
        start = jnp.where(index >= end, end, start)
    return start


def scalar_start(ends_ref, index):
    start = jnp.int32(0)
    for entry in range(ends_ref.shape[0]):
        start = jnp.where(index >= ends_ref[entry], ends_ref[entry], start)
    return start


def scalar_end(ends_ref, index):
    end = ends_ref[ends_ref.shape[0] - 1]
    for entry in range(ends_ref.shape[0] - 2, -1, -1):
        end = jnp.where(index < ends_ref[entry], ends_ref[entry], end)
    return end


def dot(left, right, left_dim, right_dim):
    return lax.dot_general(
        left, right, (((left_dim,), (right_dim,)), ((), ())), preferred_element_type=jnp.float32
    )


def fold_rows(value, combine):
    rows, width = value.shape
    return combine(value.reshape(rows // 8, 8, width), axis=0)


def attention_forward_kernel(ends_ref, qkv_ref, out_ref, lse_ref, keys_ref):
    block = pl.program_id(0)
    blocks, _, width = qkv_ref.shape
    span = CHUNK * width

    @pl.when(block == 0)
    def _():
        def turn(j, carry):
            keys_ref[j] = qkv_ref[j, HD : 2 * HD, :].T
            return carry

        lax.fori_loop(0, blocks, turn, 0)

    query = qkv_ref[block, 0:HD, :]
    first = block * width
    query_index = first + lax.broadcasted_iota(jnp.int32, (1, width), 1)
    start = document_bounds(ends_ref, query_index)
    last = block // CHUNK
    low = scalar_start(ends_ref, first) // span
    high_start = scalar_start(ends_ref, first + width - 1)
    middle = jnp.clip((high_start + span - 1) // span, low, last)

    def step(chunk, carry, masked):
        top, total, acc = carry
        parts, part_tops = [], []
        for entry in range(CHUNK):
            j = chunk * CHUNK + entry
            scores = dot(keys_ref[j], query, 1, 0)
            if masked:
                key_index = j * width + lax.broadcasted_iota(jnp.int32, (width, 1), 0)
                allowed = (key_index >= start) & (key_index <= query_index)
                scores = jnp.where(allowed, scores, MASKED)
            parts.append(scores)
            part_tops.append(fold_rows(scores, jnp.max))
        chunk_top = jnp.max(functools.reduce(jnp.maximum, part_tops), axis=0, keepdims=True)
        new_top = jnp.maximum(top, chunk_top)
        shrink = jnp.exp(top - new_top)
        total = total * shrink
        acc = acc * shrink
        for entry in range(CHUNK):
            weights = jnp.exp(parts[entry] - new_top)
            total = total + fold_rows(weights, jnp.sum)
            values = qkv_ref[chunk * CHUNK + entry, 2 * HD : 3 * HD, :]
            acc = acc + dot(values, weights.astype(jnp.bfloat16), 1, 0)
        return new_top, total, acc

    carry = (
        jnp.full((1, width), MASKED, jnp.float32),
        jnp.zeros((8, width), jnp.float32),
        jnp.zeros((HD, width), jnp.float32),
    )
    carry = lax.fori_loop(low, middle, functools.partial(step, masked=True), carry)
    carry = lax.fori_loop(middle, last, functools.partial(step, masked=False), carry)
    top, total, acc = step(last, carry, True)
    total = jnp.sum(total, axis=0, keepdims=True)
    out_ref[0] = (acc / total).astype(jnp.bfloat16)
    lse_ref[0] = top + jnp.log(total)


def attention_forward(ends, qkv):
    blocks, _, width = qkv.shape
    pairs = blocks * (blocks + 1) // 2 * width * width
    return pl.pallas_call(
        attention_forward_kernel,
        grid_spec=pltpu.PrefetchScalarGridSpec(
            num_scalar_prefetch=1,
            grid=(blocks,),
            in_specs=[pl.BlockSpec(qkv.shape, lambda i, ends_ref: (0, 0, 0))],
            out_specs=[
                pl.BlockSpec((1, HD, width), lambda i, ends_ref: (i, 0, 0)),
                pl.BlockSpec((1, 1, width), lambda i, ends_ref: (i, 0, 0)),
            ],
            scratch_shapes=[pltpu.VMEM((blocks, width, HD), jnp.bfloat16)],
        ),
        out_shape=[
            jax.ShapeDtypeStruct((blocks, HD, width), jnp.bfloat16),
            jax.ShapeDtypeStruct((blocks, 1, width), jnp.float32),
        ],
        compiler_params=pltpu.CompilerParams(vmem_limit_bytes=VMEM_LIMIT),
        cost_estimate=LIGHT,
        name="attention_forward",
    )(ends, qkv)


def attention_backward_kernel(
    ends_ref, qkv_ref, out_ref, grad_ref, lse_ref, result_ref, query_grad_ref, delta_ref
):
    block = pl.program_id(0)
    blocks, _, width = qkv_ref.shape
    span = CHUNK * width

    @pl.when(block == 0)
    def _():
        def turn(i, carry):
            delta_ref[i] = jnp.sum(
                grad_ref[i].astype(jnp.float32) * out_ref[i].astype(jnp.float32),
                axis=0,
                keepdims=True,
            )
            query_grad_ref[i] = jnp.zeros((HD, width), jnp.float32)
            return carry

        lax.fori_loop(0, blocks, turn, 0)

    first = block * width
    keys_t = qkv_ref[block, HD : 2 * HD, :]
    keys = keys_t.T
    values = qkv_ref[block, 2 * HD : 3 * HD, :].T
    key_index = first + lax.broadcasted_iota(jnp.int32, (width, 1), 0)
    near_end = scalar_end(ends_ref, first)
    far_end = scalar_end(ends_ref, first + width - 1)
    own_chunk = block // CHUNK
    stop = (far_end - 1) // span + 1
    middle = jnp.clip(near_end // span, own_chunk + 1, stop)

    def step(chunk, carry, masked):
        key_grad, value_grad = carry
        for entry in range(CHUNK):
            i = chunk * CHUNK + entry
            query = qkv_ref[i, 0:HD, :]
            grad = grad_ref[i]
            weights = jnp.exp(dot(keys, query, 1, 0) - lse_ref[i])
            if masked:
                query_index = i * width + lax.broadcasted_iota(jnp.int32, (1, width), 1)
                start = document_bounds(ends_ref, query_index)
                allowed = (key_index >= start) & (key_index <= query_index)
                weights = jnp.where(allowed, weights, 0.0)
            grad_weights = dot(values, grad, 1, 0)
            grad_scores = (weights * (grad_weights - delta_ref[i])).astype(jnp.bfloat16)
            value_grad = value_grad + dot(grad, weights.astype(jnp.bfloat16), 1, 1)
            key_grad = key_grad + dot(query, grad_scores, 1, 1)
            query_grad_ref[i] += dot(keys_t, grad_scores, 1, 0)
        return key_grad, value_grad

    empty = jnp.zeros((HD, width), jnp.float32)
    carry = step(own_chunk, (empty, empty), True)
    carry = lax.fori_loop(own_chunk + 1, middle, functools.partial(step, masked=False), carry)
    key_grad, value_grad = lax.fori_loop(middle, stop, functools.partial(step, masked=True), carry)
    result_ref[0, 0:HD] = (query_grad_ref[block] * HD ** (-0.5)).astype(jnp.bfloat16)
    result_ref[0, HD : 2 * HD] = key_grad.astype(jnp.bfloat16)
    result_ref[0, 2 * HD : 3 * HD] = value_grad.astype(jnp.bfloat16)


def attention_backward(ends, qkv, out, grad, lse):
    blocks, _, width = qkv.shape
    pairs = blocks * (blocks + 1) // 2 * width * width

    def whole(value):
        return pl.BlockSpec(value.shape, lambda i, ends_ref: (0, 0, 0))

    return pl.pallas_call(
        attention_backward_kernel,
        grid_spec=pltpu.PrefetchScalarGridSpec(
            num_scalar_prefetch=1,
            grid=(blocks,),
            in_specs=[whole(qkv), whole(out), whole(grad), whole(lse)],
            out_specs=pl.BlockSpec((1, 3 * HD, width), lambda i, ends_ref: (i, 0, 0)),
            scratch_shapes=[
                pltpu.VMEM((blocks, HD, width), jnp.float32),
                pltpu.VMEM((blocks, 1, width), jnp.float32),
            ],
        ),
        out_shape=jax.ShapeDtypeStruct(qkv.shape, jnp.bfloat16),
        compiler_params=pltpu.CompilerParams(vmem_limit_bytes=VMEM_LIMIT),
        cost_estimate=LIGHT,
        name="attention_backward",
    )(ends, qkv, out, grad, lse)


def rope_pair(leading_half, trailing_half, cosine, sine_part):
    return (
        leading_half * cosine - trailing_half * sine_part,
        trailing_half * cosine + leading_half * sine_part,
    )


def low(value):
    return value.astype(jnp.bfloat16)


def wide(value):
    return value.astype(jnp.float32)


def whole_block(value):
    zeros = (0,) * value.ndim
    return pl.BlockSpec(value.shape, lambda *_: zeros)


def feed_forward_kernel(rows_ref, gate_w_ref, up_w_ref, down_w_ref, gate_ref, up_ref, act_ref, sum_ref):
    rows = rows_ref[...]
    gate = dot(gate_w_ref[...], rows, 1, 1)
    up = dot(up_w_ref[...], rows, 1, 1)
    active = (gate * jax.nn.sigmoid(gate) * up).astype(jnp.bfloat16)
    gate_ref[...] = gate.astype(jnp.bfloat16)
    up_ref[...] = up.astype(jnp.bfloat16)
    act_ref[...] = active

    @pl.when(pl.program_id(0) == 0)
    def _():
        sum_ref[...] = jnp.zeros_like(sum_ref)

    sum_ref[...] += dot(active, down_w_ref[...], 0, 0)


def feed_forward(rows, w_gate, w_up, w_down, tile):
    units, width = w_gate.shape
    count = rows.shape[0]
    weight = pl.BlockSpec((tile, width), lambda i: (i, 0))
    column = pl.BlockSpec((tile, count), lambda i: (i, 0))
    hidden = jax.ShapeDtypeStruct((units, count), jnp.bfloat16)
    return pl.pallas_call(
        feed_forward_kernel,
        grid=(units // tile,),
        in_specs=[whole_block(rows), weight, weight, weight],
        out_specs=[column, column, column, pl.BlockSpec((count, width), lambda i: (0, 0))],
        out_shape=[hidden, hidden, hidden, jax.ShapeDtypeStruct((count, width), jnp.float32)],
        compiler_params=pltpu.CompilerParams(vmem_limit_bytes=VMEM_LIMIT),
        cost_estimate=LIGHT,
        name="feed_forward",
    )(rows, w_gate, w_up, w_down)


def feed_forward_back_kernel(
    grad_ref, gate_ref, up_ref, gate_w_ref, up_w_ref, down_w_ref, grad_gate_ref, grad_up_ref, sum_ref
):
    grad_act = dot(down_w_ref[...], grad_ref[...], 1, 1)
    gate = gate_ref[...].astype(jnp.float32)
    up = up_ref[...].astype(jnp.float32)
    sigmoid_gate = jax.nn.sigmoid(gate)
    grad_gate = (grad_act * up * sigmoid_gate * (1.0 + gate * (1.0 - sigmoid_gate))).astype(
        jnp.bfloat16
    )
    grad_up = (grad_act * gate * sigmoid_gate).astype(jnp.bfloat16)
    grad_gate_ref[...] = grad_gate
    grad_up_ref[...] = grad_up

    @pl.when(pl.program_id(0) == 0)
    def _():
        sum_ref[...] = jnp.zeros_like(sum_ref)

    sum_ref[...] += dot(grad_gate, gate_w_ref[...], 0, 0) + dot(grad_up, up_w_ref[...], 0, 0)


def feed_forward_back(grad, gate, up, w_gate, w_up, w_down, tile):
    units, width = w_gate.shape
    count = grad.shape[0]
    weight = pl.BlockSpec((tile, width), lambda i: (i, 0))
    column = pl.BlockSpec((tile, count), lambda i: (i, 0))
    hidden = jax.ShapeDtypeStruct((units, count), jnp.bfloat16)
    return pl.pallas_call(
        feed_forward_back_kernel,
        grid=(units // tile,),
        in_specs=[whole_block(grad), column, column, weight, weight, weight],
        out_specs=[column, column, pl.BlockSpec((count, width), lambda i: (0, 0))],
        out_shape=[hidden, hidden, jax.ShapeDtypeStruct((count, width), jnp.float32)],
        compiler_params=pltpu.CompilerParams(vmem_limit_bytes=VMEM_LIMIT),
        cost_estimate=LIGHT,
        name="feed_forward_back",
    )(grad, gate, up, w_gate, w_up, w_down)


def half_products_kernel(layout, sizes, has_addend, which_ref, *refs):
    refs = list(refs)
    out_ref = refs.pop()
    addend_ref = refs.pop() if has_addend else None
    totals = [
        sum(dot(refs[left][...], refs[right][...], 1, 0) for left, right in pairs)
        for pairs in layout
    ]
    for piece in range(out_ref.shape[0]):
        parts = [
            total[piece * size : (piece + 1) * size] for total, size in zip(totals, sizes)
        ]
        value = jnp.concatenate(parts, axis=0) if len(parts) > 1 else parts[0]
        if has_addend:
            value = value + addend_ref[piece].astype(jnp.float32)
        out_ref[piece] = value.astype(jnp.bfloat16)


def half_products(which, groups, pieces, per_step, addend=None):
    lefts, rights, layout = [], [], []
    for group in groups:
        for left, right in group:
            if not any(left is known for known in lefts):
                lefts.append(left)
            if not any(right is known for known in rights):
                rights.append(right)
    find = lambda known, value: next(i for i, entry in enumerate(known) if entry is value)
    for group in groups:
        layout.append(
            tuple((find(lefts, left), len(lefts) + find(rights, right)) for left, right in group)
        )
    sizes = tuple(group[0][0].shape[0] // (2 * pieces) for group in groups)
    width = rights[0].shape[1]
    steps = pieces // per_step
    out_spec = pl.BlockSpec((per_step, sum(sizes), width), lambda i, which_ref: (i, 0, 0))
    left_specs = [
        pl.BlockSpec(
            (left.shape[0] // (2 * steps), left.shape[1]),
            lambda i, which_ref: (which_ref[0] * steps + i, 0),
        )
        for left in lefts
    ]
    extra = [] if addend is None else [addend]
    work = sum(left.size // 2 for left, _ in sum(groups, ()))
    return pl.pallas_call(
        functools.partial(half_products_kernel, tuple(layout), sizes, addend is not None),
        grid_spec=pltpu.PrefetchScalarGridSpec(
            num_scalar_prefetch=1,
            grid=(steps,),
            in_specs=left_specs + [whole_block(right) for right in rights] + [out_spec] * len(extra),
            out_specs=out_spec,
        ),
        out_shape=jax.ShapeDtypeStruct((pieces, sum(sizes), width), jnp.bfloat16),
        compiler_params=pltpu.CompilerParams(vmem_limit_bytes=VMEM_LIMIT),
        cost_estimate=LIGHT,
        name="half_products",
    )(which.reshape(1).astype(jnp.int32), *lefts, *rights, *extra)


def together(*values):
    return lax.optimization_barrier(values)


def after(value, *others):
    return lax.optimization_barrier((value, *others))[0]


def split_body(mesh_sizes, inputs, cotangent, lengths, gain1, wqkv, wo, gain2, wgu, wd):
    sections, contexts, parts = mesh_sizes
    half_parts = parts // 2
    section = lax.axis_index("section")
    ctx = lax.axis_index("ctx")
    tp = lax.axis_index("tp")
    row_side, column_side = ctx // 2, ctx % 2
    leading = section == 0
    batch = tp // half_parts
    model_width = inputs.shape[2]
    rows = inputs.shape[1]
    heads = wqkv.shape[2] * parts
    unit_rows = wd.shape[1] // contexts // 2
    head_rows = 3 * HD // 2
    out_rows = HD // 2
    half_width = HD // 2
    tile = 4 * unit_rows
    number = lambda s, c, t: (s * contexts + c) * parts + t
    places = [
        (s, c, t) for s in range(sections) for c in range(contexts) for t in range(parts)
    ]
    everyone = [[number(*place) for place in places]]
    token_of = lambda s, c, t: c * parts + t % half_parts + half_parts * s
    batch_groups = device_groups(mesh_sizes, lambda s, c, t: t // half_parts, token_of)
    side_groups = device_groups(mesh_sizes, lambda s, c, t: c % 2, lambda s, c, t: (s, c, t))
    crossing = [
        (number(s, c, t), number(s, c, (t + half_parts) % parts))
        for s, c, t in places
        if t // half_parts == s
    ]

    def to_batch(value):
        mine = lax.dynamic_index_in_dim(value, batch, 0, keepdims=False)
        other = lax.dynamic_index_in_dim(value, 1 - batch, 0, keepdims=False)
        moved = lax.ppermute(other, ALL_AXES, crossing)
        return jnp.where(section == batch, mine, moved)

    def to_home(value, layer):
        stay = [
            (number(s, c, t), number(layer, c, t)) for s, c, t in places if t // half_parts == s
        ]
        cross = [
            (number(s, c, t), number(layer, c, (t + half_parts) % parts))
            for s, c, t in places
            if t // half_parts != s
        ]
        return (lax.ppermute(value, ALL_AXES, stay), lax.ppermute(value, ALL_AXES, cross))

    def at_home(first_pair, second_pair):
        near = jnp.where(leading, first_pair[0], second_pair[0])
        far = jnp.where(leading, first_pair[1], second_pair[1])
        upper = batch == 0
        return jnp.stack([jnp.where(upper, near, far), jnp.where(upper, far, near)])[None]

    def swap_side(value):
        return lax.ppermute(value, "ctx", [(c, c ^ 1) for c in range(contexts)])

    def swap_far(value):
        return lax.ppermute(value, "ctx", [(c, c ^ 2) for c in range(contexts)])

    def swap_near(value):
        return lax.ppermute(value, "tp", [(t, t ^ 1) for t in range(parts)])

    def swap_half(value):
        return lax.ppermute(value, "tp", [(t, (t + half_parts) % parts) for t in range(parts)])

    def swap_section(value):
        return lax.ppermute(value, "section", [(0, 1), (1, 0)])

    def all_to_all(value, axis):
        return lax.all_to_all(value, axis, split_axis=0, concat_axis=0, tiled=True)

    def copies(value, count):
        return jnp.broadcast_to(value[None], (count, *value.shape))

    def gather(value, groups):
        return lax.all_gather(value, ALL_AXES, axis=0, tiled=True, axis_index_groups=groups)

    def ordered(index, own, other):
        return jnp.where(index == 0, own, other), jnp.where(index == 0, other, own)

    def by_core(value, which):
        return lax.dynamic_index_in_dim(value, which, 0, keepdims=False)

    def spread_plane(piece, *others):
        middle = piece.shape[0] // 2
        line = after(all_to_all(copies(piece, parts), "tp"), *others)
        line_a, line_b = line[:, :middle], line[:, middle:]
        pair_a = jnp.stack(ordered(row_side, line_a, swap_far(line_a)))
        pair_b = jnp.stack(ordered(column_side, line_b, swap_side(line_b)))
        plane_a = jnp.stack(ordered(column_side, pair_a, swap_side(pair_a)), axis=1)
        plane_b = jnp.stack(ordered(row_side, pair_b, swap_far(pair_b)), axis=0)
        plane = jnp.concatenate([plane_a, plane_b], axis=3)
        return plane.reshape(contexts * parts * piece.shape[0], piece.shape[1]), line

    def own_halves(value, axis, size):
        part = lax.dynamic_slice_in_dim(value, ctx * size, size, axis)
        return part.reshape(2, -1, model_width)

    packed = jnp.concatenate(
        [
            own_halves(wqkv[0], 1, heads // (parts * contexts)),
            own_halves(wo[0], 0, HD),
            own_halves(wgu[0, 0], 0, 2 * unit_rows),
            own_halves(wgu[0, 1], 0, 2 * unit_rows),
            own_halves(wd[0], 0, 2 * unit_rows),
        ],
        axis=1,
    )
    kept = by_core(packed, section)
    passed = swap_section(by_core(packed, 1 - section))
    pieces = ordered(section, kept, passed)
    attention_rows = head_rows + out_rows

    def feed_forward_weights(piece):
        whole = gather(piece[attention_rows:], side_groups)
        whole = whole.reshape(2 * 2 * parts, 3, unit_rows, model_width)
        return [whole[:, entry].reshape(-1, model_width) for entry in range(3)]

    rows_in = to_batch(inputs)
    own_heads, line = spread_plane(pieces[0][:head_rows], rows_in)
    first_ffn = feed_forward_weights(after(pieces[0], line))
    first_heads = (own_heads, swap_section(own_heads))
    own_outs, _ = spread_plane(after(pieces[0], own_heads)[head_rows:attention_rows])
    first_outs = jnp.concatenate(ordered(section, own_outs, swap_section(own_outs)), axis=0)
    second = gather(pieces[1][:attention_rows], everyone)
    second = second.reshape(2, heads, attention_rows, model_width)
    second_heads = [second[half, :, :head_rows].reshape(-1, model_width) for half in range(2)]
    second_outs = second[:, :, head_rows:].reshape(-1, model_width)
    second_ffn = feed_forward_weights(pieces[1])
    w_heads = (first_heads, second_heads)
    w_outs = (first_outs, second_outs)
    w_ffn = (first_ffn, second_ffn)

    gains = wide(jnp.concatenate([gain1, gain2], axis=0))
    gain_sets = ordered(section, gains, swap_section(gains))

    seq_lengths = lax.dynamic_index_in_dim(lengths, batch, 0, keepdims=False)
    ends = jnp.cumsum(seq_lengths).astype(jnp.int32)
    token_index = token_of(section, ctx, tp) * rows + jnp.arange(rows, dtype=jnp.int32)
    before = (ends[None, :] <= token_index[:, None]).astype(jnp.int32)
    position = token_index - jnp.sum(before * seq_lengths[None, :], axis=1)
    frequency = jnp.exp(
        -jnp.log(10000.0) * jnp.arange(half_width, dtype=jnp.float32) / half_width
    )
    angles = position.astype(jnp.float32)[None, :] * frequency[:, None]
    cosine, sine_part = jnp.cos(angles), jnp.sin(angles)

    def head_halves(value):
        size = value.shape[1] // 2
        return value.reshape(heads, 2, size, rows).transpose(1, 0, 2, 3).reshape(2, -1, rows)

    def whole_heads(value):
        value = value.reshape(2, heads, -1, rows)
        return value.transpose(1, 0, 2, 3).reshape(heads, -1, rows)

    def nothing(value):
        return value

    def layer_forward(whole_rows, first_values, layer, beside):
        gain_first, gain_second = gain_sets[layer][0], gain_sets[layer][1]
        scale_first = lax.rsqrt(jnp.mean(whole_rows * whole_rows, axis=-1, keepdims=True) + EPSILON)
        normed = low(whole_rows * scale_first * gain_first)
        halves = [dot(weight, normed, 1, 1) for weight in w_heads[layer]]
        if layer == 0:
            halves = ordered(section, *halves)
        upper, lower = [half.reshape(heads, head_rows, rows) for half in halves]
        query = rope_pair(upper[:, :half_width], upper[:, half_width:HD], cosine, sine_part)
        key = rope_pair(upper[:, HD:], lower[:, :half_width], cosine, sine_part)
        value = lower[:, half_width:]
        if first_values is not None:
            value = 0.5 * value + 0.5 * wide(first_values)
        mixed = low(value)
        shrunk = [low(half * HD ** (-0.5)) for half in query]
        qkv = exchange(
            jnp.concatenate([*shrunk, low(key[0]), low(key[1]), mixed], axis=1), batch_groups
        )
        out, lse = attention_forward(ends, qkv)
        out = beside(out)
        attended = head_halves(exchange(out, batch_groups))
        hidden = whole_rows + dot(attended.reshape(-1, rows), w_outs[layer], 0, 0)
        scale_second = lax.rsqrt(jnp.mean(hidden * hidden, axis=-1, keepdims=True) + EPSILON)
        normed_second = low(hidden * scale_second * gain_second)
        far_rows = swap_side(normed_second)
        near = feed_forward(normed_second, *w_ffn[layer], tile)
        far = feed_forward(after(far_rows, near[3]), *w_ffn[layer], tile)
        far_down = swap_side(low(far[3]))
        layer_out = low(hidden + (near[3] + wide(far_down)))
        saved = (
            whole_rows, scale_first, normed, qkv, out, lse, attended, hidden, scale_second,
            (normed_second, far_rows), near[:3], far[:3],
        )
        return layer_out, mixed, saved

    def norm_back(whole_rows, scale_rows, gain, grad_normed, grad_rest):
        unit = whole_rows * scale_rows
        scaled = grad_normed * gain
        grad_gain = jnp.sum(grad_normed * unit, axis=0)
        grad_whole = grad_rest + scale_rows * (
            scaled - unit * jnp.mean(scaled * unit, axis=-1, keepdims=True)
        )
        return grad_gain, grad_whole

    def pick(value, index, axis):
        return lax.dynamic_index_in_dim(value, index, axis, keepdims=False)

    def parted(value, index, axis):
        return pick(value, index, axis), pick(value, 1 - index, axis)

    def moved_pair(pair, swap):
        return pair[0], swap(pair[1])

    def halve(value, index, swap, axis):
        return moved_pair(parted(value, index, axis), swap)

    def add(pair):
        return low(wide(pair[0]) + wide(pair[1]))

    def near_sum(value):
        return halve(value.reshape(2, half_parts, *value.shape[1:]), tp % 2, swap_near, 1)

    def far_sum(pair):
        return halve(add(pair), batch, swap_half, 0)

    def layer_backward(grad_rows, extra_values, saved, layer, in_first, in_second, in_third, in_fourth, in_fifth):
        (
            whole_rows, scale_first, normed, qkv, out, lse, attended, hidden, scale_second,
            ffn_rows, near, far,
        ) = saved
        gain_first, gain_second = gain_sets[layer][0], gain_sets[layer][1]
        grad_down = low(grad_rows)
        far_down = swap_side(grad_down)
        grad_gate, grad_up, near_back = feed_forward_back(grad_down, *near[:2], *w_ffn[layer], tile)
        far_down = in_first(after(far_down, near_back))
        far_gate, far_up, far_back = feed_forward_back(far_down, *far[:2], *w_ffn[layer], tile)
        far_back = swap_side(low(far_back))
        groups = (
            ((grad_gate, ffn_rows[0]), (far_gate, ffn_rows[1])),
            ((grad_up, ffn_rows[0]), (far_up, ffn_rows[1])),
            ((near[2], grad_down), (far[2], far_down)),
        )
        products = functools.partial(
            half_products, groups=groups, pieces=2 * parts, per_step=2
        )
        sent = products(1 - section)
        moved = swap_section(sent)
        far_back = in_second(after(far_back, sent))
        grad_gain2, grad_hidden = norm_back(
            hidden, scale_second, gain_second, near_back + wide(far_back), wide(grad_rows)
        )
        grad_branch = low(grad_hidden)
        grad_heads = whole_heads(low(dot(w_outs[layer], grad_branch, 1, 1)))
        grad_heads = exchange(grad_heads, batch_groups)
        rest = products(section, addend=moved)
        out_pair = (attended.reshape(-1, rows), grad_branch)
        grad_heads, rest = in_third(grad_heads, rest, out_pair)
        grad_qkv = attention_backward(ends, qkv, out, grad_heads, lse)
        grad_qkv = in_fourth(grad_qkv)
        grad_qkv = in_fifth(exchange(grad_qkv, batch_groups))
        grad_qkv = wide(grad_qkv)
        quarter = lambda entry: grad_qkv[:, entry * half_width : (entry + 1) * half_width]
        grad_query = rope_pair(quarter(0), quarter(1), cosine, -sine_part)
        grad_key = rope_pair(quarter(2), quarter(3), cosine, -sine_part)
        grad_value = grad_qkv[:, 2 * HD :]
        send_values = None
        if extra_values is None:
            grad_value = 0.5 * grad_value
            send_values = low(grad_value)
        else:
            grad_value = grad_value + wide(extra_values)
        upper = low(jnp.concatenate([*grad_query, grad_key[0]], axis=1))
        lower = low(jnp.concatenate([grad_key[1], grad_value], axis=1))
        grad_halves = jnp.stack([upper, lower]).reshape(2, -1, rows)
        return grad_halves, send_values, grad_hidden, out_pair, grad_gain2

    def input_grads_of(grad_halves, grad_hidden, saved, layer):
        whole_rows, scale_first = saved[:2]
        places_of = (section, 1 - section) if layer == 0 else (0, 1)
        grad_normed = sum(
            dot(by_core(grad_halves, place), weight, 0, 0)
            for place, weight in zip(places_of, w_heads[layer])
        )
        return norm_back(whole_rows, scale_first, gain_sets[layer][0], grad_normed, grad_hidden)

    def piece_sum(value, groups):
        return lax.psum_scatter(
            value, ALL_AXES, scatter_dimension=0, tiled=True, axis_index_groups=groups
        )

    line_groups = device_groups(
        mesh_sizes, lambda s, c, t: (s, c % 2), lambda s, c, t: (c, t)
    )
    plane_shape = (2, 2, parts)
    pending = {}

    first_out, first_values, first_saved = layer_forward(wide(rows_in), None, 0, nothing)
    first_home = to_home(first_out, 0)
    grad_in = to_batch(after(cotangent, first_out))

    def beside_second(value):
        value, pending["first_home"], pending["grad_in"] = together(value, first_home, grad_in)
        return value

    second_out, _, second_saved = layer_forward(
        wide(first_out), first_values, 1, beside_second
    )
    first_home, grad_in = pending["first_home"], pending["grad_in"]

    def second_third(value, rest, out_pair):
        value, rest = together(value, rest)
        rest = rest.reshape(-1, model_width)
        pending["second_rest"] = piece_sum(rest, line_groups)
        pending["second_home"] = to_home(after(second_out, value), 1)
        return value, rest

    def second_fourth(value):
        value, pending["second_home"] = together(value, pending["second_home"])
        return value

    grad_halves, send_values, grad_hidden, out_pair, second_gain2 = layer_backward(
        grad_in, None, second_saved, 1, nothing, nothing, second_third, second_fourth, nothing
    )
    second_gain1, second_grad = input_grads_of(grad_halves, grad_hidden, second_saved, 1)
    second_grad = low(second_grad)
    head_products = functools.partial(
        half_products,
        groups=(((grad_halves.reshape(-1, rows), second_saved[2]),), (out_pair,)),
        pieces=heads,
        per_step=4,
    )

    def first_first(value):
        value, sent = together(value, head_products(1 - section))
        pending["moved"] = swap_section(sent)
        return value

    def crossed(value):
        middle = value.shape[3] // 2
        return (
            parted(value[:, :, :, :middle], column_side, 1),
            parted(value[:, :, :, middle:], row_side, 0),
        )

    def first_second(value):
        head = head_products(section, addend=pending["moved"])
        head = parted(head.reshape(*plane_shape, -1, model_width), column_side, 1)
        value, head, _ = together(value, head, pending["second_rest"])
        pending["head"] = moved_pair(head, swap_side)
        pending["second_grad_home"] = to_home(after(second_grad, value), 1)
        return value

    def first_third(value, rest, out_pair):
        out_products = functools.partial(
            half_products, groups=((out_pair,),), pieces=heads, per_step=8
        )
        out_sum = out_products(section, addend=swap_section(out_products(1 - section)))
        rest = rest.reshape(2, parts, -1, model_width)
        rest_a = parted(rest[:, :-1], row_side, 0)
        rest_b = parted(rest[:, -1:], row_side, 0)
        out_sum = parted(out_sum.reshape(*plane_shape, -1, model_width), column_side, 1)
        value, rest_a, rest_b, out_sum = together(value, rest_a, rest_b, out_sum)
        pending["rest_a"] = moved_pair(rest_a, swap_far)
        pending["rest_b"] = rest_b
        pending["out"] = moved_pair(out_sum, swap_side)
        pending["second_rest"] = lax.all_gather(
            after(pending["second_rest"], value), "ctx", axis=0, tiled=False
        )
        return value, rest

    def first_fourth(value):
        value, rest_a, rest_b, out_sum, head, pending["second_grad_home"] = together(
            value, pending["rest_a"], pending["rest_b"], pending["out"], pending["head"],
            pending["second_grad_home"],
        )
        pending["rest_a"] = rest_a
        pending["rest_b"] = moved_pair(rest_b, swap_far)
        pending["out"] = halve(add(out_sum), row_side, swap_far, 0)
        pending["head"] = halve(add(head), row_side, swap_far, 0)
        return value

    def first_fifth(value):
        value, rest_a, rest_b, out_sum, head = together(
            value, pending["rest_a"], pending["rest_b"], pending["out"], pending["head"]
        )
        pending["out"] = add(out_sum)
        rest = jnp.concatenate([add(rest_a), add(rest_b)], axis=0)
        pending["rest"] = near_sum(rest)
        pending["head"] = near_sum(add(head))
        return value

    first_halves, _, first_hidden, _, first_gain2 = layer_backward(
        second_grad, send_values, first_saved, 0,
        first_first, first_second, first_third, first_fourth, first_fifth,
    )
    head_products = functools.partial(
        half_products,
        groups=(((first_halves.reshape(-1, rows), first_saved[2]),),),
        pieces=heads,
        per_step=4,
    )
    sent = head_products(1 - section)
    moved = swap_section(sent)
    first_gain1, first_grad = input_grads_of(
        after(first_halves, sent), first_hidden, first_saved, 0
    )
    head = head_products(section, addend=moved).reshape(*plane_shape, head_rows, model_width)
    head, first_grad = together(head, low(first_grad))
    head_a, head_b = crossed(head)
    gain_rows = jnp.stack([first_gain1, first_gain2, second_gain1, second_gain2])
    first_grad, gain_rows, head_a, head_b = together(first_grad, gain_rows, head_a, head_b)
    head_a = moved_pair(head_a, swap_side)
    head_b = moved_pair(head_b, swap_far)
    first_grad_home = to_home(first_grad, 0)
    head_a, head_b, rest, second_head = together(
        add(head_a), add(head_b), pending["rest"], pending["head"]
    )
    head_a = parted(head_a, row_side, 0)
    head_b = parted(head_b, column_side, 0)
    gain_rows, head_a, head_b, rest, second_head = together(
        gain_rows, head_a, head_b, rest, second_head
    )
    head_a = moved_pair(head_a, swap_far)
    head_b = moved_pair(head_b, swap_side)
    rest = far_sum(rest)
    second_head = far_sum(second_head)
    gain_sums = all_to_all(copies(gain_rows, len(places)), ALL_AXES)
    head_a, head_b, first_grad_home = together(head_a, head_b, first_grad_home)
    head = near_sum(jnp.concatenate([add(head_a), add(head_b), pending["out"]], axis=1))
    head, rest, second_head, gain_sums = together(head, rest, second_head, gain_sums)
    head = far_sum(head)
    rest = jnp.concatenate([add(rest), add(second_head)], axis=0)
    rest = all_to_all(copies(rest, contexts), "ctx")
    head, rest = together(head, rest)
    first_head = all_to_all(copies(add(head), contexts), "ctx")
    second_head = rest[:, 3 * unit_rows :]
    rest = rest[:, : 3 * unit_rows]
    first_grads = jnp.concatenate([rest, first_head], axis=1)
    second_grads = jnp.concatenate([pending["second_rest"], second_head], axis=1)
    second_home, second_grad_home = pending["second_home"], pending["second_grad_home"]
    gain_total = jnp.sum(gain_sums.reshape(len(places), 4, model_width), axis=0)
    gain_total = jnp.where(leading, gain_total[:2], gain_total[2:])

    def finish(first, second):
        mine = jnp.where(leading, first, second)
        moved = swap_section(jnp.where(leading, second, first))
        return ordered(section, mine, moved)

    def joined(halves, first, count):
        both = jnp.stack([half[:, first : first + count] for half in halves], axis=1)
        return wide(both).reshape(-1, model_width)

    grads = finish(first_grads, second_grads)
    grad_wgate, grad_wup, grad_wd = [
        joined(grads, entry * unit_rows, unit_rows) for entry in range(3)
    ]
    grad_wqkv = joined(grads, 3 * unit_rows, head_rows).reshape(contexts, 3, HD, model_width)
    grad_wo = joined(grads, 3 * unit_rows + head_rows, out_rows)
    return (
        at_home(first_home, second_home),
        wide(at_home(first_grad_home, second_grad_home)),
        gain_total[0:1],
        grad_wqkv.transpose(1, 0, 2, 3)[None],
        grad_wo[None],
        gain_total[1:2],
        jnp.stack([grad_wgate, grad_wup])[None],
        grad_wd[None],
    )


def body(mesh_sizes, *arguments):
    inputs, _, _, _, wqkv = arguments[:5]
    sections, contexts, parts = mesh_sizes
    own_heads, own_units = wqkv.shape[2], arguments[7].shape[2]
    fits = (
        sections == 2
        and inputs.shape[0] == 2
        and contexts == 4
        and parts % 2 == 0
        and own_heads == contexts
        and own_units % (16 * contexts) == 0
        and inputs.shape[1] % 128 == 0
    )
    if fits:
        return split_body(mesh_sizes, *arguments)
    return general_body(*arguments)


def solution(mesh):
    placed = (
        P(None, ("ctx", "tp"), None),
        P(None, ("ctx", "tp"), None),
        P(),
        P("section", None),
        P("section", None, "tp", None, None),
        P("section", "tp", None),
        P("section", None),
        P("section", None, "tp", None),
        P("section", "tp", None),
    )
    mesh_sizes = tuple(mesh.shape[axis] for axis in ALL_AXES)
    return jax.shard_map(
        functools.partial(body, mesh_sizes),
        mesh=mesh,
        in_specs=placed,
        out_specs=(
            P("section", None, ("ctx", "tp"), None),
            P("section", None, ("ctx", "tp"), None),
            P("section", None),
            P("section", None, "tp", None, None),
            P("section", "tp", None),
            P("section", None),
            P("section", None, "tp", None),
            P("section", "tp", None),
        ),
        check_vma=False,
    )
```

```python
import functools

import jax
import jax.numpy as jnp
from jax import lax
from jax.experimental import pallas as pl
from jax.experimental.pallas import tpu as pltpu
from jax.sharding import PartitionSpec as P

HD = 64
EPSILON = 1e-06
MASKED = -1e30
ALL_AXES = ("section", "ctx", "tp")
CHUNK = 2
ONES = 16
LOG_2 = 0.6931471805599453
LIGHT = pl.CostEstimate(flops=1, bytes_accessed=1, transcendentals=0)
VMEM_LIMIT = 40 * 1024 * 1024


def shifted(block, axis, distance):
    devices = range(lax.axis_size(axis))
    route = [(i - distance, i) for i in devices if i - distance in devices]
    return lax.ppermute(block, axis, route)


def rope_parts(position):
    half_width = HD // 2
    frequency = jnp.exp(-jnp.log(10000.0) * jnp.arange(half_width, dtype=jnp.float32) / half_width)
    angles = position.astype(jnp.float32)[:, None] * frequency[None, :]
    return (jnp.cos(angles), jnp.sin(angles))


def rotate(vectors, cosine, sine_part):
    half_width = HD // 2
    leading_half = vectors[..., :half_width]
    trailing_half = vectors[..., half_width:]
    cosine = cosine[:, None, :]
    sine_part = sine_part[:, None, :]
    return jnp.concatenate(
        [
            leading_half * cosine - trailing_half * sine_part,
            trailing_half * cosine + leading_half * sine_part,
        ],
        axis=-1,
    )


def rotate_back(vectors, cosine, sine_part):
    half_width = HD // 2
    leading_half = vectors[..., :half_width]
    trailing_half = vectors[..., half_width:]
    cosine = cosine[:, None, :]
    sine_part = sine_part[:, None, :]
    return jnp.concatenate(
        [
            leading_half * cosine + trailing_half * sine_part,
            trailing_half * cosine - leading_half * sine_part,
        ],
        axis=-1,
    )


def inner_rows(left, right):
    return lax.dot_general(
        left, right, (((0,), (0,)), ((), ())), preferred_element_type=jnp.float32
    )


def outer_cols(left, right):
    return lax.dot_general(
        left, right, (((1,), (1,)), ((), ())), preferred_element_type=jnp.float32
    )


def spread(row_block):
    return lax.all_gather(row_block, "tp", axis=0, tiled=True)


def collect(partial_value):
    return lax.psum_scatter(
        partial_value.astype(jnp.bfloat16), "tp", scatter_dimension=0, tiled=True
    ).astype(jnp.float32)


def fetch_keys(key_value):
    return lax.all_gather(key_value, "ctx", axis=0, tiled=True)


def query_bounds(seq_lengths, block_first, row_count):
    token_index = block_first + jnp.arange(row_count, dtype=jnp.int32)
    doc_ends = jnp.cumsum(seq_lengths)
    before = (doc_ends[None, :] <= token_index[:, None]).astype(jnp.int32)
    doc_start = jnp.sum(before * seq_lengths[None, :], axis=1)
    return (token_index, doc_start)


def block_scores(query_heads, pair_block, block_first, token_index, doc_start, head_width):
    row_count = pair_block.shape[0]
    key_heads = pair_block[:, :head_width].reshape(row_count, head_width // HD, HD)
    value_heads = pair_block[:, head_width:].reshape(row_count, head_width // HD, HD)
    scores = jnp.einsum(
        "qhd,khd->hqk", query_heads, key_heads, preferred_element_type=jnp.float32
    ) * HD ** (-0.5)
    key_index = block_first + jnp.arange(row_count, dtype=jnp.int32)
    allowed = (key_index[None, :] >= doc_start[:, None]) & (
        key_index[None, :] <= token_index[:, None]
    )
    return (scores, allowed[None], key_heads, value_heads)


def split_blocks(pairs_all, row_count):
    blocks = pairs_all.reshape(-1, row_count, pairs_all.shape[1])
    block_starts = jnp.arange(blocks.shape[0], dtype=jnp.int32) * row_count
    return (blocks, block_starts)


def attend(query_heads, pairs_all, token_index, doc_start, head_width):
    row_count = query_heads.shape[0]
    head_count = head_width // HD
    blocks, block_starts = split_blocks(pairs_all, row_count)
    last_query = token_index[row_count - 1]
    first_query = doc_start[0]

    def rowmax_live(carried, block_parts):
        running_top, running_sum = carried
        scores, allowed, unused_keys, unused_values = block_scores(
            query_heads, block_parts[0], block_parts[1], token_index, doc_start, head_width
        )
        masked = jnp.where(allowed, scores, -1e30)
        new_top = jnp.maximum(running_top, jnp.max(masked, axis=-1))
        running_sum = running_sum * jnp.exp(running_top - new_top) + jnp.sum(
            jnp.where(allowed, jnp.exp(masked - new_top[..., None]), 0.0), axis=-1
        )
        return (new_top, running_sum)

    def rowmax_step(carried, block_parts):
        live = (block_parts[1] <= last_query) & (block_parts[1] + row_count > first_query)
        return (
            lax.cond(live, lambda held: rowmax_live(held, block_parts), lambda held: held, carried),
            None,
        )

    initial = (
        jnp.full((head_count, row_count), -1e30, jnp.float32),
        jnp.zeros((head_count, row_count), jnp.float32),
    )
    (running_top, running_sum), unused = lax.scan(rowmax_step, initial, (blocks, block_starts))
    log_total = running_top + jnp.log(running_sum)

    def output_live(accumulated, block_parts):
        scores, allowed, unused_keys, value_heads = block_scores(
            query_heads, block_parts[0], block_parts[1], token_index, doc_start, head_width
        )
        soft_weights = jnp.where(allowed, jnp.exp(scores - log_total[..., None]), 0.0).astype(
            jnp.bfloat16
        )
        return accumulated + jnp.einsum(
            "hqk,khd->qhd", soft_weights, value_heads, preferred_element_type=jnp.float32
        )

    def output_step(accumulated, block_parts):
        live = (block_parts[1] <= last_query) & (block_parts[1] + row_count > first_query)
        return (
            lax.cond(
                live, lambda held: output_live(held, block_parts), lambda held: held, accumulated
            ),
            None,
        )

    accumulated, unused = lax.scan(
        output_step, jnp.zeros((row_count, head_count, HD), jnp.float32), (blocks, block_starts)
    )
    return (accumulated, log_total)


def attend_back(
    query_heads, pairs_all, token_index, doc_start, head_width, log_total, accumulated, grad_heads
):
    row_count = query_heads.shape[0]
    head_count = head_width // HD
    blocks, block_starts = split_blocks(pairs_all, row_count)
    last_query = token_index[row_count - 1]
    first_query = doc_start[0]
    rowdot = jnp.sum(grad_heads.astype(jnp.float32) * accumulated, axis=-1).T

    def grad_live(grad_acc, block_parts):
        scores, allowed, key_heads, value_heads = block_scores(
            query_heads, block_parts[0], block_parts[1], token_index, doc_start, head_width
        )
        soft_weights = jnp.where(allowed, jnp.exp(scores - log_total[..., None]), 0.0)
        grad_soft = jnp.einsum(
            "qhd,khd->hqk", grad_heads, value_heads, preferred_element_type=jnp.float32
        )
        grad_scores = (soft_weights * (grad_soft - rowdot[..., None])).astype(jnp.bfloat16)
        grad_acc = grad_acc + jnp.einsum(
            "hqk,khd->qhd", grad_scores, key_heads, preferred_element_type=jnp.float32
        )
        grad_keys = jnp.einsum(
            "hqk,qhd->khd", grad_scores, query_heads, preferred_element_type=jnp.float32
        ) * HD ** (-0.5)
        grad_values = jnp.einsum(
            "hqk,qhd->khd",
            soft_weights.astype(jnp.bfloat16),
            grad_heads,
            preferred_element_type=jnp.float32,
        )
        return (grad_acc, (grad_keys, grad_values))

    def grad_skip(grad_acc):
        empty = jnp.zeros((row_count, head_count, HD), jnp.float32)
        return (grad_acc, (empty, empty))

    def grad_step(grad_acc, block_parts):
        live = (block_parts[1] <= last_query) & (block_parts[1] + row_count > first_query)
        return lax.cond(live, lambda held: grad_live(held, block_parts), grad_skip, grad_acc)

    grad_query, (grad_keys, grad_values) = lax.scan(
        grad_step, jnp.zeros((row_count, head_count, HD), jnp.float32), (blocks, block_starts)
    )
    grad_query = grad_query * HD ** (-0.5)
    grad_pairs = jnp.concatenate(
        [grad_keys.reshape(-1, head_width), grad_values.reshape(-1, head_width)], axis=1
    )
    return (grad_query, grad_pairs)


def norm_back(whole_rows, scale_rows, gain, grad_normed, grad_rest):
    unit_rows = whole_rows * scale_rows
    scaled = grad_normed * gain.astype(jnp.float32)
    grad_gain = jnp.sum(grad_normed * unit_rows, axis=0)
    grad_whole = grad_rest + scale_rows * (
        scaled - unit_rows * jnp.mean(scaled * unit_rows, axis=-1, keepdims=True)
    )
    return (grad_gain, grad_whole)


def layer_forward(row_block, first_values, value_mix, weights, seq_lengths):
    gain_first, w_qkv, w_out, gain_second, w_gateup, w_down = weights
    head_count = w_qkv.shape[1]
    head_width = head_count * HD
    model_width = row_block.shape[1]
    whole_rows = row_block.astype(jnp.float32)
    scale_first = lax.rsqrt(jnp.mean(whole_rows * whole_rows, axis=-1, keepdims=True) + EPSILON)
    normed = (whole_rows * scale_first * gain_first.astype(jnp.float32)).astype(jnp.bfloat16)
    normed_all = spread(normed)
    row_count = normed_all.shape[0]
    projected = outer_cols(normed_all, w_qkv.reshape(3 * head_width, model_width))
    token_index, doc_start = query_bounds(seq_lengths, lax.axis_index("ctx") * row_count, row_count)
    cosine, sine_part = rope_parts(token_index - doc_start)
    query_heads = rotate(
        projected[:, :head_width].reshape(row_count, head_count, HD), cosine, sine_part
    ).astype(jnp.bfloat16)
    key_heads = rotate(
        projected[:, head_width : 2 * head_width].reshape(row_count, head_count, HD),
        cosine,
        sine_part,
    ).astype(jnp.bfloat16)
    mixed = (
        (1.0 - value_mix) * projected[:, 2 * head_width :]
        + value_mix * first_values.astype(jnp.float32)
    ).astype(jnp.bfloat16)
    key_value = jnp.concatenate([key_heads.reshape(row_count, head_width), mixed], axis=1)
    pairs_all = fetch_keys(key_value)
    accumulated, log_total = attend(query_heads, pairs_all, token_index, doc_start, head_width)
    attended = accumulated.reshape(row_count, head_width).astype(jnp.bfloat16)
    hidden = whole_rows + collect(jnp.dot(attended, w_out, preferred_element_type=jnp.float32))
    scale_second = lax.rsqrt(jnp.mean(hidden * hidden, axis=-1, keepdims=True) + EPSILON)
    normed_second = (hidden * scale_second * gain_second.astype(jnp.float32)).astype(jnp.bfloat16)
    ffn_rows = spread(normed_second)
    gate_up = outer_cols(ffn_rows, w_gateup.reshape(-1, model_width))
    unit_count = gate_up.shape[1] // 2
    gate_part = gate_up[:, :unit_count]
    up_part = gate_up[:, unit_count:]
    activated = (jax.nn.silu(gate_part) * up_part).astype(jnp.bfloat16)
    down_part = jnp.dot(activated, w_down, preferred_element_type=jnp.float32)
    branch_out = collect(down_part)
    layer_out = (hidden + branch_out).astype(jnp.bfloat16)
    saved = (
        whole_rows,
        scale_first,
        normed_all,
        query_heads,
        pairs_all,
        token_index,
        doc_start,
        cosine,
        sine_part,
        log_total,
        accumulated,
        attended,
        hidden,
        scale_second,
        ffn_rows,
        gate_part,
        up_part,
        activated,
    )
    return (layer_out, mixed, pairs_all, saved)


def layer_backward(grad_rows, extra_values, value_mix, weights, saved):
    gain_first, w_qkv, w_out, gain_second, w_gateup, w_down = weights
    (
        whole_rows,
        scale_first,
        normed_all,
        query_heads,
        pairs_all,
        token_index,
        doc_start,
        cosine,
        sine_part,
        log_total,
        accumulated,
        attended,
        hidden,
        scale_second,
        ffn_rows,
        gate_part,
        up_part,
        activated,
    ) = saved
    model_width = whole_rows.shape[1]
    head_count = w_qkv.shape[1]
    head_width = head_count * HD
    row_count = normed_all.shape[0]
    grad_hidden = grad_rows.astype(jnp.float32)
    grad_down = spread(grad_rows)
    grad_wd = inner_rows(activated, grad_down)
    grad_act = outer_cols(grad_down, w_down)
    sigmoid_gate = jax.nn.sigmoid(gate_part)
    grad_gate = grad_act * up_part * sigmoid_gate * (1.0 + gate_part * (1.0 - sigmoid_gate))
    grad_up = grad_act * gate_part * sigmoid_gate
    grad_gate_up = jnp.concatenate([grad_gate, grad_up], axis=1).astype(jnp.bfloat16)
    grad_wgu = inner_rows(grad_gate_up, ffn_rows).reshape(w_gateup.shape)
    back_second = jnp.dot(
        grad_gate_up, w_gateup.reshape(-1, model_width), preferred_element_type=jnp.float32
    )
    grad_normed_second = collect(back_second)
    grad_gain2, grad_hidden = norm_back(
        hidden, scale_second, gain_second, grad_normed_second, grad_hidden
    )
    grad_branch_all = spread(grad_hidden.astype(jnp.bfloat16))
    grad_wo = inner_rows(attended, grad_branch_all)
    grad_heads = (
        outer_cols(grad_branch_all, w_out).astype(jnp.bfloat16).reshape(row_count, head_count, HD)
    )
    grad_query, grad_pairs_all = attend_back(
        query_heads,
        pairs_all,
        token_index,
        doc_start,
        head_width,
        log_total,
        accumulated,
        grad_heads,
    )
    grad_pairs = lax.psum_scatter(
        grad_pairs_all.astype(jnp.bfloat16), "ctx", scatter_dimension=0, tiled=True
    ).astype(jnp.float32)
    grad_mixed = grad_pairs[:, head_width:] + extra_values.astype(jnp.float32)
    grad_keys = rotate_back(
        grad_pairs[:, :head_width].reshape(row_count, head_count, HD), cosine, sine_part
    )
    grad_query = rotate_back(grad_query, cosine, sine_part)
    grad_projected = jnp.concatenate(
        [
            grad_query.reshape(row_count, head_width),
            grad_keys.reshape(row_count, head_width),
            (1.0 - value_mix) * grad_mixed,
        ],
        axis=1,
    ).astype(jnp.bfloat16)
    send_values = (value_mix * grad_mixed).astype(jnp.bfloat16)
    grad_wqkv = inner_rows(grad_projected, normed_all).reshape(w_qkv.shape)
    grad_normed = collect(
        jnp.dot(
            grad_projected,
            w_qkv.reshape(3 * head_width, model_width),
            preferred_element_type=jnp.float32,
        )
    )
    grad_gain1, grad_whole = norm_back(
        whole_rows, scale_first, gain_first, grad_normed, grad_hidden
    )
    return (
        grad_whole,
        send_values,
        (grad_gain1, grad_wqkv, grad_wo, grad_gain2, grad_wgu, grad_wd),
    )


def general_body(inputs, cotangent, lengths, gain1, wqkv, wo, gain2, wgu, wd):
    section_index = lax.axis_index("section")
    leading = section_index == 0
    value_mix = jnp.where(leading, 0.0, 0.5).astype(jnp.float32)
    micro_count = inputs.shape[0]
    local_rows = inputs.shape[1]
    model_width = inputs.shape[2]
    head_width = wqkv.shape[2] * HD
    row_count = local_rows * lax.axis_size("tp")
    gateup_use, down_use = (wgu[0], wd[0])
    weights = (gain1[0], wqkv[0], wo[0], gain2[0], gateup_use, down_use)
    recv_rows = jnp.zeros((local_rows, model_width), jnp.bfloat16)
    recv_values = jnp.zeros((row_count, head_width), jnp.bfloat16)
    states = []
    outputs = []
    for turn_index in range(micro_count + 1):
        own_rows = inputs[min(turn_index, micro_count - 1)]
        row_block = jnp.where(leading, own_rows, recv_rows)
        seq_lengths = jnp.where(
            leading, lengths[min(turn_index, micro_count - 1)], lengths[max(turn_index - 1, 0)]
        )
        layer_out, mixed, pairs_all, unused = layer_forward(
            row_block, recv_values, value_mix, weights, seq_lengths
        )
        kept_pairs = None
        states.append((row_block, recv_values, seq_lengths, kept_pairs))
        outputs.append(layer_out)
        if turn_index < micro_count:
            recv_rows, recv_values = shifted((layer_out, mixed), "section", 1)
    grad_rows_in = jnp.zeros((local_rows, model_width), jnp.bfloat16)
    grad_values_in = jnp.zeros((row_count, head_width), jnp.bfloat16)
    totals = None
    turn_grads = []
    for turn_index in range(micro_count + 1):
        row_block, first_values, seq_lengths, kept_pairs = states[micro_count - turn_index]
        if turn_index < micro_count:
            fed_grad = cotangent[micro_count - 1 - turn_index]
        else:
            fed_grad = jnp.zeros_like(cotangent[0])
        grad_out = jnp.where(leading, grad_rows_in, fed_grad)
        unused_out, unused_mixed, unused_pairs, saved = layer_forward(
            row_block, first_values, value_mix, weights, seq_lengths
        )
        grad_whole, send_values, grads = layer_backward(
            grad_out, grad_values_in, value_mix, weights, saved
        )
        totals = grads if totals is None else jax.tree.map(jnp.add, totals, grads)
        sent_rows = grad_whole.astype(jnp.bfloat16)
        turn_grads.append(jnp.where(leading, grad_whole, sent_rows.astype(jnp.float32)))
        if turn_index < micro_count:
            grad_rows_in, grad_values_in = shifted((sent_rows, send_values), "section", -1)
    grad_gain1, grad_wqkv, grad_wo, grad_gain2, grad_wgu, grad_wd = totals
    grad_wqkv, grad_wo, grad_wgu, grad_wd = (
        lax.psum(grad_wqkv.astype(jnp.bfloat16), "ctx").astype(jnp.float32),
        lax.psum(grad_wo.astype(jnp.bfloat16), "ctx").astype(jnp.float32),
        lax.psum(grad_wgu.astype(jnp.bfloat16), "ctx").astype(jnp.float32),
        lax.psum(grad_wd.astype(jnp.bfloat16), "ctx").astype(jnp.float32),
    )
    grad_gain1, grad_gain2 = lax.psum((grad_gain1, grad_gain2), ("ctx", "tp"))
    acts = jnp.stack(
        [
            jnp.where(leading, outputs[batch_index], outputs[batch_index + 1])
            for batch_index in range(micro_count)
        ]
    )[None]
    input_grads = jnp.stack(
        [
            jnp.where(
                leading,
                turn_grads[micro_count - batch_index],
                turn_grads[micro_count - 1 - batch_index],
            )
            for batch_index in range(micro_count)
        ]
    )[None]
    return (
        acts,
        input_grads,
        grad_gain1[None],
        grad_wqkv[None],
        grad_wo[None],
        grad_gain2[None],
        grad_wgu[None],
        grad_wd[None],
    )


def device_groups(mesh_sizes, key, order):
    sections, contexts, parts = mesh_sizes
    groups = {}
    for section in range(sections):
        for ctx in range(contexts):
            for tp in range(parts):
                place = (section, ctx, tp)
                number = (section * contexts + ctx) * parts + tp
                groups.setdefault(key(*place), []).append((order(*place), number))
    return [[number for _, number in sorted(members)] for _, members in sorted(groups.items())]


def exchange(value, groups):
    return lax.all_to_all(
        value, ALL_AXES, split_axis=0, concat_axis=0, tiled=True, axis_index_groups=groups
    )


def document_bounds(ends_ref, index):
    start = jnp.zeros_like(index)
    for entry in range(ends_ref.shape[0]):
        end = ends_ref[entry]
        start = jnp.where(index >= end, end, start)
    return start


def scalar_start(ends_ref, index):
    start = jnp.int32(0)
    for entry in range(ends_ref.shape[0]):
        start = jnp.where(index >= ends_ref[entry], ends_ref[entry], start)
    return start


def scalar_end(ends_ref, index):
    end = ends_ref[ends_ref.shape[0] - 1]
    for entry in range(ends_ref.shape[0] - 2, -1, -1):
        end = jnp.where(index < ends_ref[entry], ends_ref[entry], end)
    return end


def dot(left, right, left_dim, right_dim):
    return lax.dot_general(
        left, right, (((left_dim,), (right_dim,)), ((), ())), preferred_element_type=jnp.float32
    )


def fold_rows(value, combine):
    rows, width = value.shape
    return combine(value.reshape(rows // 8, 8, width), axis=0)


def attention_forward_kernel(ends_ref, qkv_ref, out_ref, lse_ref, keys_ref, values_ref):
    program = pl.program_id(0)
    blocks, _, block_width = qkv_ref.shape
    width = CHUNK * block_width

    @pl.when(program == 0)
    def _():
        def turn(j, carry):
            keys_ref[j] = qkv_ref[j, HD : 2 * HD, :].T
            values_ref[j, 0:HD, :] = qkv_ref[j, 2 * HD : 3 * HD, :]
            values_ref[j, HD : HD + ONES, :] = jnp.ones((ONES, block_width), jnp.bfloat16)
            return carry

        lax.fori_loop(0, blocks, turn, 0)

    query = jnp.concatenate(
        [qkv_ref[program * CHUNK + entry, 0:HD, :] for entry in range(CHUNK)], axis=1
    )
    first = program * width
    query_index = first + lax.broadcasted_iota(jnp.int32, (1, width), 1)
    start = document_bounds(ends_ref, query_index)
    low_chunk = scalar_start(ends_ref, first) // width
    high_start = scalar_start(ends_ref, first + width - 1)
    middle = jnp.clip((high_start + width - 1) // width, low_chunk, program)

    def step(chunk, carry, masked):
        top, acc = carry
        parts = []
        for entry in range(CHUNK):
            j = chunk * CHUNK + entry
            scores = dot(keys_ref[j], query, 1, 0)
            if masked:
                key_index = j * block_width + lax.broadcasted_iota(jnp.int32, (block_width, 1), 0)
                allowed = (key_index >= start) & (key_index <= query_index)
                scores = jnp.where(allowed, scores, MASKED)
            parts.append(scores)
        part_top = functools.reduce(jnp.maximum, [fold_rows(part, jnp.max) for part in parts])
        new_top = jnp.maximum(top, jnp.max(part_top, axis=0, keepdims=True))
        acc = acc * jnp.exp2(top - new_top)
        for entry in range(CHUNK):
            weights = jnp.exp2(parts[entry] - new_top).astype(jnp.bfloat16)
            acc = acc + dot(values_ref[chunk * CHUNK + entry], weights, 1, 0)
        return new_top, acc

    carry = (
        jnp.full((1, width), MASKED, jnp.float32),
        jnp.zeros((HD + ONES, width), jnp.float32),
    )
    carry = lax.fori_loop(low_chunk, middle, functools.partial(step, masked=True), carry)
    carry = lax.fori_loop(middle, program, functools.partial(step, masked=False), carry)
    top, acc = step(program, carry, True)
    total = acc[HD : HD + 1]
    out = (acc[:HD] / total).astype(jnp.bfloat16)
    lse = top + jnp.log2(total)
    for entry in range(CHUNK):
        columns = slice(entry * block_width, (entry + 1) * block_width)
        out_ref[entry] = out[:, columns]
        lse_ref[entry] = lse[:, columns]


def attention_forward(ends, qkv):
    blocks, _, width = qkv.shape
    return pl.pallas_call(
        attention_forward_kernel,
        grid_spec=pltpu.PrefetchScalarGridSpec(
            num_scalar_prefetch=1,
            grid=(blocks // CHUNK,),
            in_specs=[pl.BlockSpec(qkv.shape, lambda i, ends_ref: (0, 0, 0))],
            out_specs=[
                pl.BlockSpec((CHUNK, HD, width), lambda i, ends_ref: (i, 0, 0)),
                pl.BlockSpec((CHUNK, 1, width), lambda i, ends_ref: (i, 0, 0)),
            ],
            scratch_shapes=[
                pltpu.VMEM((blocks, width, HD), jnp.bfloat16),
                pltpu.VMEM((blocks, HD + ONES, width), jnp.bfloat16),
            ],
        ),
        out_shape=[
            jax.ShapeDtypeStruct((blocks, HD, width), jnp.bfloat16),
            jax.ShapeDtypeStruct((blocks, 1, width), jnp.float32),
        ],
        compiler_params=pltpu.CompilerParams(vmem_limit_bytes=VMEM_LIMIT),
        cost_estimate=LIGHT,
        name="attention_forward",
    )(ends, qkv)


def attention_backward_kernel(
    ends_ref, qkv_ref, out_ref, grad_ref, lse_ref, result_ref,
    query_grad_ref, delta_ref, queries_ref, grads_ref, lses_ref,
):
    program = pl.program_id(0)
    blocks, _, block_width = qkv_ref.shape
    width = CHUNK * block_width

    @pl.when(program == 0)
    def _():
        def turn(i, carry):
            for entry in range(CHUNK):
                block = i * CHUNK + entry
                columns = slice(entry * block_width, (entry + 1) * block_width)
                grad = grad_ref[block]
                queries_ref[i, :, columns] = qkv_ref[block, 0:HD, :]
                grads_ref[i, :, columns] = grad
                lses_ref[i, :, columns] = lse_ref[block]
                delta_ref[i, :, columns] = jnp.sum(
                    grad.astype(jnp.float32) * out_ref[block].astype(jnp.float32),
                    axis=0,
                    keepdims=True,
                )
            query_grad_ref[i] = jnp.zeros((HD, width), jnp.float32)
            return carry

        lax.fori_loop(0, blocks // CHUNK, turn, 0)

    def joined(low_row, high_row):
        return jnp.concatenate(
            [qkv_ref[program * CHUNK + entry, low_row:high_row, :] for entry in range(CHUNK)],
            axis=1,
        )

    first = program * width
    keys_t = joined(HD, 2 * HD)
    keys = keys_t.T
    values = joined(2 * HD, 3 * HD).T
    key_index = first + lax.broadcasted_iota(jnp.int32, (width, 1), 0)
    near_end = scalar_end(ends_ref, first)
    far_end = scalar_end(ends_ref, first + width - 1)
    stop = (far_end - 1) // width + 1
    middle = jnp.clip(near_end // width, program + 1, stop)

    def step(i, carry, masked):
        key_grad, value_grad = carry
        query = queries_ref[i]
        grad = grads_ref[i]
        weights = jnp.exp2(dot(keys, query, 1, 0) - lses_ref[i])
        if masked:
            query_index = i * width + lax.broadcasted_iota(jnp.int32, (1, width), 1)
            start = document_bounds(ends_ref, query_index)
            allowed = (key_index >= start) & (key_index <= query_index)
            weights = jnp.where(allowed, weights, 0.0)
        grad_weights = dot(values, grad, 1, 0)
        grad_scores = (weights * (grad_weights - delta_ref[i])).astype(jnp.bfloat16)
        query_grad_ref[i] += dot(keys_t, grad_scores, 1, 0)
        value_grad = value_grad + dot(grad, weights.astype(jnp.bfloat16), 1, 1)
        key_grad = key_grad + dot(query, grad_scores, 1, 1)
        return key_grad, value_grad

    empty = jnp.zeros((HD, width), jnp.float32)
    carry = step(program, (empty, empty), True)
    carry = lax.fori_loop(program + 1, middle, functools.partial(step, masked=False), carry)
    key_grad, value_grad = lax.fori_loop(middle, stop, functools.partial(step, masked=True), carry)
    query_grad = query_grad_ref[program] * HD ** (-0.5)
    key_grad = key_grad * LOG_2
    for entry in range(CHUNK):
        columns = slice(entry * block_width, (entry + 1) * block_width)
        result_ref[entry, 0:HD] = query_grad[:, columns].astype(jnp.bfloat16)
        result_ref[entry, HD : 2 * HD] = key_grad[:, columns].astype(jnp.bfloat16)
        result_ref[entry, 2 * HD : 3 * HD] = value_grad[:, columns].astype(jnp.bfloat16)


def attention_backward(ends, qkv, out, grad, lse):
    blocks, _, block_width = qkv.shape
    chunks, width = blocks // CHUNK, CHUNK * block_width

    def whole(value):
        return pl.BlockSpec(value.shape, lambda i, ends_ref: (0, 0, 0))

    return pl.pallas_call(
        attention_backward_kernel,
        grid_spec=pltpu.PrefetchScalarGridSpec(
            num_scalar_prefetch=1,
            grid=(chunks,),
            in_specs=[whole(qkv), whole(out), whole(grad), whole(lse)],
            out_specs=pl.BlockSpec((CHUNK, 3 * HD, block_width), lambda i, ends_ref: (i, 0, 0)),
            scratch_shapes=[
                pltpu.VMEM((chunks, HD, width), jnp.float32),
                pltpu.VMEM((chunks, 1, width), jnp.float32),
                pltpu.VMEM((chunks, HD, width), jnp.bfloat16),
                pltpu.VMEM((chunks, HD, width), jnp.bfloat16),
                pltpu.VMEM((chunks, 1, width), jnp.float32),
            ],
        ),
        out_shape=jax.ShapeDtypeStruct(qkv.shape, jnp.bfloat16),
        compiler_params=pltpu.CompilerParams(vmem_limit_bytes=VMEM_LIMIT),
        cost_estimate=LIGHT,
        name="attention_backward",
    )(ends, qkv, out, grad, lse)


def rope_pair(leading_half, trailing_half, cosine, sine_part):
    return (
        leading_half * cosine - trailing_half * sine_part,
        trailing_half * cosine + leading_half * sine_part,
    )


def low(value):
    return value.astype(jnp.bfloat16)


def wide(value):
    return value.astype(jnp.float32)


def whole_block(value):
    zeros = (0,) * value.ndim
    return pl.BlockSpec(value.shape, lambda *_: zeros)


def feed_forward_kernel(rows_ref, gate_w_ref, up_w_ref, down_w_ref, gate_ref, up_ref, act_ref, sum_ref):
    rows = rows_ref[...]
    gate = dot(gate_w_ref[...], rows, 1, 1)
    up = dot(up_w_ref[...], rows, 1, 1)
    active = (gate * jax.nn.sigmoid(gate) * up).astype(jnp.bfloat16)
    gate_ref[...] = gate.astype(jnp.bfloat16)
    up_ref[...] = up.astype(jnp.bfloat16)
    act_ref[...] = active

    @pl.when(pl.program_id(0) == 0)
    def _():
        sum_ref[...] = jnp.zeros_like(sum_ref)

    sum_ref[...] += dot(active, down_w_ref[...], 0, 0)


def feed_forward(rows, w_gate, w_up, w_down, tile):
    units, width = w_gate.shape
    count = rows.shape[0]
    weight = pl.BlockSpec((tile, width), lambda i: (i, 0))
    column = pl.BlockSpec((tile, count), lambda i: (i, 0))
    hidden = jax.ShapeDtypeStruct((units, count), jnp.bfloat16)
    return pl.pallas_call(
        feed_forward_kernel,
        grid=(units // tile,),
        in_specs=[whole_block(rows), weight, weight, weight],
        out_specs=[column, column, column, pl.BlockSpec((count, width), lambda i: (0, 0))],
        out_shape=[hidden, hidden, hidden, jax.ShapeDtypeStruct((count, width), jnp.float32)],
        compiler_params=pltpu.CompilerParams(vmem_limit_bytes=VMEM_LIMIT),
        cost_estimate=LIGHT,
        name="feed_forward",
    )(rows, w_gate, w_up, w_down)


def feed_forward_back_kernel(
    grad_ref, gate_ref, up_ref, gate_w_ref, up_w_ref, down_w_ref, grad_gate_ref, grad_up_ref, sum_ref
):
    grad_act = dot(down_w_ref[...], grad_ref[...], 1, 1)
    gate = gate_ref[...].astype(jnp.float32)
    up = up_ref[...].astype(jnp.float32)
    sigmoid_gate = jax.nn.sigmoid(gate)
    grad_gate = (grad_act * up * sigmoid_gate * (1.0 + gate * (1.0 - sigmoid_gate))).astype(
        jnp.bfloat16
    )
    grad_up = (grad_act * gate * sigmoid_gate).astype(jnp.bfloat16)
    grad_gate_ref[...] = grad_gate
    grad_up_ref[...] = grad_up

    @pl.when(pl.program_id(0) == 0)
    def _():
        sum_ref[...] = jnp.zeros_like(sum_ref)

    sum_ref[...] += dot(grad_gate, gate_w_ref[...], 0, 0) + dot(grad_up, up_w_ref[...], 0, 0)


def feed_forward_back(grad, gate, up, w_gate, w_up, w_down, tile):
    units, width = w_gate.shape
    count = grad.shape[0]
    weight = pl.BlockSpec((tile, width), lambda i: (i, 0))
    column = pl.BlockSpec((tile, count), lambda i: (i, 0))
    hidden = jax.ShapeDtypeStruct((units, count), jnp.bfloat16)
    return pl.pallas_call(
        feed_forward_back_kernel,
        grid=(units // tile,),
        in_specs=[whole_block(grad), column, column, weight, weight, weight],
        out_specs=[column, column, pl.BlockSpec((count, width), lambda i: (0, 0))],
        out_shape=[hidden, hidden, jax.ShapeDtypeStruct((count, width), jnp.float32)],
        compiler_params=pltpu.CompilerParams(vmem_limit_bytes=VMEM_LIMIT),
        cost_estimate=LIGHT,
        name="feed_forward_back",
    )(grad, gate, up, w_gate, w_up, w_down)


def half_products_kernel(layout, sizes, has_addend, which_ref, *refs):
    refs = list(refs)
    out_ref = refs.pop()
    addend_ref = refs.pop() if has_addend else None
    totals = [
        sum(dot(refs[left][...], refs[right][...], 1, 0) for left, right in pairs)
        for pairs in layout
    ]
    for piece in range(out_ref.shape[0]):
        parts = [
            total[piece * size : (piece + 1) * size] for total, size in zip(totals, sizes)
        ]
        value = jnp.concatenate(parts, axis=0) if len(parts) > 1 else parts[0]
        if has_addend:
            value = value + addend_ref[piece].astype(jnp.float32)
        out_ref[piece] = value.astype(jnp.bfloat16)


def half_products(which, groups, pieces, per_step, addend=None):
    lefts, rights, layout = [], [], []
    for group in groups:
        for left, right in group:
            if not any(left is known for known in lefts):
                lefts.append(left)
            if not any(right is known for known in rights):
                rights.append(right)
    find = lambda known, value: next(i for i, entry in enumerate(known) if entry is value)
    for group in groups:
        layout.append(
            tuple((find(lefts, left), len(lefts) + find(rights, right)) for left, right in group)
        )
    sizes = tuple(group[0][0].shape[0] // (2 * pieces) for group in groups)
    width = rights[0].shape[1]
    steps = pieces // per_step
    out_spec = pl.BlockSpec((per_step, sum(sizes), width), lambda i, which_ref: (i, 0, 0))
    left_specs = [
        pl.BlockSpec(
            (left.shape[0] // (2 * steps), left.shape[1]),
            lambda i, which_ref: (which_ref[0] * steps + i, 0),
        )
        for left in lefts
    ]
    extra = [] if addend is None else [addend]
    work = sum(left.size // 2 for left, _ in sum(groups, ()))
    return pl.pallas_call(
        functools.partial(half_products_kernel, tuple(layout), sizes, addend is not None),
        grid_spec=pltpu.PrefetchScalarGridSpec(
            num_scalar_prefetch=1,
            grid=(steps,),
            in_specs=left_specs + [whole_block(right) for right in rights] + [out_spec] * len(extra),
            out_specs=out_spec,
        ),
        out_shape=jax.ShapeDtypeStruct((pieces, sum(sizes), width), jnp.bfloat16),
        compiler_params=pltpu.CompilerParams(vmem_limit_bytes=VMEM_LIMIT),
        cost_estimate=LIGHT,
        name="half_products",
    )(which.reshape(1).astype(jnp.int32), *lefts, *rights, *extra)


def together(*values):
    return lax.optimization_barrier(values)


def after(value, *others):
    return lax.optimization_barrier((value, *others))[0]


def split_body(mesh_sizes, inputs, cotangent, lengths, gain1, wqkv, wo, gain2, wgu, wd):
    sections, contexts, parts = mesh_sizes
    half_parts = parts // 2
    section = lax.axis_index("section")
    ctx = lax.axis_index("ctx")
    tp = lax.axis_index("tp")
    row_side, column_side = ctx // 2, ctx % 2
    leading = section == 0
    batch = tp // half_parts
    model_width = inputs.shape[2]
    rows = inputs.shape[1]
    heads = wqkv.shape[2] * parts
    unit_rows = wd.shape[1] // contexts // 2
    head_rows = 3 * HD // 2
    out_rows = HD // 2
    half_width = HD // 2
    tile = 4 * unit_rows
    number = lambda s, c, t: (s * contexts + c) * parts + t
    places = [
        (s, c, t) for s in range(sections) for c in range(contexts) for t in range(parts)
    ]
    everyone = [[number(*place) for place in places]]
    token_of = lambda s, c, t: c * parts + t % half_parts + half_parts * s
    batch_groups = device_groups(mesh_sizes, lambda s, c, t: t // half_parts, token_of)
    side_groups = device_groups(mesh_sizes, lambda s, c, t: c % 2, lambda s, c, t: (s, c, t))
    crossing = [
        (number(s, c, t), number(s, c, (t + half_parts) % parts))
        for s, c, t in places
        if t // half_parts == s
    ]

    def to_batch(value):
        mine = lax.dynamic_index_in_dim(value, batch, 0, keepdims=False)
        other = lax.dynamic_index_in_dim(value, 1 - batch, 0, keepdims=False)
        moved = lax.ppermute(other, ALL_AXES, crossing)
        return jnp.where(section == batch, mine, moved)

    def to_home(value, layer):
        stay = [
            (number(s, c, t), number(layer, c, t)) for s, c, t in places if t // half_parts == s
        ]
        cross = [
            (number(s, c, t), number(layer, c, (t + half_parts) % parts))
            for s, c, t in places
            if t // half_parts != s
        ]
        return (lax.ppermute(value, ALL_AXES, stay), lax.ppermute(value, ALL_AXES, cross))

    def at_home(first_pair, second_pair):
        near = jnp.where(leading, first_pair[0], second_pair[0])
        far = jnp.where(leading, first_pair[1], second_pair[1])
        upper = batch == 0
        return jnp.stack([jnp.where(upper, near, far), jnp.where(upper, far, near)])[None]

    def swap_side(value):
        return lax.ppermute(value, "ctx", [(c, c ^ 1) for c in range(contexts)])

    def swap_far(value):
        return lax.ppermute(value, "ctx", [(c, c ^ 2) for c in range(contexts)])

    def swap_near(value):
        return lax.ppermute(value, "tp", [(t, t ^ 1) for t in range(parts)])

    def swap_half(value):
        return lax.ppermute(value, "tp", [(t, (t + half_parts) % parts) for t in range(parts)])

    def swap_section(value):
        return lax.ppermute(value, "section", [(0, 1), (1, 0)])

    def all_to_all(value, axis):
        return lax.all_to_all(value, axis, split_axis=0, concat_axis=0, tiled=True)

    def copies(value, count):
        return jnp.broadcast_to(value[None], (count, *value.shape))

    def gather(value, groups):
        return lax.all_gather(value, ALL_AXES, axis=0, tiled=True, axis_index_groups=groups)

    def ordered(index, own, other):
        return jnp.where(index == 0, own, other), jnp.where(index == 0, other, own)

    def by_core(value, which):
        return lax.dynamic_index_in_dim(value, which, 0, keepdims=False)

    def spread_line(piece):
        return all_to_all(copies(piece, parts), "tp")

    def spread_sides(line):
        middle = line.shape[1] // 2
        line_a, line_b = line[:, :middle], line[:, middle:]
        return (line_a, swap_far(line_a)), (line_b, swap_side(line_b))

    def spread_corners(line_pairs):
        pair_a = jnp.stack(ordered(row_side, *line_pairs[0]))
        pair_b = jnp.stack(ordered(column_side, *line_pairs[1]))
        return (pair_a, swap_side(pair_a)), (pair_b, swap_far(pair_b))

    def spread_cores(plane_pairs):
        plane_a = jnp.stack(ordered(column_side, *plane_pairs[0]), axis=1)
        plane_b = jnp.stack(ordered(row_side, *plane_pairs[1]), axis=0)
        rest = head_rows - plane_a.shape[3]
        own_heads = jnp.concatenate([plane_a, plane_b[:, :, :, :rest]], axis=3)
        own_heads = own_heads.reshape(-1, model_width)
        own_outs = plane_b[:, :, :, rest:].reshape(-1, model_width)
        return (own_heads, swap_section(own_heads)), (own_outs, swap_section(own_outs))

    def own_halves(value, axis, size):
        part = lax.dynamic_slice_in_dim(value, ctx * size, size, axis)
        return part.reshape(2, -1, model_width)

    packed = jnp.concatenate(
        [
            own_halves(wqkv[0], 1, heads // (parts * contexts)),
            own_halves(wo[0], 0, HD),
            own_halves(wgu[0, 0], 0, 2 * unit_rows),
            own_halves(wgu[0, 1], 0, 2 * unit_rows),
            own_halves(wd[0], 0, 2 * unit_rows),
        ],
        axis=1,
    )
    kept = by_core(packed, section)
    passed = swap_section(by_core(packed, 1 - section))
    pieces = ordered(section, kept, passed)
    attention_rows = head_rows + out_rows

    def feed_forward_weights(piece):
        whole = gather(piece[attention_rows:], side_groups)
        whole = whole.reshape(2 * 2 * parts, 3, unit_rows, model_width)
        return [whole[:, entry].reshape(-1, model_width) for entry in range(3)]

    rows_in = to_batch(inputs)
    line, rows_in = together(spread_line(pieces[0][:attention_rows]), rows_in)
    w_ffn = [feed_forward_weights(after(piece, line)) for piece in pieces]
    line_pairs = together(*spread_sides(line))
    w_heads, w_outs = [None, None], [None, None]
    w_heads[0], out_halves = spread_cores(spread_corners(line_pairs))
    w_outs[0] = jnp.concatenate(ordered(section, *out_halves), axis=0)

    gains = wide(jnp.concatenate([gain1, gain2], axis=0))
    gain_sets = ordered(section, gains, swap_section(gains))

    seq_lengths = lax.dynamic_index_in_dim(lengths, batch, 0, keepdims=False)
    ends = jnp.cumsum(seq_lengths).astype(jnp.int32)
    token_index = token_of(section, ctx, tp) * rows + jnp.arange(rows, dtype=jnp.int32)
    before = (ends[None, :] <= token_index[:, None]).astype(jnp.int32)
    position = token_index - jnp.sum(before * seq_lengths[None, :], axis=1)
    frequency = jnp.exp(
        -jnp.log(10000.0) * jnp.arange(half_width, dtype=jnp.float32) / half_width
    )
    angles = position.astype(jnp.float32)[None, :] * frequency[:, None]
    cosine, sine_part = jnp.cos(angles), jnp.sin(angles)

    def head_halves(value):
        size = value.shape[1] // 2
        return value.reshape(heads, 2, size, rows).transpose(1, 0, 2, 3).reshape(2, -1, rows)

    def whole_heads(value):
        value = value.reshape(2, heads, -1, rows)
        return value.transpose(1, 0, 2, 3).reshape(heads, -1, rows)

    def nothing(value):
        return value

    def layer_forward(whole_rows, first_values, layer, in_first, in_second, in_third, in_fourth):
        gain_first, gain_second = gain_sets[layer][0], gain_sets[layer][1]
        scale_first = lax.rsqrt(jnp.mean(whole_rows * whole_rows, axis=-1, keepdims=True) + EPSILON)
        normed = low(whole_rows * scale_first * gain_first)
        halves = [dot(weight, normed, 1, 1) for weight in w_heads[layer]]
        halves = ordered(section, *halves)
        upper, lower = [half.reshape(heads, head_rows, rows) for half in halves]
        query = rope_pair(upper[:, :half_width], upper[:, half_width:HD], cosine, sine_part)
        key = rope_pair(upper[:, HD:], lower[:, :half_width], cosine, sine_part)
        value = lower[:, half_width:]
        if first_values is not None:
            value = 0.5 * value + 0.5 * wide(first_values)
        mixed = low(value)
        shrunk = [low(half * (HD ** (-0.5) / LOG_2)) for half in query]
        qkv = exchange(
            jnp.concatenate([*shrunk, low(key[0]), low(key[1]), mixed], axis=1), batch_groups
        )
        qkv = in_first(qkv)
        out, lse = attention_forward(ends, qkv)
        out = in_second(out)
        attended = head_halves(exchange(out, batch_groups))
        hidden = whole_rows + dot(attended.reshape(-1, rows), w_outs[layer], 0, 0)
        scale_second = lax.rsqrt(jnp.mean(hidden * hidden, axis=-1, keepdims=True) + EPSILON)
        normed_second = low(hidden * scale_second * gain_second)
        far_rows = swap_side(normed_second)
        near = feed_forward(normed_second, *w_ffn[layer], tile)
        far_rows = in_third(after(far_rows, near[3]))
        far = feed_forward(far_rows, *w_ffn[layer], tile)
        far_down = in_fourth(swap_side(low(far[3])))
        layer_out = low(hidden + (near[3] + wide(far_down)))
        saved = (
            whole_rows, scale_first, normed, qkv, out, lse, attended, hidden, scale_second,
            (normed_second, far_rows), near[:3], far[:3],
        )
        return layer_out, mixed, saved

    def norm_back(whole_rows, scale_rows, gain, grad_normed, grad_rest):
        unit = whole_rows * scale_rows
        scaled = grad_normed * gain
        grad_gain = jnp.sum(grad_normed * unit, axis=0)
        grad_whole = grad_rest + scale_rows * (
            scaled - unit * jnp.mean(scaled * unit, axis=-1, keepdims=True)
        )
        return grad_gain, grad_whole

    def pick(value, index, axis):
        return lax.dynamic_index_in_dim(value, index, axis, keepdims=False)

    def parted(value, index, axis):
        return pick(value, index, axis), pick(value, 1 - index, axis)

    def moved_pair(pair, swap):
        return pair[0], swap(pair[1])

    def halve(value, index, swap, axis):
        return moved_pair(parted(value, index, axis), swap)

    def add(pair):
        return low(wide(pair[0]) + wide(pair[1]))

    def near_sum(value):
        return halve(value.reshape(2, half_parts, *value.shape[1:]), tp % 2, swap_near, 1)

    def far_sum(pair):
        return halve(add(pair), batch, swap_half, 0)

    def layer_backward(grad_rows, extra_values, saved, layer, in_first, in_second, in_third, in_fourth, in_fifth):
        (
            whole_rows, scale_first, normed, qkv, out, lse, attended, hidden, scale_second,
            ffn_rows, near, far,
        ) = saved
        gain_first, gain_second = gain_sets[layer][0], gain_sets[layer][1]
        grad_down = low(grad_rows)
        far_down = swap_side(grad_down)
        grad_gate, grad_up, near_back = feed_forward_back(grad_down, *near[:2], *w_ffn[layer], tile)
        far_down = in_first(after(far_down, near_back))
        far_gate, far_up, far_back = feed_forward_back(far_down, *far[:2], *w_ffn[layer], tile)
        far_back = swap_side(low(far_back))
        groups = (
            ((grad_gate, ffn_rows[0]), (far_gate, ffn_rows[1])),
            ((grad_up, ffn_rows[0]), (far_up, ffn_rows[1])),
            ((near[2], grad_down), (far[2], far_down)),
        )
        products = functools.partial(
            half_products, groups=groups, pieces=2 * parts, per_step=2
        )
        sent = products(1 - section)
        moved = swap_section(sent)
        far_back = in_second(after(far_back, sent))
        grad_gain2, grad_hidden = norm_back(
            hidden, scale_second, gain_second, near_back + wide(far_back), wide(grad_rows)
        )
        grad_branch = low(grad_hidden)
        grad_heads = whole_heads(low(dot(w_outs[layer], grad_branch, 1, 1)))
        grad_heads = exchange(grad_heads, batch_groups)
        rest = products(section, addend=moved)
        out_pair = (attended.reshape(-1, rows), grad_branch)
        grad_heads, rest = in_third(grad_heads, rest, out_pair)
        grad_qkv = attention_backward(ends, qkv, out, grad_heads, lse)
        grad_qkv = in_fourth(grad_qkv)
        grad_qkv = in_fifth(exchange(grad_qkv, batch_groups))
        grad_qkv = wide(grad_qkv)
        quarter = lambda entry: grad_qkv[:, entry * half_width : (entry + 1) * half_width]
        grad_query = rope_pair(quarter(0), quarter(1), cosine, -sine_part)
        grad_key = rope_pair(quarter(2), quarter(3), cosine, -sine_part)
        grad_value = grad_qkv[:, 2 * HD :]
        send_values = None
        if extra_values is None:
            grad_value = 0.5 * grad_value
            send_values = low(grad_value)
        else:
            grad_value = grad_value + wide(extra_values)
        upper = low(jnp.concatenate([*grad_query, grad_key[0]], axis=1))
        lower = low(jnp.concatenate([grad_key[1], grad_value], axis=1))
        grad_halves = jnp.stack([upper, lower]).reshape(2, -1, rows)
        return grad_halves, send_values, grad_hidden, out_pair, grad_gain2

    def input_grads_of(grad_halves, grad_hidden, saved, layer):
        whole_rows, scale_first = saved[:2]
        places_of = (section, 1 - section)
        grad_normed = sum(
            dot(by_core(grad_halves, place), weight, 0, 0)
            for place, weight in zip(places_of, w_heads[layer])
        )
        return norm_back(whole_rows, scale_first, gain_sets[layer][0], grad_normed, grad_hidden)

    def piece_sum(value, groups):
        return lax.psum_scatter(
            value, ALL_AXES, scatter_dimension=0, tiled=True, axis_index_groups=groups
        )

    line_groups = device_groups(
        mesh_sizes, lambda s, c, t: (s, c % 2), lambda s, c, t: (c, t)
    )
    core_groups = device_groups(mesh_sizes, lambda s, c, t: s, lambda s, c, t: (c, t))
    plane_shape = (2, 2, parts)
    pending = {}

    def weights_line(value):
        value, piece = together(value, pieces[1][:attention_rows])
        pending["weights"] = spread_line(piece)
        return value

    def weights_sides(value):
        value, line = together(value, pending["weights"])
        pending["weights"] = spread_sides(line)
        return value

    def weights_corners(value):
        value, pairs = together(value, pending["weights"])
        pending["weights"] = spread_corners(pairs)
        return value

    def weights_cores(value):
        value, pairs = together(value, pending["weights"])
        w_heads[1], pending["outs"] = spread_cores(pairs)
        return value

    first_out, first_values, first_saved = layer_forward(
        wide(rows_in), None, 0, weights_line, weights_sides, weights_corners, weights_cores
    )

    def start_homes(value):
        w_outs[1] = jnp.concatenate(ordered(section, *pending["outs"]), axis=0)
        value, home = together(value, first_out)
        pending["first_home"] = to_home(home, 0)
        pending["grad_in"] = to_batch(after(cotangent, home))
        return value

    def end_homes(value):
        value, pending["first_home"], pending["grad_in"], w_outs[1] = together(
            value, pending["first_home"], pending["grad_in"], w_outs[1]
        )
        return value

    second_out, _, second_saved = layer_forward(
        wide(first_out), first_values, 1, start_homes, end_homes, nothing, nothing
    )
    first_home, grad_in = pending["first_home"], pending["grad_in"]

    def second_third(value, rest, out_pair):
        value, rest = together(value, rest)
        rest = rest.reshape(-1, model_width)
        pending["second_rest"] = piece_sum(rest, line_groups)
        pending["second_home"] = to_home(after(second_out, value), 1)
        return value, rest

    def second_fourth(value):
        value, pending["second_home"] = together(value, pending["second_home"])
        return value

    grad_halves, send_values, grad_hidden, out_pair, second_gain2 = layer_backward(
        grad_in, None, second_saved, 1, nothing, nothing, second_third, second_fourth, nothing
    )
    second_gain1, second_grad = input_grads_of(grad_halves, grad_hidden, second_saved, 1)
    second_grad = low(second_grad)
    head_products = functools.partial(
        half_products,
        groups=(((grad_halves.reshape(-1, rows), second_saved[2]),), (out_pair,)),
        pieces=heads,
        per_step=4,
    )

    def first_first(value):
        value, sent = together(value, head_products(1 - section))
        pending["moved"] = swap_section(sent)
        return value

    def crossed(value):
        middle = value.shape[3] // 2
        return (
            parted(value[:, :, :, :middle], column_side, 1),
            parted(value[:, :, :, middle:], row_side, 0),
        )

    def first_second(value):
        head = head_products(section, addend=pending["moved"])
        value, head = together(value, head)
        pending["head"] = piece_sum(head.reshape(-1, model_width), core_groups)
        pending["second_grad_home"] = to_home(after(second_grad, value), 1)
        return value

    def first_third(value, rest, out_pair):
        out_products = functools.partial(
            half_products, groups=((out_pair,),), pieces=heads, per_step=8
        )
        out_sum = out_products(section, addend=swap_section(out_products(1 - section)))
        rest = rest.reshape(2, parts, -1, model_width)
        rest_a = parted(rest[:, :-1], row_side, 0)
        rest_b = parted(rest[:, -1:], row_side, 0)
        out_sum = parted(out_sum.reshape(*plane_shape, -1, model_width), column_side, 1)
        value, rest_a, rest_b, out_sum = together(value, rest_a, rest_b, out_sum)
        pending["rest_a"] = moved_pair(rest_a, swap_far)
        pending["rest_b"] = rest_b
        pending["out"] = moved_pair(out_sum, swap_side)
        return value, rest

    def first_fourth(value):
        value, rest_a, rest_b, out_sum, pending["second_grad_home"] = together(
            value, pending["rest_a"], pending["rest_b"], pending["out"],
            pending["second_grad_home"],
        )
        pending["rest_a"] = rest_a
        pending["rest_b"] = moved_pair(rest_b, swap_far)
        pending["out"] = halve(add(out_sum), row_side, swap_far, 0)
        return value

    def first_fifth(value):
        value, rest_a, rest_b, out_sum = together(
            value, pending["rest_a"], pending["rest_b"], pending["out"]
        )
        pending["out"] = add(out_sum)
        rest = jnp.concatenate([add(rest_a), add(rest_b)], axis=0)
        pending["rest"] = near_sum(rest)
        return value

    first_halves, _, first_hidden, _, first_gain2 = layer_backward(
        second_grad, send_values, first_saved, 0,
        first_first, first_second, first_third, first_fourth, first_fifth,
    )
    head_products = functools.partial(
        half_products,
        groups=(((first_halves.reshape(-1, rows), first_saved[2]),),),
        pieces=heads,
        per_step=4,
    )
    sent = head_products(1 - section)
    moved = swap_section(sent)
    first_gain1, first_grad = input_grads_of(
        after(first_halves, sent), first_hidden, first_saved, 0
    )
    head = head_products(section, addend=moved).reshape(*plane_shape, head_rows, model_width)
    head, first_grad, rest = together(head, low(first_grad), pending["rest"])
    head_a, head_b = crossed(head)
    gain_rows = jnp.stack([first_gain1, first_gain2, second_gain1, second_gain2])
    first_grad, gain_rows, head_a, head_b, rest = together(
        first_grad, gain_rows, head_a, head_b, rest
    )
    head_a = moved_pair(head_a, swap_side)
    head_b = moved_pair(head_b, swap_far)
    rest = far_sum(rest)
    first_grad_home = to_home(first_grad, 0)
    head_a, head_b = together(add(head_a), add(head_b))
    head_a = parted(head_a, row_side, 0)
    head_b = parted(head_b, column_side, 0)
    gain_rows, head_a, head_b = together(gain_rows, head_a, head_b)
    head_a = moved_pair(head_a, swap_far)
    head_b = moved_pair(head_b, swap_side)
    gain_sums = all_to_all(copies(gain_rows, len(places)), ALL_AXES)
    head_a, head_b, rest, first_grad_home = together(head_a, head_b, rest, first_grad_home)
    head = near_sum(jnp.concatenate([add(head_a), add(head_b), pending["out"]], axis=1))
    rest = all_to_all(copies(add(rest), contexts), "ctx")
    head, gain_sums = together(head, gain_sums)
    head = together(*far_sum(head))
    first_head = all_to_all(copies(add(head), contexts), "ctx")
    second = lax.all_gather(
        jnp.concatenate([pending["second_rest"], pending["head"]], axis=0), "ctx", axis=0, tiled=False
    )
    rest, first_head, second = together(rest, first_head, second)
    first_grads = jnp.concatenate([rest, first_head], axis=1)
    second_grads = second
    second_home, second_grad_home = pending["second_home"], pending["second_grad_home"]
    gain_total = jnp.sum(gain_sums.reshape(len(places), 4, model_width), axis=0)
    gain_total = jnp.where(leading, gain_total[:2], gain_total[2:])

    def finish(first, second):
        mine = jnp.where(leading, first, second)
        moved = swap_section(jnp.where(leading, second, first))
        return ordered(section, mine, moved)

    def joined(halves, first, count):
        both = jnp.stack([half[:, first : first + count] for half in halves], axis=1)
        return wide(both).reshape(-1, model_width)

    grads = finish(first_grads, second_grads)
    grad_wgate, grad_wup, grad_wd = [
        joined(grads, entry * unit_rows, unit_rows) for entry in range(3)
    ]
    grad_wqkv = joined(grads, 3 * unit_rows, head_rows).reshape(contexts, 3, HD, model_width)
    grad_wo = joined(grads, 3 * unit_rows + head_rows, out_rows)
    return (
        at_home(first_home, second_home),
        wide(at_home(first_grad_home, second_grad_home)),
        gain_total[0:1],
        grad_wqkv.transpose(1, 0, 2, 3)[None],
        grad_wo[None],
        gain_total[1:2],
        jnp.stack([grad_wgate, grad_wup])[None],
        grad_wd[None],
    )


def body(mesh_sizes, *arguments):
    inputs, _, _, _, wqkv = arguments[:5]
    sections, contexts, parts = mesh_sizes
    own_heads, own_units = wqkv.shape[2], arguments[7].shape[2]
    fits = (
        sections == 2
        and inputs.shape[0] == 2
        and contexts == 4
        and parts % 2 == 0
        and own_heads == contexts
        and own_units % (16 * contexts) == 0
        and inputs.shape[1] % 128 == 0
    )
    if fits:
        return split_body(mesh_sizes, *arguments)
    return general_body(*arguments)


def solution(mesh):
    placed = (
        P(None, ("ctx", "tp"), None),
        P(None, ("ctx", "tp"), None),
        P(),
        P("section", None),
        P("section", None, "tp", None, None),
        P("section", "tp", None),
        P("section", None),
        P("section", None, "tp", None),
        P("section", "tp", None),
    )
    mesh_sizes = tuple(mesh.shape[axis] for axis in ALL_AXES)
    return jax.shard_map(
        functools.partial(body, mesh_sizes),
        mesh=mesh,
        in_specs=placed,
        out_specs=(
            P("section", None, ("ctx", "tp"), None),
            P("section", None, ("ctx", "tp"), None),
            P("section", None),
            P("section", None, "tp", None, None),
            P("section", "tp", None),
            P("section", None),
            P("section", None, "tp", None),
            P("section", "tp", None),
        ),
        check_vma=False,
    )
```

```python
import functools

import jax
import jax.numpy as jnp
from jax import lax
from jax.experimental import pallas as pl
from jax.experimental.pallas import tpu as pltpu
from jax.sharding import PartitionSpec as P

HD = 64
EPSILON = 1e-06
MASKED = -1e30
ALL_AXES = ("section", "ctx", "tp")
CHUNK = 2
ONES = 16
LOG_2 = 0.6931471805599453
LIGHT = pl.CostEstimate(flops=1, bytes_accessed=1, transcendentals=0)
VMEM_LIMIT = 40 * 1024 * 1024


def shifted(block, axis, distance):
    devices = range(lax.axis_size(axis))
    route = [(i - distance, i) for i in devices if i - distance in devices]
    return lax.ppermute(block, axis, route)


def rope_parts(position):
    half_width = HD // 2
    frequency = jnp.exp(-jnp.log(10000.0) * jnp.arange(half_width, dtype=jnp.float32) / half_width)
    angles = position.astype(jnp.float32)[:, None] * frequency[None, :]
    return (jnp.cos(angles), jnp.sin(angles))


def rotate(vectors, cosine, sine_part):
    half_width = HD // 2
    leading_half = vectors[..., :half_width]
    trailing_half = vectors[..., half_width:]
    cosine = cosine[:, None, :]
    sine_part = sine_part[:, None, :]
    return jnp.concatenate(
        [
            leading_half * cosine - trailing_half * sine_part,
            trailing_half * cosine + leading_half * sine_part,
        ],
        axis=-1,
    )


def rotate_back(vectors, cosine, sine_part):
    half_width = HD // 2
    leading_half = vectors[..., :half_width]
    trailing_half = vectors[..., half_width:]
    cosine = cosine[:, None, :]
    sine_part = sine_part[:, None, :]
    return jnp.concatenate(
        [
            leading_half * cosine + trailing_half * sine_part,
            trailing_half * cosine - leading_half * sine_part,
        ],
        axis=-1,
    )


def inner_rows(left, right):
    return lax.dot_general(
        left, right, (((0,), (0,)), ((), ())), preferred_element_type=jnp.float32
    )


def outer_cols(left, right):
    return lax.dot_general(
        left, right, (((1,), (1,)), ((), ())), preferred_element_type=jnp.float32
    )


def spread(row_block):
    return lax.all_gather(row_block, "tp", axis=0, tiled=True)


def collect(partial_value):
    return lax.psum_scatter(
        partial_value.astype(jnp.bfloat16), "tp", scatter_dimension=0, tiled=True
    ).astype(jnp.float32)


def fetch_keys(key_value):
    return lax.all_gather(key_value, "ctx", axis=0, tiled=True)


def query_bounds(seq_lengths, block_first, row_count):
    token_index = block_first + jnp.arange(row_count, dtype=jnp.int32)
    doc_ends = jnp.cumsum(seq_lengths)
    before = (doc_ends[None, :] <= token_index[:, None]).astype(jnp.int32)
    doc_start = jnp.sum(before * seq_lengths[None, :], axis=1)
    return (token_index, doc_start)


def block_scores(query_heads, pair_block, block_first, token_index, doc_start, head_width):
    row_count = pair_block.shape[0]
    key_heads = pair_block[:, :head_width].reshape(row_count, head_width // HD, HD)
    value_heads = pair_block[:, head_width:].reshape(row_count, head_width // HD, HD)
    scores = jnp.einsum(
        "qhd,khd->hqk", query_heads, key_heads, preferred_element_type=jnp.float32
    ) * HD ** (-0.5)
    key_index = block_first + jnp.arange(row_count, dtype=jnp.int32)
    allowed = (key_index[None, :] >= doc_start[:, None]) & (
        key_index[None, :] <= token_index[:, None]
    )
    return (scores, allowed[None], key_heads, value_heads)


def split_blocks(pairs_all, row_count):
    blocks = pairs_all.reshape(-1, row_count, pairs_all.shape[1])
    block_starts = jnp.arange(blocks.shape[0], dtype=jnp.int32) * row_count
    return (blocks, block_starts)


def attend(query_heads, pairs_all, token_index, doc_start, head_width):
    row_count = query_heads.shape[0]
    head_count = head_width // HD
    blocks, block_starts = split_blocks(pairs_all, row_count)
    last_query = token_index[row_count - 1]
    first_query = doc_start[0]

    def rowmax_live(carried, block_parts):
        running_top, running_sum = carried
        scores, allowed, unused_keys, unused_values = block_scores(
            query_heads, block_parts[0], block_parts[1], token_index, doc_start, head_width
        )
        masked = jnp.where(allowed, scores, -1e30)
        new_top = jnp.maximum(running_top, jnp.max(masked, axis=-1))
        running_sum = running_sum * jnp.exp(running_top - new_top) + jnp.sum(
            jnp.where(allowed, jnp.exp(masked - new_top[..., None]), 0.0), axis=-1
        )
        return (new_top, running_sum)

    def rowmax_step(carried, block_parts):
        live = (block_parts[1] <= last_query) & (block_parts[1] + row_count > first_query)
        return (
            lax.cond(live, lambda held: rowmax_live(held, block_parts), lambda held: held, carried),
            None,
        )

    initial = (
        jnp.full((head_count, row_count), -1e30, jnp.float32),
        jnp.zeros((head_count, row_count), jnp.float32),
    )
    (running_top, running_sum), unused = lax.scan(rowmax_step, initial, (blocks, block_starts))
    log_total = running_top + jnp.log(running_sum)

    def output_live(accumulated, block_parts):
        scores, allowed, unused_keys, value_heads = block_scores(
            query_heads, block_parts[0], block_parts[1], token_index, doc_start, head_width
        )
        soft_weights = jnp.where(allowed, jnp.exp(scores - log_total[..., None]), 0.0).astype(
            jnp.bfloat16
        )
        return accumulated + jnp.einsum(
            "hqk,khd->qhd", soft_weights, value_heads, preferred_element_type=jnp.float32
        )

    def output_step(accumulated, block_parts):
        live = (block_parts[1] <= last_query) & (block_parts[1] + row_count > first_query)
        return (
            lax.cond(
                live, lambda held: output_live(held, block_parts), lambda held: held, accumulated
            ),
            None,
        )

    accumulated, unused = lax.scan(
        output_step, jnp.zeros((row_count, head_count, HD), jnp.float32), (blocks, block_starts)
    )
    return (accumulated, log_total)


def attend_back(
    query_heads, pairs_all, token_index, doc_start, head_width, log_total, accumulated, grad_heads
):
    row_count = query_heads.shape[0]
    head_count = head_width // HD
    blocks, block_starts = split_blocks(pairs_all, row_count)
    last_query = token_index[row_count - 1]
    first_query = doc_start[0]
    rowdot = jnp.sum(grad_heads.astype(jnp.float32) * accumulated, axis=-1).T

    def grad_live(grad_acc, block_parts):
        scores, allowed, key_heads, value_heads = block_scores(
            query_heads, block_parts[0], block_parts[1], token_index, doc_start, head_width
        )
        soft_weights = jnp.where(allowed, jnp.exp(scores - log_total[..., None]), 0.0)
        grad_soft = jnp.einsum(
            "qhd,khd->hqk", grad_heads, value_heads, preferred_element_type=jnp.float32
        )
        grad_scores = (soft_weights * (grad_soft - rowdot[..., None])).astype(jnp.bfloat16)
        grad_acc = grad_acc + jnp.einsum(
            "hqk,khd->qhd", grad_scores, key_heads, preferred_element_type=jnp.float32
        )
        grad_keys = jnp.einsum(
            "hqk,qhd->khd", grad_scores, query_heads, preferred_element_type=jnp.float32
        ) * HD ** (-0.5)
        grad_values = jnp.einsum(
            "hqk,qhd->khd",
            soft_weights.astype(jnp.bfloat16),
            grad_heads,
            preferred_element_type=jnp.float32,
        )
        return (grad_acc, (grad_keys, grad_values))

    def grad_skip(grad_acc):
        empty = jnp.zeros((row_count, head_count, HD), jnp.float32)
        return (grad_acc, (empty, empty))

    def grad_step(grad_acc, block_parts):
        live = (block_parts[1] <= last_query) & (block_parts[1] + row_count > first_query)
        return lax.cond(live, lambda held: grad_live(held, block_parts), grad_skip, grad_acc)

    grad_query, (grad_keys, grad_values) = lax.scan(
        grad_step, jnp.zeros((row_count, head_count, HD), jnp.float32), (blocks, block_starts)
    )
    grad_query = grad_query * HD ** (-0.5)
    grad_pairs = jnp.concatenate(
        [grad_keys.reshape(-1, head_width), grad_values.reshape(-1, head_width)], axis=1
    )
    return (grad_query, grad_pairs)


def norm_back(whole_rows, scale_rows, gain, grad_normed, grad_rest):
    unit_rows = whole_rows * scale_rows
    scaled = grad_normed * gain.astype(jnp.float32)
    grad_gain = jnp.sum(grad_normed * unit_rows, axis=0)
    grad_whole = grad_rest + scale_rows * (
        scaled - unit_rows * jnp.mean(scaled * unit_rows, axis=-1, keepdims=True)
    )
    return (grad_gain, grad_whole)


def layer_forward(row_block, first_values, value_mix, weights, seq_lengths):
    gain_first, w_qkv, w_out, gain_second, w_gateup, w_down = weights
    head_count = w_qkv.shape[1]
    head_width = head_count * HD
    model_width = row_block.shape[1]
    whole_rows = row_block.astype(jnp.float32)
    scale_first = lax.rsqrt(jnp.mean(whole_rows * whole_rows, axis=-1, keepdims=True) + EPSILON)
    normed = (whole_rows * scale_first * gain_first.astype(jnp.float32)).astype(jnp.bfloat16)
    normed_all = spread(normed)
    row_count = normed_all.shape[0]
    projected = outer_cols(normed_all, w_qkv.reshape(3 * head_width, model_width))
    token_index, doc_start = query_bounds(seq_lengths, lax.axis_index("ctx") * row_count, row_count)
    cosine, sine_part = rope_parts(token_index - doc_start)
    query_heads = rotate(
        projected[:, :head_width].reshape(row_count, head_count, HD), cosine, sine_part
    ).astype(jnp.bfloat16)
    key_heads = rotate(
        projected[:, head_width : 2 * head_width].reshape(row_count, head_count, HD),
        cosine,
        sine_part,
    ).astype(jnp.bfloat16)
    mixed = (
        (1.0 - value_mix) * projected[:, 2 * head_width :]
        + value_mix * first_values.astype(jnp.float32)
    ).astype(jnp.bfloat16)
    key_value = jnp.concatenate([key_heads.reshape(row_count, head_width), mixed], axis=1)
    pairs_all = fetch_keys(key_value)
    accumulated, log_total = attend(query_heads, pairs_all, token_index, doc_start, head_width)
    attended = accumulated.reshape(row_count, head_width).astype(jnp.bfloat16)
    hidden = whole_rows + collect(jnp.dot(attended, w_out, preferred_element_type=jnp.float32))
    scale_second = lax.rsqrt(jnp.mean(hidden * hidden, axis=-1, keepdims=True) + EPSILON)
    normed_second = (hidden * scale_second * gain_second.astype(jnp.float32)).astype(jnp.bfloat16)
    ffn_rows = spread(normed_second)
    gate_up = outer_cols(ffn_rows, w_gateup.reshape(-1, model_width))
    unit_count = gate_up.shape[1] // 2
    gate_part = gate_up[:, :unit_count]
    up_part = gate_up[:, unit_count:]
    activated = (jax.nn.silu(gate_part) * up_part).astype(jnp.bfloat16)
    down_part = jnp.dot(activated, w_down, preferred_element_type=jnp.float32)
    branch_out = collect(down_part)
    layer_out = (hidden + branch_out).astype(jnp.bfloat16)
    saved = (
        whole_rows,
        scale_first,
        normed_all,
        query_heads,
        pairs_all,
        token_index,
        doc_start,
        cosine,
        sine_part,
        log_total,
        accumulated,
        attended,
        hidden,
        scale_second,
        ffn_rows,
        gate_part,
        up_part,
        activated,
    )
    return (layer_out, mixed, pairs_all, saved)


def layer_backward(grad_rows, extra_values, value_mix, weights, saved):
    gain_first, w_qkv, w_out, gain_second, w_gateup, w_down = weights
    (
        whole_rows,
        scale_first,
        normed_all,
        query_heads,
        pairs_all,
        token_index,
        doc_start,
        cosine,
        sine_part,
        log_total,
        accumulated,
        attended,
        hidden,
        scale_second,
        ffn_rows,
        gate_part,
        up_part,
        activated,
    ) = saved
    model_width = whole_rows.shape[1]
    head_count = w_qkv.shape[1]
    head_width = head_count * HD
    row_count = normed_all.shape[0]
    grad_hidden = grad_rows.astype(jnp.float32)
    grad_down = spread(grad_rows)
    grad_wd = inner_rows(activated, grad_down)
    grad_act = outer_cols(grad_down, w_down)
    sigmoid_gate = jax.nn.sigmoid(gate_part)
    grad_gate = grad_act * up_part * sigmoid_gate * (1.0 + gate_part * (1.0 - sigmoid_gate))
    grad_up = grad_act * gate_part * sigmoid_gate
    grad_gate_up = jnp.concatenate([grad_gate, grad_up], axis=1).astype(jnp.bfloat16)
    grad_wgu = inner_rows(grad_gate_up, ffn_rows).reshape(w_gateup.shape)
    back_second = jnp.dot(
        grad_gate_up, w_gateup.reshape(-1, model_width), preferred_element_type=jnp.float32
    )
    grad_normed_second = collect(back_second)
    grad_gain2, grad_hidden = norm_back(
        hidden, scale_second, gain_second, grad_normed_second, grad_hidden
    )
    grad_branch_all = spread(grad_hidden.astype(jnp.bfloat16))
    grad_wo = inner_rows(attended, grad_branch_all)
    grad_heads = (
        outer_cols(grad_branch_all, w_out).astype(jnp.bfloat16).reshape(row_count, head_count, HD)
    )
    grad_query, grad_pairs_all = attend_back(
        query_heads,
        pairs_all,
        token_index,
        doc_start,
        head_width,
        log_total,
        accumulated,
        grad_heads,
    )
    grad_pairs = lax.psum_scatter(
        grad_pairs_all.astype(jnp.bfloat16), "ctx", scatter_dimension=0, tiled=True
    ).astype(jnp.float32)
    grad_mixed = grad_pairs[:, head_width:] + extra_values.astype(jnp.float32)
    grad_keys = rotate_back(
        grad_pairs[:, :head_width].reshape(row_count, head_count, HD), cosine, sine_part
    )
    grad_query = rotate_back(grad_query, cosine, sine_part)
    grad_projected = jnp.concatenate(
        [
            grad_query.reshape(row_count, head_width),
            grad_keys.reshape(row_count, head_width),
            (1.0 - value_mix) * grad_mixed,
        ],
        axis=1,
    ).astype(jnp.bfloat16)
    send_values = (value_mix * grad_mixed).astype(jnp.bfloat16)
    grad_wqkv = inner_rows(grad_projected, normed_all).reshape(w_qkv.shape)
    grad_normed = collect(
        jnp.dot(
            grad_projected,
            w_qkv.reshape(3 * head_width, model_width),
            preferred_element_type=jnp.float32,
        )
    )
    grad_gain1, grad_whole = norm_back(
        whole_rows, scale_first, gain_first, grad_normed, grad_hidden
    )
    return (
        grad_whole,
        send_values,
        (grad_gain1, grad_wqkv, grad_wo, grad_gain2, grad_wgu, grad_wd),
    )


def general_body(inputs, cotangent, lengths, gain1, wqkv, wo, gain2, wgu, wd):
    section_index = lax.axis_index("section")
    leading = section_index == 0
    value_mix = jnp.where(leading, 0.0, 0.5).astype(jnp.float32)
    micro_count = inputs.shape[0]
    local_rows = inputs.shape[1]
    model_width = inputs.shape[2]
    head_width = wqkv.shape[2] * HD
    row_count = local_rows * lax.axis_size("tp")
    gateup_use, down_use = (wgu[0], wd[0])
    weights = (gain1[0], wqkv[0], wo[0], gain2[0], gateup_use, down_use)
    recv_rows = jnp.zeros((local_rows, model_width), jnp.bfloat16)
    recv_values = jnp.zeros((row_count, head_width), jnp.bfloat16)
    states = []
    outputs = []
    for turn_index in range(micro_count + 1):
        own_rows = inputs[min(turn_index, micro_count - 1)]
        row_block = jnp.where(leading, own_rows, recv_rows)
        seq_lengths = jnp.where(
            leading, lengths[min(turn_index, micro_count - 1)], lengths[max(turn_index - 1, 0)]
        )
        layer_out, mixed, pairs_all, unused = layer_forward(
            row_block, recv_values, value_mix, weights, seq_lengths
        )
        kept_pairs = None
        states.append((row_block, recv_values, seq_lengths, kept_pairs))
        outputs.append(layer_out)
        if turn_index < micro_count:
            recv_rows, recv_values = shifted((layer_out, mixed), "section", 1)
    grad_rows_in = jnp.zeros((local_rows, model_width), jnp.bfloat16)
    grad_values_in = jnp.zeros((row_count, head_width), jnp.bfloat16)
    totals = None
    turn_grads = []
    for turn_index in range(micro_count + 1):
        row_block, first_values, seq_lengths, kept_pairs = states[micro_count - turn_index]
        if turn_index < micro_count:
            fed_grad = cotangent[micro_count - 1 - turn_index]
        else:
            fed_grad = jnp.zeros_like(cotangent[0])
        grad_out = jnp.where(leading, grad_rows_in, fed_grad)
        unused_out, unused_mixed, unused_pairs, saved = layer_forward(
            row_block, first_values, value_mix, weights, seq_lengths
        )
        grad_whole, send_values, grads = layer_backward(
            grad_out, grad_values_in, value_mix, weights, saved
        )
        totals = grads if totals is None else jax.tree.map(jnp.add, totals, grads)
        sent_rows = grad_whole.astype(jnp.bfloat16)
        turn_grads.append(jnp.where(leading, grad_whole, sent_rows.astype(jnp.float32)))
        if turn_index < micro_count:
            grad_rows_in, grad_values_in = shifted((sent_rows, send_values), "section", -1)
    grad_gain1, grad_wqkv, grad_wo, grad_gain2, grad_wgu, grad_wd = totals
    grad_wqkv, grad_wo, grad_wgu, grad_wd = (
        lax.psum(grad_wqkv.astype(jnp.bfloat16), "ctx").astype(jnp.float32),
        lax.psum(grad_wo.astype(jnp.bfloat16), "ctx").astype(jnp.float32),
        lax.psum(grad_wgu.astype(jnp.bfloat16), "ctx").astype(jnp.float32),
        lax.psum(grad_wd.astype(jnp.bfloat16), "ctx").astype(jnp.float32),
    )
    grad_gain1, grad_gain2 = lax.psum((grad_gain1, grad_gain2), ("ctx", "tp"))
    acts = jnp.stack(
        [
            jnp.where(leading, outputs[batch_index], outputs[batch_index + 1])
            for batch_index in range(micro_count)
        ]
    )[None]
    input_grads = jnp.stack(
        [
            jnp.where(
                leading,
                turn_grads[micro_count - batch_index],
                turn_grads[micro_count - 1 - batch_index],
            )
            for batch_index in range(micro_count)
        ]
    )[None]
    return (
        acts,
        input_grads,
        grad_gain1[None],
        grad_wqkv[None],
        grad_wo[None],
        grad_gain2[None],
        grad_wgu[None],
        grad_wd[None],
    )


def device_groups(mesh_sizes, key, order):
    sections, contexts, parts = mesh_sizes
    groups = {}
    for section in range(sections):
        for ctx in range(contexts):
            for tp in range(parts):
                place = (section, ctx, tp)
                number = (section * contexts + ctx) * parts + tp
                groups.setdefault(key(*place), []).append((order(*place), number))
    return [[number for _, number in sorted(members)] for _, members in sorted(groups.items())]


def exchange(value, groups):
    return lax.all_to_all(
        value, ALL_AXES, split_axis=0, concat_axis=0, tiled=True, axis_index_groups=groups
    )


def document_bounds(ends_ref, index):
    start = jnp.zeros_like(index)
    for entry in range(ends_ref.shape[0]):
        end = ends_ref[entry]
        start = jnp.where(index >= end, end, start)
    return start


def scalar_start(ends_ref, index):
    start = jnp.int32(0)
    for entry in range(ends_ref.shape[0]):
        start = jnp.where(index >= ends_ref[entry], ends_ref[entry], start)
    return start


def scalar_end(ends_ref, index):
    end = ends_ref[ends_ref.shape[0] - 1]
    for entry in range(ends_ref.shape[0] - 2, -1, -1):
        end = jnp.where(index < ends_ref[entry], ends_ref[entry], end)
    return end


def dot(left, right, left_dim, right_dim):
    return lax.dot_general(
        left, right, (((left_dim,), (right_dim,)), ((), ())), preferred_element_type=jnp.float32
    )


def fold_rows(value, combine):
    rows, width = value.shape
    return combine(value.reshape(rows // 8, 8, width), axis=0)


def block_place(block, parts, width):
    entry = (block // (2 * parts)) * parts + block % parts
    return entry, pl.ds(pl.multiple_of((block // parts % 2) * width, width), width)


def attention_forward_kernel(parts, ends_ref, qkv_ref, out_ref, lse_ref, keys_ref, values_ref):
    program = pl.program_id(0)
    blocks, block_width = 2 * qkv_ref.shape[0], qkv_ref.shape[2] // 2
    width = CHUNK * block_width

    @pl.when(program == 0)
    def _():
        def turn(j, carry):
            entry, columns = block_place(j, parts, block_width)
            keys_ref[j] = qkv_ref[entry, HD : 2 * HD, columns].T
            values_ref[j, 0:HD, :] = qkv_ref[entry, 2 * HD : 3 * HD, columns]
            values_ref[j, HD : HD + ONES, :] = jnp.ones((ONES, block_width), jnp.bfloat16)
            return carry

        lax.fori_loop(0, blocks, turn, 0)

    query = []
    for block in range(CHUNK):
        entry, columns = block_place(program * CHUNK + block, parts, block_width)
        query.append(qkv_ref[entry, 0:HD, columns])
    query = jnp.concatenate(query, axis=1)
    first = program * width
    query_index = first + lax.broadcasted_iota(jnp.int32, (1, width), 1)
    start = document_bounds(ends_ref, query_index)
    low_chunk = scalar_start(ends_ref, first) // width
    high_start = scalar_start(ends_ref, first + width - 1)
    middle = jnp.clip((high_start + width - 1) // width, low_chunk, program)

    def step(chunk, carry, masked):
        top, acc = carry
        parts = []
        for entry in range(CHUNK):
            j = chunk * CHUNK + entry
            scores = dot(keys_ref[j], query, 1, 0)
            if masked:
                key_index = j * block_width + lax.broadcasted_iota(jnp.int32, (block_width, 1), 0)
                allowed = (key_index >= start) & (key_index <= query_index)
                scores = jnp.where(allowed, scores, MASKED)
            parts.append(scores)
        part_top = functools.reduce(jnp.maximum, [fold_rows(part, jnp.max) for part in parts])
        new_top = jnp.maximum(top, jnp.max(part_top, axis=0, keepdims=True))
        acc = acc * jnp.exp2(top - new_top)
        for entry in range(CHUNK):
            weights = jnp.exp2(parts[entry] - new_top).astype(jnp.bfloat16)
            acc = acc + dot(values_ref[chunk * CHUNK + entry], weights, 1, 0)
        return new_top, acc

    carry = (
        jnp.full((1, width), MASKED, jnp.float32),
        jnp.zeros((HD + ONES, width), jnp.float32),
    )
    carry = lax.fori_loop(low_chunk, middle, functools.partial(step, masked=True), carry)
    carry = lax.fori_loop(middle, program, functools.partial(step, masked=False), carry)
    top, acc = step(program, carry, True)
    total = acc[HD : HD + 1]
    out = (acc[:HD] / total).astype(jnp.bfloat16)
    lse = top + jnp.log2(total)
    for entry in range(CHUNK):
        columns = slice(entry * block_width, (entry + 1) * block_width)
        out_ref[entry] = out[:, columns]
        lse_ref[entry] = lse[:, columns]


def attention_forward(ends, qkv, parts):
    blocks, width = 2 * qkv.shape[0], qkv.shape[2] // 2
    return pl.pallas_call(
        functools.partial(attention_forward_kernel, parts),
        grid_spec=pltpu.PrefetchScalarGridSpec(
            num_scalar_prefetch=1,
            grid=(blocks // CHUNK,),
            in_specs=[pl.BlockSpec(qkv.shape, lambda i, ends_ref: (0, 0, 0))],
            out_specs=[
                pl.BlockSpec((CHUNK, HD, width), lambda i, ends_ref: (i, 0, 0)),
                pl.BlockSpec((CHUNK, 1, width), lambda i, ends_ref: (i, 0, 0)),
            ],
            scratch_shapes=[
                pltpu.VMEM((blocks, width, HD), jnp.bfloat16),
                pltpu.VMEM((blocks, HD + ONES, width), jnp.bfloat16),
            ],
        ),
        out_shape=[
            jax.ShapeDtypeStruct((blocks, HD, width), jnp.bfloat16),
            jax.ShapeDtypeStruct((blocks, 1, width), jnp.float32),
        ],
        compiler_params=pltpu.CompilerParams(vmem_limit_bytes=VMEM_LIMIT),
        cost_estimate=LIGHT,
        name="attention_forward",
    )(ends, qkv)


def attention_backward_kernel(
    parts, ends_ref, qkv_ref, out_ref, grad_ref, lse_ref, result_ref,
    query_grad_ref, delta_ref, queries_ref, grads_ref, lses_ref,
):
    program = pl.program_id(0)
    blocks, block_width = 2 * qkv_ref.shape[0], qkv_ref.shape[2] // 2
    width = CHUNK * block_width

    @pl.when(program == 0)
    def _():
        def turn(i, carry):
            for entry in range(CHUNK):
                block = i * CHUNK + entry
                columns = slice(entry * block_width, (entry + 1) * block_width)
                grad = grad_ref[block]
                place, tokens = block_place(block, parts, block_width)
                queries_ref[i, :, columns] = qkv_ref[place, 0:HD, tokens]
                grads_ref[i, :, columns] = grad
                lses_ref[i, :, columns] = lse_ref[block]
                delta_ref[i, :, columns] = jnp.sum(
                    grad.astype(jnp.float32) * out_ref[block].astype(jnp.float32),
                    axis=0,
                    keepdims=True,
                )
            query_grad_ref[i] = jnp.zeros((HD, width), jnp.float32)
            return carry

        lax.fori_loop(0, blocks // CHUNK, turn, 0)

    own_places = [
        block_place(program * CHUNK + block, parts, block_width) for block in range(CHUNK)
    ]

    def joined(low_row, high_row):
        return jnp.concatenate(
            [qkv_ref[place, low_row:high_row, tokens] for place, tokens in own_places], axis=1
        )

    first = program * width
    keys_t = joined(HD, 2 * HD)
    keys = keys_t.T
    values = joined(2 * HD, 3 * HD).T
    key_index = first + lax.broadcasted_iota(jnp.int32, (width, 1), 0)
    near_end = scalar_end(ends_ref, first)
    far_end = scalar_end(ends_ref, first + width - 1)
    stop = (far_end - 1) // width + 1
    middle = jnp.clip(near_end // width, program + 1, stop)

    def step(i, carry, masked):
        key_grad, value_grad = carry
        query = queries_ref[i]
        grad = grads_ref[i]
        weights = jnp.exp2(dot(keys, query, 1, 0) - lses_ref[i])
        if masked:
            query_index = i * width + lax.broadcasted_iota(jnp.int32, (1, width), 1)
            start = document_bounds(ends_ref, query_index)
            allowed = (key_index >= start) & (key_index <= query_index)
            weights = jnp.where(allowed, weights, 0.0)
        grad_weights = dot(values, grad, 1, 0)
        grad_scores = (weights * (grad_weights - delta_ref[i])).astype(jnp.bfloat16)
        query_grad_ref[i] += dot(keys_t, grad_scores, 1, 0)
        value_grad = value_grad + dot(grad, weights.astype(jnp.bfloat16), 1, 1)
        key_grad = key_grad + dot(query, grad_scores, 1, 1)
        return key_grad, value_grad

    empty = jnp.zeros((HD, width), jnp.float32)
    carry = step(program, (empty, empty), True)
    carry = lax.fori_loop(program + 1, middle, functools.partial(step, masked=False), carry)
    key_grad, value_grad = lax.fori_loop(middle, stop, functools.partial(step, masked=True), carry)
    query_grad = query_grad_ref[program] * HD ** (-0.5)
    key_grad = key_grad * LOG_2
    for block, (place, tokens) in enumerate(own_places):
        columns = slice(block * block_width, (block + 1) * block_width)
        result_ref[place, 0:HD, tokens] = query_grad[:, columns].astype(jnp.bfloat16)
        result_ref[place, HD : 2 * HD, tokens] = key_grad[:, columns].astype(jnp.bfloat16)
        result_ref[place, 2 * HD : 3 * HD, tokens] = value_grad[:, columns].astype(jnp.bfloat16)


def attention_backward(ends, qkv, out, grad, lse, parts):
    blocks, block_width = 2 * qkv.shape[0], qkv.shape[2] // 2
    chunks, width = blocks // CHUNK, CHUNK * block_width

    def whole(value):
        return pl.BlockSpec(value.shape, lambda i, ends_ref: (0, 0, 0))

    return pl.pallas_call(
        functools.partial(attention_backward_kernel, parts),
        grid_spec=pltpu.PrefetchScalarGridSpec(
            num_scalar_prefetch=1,
            grid=(chunks,),
            in_specs=[whole(qkv), whole(out), whole(grad), whole(lse)],
            out_specs=whole(qkv),
            scratch_shapes=[
                pltpu.VMEM((chunks, HD, width), jnp.float32),
                pltpu.VMEM((chunks, 1, width), jnp.float32),
                pltpu.VMEM((chunks, HD, width), jnp.bfloat16),
                pltpu.VMEM((chunks, HD, width), jnp.bfloat16),
                pltpu.VMEM((chunks, 1, width), jnp.float32),
            ],
        ),
        out_shape=jax.ShapeDtypeStruct(qkv.shape, jnp.bfloat16),
        compiler_params=pltpu.CompilerParams(vmem_limit_bytes=VMEM_LIMIT),
        cost_estimate=LIGHT,
        name="attention_backward",
    )(ends, qkv, out, grad, lse)


def rope_pair(leading_half, trailing_half, cosine, sine_part):
    return (
        leading_half * cosine - trailing_half * sine_part,
        trailing_half * cosine + leading_half * sine_part,
    )


def low(value):
    return value.astype(jnp.bfloat16)


def wide(value):
    return value.astype(jnp.float32)


def whole_block(value):
    zeros = (0,) * value.ndim
    return pl.BlockSpec(value.shape, lambda *_: zeros)


def feed_forward_kernel(rows_ref, gate_w_ref, up_w_ref, down_w_ref, gate_ref, up_ref, act_ref, sum_ref):
    rows = rows_ref[...]
    gate = dot(gate_w_ref[...], rows, 1, 1)
    up = dot(up_w_ref[...], rows, 1, 1)
    active = (gate * jax.nn.sigmoid(gate) * up).astype(jnp.bfloat16)
    gate_ref[...] = gate.astype(jnp.bfloat16)
    up_ref[...] = up.astype(jnp.bfloat16)
    act_ref[...] = active

    @pl.when(pl.program_id(0) == 0)
    def _():
        sum_ref[...] = jnp.zeros_like(sum_ref)

    sum_ref[...] += dot(active, down_w_ref[...], 0, 0)


def feed_forward(rows, w_gate, w_up, w_down, tile):
    units, width = w_gate.shape
    count = rows.shape[0]
    weight = pl.BlockSpec((tile, width), lambda i: (i, 0))
    column = pl.BlockSpec((tile, count), lambda i: (i, 0))
    hidden = jax.ShapeDtypeStruct((units, count), jnp.bfloat16)
    return pl.pallas_call(
        feed_forward_kernel,
        grid=(units // tile,),
        in_specs=[whole_block(rows), weight, weight, weight],
        out_specs=[column, column, column, pl.BlockSpec((count, width), lambda i: (0, 0))],
        out_shape=[hidden, hidden, hidden, jax.ShapeDtypeStruct((count, width), jnp.float32)],
        compiler_params=pltpu.CompilerParams(vmem_limit_bytes=VMEM_LIMIT),
        cost_estimate=LIGHT,
        name="feed_forward",
    )(rows, w_gate, w_up, w_down)


def feed_forward_back_kernel(
    grad_ref, gate_ref, up_ref, gate_w_ref, up_w_ref, down_w_ref, grad_gate_ref, grad_up_ref, sum_ref
):
    grad_act = dot(down_w_ref[...], grad_ref[...], 1, 1)
    gate = gate_ref[...].astype(jnp.float32)
    up = up_ref[...].astype(jnp.float32)
    sigmoid_gate = jax.nn.sigmoid(gate)
    grad_gate = (grad_act * up * sigmoid_gate * (1.0 + gate * (1.0 - sigmoid_gate))).astype(
        jnp.bfloat16
    )
    grad_up = (grad_act * gate * sigmoid_gate).astype(jnp.bfloat16)
    grad_gate_ref[...] = grad_gate
    grad_up_ref[...] = grad_up

    @pl.when(pl.program_id(0) == 0)
    def _():
        sum_ref[...] = jnp.zeros_like(sum_ref)

    sum_ref[...] += dot(grad_gate, gate_w_ref[...], 0, 0) + dot(grad_up, up_w_ref[...], 0, 0)


def feed_forward_back(grad, gate, up, w_gate, w_up, w_down, tile):
    units, width = w_gate.shape
    count = grad.shape[0]
    weight = pl.BlockSpec((tile, width), lambda i: (i, 0))
    column = pl.BlockSpec((tile, count), lambda i: (i, 0))
    hidden = jax.ShapeDtypeStruct((units, count), jnp.bfloat16)
    return pl.pallas_call(
        feed_forward_back_kernel,
        grid=(units // tile,),
        in_specs=[whole_block(grad), column, column, weight, weight, weight],
        out_specs=[column, column, pl.BlockSpec((count, width), lambda i: (0, 0))],
        out_shape=[hidden, hidden, jax.ShapeDtypeStruct((count, width), jnp.float32)],
        compiler_params=pltpu.CompilerParams(vmem_limit_bytes=VMEM_LIMIT),
        cost_estimate=LIGHT,
        name="feed_forward_back",
    )(grad, gate, up, w_gate, w_up, w_down)


def half_products_kernel(layout, sizes, has_addend, which_ref, *refs):
    refs = list(refs)
    out_ref = refs.pop()
    addend_ref = refs.pop() if has_addend else None
    totals = [
        sum(dot(refs[left][...], refs[right][...], 1, 0) for left, right in pairs)
        for pairs in layout
    ]
    for piece in range(out_ref.shape[0]):
        parts = [
            total[piece * size : (piece + 1) * size] for total, size in zip(totals, sizes)
        ]
        value = jnp.concatenate(parts, axis=0) if len(parts) > 1 else parts[0]
        if has_addend:
            value = value + addend_ref[piece].astype(jnp.float32)
        out_ref[piece] = value.astype(jnp.bfloat16)


def half_products(which, groups, pieces, per_step, addend=None):
    lefts, rights, layout = [], [], []
    for group in groups:
        for left, right in group:
            if not any(left is known for known in lefts):
                lefts.append(left)
            if not any(right is known for known in rights):
                rights.append(right)
    find = lambda known, value: next(i for i, entry in enumerate(known) if entry is value)
    for group in groups:
        layout.append(
            tuple((find(lefts, left), len(lefts) + find(rights, right)) for left, right in group)
        )
    sizes = tuple(group[0][0].shape[0] // (2 * pieces) for group in groups)
    width = rights[0].shape[1]
    steps = pieces // per_step
    out_spec = pl.BlockSpec((per_step, sum(sizes), width), lambda i, which_ref: (i, 0, 0))
    left_specs = [
        pl.BlockSpec(
            (left.shape[0] // (2 * steps), left.shape[1]),
            lambda i, which_ref: (which_ref[0] * steps + i, 0),
        )
        for left in lefts
    ]
    extra = [] if addend is None else [addend]
    work = sum(left.size // 2 for left, _ in sum(groups, ()))
    return pl.pallas_call(
        functools.partial(half_products_kernel, tuple(layout), sizes, addend is not None),
        grid_spec=pltpu.PrefetchScalarGridSpec(
            num_scalar_prefetch=1,
            grid=(steps,),
            in_specs=left_specs + [whole_block(right) for right in rights] + [out_spec] * len(extra),
            out_specs=out_spec,
        ),
        out_shape=jax.ShapeDtypeStruct((pieces, sum(sizes), width), jnp.bfloat16),
        compiler_params=pltpu.CompilerParams(vmem_limit_bytes=VMEM_LIMIT),
        cost_estimate=LIGHT,
        name="half_products",
    )(which.reshape(1).astype(jnp.int32), *lefts, *rights, *extra)


def together(*values):
    return lax.optimization_barrier(values)


def after(value, *others):
    return lax.optimization_barrier((value, *others))[0]


def split_body(mesh_sizes, inputs, cotangent, lengths, gain1, wqkv, wo, gain2, wgu, wd):
    sections, contexts, parts = mesh_sizes
    half_parts = parts // 2
    section = lax.axis_index("section")
    ctx = lax.axis_index("ctx")
    tp = lax.axis_index("tp")
    row_side, column_side = ctx // 2, ctx % 2
    leading = section == 0
    batch = tp // half_parts
    model_width = inputs.shape[2]
    rows = inputs.shape[1]
    heads = wqkv.shape[2] * parts
    side_heads = heads // 2
    unit_rows = wd.shape[1] // contexts // 2
    head_rows = 3 * HD // 2
    out_rows = HD // 2
    half_width = HD // 2
    tile = 4 * unit_rows
    number = lambda s, c, t: (s * contexts + c) * parts + t
    places = [
        (s, c, t) for s in range(sections) for c in range(contexts) for t in range(parts)
    ]
    everyone = [[number(*place) for place in places]]
    token_of = lambda s, c, t: c * parts + t % half_parts + half_parts * s
    batch_groups = device_groups(mesh_sizes, lambda s, c, t: t // half_parts, token_of)
    head_groups = device_groups(
        mesh_sizes,
        lambda s, c, t: (c % 2, t // half_parts),
        lambda s, c, t: (c // 2, t % half_parts + half_parts * s),
    )
    side_groups = device_groups(mesh_sizes, lambda s, c, t: c % 2, lambda s, c, t: (s, c, t))
    crossing = [
        (number(s, c, t), number(s, c, (t + half_parts) % parts))
        for s, c, t in places
        if t // half_parts == s
    ]

    def to_batch(value):
        mine = lax.dynamic_index_in_dim(value, batch, 0, keepdims=False)
        other = lax.dynamic_index_in_dim(value, 1 - batch, 0, keepdims=False)
        moved = lax.ppermute(other, ALL_AXES, crossing)
        return jnp.where(section == batch, mine, moved)

    def to_home(value, layer):
        stay = [
            (number(s, c, t), number(layer, c, t)) for s, c, t in places if t // half_parts == s
        ]
        cross = [
            (number(s, c, t), number(layer, c, (t + half_parts) % parts))
            for s, c, t in places
            if t // half_parts != s
        ]
        return (lax.ppermute(value, ALL_AXES, stay), lax.ppermute(value, ALL_AXES, cross))

    def at_home(first_pair, second_pair):
        near = jnp.where(leading, first_pair[0], second_pair[0])
        far = jnp.where(leading, first_pair[1], second_pair[1])
        upper = batch == 0
        return jnp.stack([jnp.where(upper, near, far), jnp.where(upper, far, near)])[None]

    def swap_side(value):
        return lax.ppermute(value, "ctx", [(c, c ^ 1) for c in range(contexts)])

    def swap_far(value):
        return lax.ppermute(value, "ctx", [(c, c ^ 2) for c in range(contexts)])

    def swap_near(value):
        return lax.ppermute(value, "tp", [(t, t ^ 1) for t in range(parts)])

    def swap_half(value):
        return lax.ppermute(value, "tp", [(t, (t + half_parts) % parts) for t in range(parts)])

    def swap_section(value):
        return lax.ppermute(value, "section", [(0, 1), (1, 0)])

    def all_to_all(value, axis):
        return lax.all_to_all(value, axis, split_axis=0, concat_axis=0, tiled=True)

    def copies(value, count):
        return jnp.broadcast_to(value[None], (count, *value.shape))

    def gather(value, groups):
        return lax.all_gather(value, ALL_AXES, axis=0, tiled=True, axis_index_groups=groups)

    def ordered(index, own, other):
        return jnp.where(index == 0, own, other), jnp.where(index == 0, other, own)

    def by_core(value, which):
        return lax.dynamic_index_in_dim(value, which, 0, keepdims=False)

    def spread_line(piece):
        pair = jnp.stack(ordered(batch, piece, swap_half(piece)))
        line = jnp.stack(ordered(tp % 2, pair, swap_near(pair)), axis=1)
        return line.reshape(parts, *piece.shape)

    def spread_far(line):
        return line, swap_far(line)

    def spread_heads(pair):
        pair = jnp.stack(ordered(row_side, *pair))
        own_heads = pair[:, :, :head_rows].reshape(-1, model_width)
        own_outs = pair[:, :, head_rows:]
        return (own_heads, swap_section(own_heads)), (own_outs, swap_side(own_outs))

    def spread_outs(pair):
        own_outs = jnp.stack(ordered(column_side, *pair), axis=1).reshape(-1, model_width)
        return own_outs, swap_section(own_outs)

    def join_outs(pair):
        return jnp.concatenate(ordered(section, *pair), axis=0)

    def own_halves(value, axis, size):
        part = lax.dynamic_slice_in_dim(value, ctx * size, size, axis)
        return part.reshape(2, -1, model_width)

    packed = jnp.concatenate(
        [
            own_halves(wqkv[0], 1, heads // (parts * contexts)),
            own_halves(wo[0], 0, HD),
            own_halves(wgu[0, 0], 0, 2 * unit_rows),
            own_halves(wgu[0, 1], 0, 2 * unit_rows),
            own_halves(wd[0], 0, 2 * unit_rows),
        ],
        axis=1,
    )
    kept = by_core(packed, section)
    passed = swap_section(by_core(packed, 1 - section))
    pieces = ordered(section, kept, passed)
    attention_rows = head_rows + out_rows

    def feed_forward_weights(piece):
        whole = gather(piece[attention_rows:], side_groups)
        whole = whole.reshape(2 * 2 * parts, 3, unit_rows, model_width)
        return [whole[:, entry].reshape(-1, model_width) for entry in range(3)]

    rows_in = to_batch(inputs)
    line, rows_in = together(spread_line(pieces[0][:attention_rows]), rows_in)
    w_ffn = [feed_forward_weights(after(piece, line)) for piece in pieces]
    w_heads, w_outs = [None, None], [None, None]
    first_pair = spread_far(line)

    gains = wide(jnp.concatenate([gain1, gain2], axis=0))
    gain_sets = ordered(section, gains, swap_section(gains))

    seq_lengths = lax.dynamic_index_in_dim(lengths, batch, 0, keepdims=False)
    ends = jnp.cumsum(seq_lengths).astype(jnp.int32)
    token_index = jnp.concatenate(
        [
            token_of(section, 2 * row_side + side, tp) * rows + jnp.arange(rows, dtype=jnp.int32)
            for side in range(2)
        ]
    )
    before = (ends[None, :] <= token_index[:, None]).astype(jnp.int32)
    position = token_index - jnp.sum(before * seq_lengths[None, :], axis=1)
    frequency = jnp.exp(
        -jnp.log(10000.0) * jnp.arange(half_width, dtype=jnp.float32) / half_width
    )
    angles = position.astype(jnp.float32)[None, :] * frequency[:, None]
    cosine, sine_part = jnp.cos(angles), jnp.sin(angles)

    def head_halves(value):
        size = value.shape[1] // 2
        return value.reshape(heads, 2, size, rows).transpose(1, 0, 2, 3).reshape(2, -1, rows)

    def whole_heads(value):
        value = value.reshape(2, heads, -1, rows)
        return value.transpose(1, 0, 2, 3).reshape(heads, -1, rows)

    def nothing(value):
        return value

    def layer_forward(whole_rows, first_values, layer, in_zero, in_first, in_second, in_third, in_fourth):
        gain_first, gain_second = gain_sets[layer][0], gain_sets[layer][1]
        scale_first = lax.rsqrt(jnp.mean(whole_rows * whole_rows, axis=-1, keepdims=True) + EPSILON)
        normed = low(whole_rows * scale_first * gain_first)
        far_normed = in_zero(swap_side(normed))
        side_rows = jnp.concatenate(ordered(column_side, normed, far_normed), axis=0)
        halves = ordered(section, *[dot(weight, side_rows, 1, 1) for weight in w_heads[layer]])
        upper, lower = [half.reshape(side_heads, head_rows, 2 * rows) for half in halves]
        query = rope_pair(upper[:, :half_width], upper[:, half_width:HD], cosine, sine_part)
        key = rope_pair(upper[:, HD:], lower[:, :half_width], cosine, sine_part)
        value = lower[:, half_width:]
        if first_values is not None:
            value = 0.5 * value + 0.5 * wide(first_values)
        mixed = low(value)
        shrunk = [low(half * (HD ** (-0.5) / LOG_2)) for half in query]
        qkv = exchange(
            jnp.concatenate([*shrunk, low(key[0]), low(key[1]), mixed], axis=1), head_groups
        )
        qkv = in_first(qkv)
        out, lse = attention_forward(ends, qkv, parts)
        out = in_second(out)
        attended = head_halves(exchange(out, batch_groups))
        hidden = whole_rows + dot(attended.reshape(-1, rows), w_outs[layer], 0, 0)
        scale_second = lax.rsqrt(jnp.mean(hidden * hidden, axis=-1, keepdims=True) + EPSILON)
        normed_second = low(hidden * scale_second * gain_second)
        far_rows = swap_side(normed_second)
        near = feed_forward(normed_second, *w_ffn[layer], tile)
        far_rows = in_third(after(far_rows, near[3]))
        far = feed_forward(far_rows, *w_ffn[layer], tile)
        sent_down = low(far[3])

        def layer_out(*others):
            far_down = in_fourth(swap_side(after(sent_down, *others)))
            return low(hidden + (near[3] + wide(far_down)))

        saved = (
            whole_rows, scale_first, side_rows, qkv, out, lse, attended, hidden, scale_second,
            (normed_second, far_rows), near[:3], far[:3],
        )
        return layer_out, mixed, saved

    def norm_back(whole_rows, scale_rows, gain, grad_normed, grad_rest):
        unit = whole_rows * scale_rows
        scaled = grad_normed * gain
        grad_gain = jnp.sum(grad_normed * unit, axis=0)
        grad_whole = grad_rest + scale_rows * (
            scaled - unit * jnp.mean(scaled * unit, axis=-1, keepdims=True)
        )
        return grad_gain, grad_whole

    def pick(value, index, axis):
        return lax.dynamic_index_in_dim(value, index, axis, keepdims=False)

    def parted(value, index, axis):
        return pick(value, index, axis), pick(value, 1 - index, axis)

    def moved_pair(pair, swap):
        return pair[0], swap(pair[1])

    def halve(value, index, swap, axis):
        return moved_pair(parted(value, index, axis), swap)

    def add(pair):
        return low(wide(pair[0]) + wide(pair[1]))

    def near_parts(value):
        return parted(value.reshape(2, half_parts, *value.shape[1:]), tp % 2, 1)

    def near_sum(value):
        return moved_pair(near_parts(value), swap_near)

    def far_sum(pair):
        return halve(add(pair), batch, swap_half, 0)

    def layer_backward(grad_rows, extra_values, saved, layer, in_first, in_second, in_third, in_fourth, in_fifth):
        (
            whole_rows, scale_first, _, qkv, out, lse, attended, hidden, scale_second,
            ffn_rows, near, far,
        ) = saved
        gain_first, gain_second = gain_sets[layer][0], gain_sets[layer][1]
        grad_down = low(grad_rows)
        far_down = swap_side(grad_down)
        grad_gate, grad_up, near_back = feed_forward_back(grad_down, *near[:2], *w_ffn[layer], tile)
        far_down = in_first(after(far_down, near_back))
        far_gate, far_up, far_back = feed_forward_back(far_down, *far[:2], *w_ffn[layer], tile)
        far_back = swap_side(low(far_back))
        groups = (
            ((grad_gate, ffn_rows[0]), (far_gate, ffn_rows[1])),
            ((grad_up, ffn_rows[0]), (far_up, ffn_rows[1])),
            ((near[2], grad_down), (far[2], far_down)),
        )
        products = functools.partial(
            half_products, groups=groups, pieces=2 * parts, per_step=2
        )
        sent = products(1 - section)
        moved = swap_section(sent)
        far_back = in_second(after(far_back, sent))
        grad_gain2, grad_hidden = norm_back(
            hidden, scale_second, gain_second, near_back + wide(far_back), wide(grad_rows)
        )
        grad_branch = low(grad_hidden)
        grad_heads = whole_heads(low(dot(w_outs[layer], grad_branch, 1, 1)))
        grad_heads = exchange(grad_heads, batch_groups)
        rest = products(section, addend=moved)
        out_pair = (attended.reshape(-1, rows), grad_branch)
        grad_heads, rest = in_third(grad_heads, rest, out_pair)
        grad_qkv = attention_backward(ends, qkv, out, grad_heads, lse, parts)
        grad_qkv = in_fourth(grad_qkv)
        grad_qkv = in_fifth(exchange(grad_qkv, head_groups))
        grad_qkv = wide(grad_qkv)
        quarter = lambda entry: grad_qkv[:, entry * half_width : (entry + 1) * half_width]
        grad_query = rope_pair(quarter(0), quarter(1), cosine, -sine_part)
        grad_key = rope_pair(quarter(2), quarter(3), cosine, -sine_part)
        grad_value = grad_qkv[:, 2 * HD :]
        send_values = None
        if extra_values is None:
            grad_value = 0.5 * grad_value
            send_values = low(grad_value)
        else:
            grad_value = grad_value + wide(extra_values)
        upper = low(jnp.concatenate([*grad_query, grad_key[0]], axis=1))
        lower = low(jnp.concatenate([grad_key[1], grad_value], axis=1))
        grad_halves = jnp.stack([upper, lower]).reshape(2, -1, 2 * rows)
        return grad_halves, send_values, grad_hidden, out_pair, grad_gain2

    def input_grads_of(grad_halves, grad_hidden, saved, layer, beside):
        whole_rows, scale_first = saved[:2]
        places_of = (section, 1 - section)
        grad_side = sum(
            dot(by_core(grad_halves, place), weight, 0, 0)
            for place, weight in zip(places_of, w_heads[layer])
        ).reshape(2, rows, model_width)
        grad_far = swap_side(low(by_core(grad_side, 1 - column_side)))
        grad_normed = by_core(grad_side, column_side) + wide(beside(grad_far))
        return norm_back(whole_rows, scale_first, gain_sets[layer][0], grad_normed, grad_hidden)

    def piece_sum(value, groups):
        return lax.psum_scatter(
            value, ALL_AXES, scatter_dimension=0, tiled=True, axis_index_groups=groups
        )

    line_groups = device_groups(
        mesh_sizes, lambda s, c, t: (s, c % 2), lambda s, c, t: (c, t)
    )
    plane_shape = (2, 2, parts)
    pending = {}

    def weights_zero(value):
        value, pair = together(value, first_pair)
        w_heads[0], pending["outs"] = spread_heads(pair)
        return value

    def weights_line(value):
        value, piece = together(value, pieces[1][:attention_rows])
        pending["weights"] = spread_line(piece)
        return value

    def weights_outs_first(value):
        value, pending["outs"], w_ffn[0] = together(value, pending["outs"], w_ffn[0])
        w_outs[0] = join_outs(spread_outs(pending["outs"]))
        pending["grad_in"] = to_batch(after(cotangent, value))
        return value

    def weights_far(value):
        value, line = together(value, pending["weights"])
        pending["weights"] = spread_far(line)
        return value

    def weights_heads(value):
        value, pairs, pending["grad_in"] = together(value, pending["weights"], pending["grad_in"])
        w_heads[1], pending["outs"] = spread_heads(pairs)
        return value

    first_result, first_values, first_saved = layer_forward(
        wide(rows_in), None, 0,
        weights_zero, weights_line, weights_outs_first, weights_far, weights_heads,
    )

    first_out = first_result()

    def start_outs(value):
        value, outs, w_ffn[1] = together(value, pending["outs"], w_ffn[1])
        pending["outs"] = spread_outs(outs)
        return value

    def end_outs(value):
        value, outs = together(value, pending["outs"])
        w_outs[1] = join_outs(outs)
        pending["first_home"] = to_home(after(first_out, value), 0)
        return value

    second_result, _, second_saved = layer_forward(
        wide(first_out), first_values, 1, nothing, start_outs, end_outs, nothing, nothing
    )
    grad_in = pending["grad_in"]

    def out_sides(out_pair):
        products = functools.partial(half_products, groups=((out_pair,),), pieces=heads, per_step=8)
        out_sum = products(section, addend=swap_section(products(1 - section)))
        return parted(out_sum.reshape(*plane_shape, out_rows, model_width), column_side, 1)

    def second_third(value, rest, out_pair):
        value, rest = together(value, rest)
        rest = rest.reshape(-1, model_width)
        pending["second_rest"] = piece_sum(rest, line_groups)
        pending["second_out_rows"] = second_result(value)
        pending["out"] = out_sides(out_pair)
        value = after(value, pending["out"])
        pending["out"] = moved_pair(pending["out"], swap_side)
        return value, rest

    def second_fourth(value):
        value, pending["first_home"], second_out, out_sum = together(
            value, pending["first_home"], pending["second_out_rows"], pending["out"]
        )
        pending["second_home"] = to_home(second_out, 1)
        pending["second_out"] = add(out_sum).reshape(2 * parts, out_rows, model_width)
        return value

    grad_halves, send_values, grad_hidden, _, second_gain2 = layer_backward(
        grad_in, None, second_saved, 1, nothing, nothing, second_third, second_fourth, nothing
    )
    head_products = functools.partial(
        half_products,
        groups=(((grad_halves.reshape(-1, 2 * rows), second_saved[2]),),),
        pieces=side_heads,
        per_step=4,
    )

    def head_start(value):
        value, sent = together(value, head_products(1 - section))
        pending["moved"] = swap_section(sent)
        return value

    second_gain1, second_grad = input_grads_of(
        grad_halves, grad_hidden, second_saved, 1, head_start
    )
    second_grad = low(second_grad)

    def first_first(value):
        head = head_products(section, addend=pending["moved"])
        value, pending["head"] = together(value, head)
        return value

    def first_second(value):
        head = jnp.concatenate([pending["head"], pending["second_out"]], axis=1)
        head = parted(head.reshape(2, parts, -1, model_width), row_side, 0)
        value, head = together(value, head)
        pending["head"] = moved_pair(head, swap_far)
        pending["second_grad_home"] = to_home(after(second_grad, value), 1)
        return value

    def first_third(value, rest, out_pair):
        out_sum = out_sides(out_pair)
        rest = rest.reshape(2, parts, -1, model_width)
        rest_a = parted(rest[:, :, : 2 * unit_rows], row_side, 0)
        rest_b = parted(rest[:, :, 2 * unit_rows :], row_side, 0)
        value, rest_a, rest_b, out_sum, pending["second_rest"], pending["second_home"] = together(
            value, rest_a, rest_b, out_sum, pending["second_rest"], pending["second_home"]
        )
        pending["rest_a"] = moved_pair(rest_a, swap_far)
        pending["rest_b"] = rest_b
        pending["out"] = moved_pair(out_sum, swap_side)
        return value, rest

    def first_fourth(value):
        value, rest_a, rest_b, out_sum, head, pending["second_grad_home"] = together(
            value, pending["rest_a"], pending["rest_b"], pending["out"], pending["head"],
            pending["second_grad_home"],
        )
        pending["rest_b"] = moved_pair(rest_b, swap_far)
        pending["rest_a"] = add(rest_a)
        pending["out"] = halve(add(out_sum), row_side, swap_far, 0)
        pending["head"] = near_sum(add(head))
        return value

    def first_fifth(value):
        value, rest_a, rest_b, out_sum, head = together(
            value, pending["rest_a"], pending["rest_b"], pending["out"], pending["head"]
        )
        pending["out"] = add(out_sum)
        pending["head2"] = far_sum(head)
        pending["rest"] = near_sum(jnp.concatenate([rest_a, add(rest_b)], axis=1))
        return value

    first_halves, _, first_hidden, _, first_gain2 = layer_backward(
        second_grad, send_values, first_saved, 0,
        first_first, first_second, first_third, first_fourth, first_fifth,
    )
    head_products = functools.partial(
        half_products,
        groups=(((first_halves.reshape(-1, 2 * rows), first_saved[2]),),),
        pieces=side_heads,
        per_step=4,
    )
    sent = head_products(1 - section)
    moved = swap_section(sent)
    def head_end(value):
        head = head_products(section, addend=moved).reshape(2, parts, head_rows, model_width)
        value, head = together(value, parted(head, row_side, 0))
        pending["head"] = moved_pair(head, swap_far)
        return value

    first_gain1, first_grad = input_grads_of(
        after(first_halves, sent), first_hidden, first_saved, 0, head_end
    )
    def summed(value, swap):
        return value + swap(value)

    gain_rows = jnp.stack([first_gain1, first_gain2, second_gain1, second_gain2])
    gain_rows = summed(gain_rows, swap_section)
    head, rest, gain_rows, second_head, first_grad = together(
        pending["head"], pending["rest"], gain_rows, pending["head2"], low(first_grad)
    )
    head = near_sum(jnp.concatenate([add(head), pending["out"]], axis=1))
    rest = far_sum(rest)
    second = jnp.concatenate([pending["second_rest"], add(second_head)], axis=0)
    second = lax.all_gather(second, "ctx", axis=0, tiled=False)
    first_grad_home = to_home(first_grad, 0)
    gain_rows = summed(gain_rows, swap_side)
    head, gain_rows = together(head, gain_rows)
    head = far_sum(head)
    gain_rows = summed(gain_rows, swap_far)
    rest, first_grad_home, gain_rows = together(rest, first_grad_home, gain_rows)
    rest = all_to_all(copies(add(rest), contexts), "ctx")
    gain_rows = summed(gain_rows, swap_near)
    head, gain_rows = together(head, gain_rows)
    head = all_to_all(copies(add(head), contexts), "ctx")
    gain_total = summed(gain_rows, swap_half)
    rest, second = together(rest, second)
    first_grads = (rest, head)
    second_grads = (second[:, : 3 * unit_rows], second[:, 3 * unit_rows :])
    first_home, second_home = pending["first_home"], pending["second_home"]
    second_grad_home = pending["second_grad_home"]
    gain_total = jnp.where(leading, gain_total[:2], gain_total[2:])

    def finish(first, second):
        mine = jnp.where(leading, first, second)
        moved = swap_section(jnp.where(leading, second, first))
        return ordered(section, mine, moved)

    def joined(halves, first, count):
        both = jnp.stack([half[:, first : first + count] for half in halves], axis=1)
        return wide(both).reshape(-1, model_width)

    rest_grads = finish(first_grads[0], second_grads[0])
    grad_wgate, grad_wup, grad_wd = [
        joined(rest_grads, entry * unit_rows, unit_rows) for entry in range(3)
    ]
    head, grad_wgate, grad_wup, grad_wd = together(first_grads[1], grad_wgate, grad_wup, grad_wd)
    head_grads = finish(head, second_grads[1])
    grad_wqkv = joined(head_grads, 0, head_rows).reshape(contexts, 3, HD, model_width)
    grad_wo = joined(head_grads, head_rows, out_rows)
    return (
        at_home(first_home, second_home),
        wide(at_home(first_grad_home, second_grad_home)),
        gain_total[0:1],
        grad_wqkv.transpose(1, 0, 2, 3)[None],
        grad_wo[None],
        gain_total[1:2],
        jnp.stack([grad_wgate, grad_wup])[None],
        grad_wd[None],
    )


def body(mesh_sizes, *arguments):
    inputs, _, _, _, wqkv = arguments[:5]
    sections, contexts, parts = mesh_sizes
    own_heads, own_units = wqkv.shape[2], arguments[7].shape[2]
    fits = (
        sections == 2
        and inputs.shape[0] == 2
        and contexts == 4
        and parts % 2 == 0
        and own_heads == contexts
        and own_units % (16 * contexts) == 0
        and inputs.shape[1] % 128 == 0
    )
    if fits:
        return split_body(mesh_sizes, *arguments)
    return general_body(*arguments)


def solution(mesh):
    placed = (
        P(None, ("ctx", "tp"), None),
        P(None, ("ctx", "tp"), None),
        P(),
        P("section", None),
        P("section", None, "tp", None, None),
        P("section", "tp", None),
        P("section", None),
        P("section", None, "tp", None),
        P("section", "tp", None),
    )
    mesh_sizes = tuple(mesh.shape[axis] for axis in ALL_AXES)
    return jax.shard_map(
        functools.partial(body, mesh_sizes),
        mesh=mesh,
        in_specs=placed,
        out_specs=(
            P("section", None, ("ctx", "tp"), None),
            P("section", None, ("ctx", "tp"), None),
            P("section", None),
            P("section", None, "tp", None, None),
            P("section", "tp", None),
            P("section", None),
            P("section", None, "tp", None),
            P("section", "tp", None),
        ),
        check_vma=False,
    )
```

```python
import functools

import jax
import jax.numpy as jnp
from jax import lax
from jax.experimental import pallas as pl
from jax.experimental.pallas import tpu as pltpu
from jax.sharding import PartitionSpec as P

HD = 64
EPSILON = 1e-06
MASKED = -1e30
ALL_AXES = ("section", "ctx", "tp")
CHUNK = 2
ONES = 16
LOG_2 = 0.6931471805599453
LIGHT = pl.CostEstimate(flops=1, bytes_accessed=1, transcendentals=0)
VMEM_LIMIT = 40 * 1024 * 1024


def shifted(block, axis, distance):
    devices = range(lax.axis_size(axis))
    route = [(i - distance, i) for i in devices if i - distance in devices]
    return lax.ppermute(block, axis, route)


def rope_parts(position):
    half_width = HD // 2
    frequency = jnp.exp(-jnp.log(10000.0) * jnp.arange(half_width, dtype=jnp.float32) / half_width)
    angles = position.astype(jnp.float32)[:, None] * frequency[None, :]
    return (jnp.cos(angles), jnp.sin(angles))


def rotate(vectors, cosine, sine_part):
    half_width = HD // 2
    leading_half = vectors[..., :half_width]
    trailing_half = vectors[..., half_width:]
    cosine = cosine[:, None, :]
    sine_part = sine_part[:, None, :]
    return jnp.concatenate(
        [
            leading_half * cosine - trailing_half * sine_part,
            trailing_half * cosine + leading_half * sine_part,
        ],
        axis=-1,
    )


def rotate_back(vectors, cosine, sine_part):
    half_width = HD // 2
    leading_half = vectors[..., :half_width]
    trailing_half = vectors[..., half_width:]
    cosine = cosine[:, None, :]
    sine_part = sine_part[:, None, :]
    return jnp.concatenate(
        [
            leading_half * cosine + trailing_half * sine_part,
            trailing_half * cosine - leading_half * sine_part,
        ],
        axis=-1,
    )


def inner_rows(left, right):
    return lax.dot_general(
        left, right, (((0,), (0,)), ((), ())), preferred_element_type=jnp.float32
    )


def outer_cols(left, right):
    return lax.dot_general(
        left, right, (((1,), (1,)), ((), ())), preferred_element_type=jnp.float32
    )


def spread(row_block):
    return lax.all_gather(row_block, "tp", axis=0, tiled=True)


def collect(partial_value):
    return lax.psum_scatter(
        partial_value.astype(jnp.bfloat16), "tp", scatter_dimension=0, tiled=True
    ).astype(jnp.float32)


def fetch_keys(key_value):
    return lax.all_gather(key_value, "ctx", axis=0, tiled=True)


def query_bounds(seq_lengths, block_first, row_count):
    token_index = block_first + jnp.arange(row_count, dtype=jnp.int32)
    doc_ends = jnp.cumsum(seq_lengths)
    before = (doc_ends[None, :] <= token_index[:, None]).astype(jnp.int32)
    doc_start = jnp.sum(before * seq_lengths[None, :], axis=1)
    return (token_index, doc_start)


def block_scores(query_heads, pair_block, block_first, token_index, doc_start, head_width):
    row_count = pair_block.shape[0]
    key_heads = pair_block[:, :head_width].reshape(row_count, head_width // HD, HD)
    value_heads = pair_block[:, head_width:].reshape(row_count, head_width // HD, HD)
    scores = jnp.einsum(
        "qhd,khd->hqk", query_heads, key_heads, preferred_element_type=jnp.float32
    ) * HD ** (-0.5)
    key_index = block_first + jnp.arange(row_count, dtype=jnp.int32)
    allowed = (key_index[None, :] >= doc_start[:, None]) & (
        key_index[None, :] <= token_index[:, None]
    )
    return (scores, allowed[None], key_heads, value_heads)


def split_blocks(pairs_all, row_count):
    blocks = pairs_all.reshape(-1, row_count, pairs_all.shape[1])
    block_starts = jnp.arange(blocks.shape[0], dtype=jnp.int32) * row_count
    return (blocks, block_starts)


def attend(query_heads, pairs_all, token_index, doc_start, head_width):
    row_count = query_heads.shape[0]
    head_count = head_width // HD
    blocks, block_starts = split_blocks(pairs_all, row_count)
    last_query = token_index[row_count - 1]
    first_query = doc_start[0]

    def rowmax_live(carried, block_parts):
        running_top, running_sum = carried
        scores, allowed, unused_keys, unused_values = block_scores(
            query_heads, block_parts[0], block_parts[1], token_index, doc_start, head_width
        )
        masked = jnp.where(allowed, scores, -1e30)
        new_top = jnp.maximum(running_top, jnp.max(masked, axis=-1))
        running_sum = running_sum * jnp.exp(running_top - new_top) + jnp.sum(
            jnp.where(allowed, jnp.exp(masked - new_top[..., None]), 0.0), axis=-1
        )
        return (new_top, running_sum)

    def rowmax_step(carried, block_parts):
        live = (block_parts[1] <= last_query) & (block_parts[1] + row_count > first_query)
        return (
            lax.cond(live, lambda held: rowmax_live(held, block_parts), lambda held: held, carried),
            None,
        )

    initial = (
        jnp.full((head_count, row_count), -1e30, jnp.float32),
        jnp.zeros((head_count, row_count), jnp.float32),
    )
    (running_top, running_sum), unused = lax.scan(rowmax_step, initial, (blocks, block_starts))
    log_total = running_top + jnp.log(running_sum)

    def output_live(accumulated, block_parts):
        scores, allowed, unused_keys, value_heads = block_scores(
            query_heads, block_parts[0], block_parts[1], token_index, doc_start, head_width
        )
        soft_weights = jnp.where(allowed, jnp.exp(scores - log_total[..., None]), 0.0).astype(
            jnp.bfloat16
        )
        return accumulated + jnp.einsum(
            "hqk,khd->qhd", soft_weights, value_heads, preferred_element_type=jnp.float32
        )

    def output_step(accumulated, block_parts):
        live = (block_parts[1] <= last_query) & (block_parts[1] + row_count > first_query)
        return (
            lax.cond(
                live, lambda held: output_live(held, block_parts), lambda held: held, accumulated
            ),
            None,
        )

    accumulated, unused = lax.scan(
        output_step, jnp.zeros((row_count, head_count, HD), jnp.float32), (blocks, block_starts)
    )
    return (accumulated, log_total)


def attend_back(
    query_heads, pairs_all, token_index, doc_start, head_width, log_total, accumulated, grad_heads
):
    row_count = query_heads.shape[0]
    head_count = head_width // HD
    blocks, block_starts = split_blocks(pairs_all, row_count)
    last_query = token_index[row_count - 1]
    first_query = doc_start[0]
    rowdot = jnp.sum(grad_heads.astype(jnp.float32) * accumulated, axis=-1).T

    def grad_live(grad_acc, block_parts):
        scores, allowed, key_heads, value_heads = block_scores(
            query_heads, block_parts[0], block_parts[1], token_index, doc_start, head_width
        )
        soft_weights = jnp.where(allowed, jnp.exp(scores - log_total[..., None]), 0.0)
        grad_soft = jnp.einsum(
            "qhd,khd->hqk", grad_heads, value_heads, preferred_element_type=jnp.float32
        )
        grad_scores = (soft_weights * (grad_soft - rowdot[..., None])).astype(jnp.bfloat16)
        grad_acc = grad_acc + jnp.einsum(
            "hqk,khd->qhd", grad_scores, key_heads, preferred_element_type=jnp.float32
        )
        grad_keys = jnp.einsum(
            "hqk,qhd->khd", grad_scores, query_heads, preferred_element_type=jnp.float32
        ) * HD ** (-0.5)
        grad_values = jnp.einsum(
            "hqk,qhd->khd",
            soft_weights.astype(jnp.bfloat16),
            grad_heads,
            preferred_element_type=jnp.float32,
        )
        return (grad_acc, (grad_keys, grad_values))

    def grad_skip(grad_acc):
        empty = jnp.zeros((row_count, head_count, HD), jnp.float32)
        return (grad_acc, (empty, empty))

    def grad_step(grad_acc, block_parts):
        live = (block_parts[1] <= last_query) & (block_parts[1] + row_count > first_query)
        return lax.cond(live, lambda held: grad_live(held, block_parts), grad_skip, grad_acc)

    grad_query, (grad_keys, grad_values) = lax.scan(
        grad_step, jnp.zeros((row_count, head_count, HD), jnp.float32), (blocks, block_starts)
    )
    grad_query = grad_query * HD ** (-0.5)
    grad_pairs = jnp.concatenate(
        [grad_keys.reshape(-1, head_width), grad_values.reshape(-1, head_width)], axis=1
    )
    return (grad_query, grad_pairs)


def norm_back(whole_rows, scale_rows, gain, grad_normed, grad_rest):
    unit_rows = whole_rows * scale_rows
    scaled = grad_normed * gain.astype(jnp.float32)
    grad_gain = jnp.sum(grad_normed * unit_rows, axis=0)
    grad_whole = grad_rest + scale_rows * (
        scaled - unit_rows * jnp.mean(scaled * unit_rows, axis=-1, keepdims=True)
    )
    return (grad_gain, grad_whole)


def layer_forward(row_block, first_values, value_mix, weights, seq_lengths):
    gain_first, w_qkv, w_out, gain_second, w_gateup, w_down = weights
    head_count = w_qkv.shape[1]
    head_width = head_count * HD
    model_width = row_block.shape[1]
    whole_rows = row_block.astype(jnp.float32)
    scale_first = lax.rsqrt(jnp.mean(whole_rows * whole_rows, axis=-1, keepdims=True) + EPSILON)
    normed = (whole_rows * scale_first * gain_first.astype(jnp.float32)).astype(jnp.bfloat16)
    normed_all = spread(normed)
    row_count = normed_all.shape[0]
    projected = outer_cols(normed_all, w_qkv.reshape(3 * head_width, model_width))
    token_index, doc_start = query_bounds(seq_lengths, lax.axis_index("ctx") * row_count, row_count)
    cosine, sine_part = rope_parts(token_index - doc_start)
    query_heads = rotate(
        projected[:, :head_width].reshape(row_count, head_count, HD), cosine, sine_part
    ).astype(jnp.bfloat16)
    key_heads = rotate(
        projected[:, head_width : 2 * head_width].reshape(row_count, head_count, HD),
        cosine,
        sine_part,
    ).astype(jnp.bfloat16)
    mixed = (
        (1.0 - value_mix) * projected[:, 2 * head_width :]
        + value_mix * first_values.astype(jnp.float32)
    ).astype(jnp.bfloat16)
    key_value = jnp.concatenate([key_heads.reshape(row_count, head_width), mixed], axis=1)
    pairs_all = fetch_keys(key_value)
    accumulated, log_total = attend(query_heads, pairs_all, token_index, doc_start, head_width)
    attended = accumulated.reshape(row_count, head_width).astype(jnp.bfloat16)
    hidden = whole_rows + collect(jnp.dot(attended, w_out, preferred_element_type=jnp.float32))
    scale_second = lax.rsqrt(jnp.mean(hidden * hidden, axis=-1, keepdims=True) + EPSILON)
    normed_second = (hidden * scale_second * gain_second.astype(jnp.float32)).astype(jnp.bfloat16)
    ffn_rows = spread(normed_second)
    gate_up = outer_cols(ffn_rows, w_gateup.reshape(-1, model_width))
    unit_count = gate_up.shape[1] // 2
    gate_part = gate_up[:, :unit_count]
    up_part = gate_up[:, unit_count:]
    activated = (jax.nn.silu(gate_part) * up_part).astype(jnp.bfloat16)
    down_part = jnp.dot(activated, w_down, preferred_element_type=jnp.float32)
    branch_out = collect(down_part)
    layer_out = (hidden + branch_out).astype(jnp.bfloat16)
    saved = (
        whole_rows,
        scale_first,
        normed_all,
        query_heads,
        pairs_all,
        token_index,
        doc_start,
        cosine,
        sine_part,
        log_total,
        accumulated,
        attended,
        hidden,
        scale_second,
        ffn_rows,
        gate_part,
        up_part,
        activated,
    )
    return (layer_out, mixed, pairs_all, saved)


def layer_backward(grad_rows, extra_values, value_mix, weights, saved):
    gain_first, w_qkv, w_out, gain_second, w_gateup, w_down = weights
    (
        whole_rows,
        scale_first,
        normed_all,
        query_heads,
        pairs_all,
        token_index,
        doc_start,
        cosine,
        sine_part,
        log_total,
        accumulated,
        attended,
        hidden,
        scale_second,
        ffn_rows,
        gate_part,
        up_part,
        activated,
    ) = saved
    model_width = whole_rows.shape[1]
    head_count = w_qkv.shape[1]
    head_width = head_count * HD
    row_count = normed_all.shape[0]
    grad_hidden = grad_rows.astype(jnp.float32)
    grad_down = spread(grad_rows)
    grad_wd = inner_rows(activated, grad_down)
    grad_act = outer_cols(grad_down, w_down)
    sigmoid_gate = jax.nn.sigmoid(gate_part)
    grad_gate = grad_act * up_part * sigmoid_gate * (1.0 + gate_part * (1.0 - sigmoid_gate))
    grad_up = grad_act * gate_part * sigmoid_gate
    grad_gate_up = jnp.concatenate([grad_gate, grad_up], axis=1).astype(jnp.bfloat16)
    grad_wgu = inner_rows(grad_gate_up, ffn_rows).reshape(w_gateup.shape)
    back_second = jnp.dot(
        grad_gate_up, w_gateup.reshape(-1, model_width), preferred_element_type=jnp.float32
    )
    grad_normed_second = collect(back_second)
    grad_gain2, grad_hidden = norm_back(
        hidden, scale_second, gain_second, grad_normed_second, grad_hidden
    )
    grad_branch_all = spread(grad_hidden.astype(jnp.bfloat16))
    grad_wo = inner_rows(attended, grad_branch_all)
    grad_heads = (
        outer_cols(grad_branch_all, w_out).astype(jnp.bfloat16).reshape(row_count, head_count, HD)
    )
    grad_query, grad_pairs_all = attend_back(
        query_heads,
        pairs_all,
        token_index,
        doc_start,
        head_width,
        log_total,
        accumulated,
        grad_heads,
    )
    grad_pairs = lax.psum_scatter(
        grad_pairs_all.astype(jnp.bfloat16), "ctx", scatter_dimension=0, tiled=True
    ).astype(jnp.float32)
    grad_mixed = grad_pairs[:, head_width:] + extra_values.astype(jnp.float32)
    grad_keys = rotate_back(
        grad_pairs[:, :head_width].reshape(row_count, head_count, HD), cosine, sine_part
    )
    grad_query = rotate_back(grad_query, cosine, sine_part)
    grad_projected = jnp.concatenate(
        [
            grad_query.reshape(row_count, head_width),
            grad_keys.reshape(row_count, head_width),
            (1.0 - value_mix) * grad_mixed,
        ],
        axis=1,
    ).astype(jnp.bfloat16)
    send_values = (value_mix * grad_mixed).astype(jnp.bfloat16)
    grad_wqkv = inner_rows(grad_projected, normed_all).reshape(w_qkv.shape)
    grad_normed = collect(
        jnp.dot(
            grad_projected,
            w_qkv.reshape(3 * head_width, model_width),
            preferred_element_type=jnp.float32,
        )
    )
    grad_gain1, grad_whole = norm_back(
        whole_rows, scale_first, gain_first, grad_normed, grad_hidden
    )
    return (
        grad_whole,
        send_values,
        (grad_gain1, grad_wqkv, grad_wo, grad_gain2, grad_wgu, grad_wd),
    )


def general_body(inputs, cotangent, lengths, gain1, wqkv, wo, gain2, wgu, wd):
    section_index = lax.axis_index("section")
    leading = section_index == 0
    value_mix = jnp.where(leading, 0.0, 0.5).astype(jnp.float32)
    micro_count = inputs.shape[0]
    local_rows = inputs.shape[1]
    model_width = inputs.shape[2]
    head_width = wqkv.shape[2] * HD
    row_count = local_rows * lax.axis_size("tp")
    gateup_use, down_use = (wgu[0], wd[0])
    weights = (gain1[0], wqkv[0], wo[0], gain2[0], gateup_use, down_use)
    recv_rows = jnp.zeros((local_rows, model_width), jnp.bfloat16)
    recv_values = jnp.zeros((row_count, head_width), jnp.bfloat16)
    states = []
    outputs = []
    for turn_index in range(micro_count + 1):
        own_rows = inputs[min(turn_index, micro_count - 1)]
        row_block = jnp.where(leading, own_rows, recv_rows)
        seq_lengths = jnp.where(
            leading, lengths[min(turn_index, micro_count - 1)], lengths[max(turn_index - 1, 0)]
        )
        layer_out, mixed, pairs_all, unused = layer_forward(
            row_block, recv_values, value_mix, weights, seq_lengths
        )
        kept_pairs = None
        states.append((row_block, recv_values, seq_lengths, kept_pairs))
        outputs.append(layer_out)
        if turn_index < micro_count:
            recv_rows, recv_values = shifted((layer_out, mixed), "section", 1)
    grad_rows_in = jnp.zeros((local_rows, model_width), jnp.bfloat16)
    grad_values_in = jnp.zeros((row_count, head_width), jnp.bfloat16)
    totals = None
    turn_grads = []
    for turn_index in range(micro_count + 1):
        row_block, first_values, seq_lengths, kept_pairs = states[micro_count - turn_index]
        if turn_index < micro_count:
            fed_grad = cotangent[micro_count - 1 - turn_index]
        else:
            fed_grad = jnp.zeros_like(cotangent[0])
        grad_out = jnp.where(leading, grad_rows_in, fed_grad)
        unused_out, unused_mixed, unused_pairs, saved = layer_forward(
            row_block, first_values, value_mix, weights, seq_lengths
        )
        grad_whole, send_values, grads = layer_backward(
            grad_out, grad_values_in, value_mix, weights, saved
        )
        totals = grads if totals is None else jax.tree.map(jnp.add, totals, grads)
        sent_rows = grad_whole.astype(jnp.bfloat16)
        turn_grads.append(jnp.where(leading, grad_whole, sent_rows.astype(jnp.float32)))
        if turn_index < micro_count:
            grad_rows_in, grad_values_in = shifted((sent_rows, send_values), "section", -1)
    grad_gain1, grad_wqkv, grad_wo, grad_gain2, grad_wgu, grad_wd = totals
    grad_wqkv, grad_wo, grad_wgu, grad_wd = (
        lax.psum(grad_wqkv.astype(jnp.bfloat16), "ctx").astype(jnp.float32),
        lax.psum(grad_wo.astype(jnp.bfloat16), "ctx").astype(jnp.float32),
        lax.psum(grad_wgu.astype(jnp.bfloat16), "ctx").astype(jnp.float32),
        lax.psum(grad_wd.astype(jnp.bfloat16), "ctx").astype(jnp.float32),
    )
    grad_gain1, grad_gain2 = lax.psum((grad_gain1, grad_gain2), ("ctx", "tp"))
    acts = jnp.stack(
        [
            jnp.where(leading, outputs[batch_index], outputs[batch_index + 1])
            for batch_index in range(micro_count)
        ]
    )[None]
    input_grads = jnp.stack(
        [
            jnp.where(
                leading,
                turn_grads[micro_count - batch_index],
                turn_grads[micro_count - 1 - batch_index],
            )
            for batch_index in range(micro_count)
        ]
    )[None]
    return (
        acts,
        input_grads,
        grad_gain1[None],
        grad_wqkv[None],
        grad_wo[None],
        grad_gain2[None],
        grad_wgu[None],
        grad_wd[None],
    )


def device_groups(mesh_sizes, key, order):
    sections, contexts, parts = mesh_sizes
    groups = {}
    for section in range(sections):
        for ctx in range(contexts):
            for tp in range(parts):
                place = (section, ctx, tp)
                number = (section * contexts + ctx) * parts + tp
                groups.setdefault(key(*place), []).append((order(*place), number))
    return [[number for _, number in sorted(members)] for _, members in sorted(groups.items())]


def exchange(value, groups):
    return lax.all_to_all(
        value, ALL_AXES, split_axis=0, concat_axis=0, tiled=True, axis_index_groups=groups
    )


def document_bounds(ends_ref, index):
    start = jnp.zeros_like(index)
    for entry in range(ends_ref.shape[0]):
        end = ends_ref[entry]
        start = jnp.where(index >= end, end, start)
    return start


def scalar_start(ends_ref, index):
    start = jnp.int32(0)
    for entry in range(ends_ref.shape[0]):
        start = jnp.where(index >= ends_ref[entry], ends_ref[entry], start)
    return start


def scalar_end(ends_ref, index):
    end = ends_ref[ends_ref.shape[0] - 1]
    for entry in range(ends_ref.shape[0] - 2, -1, -1):
        end = jnp.where(index < ends_ref[entry], ends_ref[entry], end)
    return end


def dot(left, right, left_dim, right_dim):
    return lax.dot_general(
        left, right, (((left_dim,), (right_dim,)), ((), ())), preferred_element_type=jnp.float32
    )


def fold_rows(value, combine):
    rows, width = value.shape
    return combine(value.reshape(rows // 8, 8, width), axis=0)


def block_place(block, parts, width):
    entry = (block // (2 * parts)) * parts + block % parts
    return entry, pl.ds(pl.multiple_of((block // parts % 2) * width, width), width)


def attention_forward_kernel(parts, ends_ref, qkv_ref, out_ref, lse_ref, keys_ref, values_ref):
    program = pl.program_id(0)
    blocks, block_width = 2 * qkv_ref.shape[0], qkv_ref.shape[2] // 2
    width = CHUNK * block_width

    @pl.when(program == 0)
    def _():
        def turn(j, carry):
            entry, columns = block_place(j, parts, block_width)
            keys_ref[j] = qkv_ref[entry, HD : 2 * HD, columns].T
            values_ref[j, 0:HD, :] = qkv_ref[entry, 2 * HD : 3 * HD, columns]
            values_ref[j, HD : HD + ONES, :] = jnp.ones((ONES, block_width), jnp.bfloat16)
            return carry

        lax.fori_loop(0, blocks, turn, 0)

    query = []
    for block in range(CHUNK):
        entry, columns = block_place(program * CHUNK + block, parts, block_width)
        query.append(qkv_ref[entry, 0:HD, columns])
    query = jnp.concatenate(query, axis=1)
    first = program * width
    query_index = first + lax.broadcasted_iota(jnp.int32, (1, width), 1)
    start = document_bounds(ends_ref, query_index)
    low_chunk = scalar_start(ends_ref, first) // width
    high_start = scalar_start(ends_ref, first + width - 1)
    middle = jnp.clip((high_start + width - 1) // width, low_chunk, program)

    def step(chunk, carry, masked):
        top, acc = carry
        parts = []
        for entry in range(CHUNK):
            j = chunk * CHUNK + entry
            scores = dot(keys_ref[j], query, 1, 0)
            if masked:
                key_index = j * block_width + lax.broadcasted_iota(jnp.int32, (block_width, 1), 0)
                allowed = (key_index >= start) & (key_index <= query_index)
                scores = jnp.where(allowed, scores, MASKED)
            parts.append(scores)
        part_top = functools.reduce(jnp.maximum, [fold_rows(part, jnp.max) for part in parts])
        new_top = jnp.maximum(top, jnp.max(part_top, axis=0, keepdims=True))
        acc = acc * jnp.exp2(top - new_top)
        for entry in range(CHUNK):
            weights = jnp.exp2(parts[entry] - new_top).astype(jnp.bfloat16)
            acc = acc + dot(values_ref[chunk * CHUNK + entry], weights, 1, 0)
        return new_top, acc

    carry = (
        jnp.full((1, width), MASKED, jnp.float32),
        jnp.zeros((HD + ONES, width), jnp.float32),
    )
    carry = lax.fori_loop(low_chunk, middle, functools.partial(step, masked=True), carry)
    carry = lax.fori_loop(middle, program, functools.partial(step, masked=False), carry)
    top, acc = step(program, carry, True)
    total = acc[HD : HD + 1]
    out = (acc[:HD] / total).astype(jnp.bfloat16)
    lse = top + jnp.log2(total)
    for entry in range(CHUNK):
        columns = slice(entry * block_width, (entry + 1) * block_width)
        out_ref[entry] = out[:, columns]
        lse_ref[entry] = lse[:, columns]


def attention_forward(ends, qkv, parts):
    blocks, width = 2 * qkv.shape[0], qkv.shape[2] // 2
    return pl.pallas_call(
        functools.partial(attention_forward_kernel, parts),
        grid_spec=pltpu.PrefetchScalarGridSpec(
            num_scalar_prefetch=1,
            grid=(blocks // CHUNK,),
            in_specs=[pl.BlockSpec(qkv.shape, lambda i, ends_ref: (0, 0, 0))],
            out_specs=[
                pl.BlockSpec((CHUNK, HD, width), lambda i, ends_ref: (i, 0, 0)),
                pl.BlockSpec((CHUNK, 1, width), lambda i, ends_ref: (i, 0, 0)),
            ],
            scratch_shapes=[
                pltpu.VMEM((blocks, width, HD), jnp.bfloat16),
                pltpu.VMEM((blocks, HD + ONES, width), jnp.bfloat16),
            ],
        ),
        out_shape=[
            jax.ShapeDtypeStruct((blocks, HD, width), jnp.bfloat16),
            jax.ShapeDtypeStruct((blocks, 1, width), jnp.float32),
        ],
        compiler_params=pltpu.CompilerParams(vmem_limit_bytes=VMEM_LIMIT),
        cost_estimate=LIGHT,
        name="attention_forward",
    )(ends, qkv)


def attention_backward_kernel(
    parts, ends_ref, qkv_ref, out_ref, grad_ref, lse_ref, result_ref,
    query_grad_ref, delta_ref, queries_ref, grads_ref, lses_ref,
):
    program = pl.program_id(0)
    blocks, block_width = 2 * qkv_ref.shape[0], qkv_ref.shape[2] // 2
    width = CHUNK * block_width

    @pl.when(program == 0)
    def _():
        def turn(i, carry):
            for entry in range(CHUNK):
                block = i * CHUNK + entry
                columns = slice(entry * block_width, (entry + 1) * block_width)
                grad = grad_ref[block]
                place, tokens = block_place(block, parts, block_width)
                queries_ref[i, :, columns] = qkv_ref[place, 0:HD, tokens]
                grads_ref[i, :, columns] = grad
                lses_ref[i, :, columns] = lse_ref[block]
                delta_ref[i, :, columns] = jnp.sum(
                    grad.astype(jnp.float32) * out_ref[block].astype(jnp.float32),
                    axis=0,
                    keepdims=True,
                )
            query_grad_ref[i] = jnp.zeros((HD, width), jnp.float32)
            return carry

        lax.fori_loop(0, blocks // CHUNK, turn, 0)

    own_places = [
        block_place(program * CHUNK + block, parts, block_width) for block in range(CHUNK)
    ]

    def joined(low_row, high_row):
        return jnp.concatenate(
            [qkv_ref[place, low_row:high_row, tokens] for place, tokens in own_places], axis=1
        )

    first = program * width
    keys_t = joined(HD, 2 * HD)
    keys = keys_t.T
    values = joined(2 * HD, 3 * HD).T
    key_index = first + lax.broadcasted_iota(jnp.int32, (width, 1), 0)
    near_end = scalar_end(ends_ref, first)
    far_end = scalar_end(ends_ref, first + width - 1)
    stop = (far_end - 1) // width + 1
    middle = jnp.clip(near_end // width, program + 1, stop)

    def step(i, carry, masked):
        key_grad, value_grad = carry
        query = queries_ref[i]
        grad = grads_ref[i]
        weights = jnp.exp2(dot(keys, query, 1, 0) - lses_ref[i])
        if masked:
            query_index = i * width + lax.broadcasted_iota(jnp.int32, (1, width), 1)
            start = document_bounds(ends_ref, query_index)
            allowed = (key_index >= start) & (key_index <= query_index)
            weights = jnp.where(allowed, weights, 0.0)
        grad_weights = dot(values, grad, 1, 0)
        grad_scores = (weights * (grad_weights - delta_ref[i])).astype(jnp.bfloat16)
        query_grad_ref[i] += dot(keys_t, grad_scores, 1, 0)
        value_grad = value_grad + dot(grad, weights.astype(jnp.bfloat16), 1, 1)
        key_grad = key_grad + dot(query, grad_scores, 1, 1)
        return key_grad, value_grad

    empty = jnp.zeros((HD, width), jnp.float32)
    carry = step(program, (empty, empty), True)
    carry = lax.fori_loop(program + 1, middle, functools.partial(step, masked=False), carry)
    key_grad, value_grad = lax.fori_loop(middle, stop, functools.partial(step, masked=True), carry)
    query_grad = query_grad_ref[program] * HD ** (-0.5)
    key_grad = key_grad * LOG_2
    for block, (place, tokens) in enumerate(own_places):
        columns = slice(block * block_width, (block + 1) * block_width)
        result_ref[place, 0:HD, tokens] = query_grad[:, columns].astype(jnp.bfloat16)
        result_ref[place, HD : 2 * HD, tokens] = key_grad[:, columns].astype(jnp.bfloat16)
        result_ref[place, 2 * HD : 3 * HD, tokens] = value_grad[:, columns].astype(jnp.bfloat16)


def attention_backward(ends, qkv, out, grad, lse, parts):
    blocks, block_width = 2 * qkv.shape[0], qkv.shape[2] // 2
    chunks, width = blocks // CHUNK, CHUNK * block_width

    def whole(value):
        return pl.BlockSpec(value.shape, lambda i, ends_ref: (0, 0, 0))

    return pl.pallas_call(
        functools.partial(attention_backward_kernel, parts),
        grid_spec=pltpu.PrefetchScalarGridSpec(
            num_scalar_prefetch=1,
            grid=(chunks,),
            in_specs=[whole(qkv), whole(out), whole(grad), whole(lse)],
            out_specs=whole(qkv),
            scratch_shapes=[
                pltpu.VMEM((chunks, HD, width), jnp.float32),
                pltpu.VMEM((chunks, 1, width), jnp.float32),
                pltpu.VMEM((chunks, HD, width), jnp.bfloat16),
                pltpu.VMEM((chunks, HD, width), jnp.bfloat16),
                pltpu.VMEM((chunks, 1, width), jnp.float32),
            ],
        ),
        out_shape=jax.ShapeDtypeStruct(qkv.shape, jnp.bfloat16),
        compiler_params=pltpu.CompilerParams(vmem_limit_bytes=VMEM_LIMIT),
        cost_estimate=LIGHT,
        name="attention_backward",
    )(ends, qkv, out, grad, lse)


def rope_pair(leading_half, trailing_half, cosine, sine_part):
    return (
        leading_half * cosine - trailing_half * sine_part,
        trailing_half * cosine + leading_half * sine_part,
    )


def low(value):
    return value.astype(jnp.bfloat16)


def wide(value):
    return value.astype(jnp.float32)


def whole_block(value):
    zeros = (0,) * value.ndim
    return pl.BlockSpec(value.shape, lambda *_: zeros)


def feed_forward_kernel(rows_ref, gate_w_ref, up_w_ref, down_w_ref, gate_ref, up_ref, act_ref, sum_ref):
    rows = rows_ref[...]
    gate = dot(gate_w_ref[...], rows, 1, 1)
    up = dot(up_w_ref[...], rows, 1, 1)
    active = (gate * jax.nn.sigmoid(gate) * up).astype(jnp.bfloat16)
    gate_ref[...] = gate.astype(jnp.bfloat16)
    up_ref[...] = up.astype(jnp.bfloat16)
    act_ref[...] = active

    @pl.when(pl.program_id(0) == 0)
    def _():
        sum_ref[...] = jnp.zeros_like(sum_ref)

    sum_ref[...] += dot(active, down_w_ref[...], 0, 0)


def feed_forward(rows, w_gate, w_up, w_down, tile):
    units, width = w_gate.shape
    count = rows.shape[0]
    weight = pl.BlockSpec((tile, width), lambda i: (i, 0))
    column = pl.BlockSpec((tile, count), lambda i: (i, 0))
    hidden = jax.ShapeDtypeStruct((units, count), jnp.bfloat16)
    return pl.pallas_call(
        feed_forward_kernel,
        grid=(units // tile,),
        in_specs=[whole_block(rows), weight, weight, weight],
        out_specs=[column, column, column, pl.BlockSpec((count, width), lambda i: (0, 0))],
        out_shape=[hidden, hidden, hidden, jax.ShapeDtypeStruct((count, width), jnp.float32)],
        compiler_params=pltpu.CompilerParams(vmem_limit_bytes=VMEM_LIMIT),
        cost_estimate=LIGHT,
        name="feed_forward",
    )(rows, w_gate, w_up, w_down)


def feed_forward_back_kernel(
    grad_ref, gate_ref, up_ref, gate_w_ref, up_w_ref, down_w_ref, grad_gate_ref, grad_up_ref, sum_ref
):
    grad_act = dot(down_w_ref[...], grad_ref[...], 1, 1)
    gate = gate_ref[...].astype(jnp.float32)
    up = up_ref[...].astype(jnp.float32)
    sigmoid_gate = jax.nn.sigmoid(gate)
    grad_gate = (grad_act * up * sigmoid_gate * (1.0 + gate * (1.0 - sigmoid_gate))).astype(
        jnp.bfloat16
    )
    grad_up = (grad_act * gate * sigmoid_gate).astype(jnp.bfloat16)
    grad_gate_ref[...] = grad_gate
    grad_up_ref[...] = grad_up

    @pl.when(pl.program_id(0) == 0)
    def _():
        sum_ref[...] = jnp.zeros_like(sum_ref)

    sum_ref[...] += dot(grad_gate, gate_w_ref[...], 0, 0) + dot(grad_up, up_w_ref[...], 0, 0)


def feed_forward_back(grad, gate, up, w_gate, w_up, w_down, tile):
    units, width = w_gate.shape
    count = grad.shape[0]
    weight = pl.BlockSpec((tile, width), lambda i: (i, 0))
    column = pl.BlockSpec((tile, count), lambda i: (i, 0))
    hidden = jax.ShapeDtypeStruct((units, count), jnp.bfloat16)
    return pl.pallas_call(
        feed_forward_back_kernel,
        grid=(units // tile,),
        in_specs=[whole_block(grad), column, column, weight, weight, weight],
        out_specs=[column, column, pl.BlockSpec((count, width), lambda i: (0, 0))],
        out_shape=[hidden, hidden, jax.ShapeDtypeStruct((count, width), jnp.float32)],
        compiler_params=pltpu.CompilerParams(vmem_limit_bytes=VMEM_LIMIT),
        cost_estimate=LIGHT,
        name="feed_forward_back",
    )(grad, gate, up, w_gate, w_up, w_down)


def half_products_kernel(layout, sizes, has_addend, which_ref, *refs):
    refs = list(refs)
    out_ref = refs.pop()
    addend_ref = refs.pop() if has_addend else None
    totals = [
        sum(dot(refs[left][...], refs[right][...], 1, 0) for left, right in pairs)
        for pairs in layout
    ]
    for piece in range(out_ref.shape[0]):
        parts = [
            total[piece * size : (piece + 1) * size] for total, size in zip(totals, sizes)
        ]
        value = jnp.concatenate(parts, axis=0) if len(parts) > 1 else parts[0]
        if has_addend:
            value = value + addend_ref[piece].astype(jnp.float32)
        out_ref[piece] = value.astype(jnp.bfloat16)


def half_products(which, groups, pieces, per_step, addend=None):
    lefts, rights, layout = [], [], []
    for group in groups:
        for left, right in group:
            if not any(left is known for known in lefts):
                lefts.append(left)
            if not any(right is known for known in rights):
                rights.append(right)
    find = lambda known, value: next(i for i, entry in enumerate(known) if entry is value)
    for group in groups:
        layout.append(
            tuple((find(lefts, left), len(lefts) + find(rights, right)) for left, right in group)
        )
    sizes = tuple(group[0][0].shape[0] // (2 * pieces) for group in groups)
    width = rights[0].shape[1]
    steps = pieces // per_step
    out_spec = pl.BlockSpec((per_step, sum(sizes), width), lambda i, which_ref: (i, 0, 0))
    left_specs = [
        pl.BlockSpec(
            (left.shape[0] // (2 * steps), left.shape[1]),
            lambda i, which_ref: (which_ref[0] * steps + i, 0),
        )
        for left in lefts
    ]
    extra = [] if addend is None else [addend]
    work = sum(left.size // 2 for left, _ in sum(groups, ()))
    return pl.pallas_call(
        functools.partial(half_products_kernel, tuple(layout), sizes, addend is not None),
        grid_spec=pltpu.PrefetchScalarGridSpec(
            num_scalar_prefetch=1,
            grid=(steps,),
            in_specs=left_specs + [whole_block(right) for right in rights] + [out_spec] * len(extra),
            out_specs=out_spec,
        ),
        out_shape=jax.ShapeDtypeStruct((pieces, sum(sizes), width), jnp.bfloat16),
        compiler_params=pltpu.CompilerParams(vmem_limit_bytes=VMEM_LIMIT),
        cost_estimate=LIGHT,
        name="half_products",
    )(which.reshape(1).astype(jnp.int32), *lefts, *rights, *extra)


def together(*values):
    return lax.optimization_barrier(values)


def after(value, *others):
    return lax.optimization_barrier((value, *others))[0]


def split_body(mesh_sizes, inputs, cotangent, lengths, gain1, wqkv, wo, gain2, wgu, wd):
    sections, contexts, parts = mesh_sizes
    half_parts = parts // 2
    section = lax.axis_index("section")
    ctx = lax.axis_index("ctx")
    tp = lax.axis_index("tp")
    row_side, column_side = ctx // 2, ctx % 2
    leading = section == 0
    batch = tp // half_parts
    model_width = inputs.shape[2]
    rows = inputs.shape[1]
    heads = wqkv.shape[2] * parts
    side_heads = heads // 2
    unit_rows = wd.shape[1] // contexts // 2
    head_rows = 3 * HD // 2
    out_rows = HD // 2
    half_width = HD // 2
    tile = 4 * unit_rows
    number = lambda s, c, t: (s * contexts + c) * parts + t
    places = [
        (s, c, t) for s in range(sections) for c in range(contexts) for t in range(parts)
    ]
    everyone = [[number(*place) for place in places]]
    token_of = lambda s, c, t: c * parts + t % half_parts + half_parts * s
    batch_groups = device_groups(mesh_sizes, lambda s, c, t: t // half_parts, token_of)
    head_groups = device_groups(
        mesh_sizes,
        lambda s, c, t: (c % 2, t // half_parts),
        lambda s, c, t: (c // 2, t % half_parts + half_parts * s),
    )
    side_groups = device_groups(mesh_sizes, lambda s, c, t: c % 2, lambda s, c, t: (s, c, t))
    crossing = [
        (number(s, c, t), number(s, c, (t + half_parts) % parts))
        for s, c, t in places
        if t // half_parts == s
    ]

    def to_batch(value):
        mine = lax.dynamic_index_in_dim(value, batch, 0, keepdims=False)
        other = lax.dynamic_index_in_dim(value, 1 - batch, 0, keepdims=False)
        moved = lax.ppermute(other, ALL_AXES, crossing)
        return jnp.where(section == batch, mine, moved)

    def to_home(value, layer):
        stay = [
            (number(s, c, t), number(layer, c, t)) for s, c, t in places if t // half_parts == s
        ]
        cross = [
            (number(s, c, t), number(layer, c, (t + half_parts) % parts))
            for s, c, t in places
            if t // half_parts != s
        ]
        return (lax.ppermute(value, ALL_AXES, stay), lax.ppermute(value, ALL_AXES, cross))

    def at_home(first_pair, second_pair):
        near = jnp.where(leading, first_pair[0], second_pair[0])
        far = jnp.where(leading, first_pair[1], second_pair[1])
        upper = batch == 0
        return jnp.stack([jnp.where(upper, near, far), jnp.where(upper, far, near)])[None]

    def swap_side(value):
        return lax.ppermute(value, "ctx", [(c, c ^ 1) for c in range(contexts)])

    def swap_far(value):
        return lax.ppermute(value, "ctx", [(c, c ^ 2) for c in range(contexts)])

    def swap_near(value):
        return lax.ppermute(value, "tp", [(t, t ^ 1) for t in range(parts)])

    def swap_half(value):
        return lax.ppermute(value, "tp", [(t, (t + half_parts) % parts) for t in range(parts)])

    def swap_section(value):
        return lax.ppermute(value, "section", [(0, 1), (1, 0)])

    def all_to_all(value, axis):
        return lax.all_to_all(value, axis, split_axis=0, concat_axis=0, tiled=True)

    def copies(value, count):
        return jnp.broadcast_to(value[None], (count, *value.shape))

    def gather(value, groups):
        return lax.all_gather(value, ALL_AXES, axis=0, tiled=True, axis_index_groups=groups)

    def ordered(index, own, other):
        return jnp.where(index == 0, own, other), jnp.where(index == 0, other, own)

    def by_core(value, which):
        return lax.dynamic_index_in_dim(value, which, 0, keepdims=False)

    def spread_half(piece):
        return piece, swap_half(piece)

    def spread_near(pieces_pair):
        pair = jnp.stack(ordered(batch, *pieces_pair))
        return pair, swap_near(pair)

    def spread_line(pairs):
        line = jnp.stack(ordered(tp % 2, *pairs), axis=1)
        return line.reshape(parts, *line.shape[2:])

    def spread_far(line):
        return line, swap_far(line)

    def spread_heads(pair):
        pair = jnp.stack(ordered(row_side, *pair))
        own_heads = pair[:, :, :head_rows].reshape(-1, model_width)
        own_outs = pair[:, :, head_rows:]
        return (own_heads, swap_section(own_heads)), (own_outs, swap_side(own_outs))

    def spread_outs(pair):
        own_outs = jnp.stack(ordered(column_side, *pair), axis=1).reshape(-1, model_width)
        return own_outs, swap_section(own_outs)

    def join_outs(pair):
        return jnp.concatenate(ordered(section, *pair), axis=0)

    def own_halves(value, axis, size):
        part = lax.dynamic_slice_in_dim(value, ctx * size, size, axis)
        return part.reshape(2, -1, model_width)

    packed = jnp.concatenate(
        [
            own_halves(wqkv[0], 1, heads // (parts * contexts)),
            own_halves(wo[0], 0, HD),
            own_halves(wgu[0, 0], 0, 2 * unit_rows),
            own_halves(wgu[0, 1], 0, 2 * unit_rows),
            own_halves(wd[0], 0, 2 * unit_rows),
        ],
        axis=1,
    )
    kept = by_core(packed, section)
    passed = swap_section(by_core(packed, 1 - section))
    pieces = ordered(section, kept, passed)
    attention_rows = head_rows + out_rows

    def feed_forward_weights(piece):
        whole = gather(piece[attention_rows:], side_groups)
        whole = whole.reshape(2 * 2 * parts, 3, unit_rows, model_width)
        return [whole[:, entry].reshape(-1, model_width) for entry in range(3)]

    rows_in = to_batch(inputs)
    line = spread_near(spread_half(pieces[0][:attention_rows]))
    line, rows_in = together(spread_line(line), rows_in)
    w_ffn = [feed_forward_weights(after(pieces[0], line)), None]
    w_heads, w_outs = [None, None], [None, None]
    first_pair = spread_far(line)

    gains = wide(jnp.concatenate([gain1, gain2], axis=0))
    gain_sets = ordered(section, gains, swap_section(gains))

    seq_lengths = lax.dynamic_index_in_dim(lengths, batch, 0, keepdims=False)
    ends = jnp.cumsum(seq_lengths).astype(jnp.int32)
    token_index = jnp.concatenate(
        [
            token_of(section, 2 * row_side + side, tp) * rows + jnp.arange(rows, dtype=jnp.int32)
            for side in range(2)
        ]
    )
    before = (ends[None, :] <= token_index[:, None]).astype(jnp.int32)
    position = token_index - jnp.sum(before * seq_lengths[None, :], axis=1)
    frequency = jnp.exp(
        -jnp.log(10000.0) * jnp.arange(half_width, dtype=jnp.float32) / half_width
    )
    angles = position.astype(jnp.float32)[None, :] * frequency[:, None]
    cosine, sine_part = jnp.cos(angles), jnp.sin(angles)

    def head_halves(value):
        size = value.shape[1] // 2
        return value.reshape(heads, 2, size, rows).transpose(1, 0, 2, 3).reshape(2, -1, rows)

    def whole_heads(value):
        value = value.reshape(2, heads, -1, rows)
        return value.transpose(1, 0, 2, 3).reshape(heads, -1, rows)

    def nothing(value):
        return value

    def layer_forward(whole_rows, first_values, layer, in_zero, in_first, in_second, in_third, in_fourth):
        gain_first, gain_second = gain_sets[layer][0], gain_sets[layer][1]
        scale_first = lax.rsqrt(jnp.mean(whole_rows * whole_rows, axis=-1, keepdims=True) + EPSILON)
        normed = low(whole_rows * scale_first * gain_first)
        far_normed = in_zero(swap_side(normed))
        side_rows = jnp.concatenate(ordered(column_side, normed, far_normed), axis=0)
        halves = ordered(section, *[dot(weight, side_rows, 1, 1) for weight in w_heads[layer]])
        upper, lower = [half.reshape(side_heads, head_rows, 2 * rows) for half in halves]
        query = rope_pair(upper[:, :half_width], upper[:, half_width:HD], cosine, sine_part)
        key = rope_pair(upper[:, HD:], lower[:, :half_width], cosine, sine_part)
        value = lower[:, half_width:]
        if first_values is not None:
            value = 0.5 * value + 0.5 * wide(first_values)
        mixed = low(value)
        shrunk = [low(half * (HD ** (-0.5) / LOG_2)) for half in query]
        qkv = exchange(
            jnp.concatenate([*shrunk, low(key[0]), low(key[1]), mixed], axis=1), head_groups
        )
        qkv = in_first(qkv)
        out, lse = attention_forward(ends, qkv, parts)
        out = in_second(out)
        attended = head_halves(exchange(out, batch_groups))
        hidden = whole_rows + dot(attended.reshape(-1, rows), w_outs[layer], 0, 0)
        scale_second = lax.rsqrt(jnp.mean(hidden * hidden, axis=-1, keepdims=True) + EPSILON)
        normed_second = low(hidden * scale_second * gain_second)
        far_rows = swap_side(normed_second)
        near = feed_forward(normed_second, *w_ffn[layer], tile)
        far_rows = in_third(after(far_rows, near[3]))
        far = feed_forward(far_rows, *w_ffn[layer], tile)
        sent_down = low(far[3])

        def layer_out(*others):
            far_down = in_fourth(swap_side(after(sent_down, *others)))
            return low(hidden + (near[3] + wide(far_down)))

        saved = (
            whole_rows, scale_first, side_rows, qkv, out, lse, attended, hidden, scale_second,
            (normed_second, far_rows), near[:3], far[:3],
        )
        return layer_out, mixed, saved

    def norm_back(whole_rows, scale_rows, gain, grad_normed, grad_rest):
        unit = whole_rows * scale_rows
        scaled = grad_normed * gain
        grad_gain = jnp.sum(grad_normed * unit, axis=0)
        grad_whole = grad_rest + scale_rows * (
            scaled - unit * jnp.mean(scaled * unit, axis=-1, keepdims=True)
        )
        return grad_gain, grad_whole

    def pick(value, index, axis):
        return lax.dynamic_index_in_dim(value, index, axis, keepdims=False)

    def parted(value, index, axis):
        return pick(value, index, axis), pick(value, 1 - index, axis)

    def moved_pair(pair, swap):
        return pair[0], swap(pair[1])

    def halve(value, index, swap, axis):
        return moved_pair(parted(value, index, axis), swap)

    def add(pair):
        return low(wide(pair[0]) + wide(pair[1]))

    def near_parts(value):
        return parted(value.reshape(2, half_parts, *value.shape[1:]), tp % 2, 1)

    def near_sum(value):
        return moved_pair(near_parts(value), swap_near)

    def far_sum(pair):
        return halve(add(pair), batch, swap_half, 0)

    def layer_backward(grad_rows, extra_values, saved, layer, in_first, in_second, in_third, in_fourth, in_fifth):
        (
            whole_rows, scale_first, _, qkv, out, lse, attended, hidden, scale_second,
            ffn_rows, near, far,
        ) = saved
        gain_first, gain_second = gain_sets[layer][0], gain_sets[layer][1]
        grad_down = low(grad_rows)
        far_down = swap_side(grad_down)
        grad_gate, grad_up, near_back = feed_forward_back(grad_down, *near[:2], *w_ffn[layer], tile)
        far_down = in_first(after(far_down, near_back))
        far_gate, far_up, far_back = feed_forward_back(far_down, *far[:2], *w_ffn[layer], tile)
        far_back = swap_side(low(far_back))
        groups = (
            ((grad_gate, ffn_rows[0]), (far_gate, ffn_rows[1])),
            ((grad_up, ffn_rows[0]), (far_up, ffn_rows[1])),
            ((near[2], grad_down), (far[2], far_down)),
        )
        products = functools.partial(
            half_products, groups=groups, pieces=2 * parts, per_step=2
        )
        sent = products(1 - section)
        moved = swap_section(sent)
        far_back = in_second(after(far_back, sent))
        grad_gain2, grad_hidden = norm_back(
            hidden, scale_second, gain_second, near_back + wide(far_back), wide(grad_rows)
        )
        grad_branch = low(grad_hidden)
        grad_heads = whole_heads(low(dot(w_outs[layer], grad_branch, 1, 1)))
        grad_heads = exchange(grad_heads, batch_groups)
        rest = products(section, addend=moved)
        out_pair = (attended.reshape(-1, rows), grad_branch)
        grad_heads, rest = in_third(grad_heads, rest, out_pair)
        grad_qkv = attention_backward(ends, qkv, out, grad_heads, lse, parts)
        grad_qkv = in_fourth(grad_qkv)
        grad_qkv = in_fifth(exchange(grad_qkv, head_groups))
        grad_qkv = wide(grad_qkv)
        quarter = lambda entry: grad_qkv[:, entry * half_width : (entry + 1) * half_width]
        grad_query = rope_pair(quarter(0), quarter(1), cosine, -sine_part)
        grad_key = rope_pair(quarter(2), quarter(3), cosine, -sine_part)
        grad_value = grad_qkv[:, 2 * HD :]
        send_values = None
        if extra_values is None:
            grad_value = 0.5 * grad_value
            send_values = low(grad_value)
        else:
            grad_value = grad_value + wide(extra_values)
        upper = low(jnp.concatenate([*grad_query, grad_key[0]], axis=1))
        lower = low(jnp.concatenate([grad_key[1], grad_value], axis=1))
        grad_halves = jnp.stack([upper, lower]).reshape(2, -1, 2 * rows)
        return grad_halves, send_values, grad_hidden, out_pair, grad_gain2

    def input_grads_of(grad_halves, grad_hidden, saved, layer, beside):
        whole_rows, scale_first = saved[:2]
        places_of = (section, 1 - section)
        grad_side = sum(
            dot(by_core(grad_halves, place), weight, 0, 0)
            for place, weight in zip(places_of, w_heads[layer])
        ).reshape(2, rows, model_width)
        grad_far = swap_side(low(by_core(grad_side, 1 - column_side)))
        grad_normed = by_core(grad_side, column_side) + wide(beside(grad_far))
        return norm_back(whole_rows, scale_first, gain_sets[layer][0], grad_normed, grad_hidden)

    def piece_sum(value, groups):
        return lax.psum_scatter(
            value, ALL_AXES, scatter_dimension=0, tiled=True, axis_index_groups=groups
        )

    line_groups = device_groups(
        mesh_sizes, lambda s, c, t: (s, c % 2), lambda s, c, t: (c, t)
    )
    plane_shape = (2, 2, parts)
    pending = {}

    def weights_zero(value):
        value, pair = together(value, first_pair)
        w_heads[0], pending["outs"] = spread_heads(pair)
        return value

    def weights_line(value):
        value, piece = together(value, pieces[1][:attention_rows])
        pending["weights"] = spread_half(piece)
        return value

    def weights_outs_first(value):
        value, pending["outs"], w_ffn[0], weights = together(
            value, pending["outs"], w_ffn[0], pending["weights"]
        )
        pending["weights"] = spread_near(weights)
        w_outs[0] = join_outs(spread_outs(pending["outs"]))
        return value

    def weights_far(value):
        value, line = together(value, pending["weights"])
        pending["weights"] = spread_far(spread_line(line))
        w_ffn[1] = feed_forward_weights(after(pieces[1], value))
        return value

    def weights_heads(value):
        value, pairs = together(value, pending["weights"])
        w_heads[1], pending["outs"] = spread_heads(pairs)
        return value

    first_result, first_values, first_saved = layer_forward(
        wide(rows_in), None, 0,
        weights_zero, weights_line, weights_outs_first, weights_far, weights_heads,
    )

    first_out = first_result()

    def start_outs(value):
        value, grads = together(value, cotangent)
        pending["grad_in"] = to_batch(grads)
        return value

    def end_outs(value):
        value, outs, w_ffn[1], pending["grad_in"] = together(
            value, pending["outs"], w_ffn[1], pending["grad_in"]
        )
        w_outs[1] = join_outs(spread_outs(outs))
        pending["first_home"] = to_home(after(first_out, value), 0)
        return value

    second_result, _, second_saved = layer_forward(
        wide(first_out), first_values, 1, nothing, start_outs, end_outs, nothing, nothing
    )
    grad_in = pending["grad_in"]

    def out_sides(out_pair):
        products = functools.partial(half_products, groups=((out_pair,),), pieces=heads, per_step=8)
        out_sum = products(section, addend=swap_section(products(1 - section)))
        return parted(out_sum.reshape(*plane_shape, out_rows, model_width), column_side, 1)

    def second_third(value, rest, out_pair):
        value, rest = together(value, rest)
        rest = rest.reshape(-1, model_width)
        pending["second_rest"] = piece_sum(rest, line_groups)
        pending["second_out_rows"] = second_result(value)
        pending["out"] = out_sides(out_pair)
        value = after(value, pending["out"])
        pending["out"] = moved_pair(pending["out"], swap_side)
        return value, rest

    def second_fourth(value):
        value, pending["first_home"], second_out, out_sum = together(
            value, pending["first_home"], pending["second_out_rows"], pending["out"]
        )
        pending["second_home"] = to_home(second_out, 1)
        pending["second_out"] = add(out_sum).reshape(2 * parts, out_rows, model_width)
        return value

    grad_halves, send_values, grad_hidden, _, second_gain2 = layer_backward(
        grad_in, None, second_saved, 1, nothing, nothing, second_third, second_fourth, nothing
    )
    head_products = functools.partial(
        half_products,
        groups=(((grad_halves.reshape(-1, 2 * rows), second_saved[2]),),),
        pieces=side_heads,
        per_step=4,
    )

    def head_start(value):
        value, sent = together(value, head_products(1 - section))
        pending["moved"] = swap_section(sent)
        return value

    second_gain1, second_grad = input_grads_of(
        grad_halves, grad_hidden, second_saved, 1, head_start
    )
    second_grad = low(second_grad)

    def first_first(value):
        head = head_products(section, addend=pending["moved"])
        head = jnp.concatenate([head, pending["second_out"]], axis=1)
        head = parted(head.reshape(2, parts, -1, model_width), row_side, 0)
        value, head = together(value, head)
        pending["head"] = moved_pair(head, swap_far)
        return value

    def first_second(value):
        return value

    def first_third(value, rest, out_pair):
        out_sum = out_sides(out_pair)
        rest = rest.reshape(2, parts, -1, model_width)
        rest_a = parted(rest[:, :, : 2 * unit_rows], row_side, 0)
        rest_b = parted(rest[:, :, 2 * unit_rows :], row_side, 0)
        (
            value, rest_a, rest_b, out_sum, head, pending["second_rest"], pending["second_home"]
        ) = together(
            value, rest_a, rest_b, out_sum, pending["head"], pending["second_rest"],
            pending["second_home"],
        )
        pending["rest_a"] = moved_pair(rest_a, swap_far)
        pending["rest_b"] = rest_b
        pending["out"] = moved_pair(out_sum, swap_side)
        pending["head"] = near_sum(add(head))
        return value, rest

    def first_fourth(value):
        value, rest_a, rest_b, out_sum, head = together(
            value, pending["rest_a"], pending["rest_b"], pending["out"], pending["head"]
        )
        pending["head"] = far_sum(head)
        pending["rest_b"] = moved_pair(rest_b, swap_far)
        pending["rest_a"] = near_sum(add(rest_a))
        pending["out"] = halve(add(out_sum), row_side, swap_far, 0)
        return value

    def first_fifth(value):
        value, rest_a, rest_b, out_sum, head = together(
            value, pending["rest_a"], pending["rest_b"], pending["out"], pending["head"]
        )
        second = jnp.concatenate([pending["second_rest"], add(head)], axis=0)
        pending["second"] = lax.all_gather(second, "ctx", axis=0, tiled=False)
        pending["out"] = add(out_sum)
        pending["rest_a"] = far_sum(rest_a)
        pending["rest_b"] = near_sum(add(rest_b))
        return value

    first_halves, _, first_hidden, _, first_gain2 = layer_backward(
        second_grad, send_values, first_saved, 0,
        first_first, first_second, first_third, first_fourth, first_fifth,
    )
    head_products = functools.partial(
        half_products,
        groups=(((first_halves.reshape(-1, 2 * rows), first_saved[2]),),),
        pieces=side_heads,
        per_step=4,
    )
    sent = head_products(1 - section)
    moved = swap_section(sent)
    def head_end(value):
        head = head_products(section, addend=moved).reshape(2, parts, head_rows, model_width)
        head = parted(head, row_side, 0)
        pending["head"] = moved_pair(head, swap_far)
        return after(value, head)

    first_gain1, first_grad = input_grads_of(
        after(first_halves, sent), first_hidden, first_saved, 0, head_end
    )
    def summed(value, swap):
        return value + swap(value)

    gain_rows = jnp.stack([first_gain1, first_gain2, second_gain1, second_gain2])
    gain_rows = summed(gain_rows, swap_section)
    head, rest_a, rest_b, gain_rows, first_grad, home = together(
        pending["head"], pending["rest_a"], pending["rest_b"], gain_rows, low(first_grad), second_grad
    )
    second_grad_home = to_home(home, 1)
    head = near_sum(jnp.concatenate([add(head), pending["out"]], axis=1))
    rest_b = far_sum(rest_b)
    first_grad_home = to_home(first_grad, 0)
    gain_rows = summed(summed(gain_rows, swap_side), swap_far)
    head, rest_b, gain_rows = together(head, rest_b, gain_rows)
    head = far_sum(head)
    rest = jnp.concatenate([add(rest_a), add(rest_b)], axis=0)
    rest = lax.all_gather(rest, "ctx", axis=0, tiled=False)
    gain_total = summed(summed(gain_rows, swap_near), swap_half)
    head, first_grad_home, second_grad_home = together(head, first_grad_home, second_grad_home)
    head = all_to_all(copies(add(head), contexts), "ctx")
    rest, second, head = together(rest, pending["second"], head)
    first_grads = (rest, head)
    second_grads = (second[:, : 3 * unit_rows], second[:, 3 * unit_rows :])
    first_home, second_home = pending["first_home"], pending["second_home"]
    gain_total = jnp.where(leading, gain_total[:2], gain_total[2:])

    def finish(first, second):
        mine = jnp.where(leading, first, second)
        moved = swap_section(jnp.where(leading, second, first))
        return ordered(section, mine, moved)

    def joined(halves, first, count):
        both = jnp.stack([half[:, first : first + count] for half in halves], axis=1)
        return wide(both).reshape(-1, model_width)

    rest_grads = finish(first_grads[0], second_grads[0])
    grad_wgate, grad_wup, grad_wd = [
        joined(rest_grads, entry * unit_rows, unit_rows) for entry in range(3)
    ]
    head, grad_wgate, grad_wup, grad_wd = together(first_grads[1], grad_wgate, grad_wup, grad_wd)
    head_grads = finish(head, second_grads[1])
    grad_wqkv = joined(head_grads, 0, head_rows).reshape(contexts, 3, HD, model_width)
    grad_wo = joined(head_grads, head_rows, out_rows)
    return (
        at_home(first_home, second_home),
        wide(at_home(first_grad_home, second_grad_home)),
        gain_total[0:1],
        grad_wqkv.transpose(1, 0, 2, 3)[None],
        grad_wo[None],
        gain_total[1:2],
        jnp.stack([grad_wgate, grad_wup])[None],
        grad_wd[None],
    )


def body(mesh_sizes, *arguments):
    inputs, _, _, _, wqkv = arguments[:5]
    sections, contexts, parts = mesh_sizes
    own_heads, own_units = wqkv.shape[2], arguments[7].shape[2]
    fits = (
        sections == 2
        and inputs.shape[0] == 2
        and contexts == 4
        and parts % 2 == 0
        and own_heads == contexts
        and own_units % (16 * contexts) == 0
        and inputs.shape[1] % 128 == 0
    )
    if fits:
        return split_body(mesh_sizes, *arguments)
    return general_body(*arguments)


def solution(mesh):
    placed = (
        P(None, ("ctx", "tp"), None),
        P(None, ("ctx", "tp"), None),
        P(),
        P("section", None),
        P("section", None, "tp", None, None),
        P("section", "tp", None),
        P("section", None),
        P("section", None, "tp", None),
        P("section", "tp", None),
    )
    mesh_sizes = tuple(mesh.shape[axis] for axis in ALL_AXES)
    return jax.shard_map(
        functools.partial(body, mesh_sizes),
        mesh=mesh,
        in_specs=placed,
        out_specs=(
            P("section", None, ("ctx", "tp"), None),
            P("section", None, ("ctx", "tp"), None),
            P("section", None),
            P("section", None, "tp", None, None),
            P("section", "tp", None),
            P("section", None),
            P("section", None, "tp", None),
            P("section", "tp", None),
        ),
        check_vma=False,
    )
```

```python
import functools

import jax
import jax.numpy as jnp
from jax import lax
from jax.experimental import pallas as pl
from jax.experimental.pallas import tpu as pltpu
from jax.sharding import PartitionSpec as P

HD = 64
EPSILON = 1e-06
MASKED = -1e30
ALL_AXES = ("section", "ctx", "tp")
CHUNK = 2
ONES = 16
LOG_2 = 0.6931471805599453
LIGHT = pl.CostEstimate(flops=1, bytes_accessed=1, transcendentals=0)
VMEM_LIMIT = 40 * 1024 * 1024


def shifted(block, axis, distance):
    devices = range(lax.axis_size(axis))
    route = [(i - distance, i) for i in devices if i - distance in devices]
    return lax.ppermute(block, axis, route)


def rope_parts(position):
    half_width = HD // 2
    frequency = jnp.exp(-jnp.log(10000.0) * jnp.arange(half_width, dtype=jnp.float32) / half_width)
    angles = position.astype(jnp.float32)[:, None] * frequency[None, :]
    return (jnp.cos(angles), jnp.sin(angles))


def rotate(vectors, cosine, sine_part):
    half_width = HD // 2
    leading_half = vectors[..., :half_width]
    trailing_half = vectors[..., half_width:]
    cosine = cosine[:, None, :]
    sine_part = sine_part[:, None, :]
    return jnp.concatenate(
        [
            leading_half * cosine - trailing_half * sine_part,
            trailing_half * cosine + leading_half * sine_part,
        ],
        axis=-1,
    )


def rotate_back(vectors, cosine, sine_part):
    half_width = HD // 2
    leading_half = vectors[..., :half_width]
    trailing_half = vectors[..., half_width:]
    cosine = cosine[:, None, :]
    sine_part = sine_part[:, None, :]
    return jnp.concatenate(
        [
            leading_half * cosine + trailing_half * sine_part,
            trailing_half * cosine - leading_half * sine_part,
        ],
        axis=-1,
    )


def inner_rows(left, right):
    return lax.dot_general(
        left, right, (((0,), (0,)), ((), ())), preferred_element_type=jnp.float32
    )


def outer_cols(left, right):
    return lax.dot_general(
        left, right, (((1,), (1,)), ((), ())), preferred_element_type=jnp.float32
    )


def spread(row_block):
    return lax.all_gather(row_block, "tp", axis=0, tiled=True)


def collect(partial_value):
    return lax.psum_scatter(
        partial_value.astype(jnp.bfloat16), "tp", scatter_dimension=0, tiled=True
    ).astype(jnp.float32)


def fetch_keys(key_value):
    return lax.all_gather(key_value, "ctx", axis=0, tiled=True)


def query_bounds(seq_lengths, block_first, row_count):
    token_index = block_first + jnp.arange(row_count, dtype=jnp.int32)
    doc_ends = jnp.cumsum(seq_lengths)
    before = (doc_ends[None, :] <= token_index[:, None]).astype(jnp.int32)
    doc_start = jnp.sum(before * seq_lengths[None, :], axis=1)
    return (token_index, doc_start)


def block_scores(query_heads, pair_block, block_first, token_index, doc_start, head_width):
    row_count = pair_block.shape[0]
    key_heads = pair_block[:, :head_width].reshape(row_count, head_width // HD, HD)
    value_heads = pair_block[:, head_width:].reshape(row_count, head_width // HD, HD)
    scores = jnp.einsum(
        "qhd,khd->hqk", query_heads, key_heads, preferred_element_type=jnp.float32
    ) * HD ** (-0.5)
    key_index = block_first + jnp.arange(row_count, dtype=jnp.int32)
    allowed = (key_index[None, :] >= doc_start[:, None]) & (
        key_index[None, :] <= token_index[:, None]
    )
    return (scores, allowed[None], key_heads, value_heads)


def split_blocks(pairs_all, row_count):
    blocks = pairs_all.reshape(-1, row_count, pairs_all.shape[1])
    block_starts = jnp.arange(blocks.shape[0], dtype=jnp.int32) * row_count
    return (blocks, block_starts)


def attend(query_heads, pairs_all, token_index, doc_start, head_width):
    row_count = query_heads.shape[0]
    head_count = head_width // HD
    blocks, block_starts = split_blocks(pairs_all, row_count)
    last_query = token_index[row_count - 1]
    first_query = doc_start[0]

    def rowmax_live(carried, block_parts):
        running_top, running_sum = carried
        scores, allowed, unused_keys, unused_values = block_scores(
            query_heads, block_parts[0], block_parts[1], token_index, doc_start, head_width
        )
        masked = jnp.where(allowed, scores, -1e30)
        new_top = jnp.maximum(running_top, jnp.max(masked, axis=-1))
        running_sum = running_sum * jnp.exp(running_top - new_top) + jnp.sum(
            jnp.where(allowed, jnp.exp(masked - new_top[..., None]), 0.0), axis=-1
        )
        return (new_top, running_sum)

    def rowmax_step(carried, block_parts):
        live = (block_parts[1] <= last_query) & (block_parts[1] + row_count > first_query)
        return (
            lax.cond(live, lambda held: rowmax_live(held, block_parts), lambda held: held, carried),
            None,
        )

    initial = (
        jnp.full((head_count, row_count), -1e30, jnp.float32),
        jnp.zeros((head_count, row_count), jnp.float32),
    )
    (running_top, running_sum), unused = lax.scan(rowmax_step, initial, (blocks, block_starts))
    log_total = running_top + jnp.log(running_sum)

    def output_live(accumulated, block_parts):
        scores, allowed, unused_keys, value_heads = block_scores(
            query_heads, block_parts[0], block_parts[1], token_index, doc_start, head_width
        )
        soft_weights = jnp.where(allowed, jnp.exp(scores - log_total[..., None]), 0.0).astype(
            jnp.bfloat16
        )
        return accumulated + jnp.einsum(
            "hqk,khd->qhd", soft_weights, value_heads, preferred_element_type=jnp.float32
        )

    def output_step(accumulated, block_parts):
        live = (block_parts[1] <= last_query) & (block_parts[1] + row_count > first_query)
        return (
            lax.cond(
                live, lambda held: output_live(held, block_parts), lambda held: held, accumulated
            ),
            None,
        )

    accumulated, unused = lax.scan(
        output_step, jnp.zeros((row_count, head_count, HD), jnp.float32), (blocks, block_starts)
    )
    return (accumulated, log_total)


def attend_back(
    query_heads, pairs_all, token_index, doc_start, head_width, log_total, accumulated, grad_heads
):
    row_count = query_heads.shape[0]
    head_count = head_width // HD
    blocks, block_starts = split_blocks(pairs_all, row_count)
    last_query = token_index[row_count - 1]
    first_query = doc_start[0]
    rowdot = jnp.sum(grad_heads.astype(jnp.float32) * accumulated, axis=-1).T

    def grad_live(grad_acc, block_parts):
        scores, allowed, key_heads, value_heads = block_scores(
            query_heads, block_parts[0], block_parts[1], token_index, doc_start, head_width
        )
        soft_weights = jnp.where(allowed, jnp.exp(scores - log_total[..., None]), 0.0)
        grad_soft = jnp.einsum(
            "qhd,khd->hqk", grad_heads, value_heads, preferred_element_type=jnp.float32
        )
        grad_scores = (soft_weights * (grad_soft - rowdot[..., None])).astype(jnp.bfloat16)
        grad_acc = grad_acc + jnp.einsum(
            "hqk,khd->qhd", grad_scores, key_heads, preferred_element_type=jnp.float32
        )
        grad_keys = jnp.einsum(
            "hqk,qhd->khd", grad_scores, query_heads, preferred_element_type=jnp.float32
        ) * HD ** (-0.5)
        grad_values = jnp.einsum(
            "hqk,qhd->khd",
            soft_weights.astype(jnp.bfloat16),
            grad_heads,
            preferred_element_type=jnp.float32,
        )
        return (grad_acc, (grad_keys, grad_values))

    def grad_skip(grad_acc):
        empty = jnp.zeros((row_count, head_count, HD), jnp.float32)
        return (grad_acc, (empty, empty))

    def grad_step(grad_acc, block_parts):
        live = (block_parts[1] <= last_query) & (block_parts[1] + row_count > first_query)
        return lax.cond(live, lambda held: grad_live(held, block_parts), grad_skip, grad_acc)

    grad_query, (grad_keys, grad_values) = lax.scan(
        grad_step, jnp.zeros((row_count, head_count, HD), jnp.float32), (blocks, block_starts)
    )
    grad_query = grad_query * HD ** (-0.5)
    grad_pairs = jnp.concatenate(
        [grad_keys.reshape(-1, head_width), grad_values.reshape(-1, head_width)], axis=1
    )
    return (grad_query, grad_pairs)


def norm_back(whole_rows, scale_rows, gain, grad_normed, grad_rest):
    unit_rows = whole_rows * scale_rows
    scaled = grad_normed * gain.astype(jnp.float32)
    grad_gain = jnp.sum(grad_normed * unit_rows, axis=0)
    grad_whole = grad_rest + scale_rows * (
        scaled - unit_rows * jnp.mean(scaled * unit_rows, axis=-1, keepdims=True)
    )
    return (grad_gain, grad_whole)


def layer_forward(row_block, first_values, value_mix, weights, seq_lengths):
    gain_first, w_qkv, w_out, gain_second, w_gateup, w_down = weights
    head_count = w_qkv.shape[1]
    head_width = head_count * HD
    model_width = row_block.shape[1]
    whole_rows = row_block.astype(jnp.float32)
    scale_first = lax.rsqrt(jnp.mean(whole_rows * whole_rows, axis=-1, keepdims=True) + EPSILON)
    normed = (whole_rows * scale_first * gain_first.astype(jnp.float32)).astype(jnp.bfloat16)
    normed_all = spread(normed)
    row_count = normed_all.shape[0]
    projected = outer_cols(normed_all, w_qkv.reshape(3 * head_width, model_width))
    token_index, doc_start = query_bounds(seq_lengths, lax.axis_index("ctx") * row_count, row_count)
    cosine, sine_part = rope_parts(token_index - doc_start)
    query_heads = rotate(
        projected[:, :head_width].reshape(row_count, head_count, HD), cosine, sine_part
    ).astype(jnp.bfloat16)
    key_heads = rotate(
        projected[:, head_width : 2 * head_width].reshape(row_count, head_count, HD),
        cosine,
        sine_part,
    ).astype(jnp.bfloat16)
    mixed = (
        (1.0 - value_mix) * projected[:, 2 * head_width :]
        + value_mix * first_values.astype(jnp.float32)
    ).astype(jnp.bfloat16)
    key_value = jnp.concatenate([key_heads.reshape(row_count, head_width), mixed], axis=1)
    pairs_all = fetch_keys(key_value)
    accumulated, log_total = attend(query_heads, pairs_all, token_index, doc_start, head_width)
    attended = accumulated.reshape(row_count, head_width).astype(jnp.bfloat16)
    hidden = whole_rows + collect(jnp.dot(attended, w_out, preferred_element_type=jnp.float32))
    scale_second = lax.rsqrt(jnp.mean(hidden * hidden, axis=-1, keepdims=True) + EPSILON)
    normed_second = (hidden * scale_second * gain_second.astype(jnp.float32)).astype(jnp.bfloat16)
    ffn_rows = spread(normed_second)
    gate_up = outer_cols(ffn_rows, w_gateup.reshape(-1, model_width))
    unit_count = gate_up.shape[1] // 2
    gate_part = gate_up[:, :unit_count]
    up_part = gate_up[:, unit_count:]
    activated = (jax.nn.silu(gate_part) * up_part).astype(jnp.bfloat16)
    down_part = jnp.dot(activated, w_down, preferred_element_type=jnp.float32)
    branch_out = collect(down_part)
    layer_out = (hidden + branch_out).astype(jnp.bfloat16)
    saved = (
        whole_rows,
        scale_first,
        normed_all,
        query_heads,
        pairs_all,
        token_index,
        doc_start,
        cosine,
        sine_part,
        log_total,
        accumulated,
        attended,
        hidden,
        scale_second,
        ffn_rows,
        gate_part,
        up_part,
        activated,
    )
    return (layer_out, mixed, pairs_all, saved)


def layer_backward(grad_rows, extra_values, value_mix, weights, saved):
    gain_first, w_qkv, w_out, gain_second, w_gateup, w_down = weights
    (
        whole_rows,
        scale_first,
        normed_all,
        query_heads,
        pairs_all,
        token_index,
        doc_start,
        cosine,
        sine_part,
        log_total,
        accumulated,
        attended,
        hidden,
        scale_second,
        ffn_rows,
        gate_part,
        up_part,
        activated,
    ) = saved
    model_width = whole_rows.shape[1]
    head_count = w_qkv.shape[1]
    head_width = head_count * HD
    row_count = normed_all.shape[0]
    grad_hidden = grad_rows.astype(jnp.float32)
    grad_down = spread(grad_rows)
    grad_wd = inner_rows(activated, grad_down)
    grad_act = outer_cols(grad_down, w_down)
    sigmoid_gate = jax.nn.sigmoid(gate_part)
    grad_gate = grad_act * up_part * sigmoid_gate * (1.0 + gate_part * (1.0 - sigmoid_gate))
    grad_up = grad_act * gate_part * sigmoid_gate
    grad_gate_up = jnp.concatenate([grad_gate, grad_up], axis=1).astype(jnp.bfloat16)
    grad_wgu = inner_rows(grad_gate_up, ffn_rows).reshape(w_gateup.shape)
    back_second = jnp.dot(
        grad_gate_up, w_gateup.reshape(-1, model_width), preferred_element_type=jnp.float32
    )
    grad_normed_second = collect(back_second)
    grad_gain2, grad_hidden = norm_back(
        hidden, scale_second, gain_second, grad_normed_second, grad_hidden
    )
    grad_branch_all = spread(grad_hidden.astype(jnp.bfloat16))
    grad_wo = inner_rows(attended, grad_branch_all)
    grad_heads = (
        outer_cols(grad_branch_all, w_out).astype(jnp.bfloat16).reshape(row_count, head_count, HD)
    )
    grad_query, grad_pairs_all = attend_back(
        query_heads,
        pairs_all,
        token_index,
        doc_start,
        head_width,
        log_total,
        accumulated,
        grad_heads,
    )
    grad_pairs = lax.psum_scatter(
        grad_pairs_all.astype(jnp.bfloat16), "ctx", scatter_dimension=0, tiled=True
    ).astype(jnp.float32)
    grad_mixed = grad_pairs[:, head_width:] + extra_values.astype(jnp.float32)
    grad_keys = rotate_back(
        grad_pairs[:, :head_width].reshape(row_count, head_count, HD), cosine, sine_part
    )
    grad_query = rotate_back(grad_query, cosine, sine_part)
    grad_projected = jnp.concatenate(
        [
            grad_query.reshape(row_count, head_width),
            grad_keys.reshape(row_count, head_width),
            (1.0 - value_mix) * grad_mixed,
        ],
        axis=1,
    ).astype(jnp.bfloat16)
    send_values = (value_mix * grad_mixed).astype(jnp.bfloat16)
    grad_wqkv = inner_rows(grad_projected, normed_all).reshape(w_qkv.shape)
    grad_normed = collect(
        jnp.dot(
            grad_projected,
            w_qkv.reshape(3 * head_width, model_width),
            preferred_element_type=jnp.float32,
        )
    )
    grad_gain1, grad_whole = norm_back(
        whole_rows, scale_first, gain_first, grad_normed, grad_hidden
    )
    return (
        grad_whole,
        send_values,
        (grad_gain1, grad_wqkv, grad_wo, grad_gain2, grad_wgu, grad_wd),
    )


def general_body(inputs, cotangent, lengths, gain1, wqkv, wo, gain2, wgu, wd):
    section_index = lax.axis_index("section")
    leading = section_index == 0
    value_mix = jnp.where(leading, 0.0, 0.5).astype(jnp.float32)
    micro_count = inputs.shape[0]
    local_rows = inputs.shape[1]
    model_width = inputs.shape[2]
    head_width = wqkv.shape[2] * HD
    row_count = local_rows * lax.axis_size("tp")
    gateup_use, down_use = (wgu[0], wd[0])
    weights = (gain1[0], wqkv[0], wo[0], gain2[0], gateup_use, down_use)
    recv_rows = jnp.zeros((local_rows, model_width), jnp.bfloat16)
    recv_values = jnp.zeros((row_count, head_width), jnp.bfloat16)
    states = []
    outputs = []
    for turn_index in range(micro_count + 1):
        own_rows = inputs[min(turn_index, micro_count - 1)]
        row_block = jnp.where(leading, own_rows, recv_rows)
        seq_lengths = jnp.where(
            leading, lengths[min(turn_index, micro_count - 1)], lengths[max(turn_index - 1, 0)]
        )
        layer_out, mixed, pairs_all, unused = layer_forward(
            row_block, recv_values, value_mix, weights, seq_lengths
        )
        kept_pairs = None
        states.append((row_block, recv_values, seq_lengths, kept_pairs))
        outputs.append(layer_out)
        if turn_index < micro_count:
            recv_rows, recv_values = shifted((layer_out, mixed), "section", 1)
    grad_rows_in = jnp.zeros((local_rows, model_width), jnp.bfloat16)
    grad_values_in = jnp.zeros((row_count, head_width), jnp.bfloat16)
    totals = None
    turn_grads = []
    for turn_index in range(micro_count + 1):
        row_block, first_values, seq_lengths, kept_pairs = states[micro_count - turn_index]
        if turn_index < micro_count:
            fed_grad = cotangent[micro_count - 1 - turn_index]
        else:
            fed_grad = jnp.zeros_like(cotangent[0])
        grad_out = jnp.where(leading, grad_rows_in, fed_grad)
        unused_out, unused_mixed, unused_pairs, saved = layer_forward(
            row_block, first_values, value_mix, weights, seq_lengths
        )
        grad_whole, send_values, grads = layer_backward(
            grad_out, grad_values_in, value_mix, weights, saved
        )
        totals = grads if totals is None else jax.tree.map(jnp.add, totals, grads)
        sent_rows = grad_whole.astype(jnp.bfloat16)
        turn_grads.append(jnp.where(leading, grad_whole, sent_rows.astype(jnp.float32)))
        if turn_index < micro_count:
            grad_rows_in, grad_values_in = shifted((sent_rows, send_values), "section", -1)
    grad_gain1, grad_wqkv, grad_wo, grad_gain2, grad_wgu, grad_wd = totals
    grad_wqkv, grad_wo, grad_wgu, grad_wd = (
        lax.psum(grad_wqkv.astype(jnp.bfloat16), "ctx").astype(jnp.float32),
        lax.psum(grad_wo.astype(jnp.bfloat16), "ctx").astype(jnp.float32),
        lax.psum(grad_wgu.astype(jnp.bfloat16), "ctx").astype(jnp.float32),
        lax.psum(grad_wd.astype(jnp.bfloat16), "ctx").astype(jnp.float32),
    )
    grad_gain1, grad_gain2 = lax.psum((grad_gain1, grad_gain2), ("ctx", "tp"))
    acts = jnp.stack(
        [
            jnp.where(leading, outputs[batch_index], outputs[batch_index + 1])
            for batch_index in range(micro_count)
        ]
    )[None]
    input_grads = jnp.stack(
        [
            jnp.where(
                leading,
                turn_grads[micro_count - batch_index],
                turn_grads[micro_count - 1 - batch_index],
            )
            for batch_index in range(micro_count)
        ]
    )[None]
    return (
        acts,
        input_grads,
        grad_gain1[None],
        grad_wqkv[None],
        grad_wo[None],
        grad_gain2[None],
        grad_wgu[None],
        grad_wd[None],
    )


def device_groups(mesh_sizes, key, order):
    sections, contexts, parts = mesh_sizes
    groups = {}
    for section in range(sections):
        for ctx in range(contexts):
            for tp in range(parts):
                place = (section, ctx, tp)
                number = (section * contexts + ctx) * parts + tp
                groups.setdefault(key(*place), []).append((order(*place), number))
    return [[number for _, number in sorted(members)] for _, members in sorted(groups.items())]


def exchange(value, groups):
    return lax.all_to_all(
        value, ALL_AXES, split_axis=0, concat_axis=0, tiled=True, axis_index_groups=groups
    )


def document_bounds(ends_ref, index):
    start = jnp.zeros_like(index)
    for entry in range(ends_ref.shape[0]):
        end = ends_ref[entry]
        start = jnp.where(index >= end, end, start)
    return start


def scalar_start(ends_ref, index):
    start = jnp.int32(0)
    for entry in range(ends_ref.shape[0]):
        start = jnp.where(index >= ends_ref[entry], ends_ref[entry], start)
    return start


def scalar_end(ends_ref, index):
    end = ends_ref[ends_ref.shape[0] - 1]
    for entry in range(ends_ref.shape[0] - 2, -1, -1):
        end = jnp.where(index < ends_ref[entry], ends_ref[entry], end)
    return end


def dot(left, right, left_dim, right_dim):
    return lax.dot_general(
        left, right, (((left_dim,), (right_dim,)), ((), ())), preferred_element_type=jnp.float32
    )


def fold_rows(value, combine):
    rows, width = value.shape
    return combine(value.reshape(rows // 8, 8, width), axis=0)


def block_place(block, parts, width):
    entry = (block // (2 * parts)) * parts + block % parts
    return entry, pl.ds(pl.multiple_of((block // parts % 2) * width, width), width)


def attention_forward_kernel(parts, ends_ref, qkv_ref, out_ref, lse_ref, keys_ref, values_ref):
    program = pl.program_id(0)
    blocks, block_width = 2 * qkv_ref.shape[0], qkv_ref.shape[2] // 2
    width = CHUNK * block_width

    @pl.when(program == 0)
    def _():
        def turn(j, carry):
            entry, columns = block_place(j, parts, block_width)
            keys_ref[j] = qkv_ref[entry, HD : 2 * HD, columns].T
            values_ref[j, 0:HD, :] = qkv_ref[entry, 2 * HD : 3 * HD, columns]
            values_ref[j, HD : HD + ONES, :] = jnp.ones((ONES, block_width), jnp.bfloat16)
            return carry

        lax.fori_loop(0, blocks, turn, 0)

    query = []
    for block in range(CHUNK):
        entry, columns = block_place(program * CHUNK + block, parts, block_width)
        query.append(qkv_ref[entry, 0:HD, columns])
    query = jnp.concatenate(query, axis=1)
    first = program * width
    query_index = first + lax.broadcasted_iota(jnp.int32, (1, width), 1)
    start = document_bounds(ends_ref, query_index)
    low_chunk = scalar_start(ends_ref, first) // width
    high_start = scalar_start(ends_ref, first + width - 1)
    middle = jnp.clip((high_start + width - 1) // width, low_chunk, program)

    def step(chunk, carry, masked):
        top, acc = carry
        parts = []
        for entry in range(CHUNK):
            j = chunk * CHUNK + entry
            scores = dot(keys_ref[j], query, 1, 0)
            if masked:
                key_index = j * block_width + lax.broadcasted_iota(jnp.int32, (block_width, 1), 0)
                allowed = (key_index >= start) & (key_index <= query_index)
                scores = jnp.where(allowed, scores, MASKED)
            parts.append(scores)
        part_top = functools.reduce(jnp.maximum, [fold_rows(part, jnp.max) for part in parts])
        new_top = jnp.maximum(top, jnp.max(part_top, axis=0, keepdims=True))
        acc = acc * jnp.exp2(top - new_top)
        for entry in range(CHUNK):
            weights = jnp.exp2(parts[entry] - new_top).astype(jnp.bfloat16)
            acc = acc + dot(values_ref[chunk * CHUNK + entry], weights, 1, 0)
        return new_top, acc

    def on_diagonal(carry):
        top, acc = carry
        parts_of, tops = [], []
        for block in range(CHUNK):
            columns = slice(block * block_width, width)
            j = program * CHUNK + block
            scores = dot(keys_ref[j], query[:, columns], 1, 0)
            key_index = j * block_width + lax.broadcasted_iota(jnp.int32, (block_width, 1), 0)
            allowed = (key_index >= start[:, columns]) & (key_index <= query_index[:, columns])
            scores = jnp.where(allowed, scores, MASKED)
            parts_of.append(scores)
            part_top = fold_rows(scores, jnp.max)
            if block > 0:
                before = jnp.full((8, block * block_width), MASKED, jnp.float32)
                part_top = jnp.concatenate([before, part_top], axis=1)
            tops.append(part_top)
        chunk_top = jnp.max(functools.reduce(jnp.maximum, tops), axis=0, keepdims=True)
        new_top = jnp.maximum(top, chunk_top)
        acc = acc * jnp.exp2(top - new_top)
        for block, scores in enumerate(parts_of):
            weights = jnp.exp2(scores - new_top[:, block * block_width :]).astype(jnp.bfloat16)
            added = dot(values_ref[program * CHUNK + block], weights, 1, 0)
            if block > 0:
                before = jnp.zeros((HD + ONES, block * block_width), jnp.float32)
                added = jnp.concatenate([before, added], axis=1)
            acc = acc + added
        return new_top, acc

    carry = (
        jnp.full((1, width), MASKED, jnp.float32),
        jnp.zeros((HD + ONES, width), jnp.float32),
    )
    carry = lax.fori_loop(low_chunk, middle, functools.partial(step, masked=True), carry)
    carry = lax.fori_loop(middle, program, functools.partial(step, masked=False), carry)
    top, acc = on_diagonal(carry)
    total = acc[HD : HD + 1]
    out = (acc[:HD] / total).astype(jnp.bfloat16)
    lse = top + jnp.log2(total)
    for entry in range(CHUNK):
        columns = slice(entry * block_width, (entry + 1) * block_width)
        out_ref[entry] = out[:, columns]
        lse_ref[entry] = lse[:, columns]


def attention_forward(ends, qkv, parts):
    blocks, width = 2 * qkv.shape[0], qkv.shape[2] // 2
    return pl.pallas_call(
        functools.partial(attention_forward_kernel, parts),
        grid_spec=pltpu.PrefetchScalarGridSpec(
            num_scalar_prefetch=1,
            grid=(blocks // CHUNK,),
            in_specs=[pl.BlockSpec(qkv.shape, lambda i, ends_ref: (0, 0, 0))],
            out_specs=[
                pl.BlockSpec((CHUNK, HD, width), lambda i, ends_ref: (i, 0, 0)),
                pl.BlockSpec((CHUNK, 1, width), lambda i, ends_ref: (i, 0, 0)),
            ],
            scratch_shapes=[
                pltpu.VMEM((blocks, width, HD), jnp.bfloat16),
                pltpu.VMEM((blocks, HD + ONES, width), jnp.bfloat16),
            ],
        ),
        out_shape=[
            jax.ShapeDtypeStruct((blocks, HD, width), jnp.bfloat16),
            jax.ShapeDtypeStruct((blocks, 1, width), jnp.float32),
        ],
        compiler_params=pltpu.CompilerParams(vmem_limit_bytes=VMEM_LIMIT),
        cost_estimate=LIGHT,
        name="attention_forward",
    )(ends, qkv)


def attention_backward_kernel(
    parts, ends_ref, qkv_ref, out_ref, grad_ref, lse_ref, result_ref,
    query_grad_ref, delta_ref, queries_ref, grads_ref, lses_ref,
):
    program = pl.program_id(0)
    blocks, block_width = 2 * qkv_ref.shape[0], qkv_ref.shape[2] // 2
    width = CHUNK * block_width

    @pl.when(program == 0)
    def _():
        def turn(i, carry):
            for entry in range(CHUNK):
                block = i * CHUNK + entry
                columns = slice(entry * block_width, (entry + 1) * block_width)
                grad = grad_ref[block]
                place, tokens = block_place(block, parts, block_width)
                queries_ref[i, :, columns] = qkv_ref[place, 0:HD, tokens]
                grads_ref[i, :, columns] = grad
                lses_ref[i, :, columns] = lse_ref[block]
                delta_ref[i, :, columns] = jnp.sum(
                    grad.astype(jnp.float32) * out_ref[block].astype(jnp.float32),
                    axis=0,
                    keepdims=True,
                )
            query_grad_ref[i] = jnp.zeros((HD, width), jnp.float32)
            return carry

        lax.fori_loop(0, blocks // CHUNK, turn, 0)

    own_places = [
        block_place(program * CHUNK + block, parts, block_width) for block in range(CHUNK)
    ]

    def joined(low_row, high_row):
        return jnp.concatenate(
            [qkv_ref[place, low_row:high_row, tokens] for place, tokens in own_places], axis=1
        )

    first = program * width
    keys_t = joined(HD, 2 * HD)
    keys = keys_t.T
    values = joined(2 * HD, 3 * HD).T
    key_index = first + lax.broadcasted_iota(jnp.int32, (width, 1), 0)
    near_end = scalar_end(ends_ref, first)
    far_end = scalar_end(ends_ref, first + width - 1)
    stop = (far_end - 1) // width + 1
    middle = jnp.clip(near_end // width, program + 1, stop)

    def step(i, carry, masked):
        key_grad, value_grad = carry
        query = queries_ref[i]
        grad = grads_ref[i]
        weights = jnp.exp2(dot(keys, query, 1, 0) - lses_ref[i])
        if masked:
            query_index = i * width + lax.broadcasted_iota(jnp.int32, (1, width), 1)
            start = document_bounds(ends_ref, query_index)
            allowed = (key_index >= start) & (key_index <= query_index)
            weights = jnp.where(allowed, weights, 0.0)
        grad_weights = dot(values, grad, 1, 0)
        grad_scores = (weights * (grad_weights - delta_ref[i])).astype(jnp.bfloat16)
        query_grad_ref[i] += dot(keys_t, grad_scores, 1, 0)
        value_grad = value_grad + dot(grad, weights.astype(jnp.bfloat16), 1, 1)
        key_grad = key_grad + dot(query, grad_scores, 1, 1)
        return key_grad, value_grad

    key_grad = jnp.zeros((HD, width), jnp.float32)
    value_grad = jnp.zeros((HD, width), jnp.float32)
    own_query_grads = []
    for block in range(CHUNK):
        columns = slice(block * block_width, (block + 1) * block_width)
        height = (block + 1) * block_width
        query = queries_ref[program, :, columns]
        grad = grads_ref[program, :, columns]
        query_index = (
            first + block * block_width + lax.broadcasted_iota(jnp.int32, (1, block_width), 1)
        )
        start = document_bounds(ends_ref, query_index)
        rows_index = key_index[:height]
        allowed = (rows_index >= start) & (rows_index <= query_index)
        scores = dot(keys[:height], query, 1, 0)
        weights = jnp.where(allowed, jnp.exp2(scores - lses_ref[program, :, columns]), 0.0)
        grad_weights = dot(values[:height], grad, 1, 0)
        grad_scores = (weights * (grad_weights - delta_ref[program, :, columns])).astype(
            jnp.bfloat16
        )
        own_query_grads.append(dot(keys_t[:, :height], grad_scores, 1, 0))
        added = (
            dot(query, grad_scores, 1, 1),
            dot(grad, weights.astype(jnp.bfloat16), 1, 1),
        )
        if height < width:
            behind = jnp.zeros((HD, width - height), jnp.float32)
            added = [jnp.concatenate([value, behind], axis=1) for value in added]
        key_grad = key_grad + added[0]
        value_grad = value_grad + added[1]
    query_grad_ref[program] += jnp.concatenate(own_query_grads, axis=1)
    carry = (key_grad, value_grad)
    carry = lax.fori_loop(program + 1, middle, functools.partial(step, masked=False), carry)
    key_grad, value_grad = lax.fori_loop(middle, stop, functools.partial(step, masked=True), carry)
    query_grad = query_grad_ref[program] * HD ** (-0.5)
    key_grad = key_grad * LOG_2
    for block, (place, tokens) in enumerate(own_places):
        columns = slice(block * block_width, (block + 1) * block_width)
        result_ref[place, 0:HD, tokens] = query_grad[:, columns].astype(jnp.bfloat16)
        result_ref[place, HD : 2 * HD, tokens] = key_grad[:, columns].astype(jnp.bfloat16)
        result_ref[place, 2 * HD : 3 * HD, tokens] = value_grad[:, columns].astype(jnp.bfloat16)


def attention_backward(ends, qkv, out, grad, lse, parts):
    blocks, block_width = 2 * qkv.shape[0], qkv.shape[2] // 2
    chunks, width = blocks // CHUNK, CHUNK * block_width

    def whole(value):
        return pl.BlockSpec(value.shape, lambda i, ends_ref: (0, 0, 0))

    return pl.pallas_call(
        functools.partial(attention_backward_kernel, parts),
        grid_spec=pltpu.PrefetchScalarGridSpec(
            num_scalar_prefetch=1,
            grid=(chunks,),
            in_specs=[whole(qkv), whole(out), whole(grad), whole(lse)],
            out_specs=whole(qkv),
            scratch_shapes=[
                pltpu.VMEM((chunks, HD, width), jnp.float32),
                pltpu.VMEM((chunks, 1, width), jnp.float32),
                pltpu.VMEM((chunks, HD, width), jnp.bfloat16),
                pltpu.VMEM((chunks, HD, width), jnp.bfloat16),
                pltpu.VMEM((chunks, 1, width), jnp.float32),
            ],
        ),
        out_shape=jax.ShapeDtypeStruct(qkv.shape, jnp.bfloat16),
        compiler_params=pltpu.CompilerParams(vmem_limit_bytes=VMEM_LIMIT),
        cost_estimate=LIGHT,
        name="attention_backward",
    )(ends, qkv, out, grad, lse)


def rope_pair(leading_half, trailing_half, cosine, sine_part):
    return (
        leading_half * cosine - trailing_half * sine_part,
        trailing_half * cosine + leading_half * sine_part,
    )


def low(value):
    return value.astype(jnp.bfloat16)


def wide(value):
    return value.astype(jnp.float32)


def whole_block(value):
    zeros = (0,) * value.ndim
    return pl.BlockSpec(value.shape, lambda *_: zeros)


def feed_forward_kernel(rows_ref, gate_w_ref, up_w_ref, down_w_ref, gate_ref, up_ref, act_ref, sum_ref):
    rows = rows_ref[...]
    gate = dot(gate_w_ref[...], rows, 1, 1)
    up = dot(up_w_ref[...], rows, 1, 1)
    active = (gate * jax.nn.sigmoid(gate) * up).astype(jnp.bfloat16)
    gate_ref[...] = gate.astype(jnp.bfloat16)
    up_ref[...] = up.astype(jnp.bfloat16)
    act_ref[...] = active

    @pl.when(pl.program_id(0) == 0)
    def _():
        sum_ref[...] = jnp.zeros_like(sum_ref)

    sum_ref[...] += dot(active, down_w_ref[...], 0, 0)


def feed_forward(rows, w_gate, w_up, w_down, tile):
    units, width = w_gate.shape
    count = rows.shape[0]
    weight = pl.BlockSpec((tile, width), lambda i: (i, 0))
    column = pl.BlockSpec((tile, count), lambda i: (i, 0))
    hidden = jax.ShapeDtypeStruct((units, count), jnp.bfloat16)
    return pl.pallas_call(
        feed_forward_kernel,
        grid=(units // tile,),
        in_specs=[whole_block(rows), weight, weight, weight],
        out_specs=[column, column, column, pl.BlockSpec((count, width), lambda i: (0, 0))],
        out_shape=[hidden, hidden, hidden, jax.ShapeDtypeStruct((count, width), jnp.float32)],
        compiler_params=pltpu.CompilerParams(vmem_limit_bytes=VMEM_LIMIT),
        cost_estimate=LIGHT,
        name="feed_forward",
    )(rows, w_gate, w_up, w_down)


def feed_forward_back_kernel(
    grad_ref, gate_ref, up_ref, gate_w_ref, up_w_ref, down_w_ref, grad_gate_ref, grad_up_ref, sum_ref
):
    grad_act = dot(down_w_ref[...], grad_ref[...], 1, 1)
    gate = gate_ref[...].astype(jnp.float32)
    up = up_ref[...].astype(jnp.float32)
    sigmoid_gate = jax.nn.sigmoid(gate)
    grad_gate = (grad_act * up * sigmoid_gate * (1.0 + gate * (1.0 - sigmoid_gate))).astype(
        jnp.bfloat16
    )
    grad_up = (grad_act * gate * sigmoid_gate).astype(jnp.bfloat16)
    grad_gate_ref[...] = grad_gate
    grad_up_ref[...] = grad_up

    @pl.when(pl.program_id(0) == 0)
    def _():
        sum_ref[...] = jnp.zeros_like(sum_ref)

    sum_ref[...] += dot(grad_gate, gate_w_ref[...], 0, 0) + dot(grad_up, up_w_ref[...], 0, 0)


def feed_forward_back(grad, gate, up, w_gate, w_up, w_down, tile):
    units, width = w_gate.shape
    count = grad.shape[0]
    weight = pl.BlockSpec((tile, width), lambda i: (i, 0))
    column = pl.BlockSpec((tile, count), lambda i: (i, 0))
    hidden = jax.ShapeDtypeStruct((units, count), jnp.bfloat16)
    return pl.pallas_call(
        feed_forward_back_kernel,
        grid=(units // tile,),
        in_specs=[whole_block(grad), column, column, weight, weight, weight],
        out_specs=[column, column, pl.BlockSpec((count, width), lambda i: (0, 0))],
        out_shape=[hidden, hidden, jax.ShapeDtypeStruct((count, width), jnp.float32)],
        compiler_params=pltpu.CompilerParams(vmem_limit_bytes=VMEM_LIMIT),
        cost_estimate=LIGHT,
        name="feed_forward_back",
    )(grad, gate, up, w_gate, w_up, w_down)


def half_products_kernel(layout, sizes, has_addend, which_ref, *refs):
    refs = list(refs)
    out_ref = refs.pop()
    addend_ref = refs.pop() if has_addend else None
    totals = [
        sum(dot(refs[left][...], refs[right][...], 1, 0) for left, right in pairs)
        for pairs in layout
    ]
    for piece in range(out_ref.shape[0]):
        parts = [
            total[piece * size : (piece + 1) * size] for total, size in zip(totals, sizes)
        ]
        value = jnp.concatenate(parts, axis=0) if len(parts) > 1 else parts[0]
        if has_addend:
            value = value + addend_ref[piece].astype(jnp.float32)
        out_ref[piece] = value.astype(jnp.bfloat16)


def half_products(which, groups, pieces, per_step, addend=None):
    lefts, rights, layout = [], [], []
    for group in groups:
        for left, right in group:
            if not any(left is known for known in lefts):
                lefts.append(left)
            if not any(right is known for known in rights):
                rights.append(right)
    find = lambda known, value: next(i for i, entry in enumerate(known) if entry is value)
    for group in groups:
        layout.append(
            tuple((find(lefts, left), len(lefts) + find(rights, right)) for left, right in group)
        )
    sizes = tuple(group[0][0].shape[0] // (2 * pieces) for group in groups)
    width = rights[0].shape[1]
    steps = pieces // per_step
    out_spec = pl.BlockSpec((per_step, sum(sizes), width), lambda i, which_ref: (i, 0, 0))
    left_specs = [
        pl.BlockSpec(
            (left.shape[0] // (2 * steps), left.shape[1]),
            lambda i, which_ref: (which_ref[0] * steps + i, 0),
        )
        for left in lefts
    ]
    extra = [] if addend is None else [addend]
    work = sum(left.size // 2 for left, _ in sum(groups, ()))
    return pl.pallas_call(
        functools.partial(half_products_kernel, tuple(layout), sizes, addend is not None),
        grid_spec=pltpu.PrefetchScalarGridSpec(
            num_scalar_prefetch=1,
            grid=(steps,),
            in_specs=left_specs + [whole_block(right) for right in rights] + [out_spec] * len(extra),
            out_specs=out_spec,
        ),
        out_shape=jax.ShapeDtypeStruct((pieces, sum(sizes), width), jnp.bfloat16),
        compiler_params=pltpu.CompilerParams(vmem_limit_bytes=VMEM_LIMIT),
        cost_estimate=LIGHT,
        name="half_products",
    )(which.reshape(1).astype(jnp.int32), *lefts, *rights, *extra)


def together(*values):
    return lax.optimization_barrier(values)


def after(value, *others):
    return lax.optimization_barrier((value, *others))[0]


def split_body(mesh_sizes, inputs, cotangent, lengths, gain1, wqkv, wo, gain2, wgu, wd):
    sections, contexts, parts = mesh_sizes
    half_parts = parts // 2
    section = lax.axis_index("section")
    ctx = lax.axis_index("ctx")
    tp = lax.axis_index("tp")
    row_side, column_side = ctx // 2, ctx % 2
    leading = section == 0
    batch = tp // half_parts
    model_width = inputs.shape[2]
    rows = inputs.shape[1]
    heads = wqkv.shape[2] * parts
    side_heads = heads // 2
    unit_rows = wd.shape[1] // contexts // 2
    head_rows = 3 * HD // 2
    out_rows = HD // 2
    half_width = HD // 2
    tile = 4 * unit_rows
    number = lambda s, c, t: (s * contexts + c) * parts + t
    places = [
        (s, c, t) for s in range(sections) for c in range(contexts) for t in range(parts)
    ]
    everyone = [[number(*place) for place in places]]
    token_of = lambda s, c, t: c * parts + t % half_parts + half_parts * s
    batch_groups = device_groups(mesh_sizes, lambda s, c, t: t // half_parts, token_of)
    head_groups = device_groups(
        mesh_sizes,
        lambda s, c, t: (c % 2, t // half_parts),
        lambda s, c, t: (c // 2, t % half_parts + half_parts * s),
    )
    side_groups = device_groups(mesh_sizes, lambda s, c, t: c % 2, lambda s, c, t: (s, c, t))
    crossing = [
        (number(s, c, t), number(s, c, (t + half_parts) % parts))
        for s, c, t in places
        if t // half_parts == s
    ]

    def to_batch(value):
        mine = lax.dynamic_index_in_dim(value, batch, 0, keepdims=False)
        other = lax.dynamic_index_in_dim(value, 1 - batch, 0, keepdims=False)
        moved = lax.ppermute(other, ALL_AXES, crossing)
        return jnp.where(section == batch, mine, moved)

    def to_home(value, layer):
        stay = [
            (number(s, c, t), number(layer, c, t)) for s, c, t in places if t // half_parts == s
        ]
        cross = [
            (number(s, c, t), number(layer, c, (t + half_parts) % parts))
            for s, c, t in places
            if t // half_parts != s
        ]
        return (lax.ppermute(value, ALL_AXES, stay), lax.ppermute(value, ALL_AXES, cross))

    def at_home(first_pair, second_pair):
        near = jnp.where(leading, first_pair[0], second_pair[0])
        far = jnp.where(leading, first_pair[1], second_pair[1])
        upper = batch == 0
        return jnp.stack([jnp.where(upper, near, far), jnp.where(upper, far, near)])[None]

    def swap_side(value):
        return lax.ppermute(value, "ctx", [(c, c ^ 1) for c in range(contexts)])

    def swap_far(value):
        return lax.ppermute(value, "ctx", [(c, c ^ 2) for c in range(contexts)])

    def swap_near(value):
        return lax.ppermute(value, "tp", [(t, t ^ 1) for t in range(parts)])

    def swap_half(value):
        return lax.ppermute(value, "tp", [(t, (t + half_parts) % parts) for t in range(parts)])

    def swap_section(value):
        return lax.ppermute(value, "section", [(0, 1), (1, 0)])

    def all_to_all(value, axis):
        return lax.all_to_all(value, axis, split_axis=0, concat_axis=0, tiled=True)

    def copies(value, count):
        return jnp.broadcast_to(value[None], (count, *value.shape))

    def gather(value, groups):
        return lax.all_gather(value, ALL_AXES, axis=0, tiled=True, axis_index_groups=groups)

    def ordered(index, own, other):
        return jnp.where(index == 0, own, other), jnp.where(index == 0, other, own)

    def by_core(value, which):
        return lax.dynamic_index_in_dim(value, which, 0, keepdims=False)

    def spread_half(piece):
        return piece, swap_half(piece)

    def spread_near(pieces_pair):
        pair = jnp.stack(ordered(batch, *pieces_pair))
        return pair, swap_near(pair)

    def spread_line(pairs):
        line = jnp.stack(ordered(tp % 2, *pairs), axis=1)
        return line.reshape(parts, *line.shape[2:])

    def spread_far(line):
        return line, swap_far(line)

    def spread_heads(pair):
        pair = jnp.stack(ordered(row_side, *pair))
        own_heads = pair[:, :, :head_rows].reshape(-1, model_width)
        own_outs = pair[:, :, head_rows:]
        return (own_heads, swap_section(own_heads)), (own_outs, swap_side(own_outs))

    def spread_outs(pair):
        own_outs = jnp.stack(ordered(column_side, *pair), axis=1).reshape(-1, model_width)
        return own_outs, swap_section(own_outs)

    def join_outs(pair):
        return jnp.concatenate(ordered(section, *pair), axis=0)

    def own_halves(value, axis, size):
        part = lax.dynamic_slice_in_dim(value, ctx * size, size, axis)
        return part.reshape(2, -1, model_width)

    packed = jnp.concatenate(
        [
            own_halves(wqkv[0], 1, heads // (parts * contexts)),
            own_halves(wo[0], 0, HD),
            own_halves(wgu[0, 0], 0, 2 * unit_rows),
            own_halves(wgu[0, 1], 0, 2 * unit_rows),
            own_halves(wd[0], 0, 2 * unit_rows),
        ],
        axis=1,
    )
    kept = by_core(packed, section)
    passed = swap_section(by_core(packed, 1 - section))
    pieces = ordered(section, kept, passed)
    attention_rows = head_rows + out_rows

    def feed_forward_weights(piece):
        whole = gather(piece[attention_rows:], side_groups)
        whole = whole.reshape(2 * 2 * parts, 3, unit_rows, model_width)
        return [whole[:, entry].reshape(-1, model_width) for entry in range(3)]

    rows_in = to_batch(inputs)
    line = spread_near(spread_half(pieces[0][:attention_rows]))
    line, rows_in = together(spread_line(line), rows_in)
    w_ffn = [feed_forward_weights(after(pieces[0], line)), None]
    w_heads, w_outs = [None, None], [None, None]
    first_pair = spread_far(line)

    gains = wide(jnp.concatenate([gain1, gain2], axis=0))
    gain_sets = ordered(section, gains, swap_section(gains))

    seq_lengths = lax.dynamic_index_in_dim(lengths, batch, 0, keepdims=False)
    ends = jnp.cumsum(seq_lengths).astype(jnp.int32)
    token_index = jnp.concatenate(
        [
            token_of(section, 2 * row_side + side, tp) * rows + jnp.arange(rows, dtype=jnp.int32)
            for side in range(2)
        ]
    )
    before = (ends[None, :] <= token_index[:, None]).astype(jnp.int32)
    position = token_index - jnp.sum(before * seq_lengths[None, :], axis=1)
    frequency = jnp.exp(
        -jnp.log(10000.0) * jnp.arange(half_width, dtype=jnp.float32) / half_width
    )
    angles = position.astype(jnp.float32)[None, :] * frequency[:, None]
    cosine, sine_part = jnp.cos(angles), jnp.sin(angles)

    def head_halves(value):
        size = value.shape[1] // 2
        return value.reshape(heads, 2, size, rows).transpose(1, 0, 2, 3).reshape(2, -1, rows)

    def whole_heads(value):
        value = value.reshape(2, heads, -1, rows)
        return value.transpose(1, 0, 2, 3).reshape(heads, -1, rows)

    def nothing(value):
        return value

    def layer_forward(whole_rows, first_values, layer, in_zero, in_first, in_second, in_middle, in_third, in_fourth):
        gain_first, gain_second = gain_sets[layer][0], gain_sets[layer][1]
        scale_first = lax.rsqrt(jnp.mean(whole_rows * whole_rows, axis=-1, keepdims=True) + EPSILON)
        normed = low(whole_rows * scale_first * gain_first)
        far_normed = in_zero(swap_side(normed))
        side_rows = jnp.concatenate(ordered(column_side, normed, far_normed), axis=0)
        halves = ordered(section, *[dot(weight, side_rows, 1, 1) for weight in w_heads[layer]])
        upper, lower = [half.reshape(side_heads, head_rows, 2 * rows) for half in halves]
        query = rope_pair(upper[:, :half_width], upper[:, half_width:HD], cosine, sine_part)
        key = rope_pair(upper[:, HD:], lower[:, :half_width], cosine, sine_part)
        value = lower[:, half_width:]
        if first_values is not None:
            value = 0.5 * value + 0.5 * wide(first_values)
        mixed = low(value)
        shrunk = [low(half * (HD ** (-0.5) / LOG_2)) for half in query]
        qkv = exchange(
            jnp.concatenate([*shrunk, low(key[0]), low(key[1]), mixed], axis=1), head_groups
        )
        qkv = in_first(qkv)
        out, lse = attention_forward(ends, qkv, parts)
        out = in_second(out)
        attended = head_halves(in_middle(exchange(out, batch_groups)))
        hidden = whole_rows + dot(attended.reshape(-1, rows), w_outs[layer], 0, 0)
        scale_second = lax.rsqrt(jnp.mean(hidden * hidden, axis=-1, keepdims=True) + EPSILON)
        normed_second = low(hidden * scale_second * gain_second)
        far_rows = swap_side(normed_second)
        near = feed_forward(normed_second, *w_ffn[layer], tile)
        far_rows = in_third(after(far_rows, near[3]))
        far = feed_forward(far_rows, *w_ffn[layer], tile)
        sent_down = low(far[3])

        def layer_out(*others):
            far_down = in_fourth(swap_side(after(sent_down, *others)))
            return low(hidden + (near[3] + wide(far_down)))

        saved = (
            whole_rows, scale_first, side_rows, qkv, out, lse, attended, hidden, scale_second,
            (normed_second, far_rows), near[:3], far[:3],
        )
        return layer_out, mixed, saved

    def norm_back(whole_rows, scale_rows, gain, grad_normed, grad_rest):
        unit = whole_rows * scale_rows
        scaled = grad_normed * gain
        grad_gain = jnp.sum(grad_normed * unit, axis=0)
        grad_whole = grad_rest + scale_rows * (
            scaled - unit * jnp.mean(scaled * unit, axis=-1, keepdims=True)
        )
        return grad_gain, grad_whole

    def pick(value, index, axis):
        return lax.dynamic_index_in_dim(value, index, axis, keepdims=False)

    def parted(value, index, axis):
        return pick(value, index, axis), pick(value, 1 - index, axis)

    def moved_pair(pair, swap):
        return pair[0], swap(pair[1])

    def halve(value, index, swap, axis):
        return moved_pair(parted(value, index, axis), swap)

    def add(pair):
        return low(wide(pair[0]) + wide(pair[1]))

    def near_parts(value):
        return parted(value.reshape(2, half_parts, *value.shape[1:]), tp % 2, 1)

    def near_sum(value):
        return moved_pair(near_parts(value), swap_near)

    def far_sum(pair):
        return halve(add(pair), batch, swap_half, 0)

    def layer_backward(grad_rows, extra_values, saved, layer, in_first, in_second, in_third, in_fourth, in_fifth):
        (
            whole_rows, scale_first, _, qkv, out, lse, attended, hidden, scale_second,
            ffn_rows, near, far,
        ) = saved
        gain_first, gain_second = gain_sets[layer][0], gain_sets[layer][1]
        grad_down = low(grad_rows)
        far_down = swap_side(grad_down)
        grad_gate, grad_up, near_back = feed_forward_back(grad_down, *near[:2], *w_ffn[layer], tile)
        far_down = in_first(after(far_down, near_back))
        far_gate, far_up, far_back = feed_forward_back(far_down, *far[:2], *w_ffn[layer], tile)
        far_back = swap_side(low(far_back))
        groups = (
            ((grad_gate, ffn_rows[0]), (far_gate, ffn_rows[1])),
            ((grad_up, ffn_rows[0]), (far_up, ffn_rows[1])),
            ((near[2], grad_down), (far[2], far_down)),
        )
        products = functools.partial(
            half_products, groups=groups, pieces=2 * parts, per_step=2
        )
        sent = products(1 - section)
        moved = swap_section(sent)
        far_back = in_second(after(far_back, sent))
        grad_gain2, grad_hidden = norm_back(
            hidden, scale_second, gain_second, near_back + wide(far_back), wide(grad_rows)
        )
        grad_branch = low(grad_hidden)
        grad_heads = whole_heads(low(dot(w_outs[layer], grad_branch, 1, 1)))
        grad_heads = exchange(grad_heads, batch_groups)
        rest = products(section, addend=moved)
        out_pair = (attended.reshape(-1, rows), grad_branch)
        grad_heads, rest = in_third(grad_heads, rest, out_pair)
        grad_qkv = attention_backward(ends, qkv, out, grad_heads, lse, parts)
        grad_qkv = in_fourth(grad_qkv)
        grad_qkv = in_fifth(exchange(grad_qkv, head_groups))
        grad_qkv = wide(grad_qkv)
        quarter = lambda entry: grad_qkv[:, entry * half_width : (entry + 1) * half_width]
        grad_query = rope_pair(quarter(0), quarter(1), cosine, -sine_part)
        grad_key = rope_pair(quarter(2), quarter(3), cosine, -sine_part)
        grad_value = grad_qkv[:, 2 * HD :]
        send_values = None
        if extra_values is None:
            grad_value = 0.5 * grad_value
            send_values = low(grad_value)
        else:
            grad_value = grad_value + wide(extra_values)
        upper = low(jnp.concatenate([*grad_query, grad_key[0]], axis=1))
        lower = low(jnp.concatenate([grad_key[1], grad_value], axis=1))
        grad_halves = jnp.stack([upper, lower]).reshape(2, -1, 2 * rows)
        return grad_halves, send_values, grad_hidden, out_pair, grad_gain2

    def input_grads_of(grad_halves, grad_hidden, saved, layer, beside):
        whole_rows, scale_first = saved[:2]
        places_of = (section, 1 - section)
        grad_side = sum(
            dot(by_core(grad_halves, place), weight, 0, 0)
            for place, weight in zip(places_of, w_heads[layer])
        ).reshape(2, rows, model_width)
        grad_far = swap_side(low(by_core(grad_side, 1 - column_side)))
        grad_normed = by_core(grad_side, column_side) + wide(beside(grad_far))
        return norm_back(whole_rows, scale_first, gain_sets[layer][0], grad_normed, grad_hidden)

    def piece_sum(value, groups):
        return lax.psum_scatter(
            value, ALL_AXES, scatter_dimension=0, tiled=True, axis_index_groups=groups
        )

    line_groups = device_groups(
        mesh_sizes, lambda s, c, t: (s, c % 2), lambda s, c, t: (c, t)
    )
    plane_shape = (2, 2, parts)
    pending = {}

    def weights_zero(value):
        value, pair = together(value, first_pair)
        w_heads[0], pending["outs"] = spread_heads(pair)
        return value

    def weights_line(value):
        value, piece = together(value, pieces[1][:attention_rows])
        pending["weights"] = spread_half(piece)
        return value

    def weights_outs_first(value):
        value, pending["outs"], w_ffn[0], weights = together(
            value, pending["outs"], w_ffn[0], pending["weights"]
        )
        pending["weights"] = spread_near(weights)
        w_outs[0] = join_outs(spread_outs(pending["outs"]))
        return value

    def weights_far(value):
        value, line = together(value, pending["weights"])
        pending["weights"] = spread_far(spread_line(line))
        w_ffn[1] = feed_forward_weights(after(pieces[1], value))
        return value

    def weights_heads(value):
        value, pairs = together(value, pending["weights"])
        w_heads[1], pending["outs"] = spread_heads(pairs)
        return value

    first_result, first_values, first_saved = layer_forward(
        wide(rows_in), None, 0,
        weights_zero, weights_line, nothing, weights_outs_first, weights_far, weights_heads,
    )

    first_out = first_result()

    def start_outs(value):
        value, grads = together(value, cotangent)
        pending["grad_in"] = to_batch(grads)
        return value

    def end_outs(value):
        value, outs, w_ffn[1], pending["grad_in"] = together(
            value, pending["outs"], w_ffn[1], pending["grad_in"]
        )
        w_outs[1] = join_outs(spread_outs(outs))
        pending["first_home"] = to_home(after(first_out, value), 0)
        return value

    second_result, _, second_saved = layer_forward(
        wide(first_out), first_values, 1,
        nothing, start_outs, end_outs, nothing, nothing, nothing,
    )
    grad_in = pending["grad_in"]

    def out_sides(out_pair):
        products = functools.partial(half_products, groups=((out_pair,),), pieces=heads, per_step=8)
        out_sum = products(section, addend=swap_section(products(1 - section)))
        return parted(out_sum.reshape(*plane_shape, out_rows, model_width), column_side, 1)

    def second_third(value, rest, out_pair):
        value, rest = together(value, rest)
        rest = rest.reshape(-1, model_width)
        pending["second_rest"] = piece_sum(rest, line_groups)
        pending["second_out_rows"] = second_result(value)
        pending["out"] = out_sides(out_pair)
        value = after(value, pending["out"])
        pending["out"] = moved_pair(pending["out"], swap_side)
        return value, rest

    def second_fourth(value):
        value, pending["first_home"], second_out, out_sum = together(
            value, pending["first_home"], pending["second_out_rows"], pending["out"]
        )
        pending["second_home"] = to_home(second_out, 1)
        pending["second_out"] = add(out_sum).reshape(2 * parts, out_rows, model_width)
        return value

    grad_halves, send_values, grad_hidden, _, second_gain2 = layer_backward(
        grad_in, None, second_saved, 1, nothing, nothing, second_third, second_fourth, nothing
    )
    head_products = functools.partial(
        half_products,
        groups=(((grad_halves.reshape(-1, 2 * rows), second_saved[2]),),),
        pieces=side_heads,
        per_step=4,
    )

    def head_start(value):
        value, sent = together(value, head_products(1 - section))
        pending["moved"] = swap_section(sent)
        return value

    second_gain1, second_grad = input_grads_of(
        grad_halves, grad_hidden, second_saved, 1, head_start
    )
    second_grad = low(second_grad)

    def first_first(value):
        head = head_products(section, addend=pending["moved"])
        head = jnp.concatenate([head, pending["second_out"]], axis=1)
        head = parted(head.reshape(2, parts, -1, model_width), row_side, 0)
        value, head = together(value, head)
        pending["head"] = moved_pair(head, swap_far)
        return value

    def first_second(value):
        return value

    def first_third(value, rest, out_pair):
        out_sum = out_sides(out_pair)
        rest = rest.reshape(2, parts, -1, model_width)
        rest_a = parted(rest[:, :, : 2 * unit_rows], row_side, 0)
        rest_b = parted(rest[:, :, 2 * unit_rows :], row_side, 0)
        (
            value, rest_a, rest_b, out_sum, head, pending["second_rest"], pending["second_home"]
        ) = together(
            value, rest_a, rest_b, out_sum, pending["head"], pending["second_rest"],
            pending["second_home"],
        )
        pending["rest_a"] = moved_pair(rest_a, swap_far)
        pending["rest_b"] = rest_b
        pending["out"] = moved_pair(out_sum, swap_side)
        pending["head"] = near_sum(add(head))
        return value, rest

    def first_fourth(value):
        value, rest_a, rest_b, out_sum, head = together(
            value, pending["rest_a"], pending["rest_b"], pending["out"], pending["head"]
        )
        pending["head"] = far_sum(head)
        pending["rest_b"] = moved_pair(rest_b, swap_far)
        pending["rest_a"] = near_sum(add(rest_a))
        pending["out"] = halve(add(out_sum), row_side, swap_far, 0)
        return value

    def first_fifth(value):
        value, rest_a, rest_b, out_sum, head = together(
            value, pending["rest_a"], pending["rest_b"], pending["out"], pending["head"]
        )
        second = jnp.concatenate([pending["second_rest"], add(head)], axis=0)
        pending["second"] = lax.all_gather(second, "ctx", axis=0, tiled=False)
        pending["out"] = add(out_sum)
        pending["rest_a"] = far_sum(rest_a)
        pending["rest_b"] = near_sum(add(rest_b))
        return value

    first_halves, _, first_hidden, _, first_gain2 = layer_backward(
        second_grad, send_values, first_saved, 0,
        first_first, first_second, first_third, first_fourth, first_fifth,
    )
    head_products = functools.partial(
        half_products,
        groups=(((first_halves.reshape(-1, 2 * rows), first_saved[2]),),),
        pieces=side_heads,
        per_step=4,
    )
    sent = head_products(1 - section)
    moved = swap_section(sent)
    def head_end(value):
        head = head_products(section, addend=moved).reshape(2, parts, head_rows, model_width)
        head = parted(head, row_side, 0)
        pending["head"] = moved_pair(head, swap_far)
        return after(value, head)

    first_gain1, first_grad = input_grads_of(
        after(first_halves, sent), first_hidden, first_saved, 0, head_end
    )
    def summed(value, swap):
        return value + swap(value)

    gain_rows = jnp.stack([first_gain1, first_gain2, second_gain1, second_gain2])
    gain_rows = summed(gain_rows, swap_section)
    head, rest_a, rest_b, gain_rows, first_grad = together(
        pending["head"], pending["rest_a"], pending["rest_b"], gain_rows, low(first_grad)
    )
    head = near_sum(jnp.concatenate([add(head), pending["out"]], axis=1))
    rest_b = far_sum(rest_b)
    gain_rows = summed(summed(gain_rows, swap_side), swap_far)
    head, rest_b, gain_rows, first_grad = together(head, rest_b, gain_rows, first_grad)
    head = parted(add(head), batch, 0)
    first_grad, home = together(after(first_grad, head), second_grad)
    head = moved_pair(head, swap_half)
    first_grad_home = to_home(first_grad, 0)
    second_grad_home = to_home(home, 1)
    rest = jnp.concatenate([add(rest_a), add(rest_b)], axis=0)
    rest = lax.all_gather(rest, "ctx", axis=0, tiled=False)
    gain_rows = summed(gain_rows, swap_near)
    head, first_grad_home, second_grad_home = together(head, first_grad_home, second_grad_home)
    head = all_to_all(copies(add(head), contexts), "ctx")
    head, gain_rows = together(head, gain_rows)
    gain_total = summed(gain_rows, swap_half)
    rest, second, head = together(rest, pending["second"], head)
    first_grads = (rest, head)
    second_grads = (second[:, : 3 * unit_rows], second[:, 3 * unit_rows :])
    first_home, second_home = pending["first_home"], pending["second_home"]
    gain_total = jnp.where(leading, gain_total[:2], gain_total[2:])

    def finish(first, second):
        mine = jnp.where(leading, first, second)
        moved = swap_section(jnp.where(leading, second, first))
        return ordered(section, mine, moved)

    def joined(halves, first, count):
        both = jnp.stack([half[:, first : first + count] for half in halves], axis=1)
        return wide(both).reshape(-1, model_width)

    rest_grads = finish(first_grads[0], second_grads[0])
    grad_wgate, grad_wup, grad_wd = [
        joined(rest_grads, entry * unit_rows, unit_rows) for entry in range(3)
    ]
    head, grad_wgate, grad_wup, grad_wd = together(first_grads[1], grad_wgate, grad_wup, grad_wd)
    head_grads = finish(head, second_grads[1])
    grad_wqkv = joined(head_grads, 0, head_rows).reshape(contexts, 3, HD, model_width)
    grad_wo = joined(head_grads, head_rows, out_rows)
    return (
        at_home(first_home, second_home),
        wide(at_home(first_grad_home, second_grad_home)),
        gain_total[0:1],
        grad_wqkv.transpose(1, 0, 2, 3)[None],
        grad_wo[None],
        gain_total[1:2],
        jnp.stack([grad_wgate, grad_wup])[None],
        grad_wd[None],
    )


def body(mesh_sizes, *arguments):
    inputs, _, _, _, wqkv = arguments[:5]
    sections, contexts, parts = mesh_sizes
    own_heads, own_units = wqkv.shape[2], arguments[7].shape[2]
    fits = (
        sections == 2
        and inputs.shape[0] == 2
        and contexts == 4
        and parts % 2 == 0
        and own_heads == contexts
        and own_units % (16 * contexts) == 0
        and inputs.shape[1] % 128 == 0
    )
    if fits:
        return split_body(mesh_sizes, *arguments)
    return general_body(*arguments)


def solution(mesh):
    placed = (
        P(None, ("ctx", "tp"), None),
        P(None, ("ctx", "tp"), None),
        P(),
        P("section", None),
        P("section", None, "tp", None, None),
        P("section", "tp", None),
        P("section", None),
        P("section", None, "tp", None),
        P("section", "tp", None),
    )
    mesh_sizes = tuple(mesh.shape[axis] for axis in ALL_AXES)
    return jax.shard_map(
        functools.partial(body, mesh_sizes),
        mesh=mesh,
        in_specs=placed,
        out_specs=(
            P("section", None, ("ctx", "tp"), None),
            P("section", None, ("ctx", "tp"), None),
            P("section", None),
            P("section", None, "tp", None, None),
            P("section", "tp", None),
            P("section", None),
            P("section", None, "tp", None),
            P("section", "tp", None),
        ),
        check_vma=False,
    )
```

```python
import functools

import jax
import jax.numpy as jnp
from jax import lax
from jax.experimental import pallas as pl
from jax.experimental.pallas import tpu as pltpu
from jax.sharding import PartitionSpec as P

HD = 64
EPSILON = 1e-06
MASKED = -1e30
ALL_AXES = ("section", "ctx", "tp")
CHUNK = 2
ONES = 16
LOG_2 = 0.6931471805599453
LIGHT = pl.CostEstimate(flops=1, bytes_accessed=1, transcendentals=0)
VMEM_LIMIT = 40 * 1024 * 1024


def shifted(block, axis, distance):
    devices = range(lax.axis_size(axis))
    route = [(i - distance, i) for i in devices if i - distance in devices]
    return lax.ppermute(block, axis, route)


def rope_parts(position):
    half_width = HD // 2
    frequency = jnp.exp(-jnp.log(10000.0) * jnp.arange(half_width, dtype=jnp.float32) / half_width)
    angles = position.astype(jnp.float32)[:, None] * frequency[None, :]
    return (jnp.cos(angles), jnp.sin(angles))


def rotate(vectors, cosine, sine_part):
    half_width = HD // 2
    leading_half = vectors[..., :half_width]
    trailing_half = vectors[..., half_width:]
    cosine = cosine[:, None, :]
    sine_part = sine_part[:, None, :]
    return jnp.concatenate(
        [
            leading_half * cosine - trailing_half * sine_part,
            trailing_half * cosine + leading_half * sine_part,
        ],
        axis=-1,
    )


def rotate_back(vectors, cosine, sine_part):
    half_width = HD // 2
    leading_half = vectors[..., :half_width]
    trailing_half = vectors[..., half_width:]
    cosine = cosine[:, None, :]
    sine_part = sine_part[:, None, :]
    return jnp.concatenate(
        [
            leading_half * cosine + trailing_half * sine_part,
            trailing_half * cosine - leading_half * sine_part,
        ],
        axis=-1,
    )


def inner_rows(left, right):
    return lax.dot_general(
        left, right, (((0,), (0,)), ((), ())), preferred_element_type=jnp.float32
    )


def outer_cols(left, right):
    return lax.dot_general(
        left, right, (((1,), (1,)), ((), ())), preferred_element_type=jnp.float32
    )


def spread(row_block):
    return lax.all_gather(row_block, "tp", axis=0, tiled=True)


def collect(partial_value):
    return lax.psum_scatter(
        partial_value.astype(jnp.bfloat16), "tp", scatter_dimension=0, tiled=True
    ).astype(jnp.float32)


def fetch_keys(key_value):
    return lax.all_gather(key_value, "ctx", axis=0, tiled=True)


def query_bounds(seq_lengths, block_first, row_count):
    token_index = block_first + jnp.arange(row_count, dtype=jnp.int32)
    doc_ends = jnp.cumsum(seq_lengths)
    before = (doc_ends[None, :] <= token_index[:, None]).astype(jnp.int32)
    doc_start = jnp.sum(before * seq_lengths[None, :], axis=1)
    return (token_index, doc_start)


def block_scores(query_heads, pair_block, block_first, token_index, doc_start, head_width):
    row_count = pair_block.shape[0]
    key_heads = pair_block[:, :head_width].reshape(row_count, head_width // HD, HD)
    value_heads = pair_block[:, head_width:].reshape(row_count, head_width // HD, HD)
    scores = jnp.einsum(
        "qhd,khd->hqk", query_heads, key_heads, preferred_element_type=jnp.float32
    ) * HD ** (-0.5)
    key_index = block_first + jnp.arange(row_count, dtype=jnp.int32)
    allowed = (key_index[None, :] >= doc_start[:, None]) & (
        key_index[None, :] <= token_index[:, None]
    )
    return (scores, allowed[None], key_heads, value_heads)


def split_blocks(pairs_all, row_count):
    blocks = pairs_all.reshape(-1, row_count, pairs_all.shape[1])
    block_starts = jnp.arange(blocks.shape[0], dtype=jnp.int32) * row_count
    return (blocks, block_starts)


def attend(query_heads, pairs_all, token_index, doc_start, head_width):
    row_count = query_heads.shape[0]
    head_count = head_width // HD
    blocks, block_starts = split_blocks(pairs_all, row_count)
    last_query = token_index[row_count - 1]
    first_query = doc_start[0]

    def rowmax_live(carried, block_parts):
        running_top, running_sum = carried
        scores, allowed, unused_keys, unused_values = block_scores(
            query_heads, block_parts[0], block_parts[1], token_index, doc_start, head_width
        )
        masked = jnp.where(allowed, scores, -1e30)
        new_top = jnp.maximum(running_top, jnp.max(masked, axis=-1))
        running_sum = running_sum * jnp.exp(running_top - new_top) + jnp.sum(
            jnp.where(allowed, jnp.exp(masked - new_top[..., None]), 0.0), axis=-1
        )
        return (new_top, running_sum)

    def rowmax_step(carried, block_parts):
        live = (block_parts[1] <= last_query) & (block_parts[1] + row_count > first_query)
        return (
            lax.cond(live, lambda held: rowmax_live(held, block_parts), lambda held: held, carried),
            None,
        )

    initial = (
        jnp.full((head_count, row_count), -1e30, jnp.float32),
        jnp.zeros((head_count, row_count), jnp.float32),
    )
    (running_top, running_sum), unused = lax.scan(rowmax_step, initial, (blocks, block_starts))
    log_total = running_top + jnp.log(running_sum)

    def output_live(accumulated, block_parts):
        scores, allowed, unused_keys, value_heads = block_scores(
            query_heads, block_parts[0], block_parts[1], token_index, doc_start, head_width
        )
        soft_weights = jnp.where(allowed, jnp.exp(scores - log_total[..., None]), 0.0).astype(
            jnp.bfloat16
        )
        return accumulated + jnp.einsum(
            "hqk,khd->qhd", soft_weights, value_heads, preferred_element_type=jnp.float32
        )

    def output_step(accumulated, block_parts):
        live = (block_parts[1] <= last_query) & (block_parts[1] + row_count > first_query)
        return (
            lax.cond(
                live, lambda held: output_live(held, block_parts), lambda held: held, accumulated
            ),
            None,
        )

    accumulated, unused = lax.scan(
        output_step, jnp.zeros((row_count, head_count, HD), jnp.float32), (blocks, block_starts)
    )
    return (accumulated, log_total)


def attend_back(
    query_heads, pairs_all, token_index, doc_start, head_width, log_total, accumulated, grad_heads
):
    row_count = query_heads.shape[0]
    head_count = head_width // HD
    blocks, block_starts = split_blocks(pairs_all, row_count)
    last_query = token_index[row_count - 1]
    first_query = doc_start[0]
    rowdot = jnp.sum(grad_heads.astype(jnp.float32) * accumulated, axis=-1).T

    def grad_live(grad_acc, block_parts):
        scores, allowed, key_heads, value_heads = block_scores(
            query_heads, block_parts[0], block_parts[1], token_index, doc_start, head_width
        )
        soft_weights = jnp.where(allowed, jnp.exp(scores - log_total[..., None]), 0.0)
        grad_soft = jnp.einsum(
            "qhd,khd->hqk", grad_heads, value_heads, preferred_element_type=jnp.float32
        )
        grad_scores = (soft_weights * (grad_soft - rowdot[..., None])).astype(jnp.bfloat16)
        grad_acc = grad_acc + jnp.einsum(
            "hqk,khd->qhd", grad_scores, key_heads, preferred_element_type=jnp.float32
        )
        grad_keys = jnp.einsum(
            "hqk,qhd->khd", grad_scores, query_heads, preferred_element_type=jnp.float32
        ) * HD ** (-0.5)
        grad_values = jnp.einsum(
            "hqk,qhd->khd",
            soft_weights.astype(jnp.bfloat16),
            grad_heads,
            preferred_element_type=jnp.float32,
        )
        return (grad_acc, (grad_keys, grad_values))

    def grad_skip(grad_acc):
        empty = jnp.zeros((row_count, head_count, HD), jnp.float32)
        return (grad_acc, (empty, empty))

    def grad_step(grad_acc, block_parts):
        live = (block_parts[1] <= last_query) & (block_parts[1] + row_count > first_query)
        return lax.cond(live, lambda held: grad_live(held, block_parts), grad_skip, grad_acc)

    grad_query, (grad_keys, grad_values) = lax.scan(
        grad_step, jnp.zeros((row_count, head_count, HD), jnp.float32), (blocks, block_starts)
    )
    grad_query = grad_query * HD ** (-0.5)
    grad_pairs = jnp.concatenate(
        [grad_keys.reshape(-1, head_width), grad_values.reshape(-1, head_width)], axis=1
    )
    return (grad_query, grad_pairs)


def norm_back(whole_rows, scale_rows, gain, grad_normed, grad_rest):
    unit_rows = whole_rows * scale_rows
    scaled = grad_normed * gain.astype(jnp.float32)
    grad_gain = jnp.sum(grad_normed * unit_rows, axis=0)
    grad_whole = grad_rest + scale_rows * (
        scaled - unit_rows * jnp.mean(scaled * unit_rows, axis=-1, keepdims=True)
    )
    return (grad_gain, grad_whole)


def layer_forward(row_block, first_values, value_mix, weights, seq_lengths):
    gain_first, w_qkv, w_out, gain_second, w_gateup, w_down = weights
    head_count = w_qkv.shape[1]
    head_width = head_count * HD
    model_width = row_block.shape[1]
    whole_rows = row_block.astype(jnp.float32)
    scale_first = lax.rsqrt(jnp.mean(whole_rows * whole_rows, axis=-1, keepdims=True) + EPSILON)
    normed = (whole_rows * scale_first * gain_first.astype(jnp.float32)).astype(jnp.bfloat16)
    normed_all = spread(normed)
    row_count = normed_all.shape[0]
    projected = outer_cols(normed_all, w_qkv.reshape(3 * head_width, model_width))
    token_index, doc_start = query_bounds(seq_lengths, lax.axis_index("ctx") * row_count, row_count)
    cosine, sine_part = rope_parts(token_index - doc_start)
    query_heads = rotate(
        projected[:, :head_width].reshape(row_count, head_count, HD), cosine, sine_part
    ).astype(jnp.bfloat16)
    key_heads = rotate(
        projected[:, head_width : 2 * head_width].reshape(row_count, head_count, HD),
        cosine,
        sine_part,
    ).astype(jnp.bfloat16)
    mixed = (
        (1.0 - value_mix) * projected[:, 2 * head_width :]
        + value_mix * first_values.astype(jnp.float32)
    ).astype(jnp.bfloat16)
    key_value = jnp.concatenate([key_heads.reshape(row_count, head_width), mixed], axis=1)
    pairs_all = fetch_keys(key_value)
    accumulated, log_total = attend(query_heads, pairs_all, token_index, doc_start, head_width)
    attended = accumulated.reshape(row_count, head_width).astype(jnp.bfloat16)
    hidden = whole_rows + collect(jnp.dot(attended, w_out, preferred_element_type=jnp.float32))
    scale_second = lax.rsqrt(jnp.mean(hidden * hidden, axis=-1, keepdims=True) + EPSILON)
    normed_second = (hidden * scale_second * gain_second.astype(jnp.float32)).astype(jnp.bfloat16)
    ffn_rows = spread(normed_second)
    gate_up = outer_cols(ffn_rows, w_gateup.reshape(-1, model_width))
    unit_count = gate_up.shape[1] // 2
    gate_part = gate_up[:, :unit_count]
    up_part = gate_up[:, unit_count:]
    activated = (jax.nn.silu(gate_part) * up_part).astype(jnp.bfloat16)
    down_part = jnp.dot(activated, w_down, preferred_element_type=jnp.float32)
    branch_out = collect(down_part)
    layer_out = (hidden + branch_out).astype(jnp.bfloat16)
    saved = (
        whole_rows,
        scale_first,
        normed_all,
        query_heads,
        pairs_all,
        token_index,
        doc_start,
        cosine,
        sine_part,
        log_total,
        accumulated,
        attended,
        hidden,
        scale_second,
        ffn_rows,
        gate_part,
        up_part,
        activated,
    )
    return (layer_out, mixed, pairs_all, saved)


def layer_backward(grad_rows, extra_values, value_mix, weights, saved):
    gain_first, w_qkv, w_out, gain_second, w_gateup, w_down = weights
    (
        whole_rows,
        scale_first,
        normed_all,
        query_heads,
        pairs_all,
        token_index,
        doc_start,
        cosine,
        sine_part,
        log_total,
        accumulated,
        attended,
        hidden,
        scale_second,
        ffn_rows,
        gate_part,
        up_part,
        activated,
    ) = saved
    model_width = whole_rows.shape[1]
    head_count = w_qkv.shape[1]
    head_width = head_count * HD
    row_count = normed_all.shape[0]
    grad_hidden = grad_rows.astype(jnp.float32)
    grad_down = spread(grad_rows)
    grad_wd = inner_rows(activated, grad_down)
    grad_act = outer_cols(grad_down, w_down)
    sigmoid_gate = jax.nn.sigmoid(gate_part)
    grad_gate = grad_act * up_part * sigmoid_gate * (1.0 + gate_part * (1.0 - sigmoid_gate))
    grad_up = grad_act * gate_part * sigmoid_gate
    grad_gate_up = jnp.concatenate([grad_gate, grad_up], axis=1).astype(jnp.bfloat16)
    grad_wgu = inner_rows(grad_gate_up, ffn_rows).reshape(w_gateup.shape)
    back_second = jnp.dot(
        grad_gate_up, w_gateup.reshape(-1, model_width), preferred_element_type=jnp.float32
    )
    grad_normed_second = collect(back_second)
    grad_gain2, grad_hidden = norm_back(
        hidden, scale_second, gain_second, grad_normed_second, grad_hidden
    )
    grad_branch_all = spread(grad_hidden.astype(jnp.bfloat16))
    grad_wo = inner_rows(attended, grad_branch_all)
    grad_heads = (
        outer_cols(grad_branch_all, w_out).astype(jnp.bfloat16).reshape(row_count, head_count, HD)
    )
    grad_query, grad_pairs_all = attend_back(
        query_heads,
        pairs_all,
        token_index,
        doc_start,
        head_width,
        log_total,
        accumulated,
        grad_heads,
    )
    grad_pairs = lax.psum_scatter(
        grad_pairs_all.astype(jnp.bfloat16), "ctx", scatter_dimension=0, tiled=True
    ).astype(jnp.float32)
    grad_mixed = grad_pairs[:, head_width:] + extra_values.astype(jnp.float32)
    grad_keys = rotate_back(
        grad_pairs[:, :head_width].reshape(row_count, head_count, HD), cosine, sine_part
    )
    grad_query = rotate_back(grad_query, cosine, sine_part)
    grad_projected = jnp.concatenate(
        [
            grad_query.reshape(row_count, head_width),
            grad_keys.reshape(row_count, head_width),
            (1.0 - value_mix) * grad_mixed,
        ],
        axis=1,
    ).astype(jnp.bfloat16)
    send_values = (value_mix * grad_mixed).astype(jnp.bfloat16)
    grad_wqkv = inner_rows(grad_projected, normed_all).reshape(w_qkv.shape)
    grad_normed = collect(
        jnp.dot(
            grad_projected,
            w_qkv.reshape(3 * head_width, model_width),
            preferred_element_type=jnp.float32,
        )
    )
    grad_gain1, grad_whole = norm_back(
        whole_rows, scale_first, gain_first, grad_normed, grad_hidden
    )
    return (
        grad_whole,
        send_values,
        (grad_gain1, grad_wqkv, grad_wo, grad_gain2, grad_wgu, grad_wd),
    )


def general_body(inputs, cotangent, lengths, gain1, wqkv, wo, gain2, wgu, wd):
    section_index = lax.axis_index("section")
    leading = section_index == 0
    value_mix = jnp.where(leading, 0.0, 0.5).astype(jnp.float32)
    micro_count = inputs.shape[0]
    local_rows = inputs.shape[1]
    model_width = inputs.shape[2]
    head_width = wqkv.shape[2] * HD
    row_count = local_rows * lax.axis_size("tp")
    gateup_use, down_use = (wgu[0], wd[0])
    weights = (gain1[0], wqkv[0], wo[0], gain2[0], gateup_use, down_use)
    recv_rows = jnp.zeros((local_rows, model_width), jnp.bfloat16)
    recv_values = jnp.zeros((row_count, head_width), jnp.bfloat16)
    states = []
    outputs = []
    for turn_index in range(micro_count + 1):
        own_rows = inputs[min(turn_index, micro_count - 1)]
        row_block = jnp.where(leading, own_rows, recv_rows)
        seq_lengths = jnp.where(
            leading, lengths[min(turn_index, micro_count - 1)], lengths[max(turn_index - 1, 0)]
        )
        layer_out, mixed, pairs_all, unused = layer_forward(
            row_block, recv_values, value_mix, weights, seq_lengths
        )
        kept_pairs = None
        states.append((row_block, recv_values, seq_lengths, kept_pairs))
        outputs.append(layer_out)
        if turn_index < micro_count:
            recv_rows, recv_values = shifted((layer_out, mixed), "section", 1)
    grad_rows_in = jnp.zeros((local_rows, model_width), jnp.bfloat16)
    grad_values_in = jnp.zeros((row_count, head_width), jnp.bfloat16)
    totals = None
    turn_grads = []
    for turn_index in range(micro_count + 1):
        row_block, first_values, seq_lengths, kept_pairs = states[micro_count - turn_index]
        if turn_index < micro_count:
            fed_grad = cotangent[micro_count - 1 - turn_index]
        else:
            fed_grad = jnp.zeros_like(cotangent[0])
        grad_out = jnp.where(leading, grad_rows_in, fed_grad)
        unused_out, unused_mixed, unused_pairs, saved = layer_forward(
            row_block, first_values, value_mix, weights, seq_lengths
        )
        grad_whole, send_values, grads = layer_backward(
            grad_out, grad_values_in, value_mix, weights, saved
        )
        totals = grads if totals is None else jax.tree.map(jnp.add, totals, grads)
        sent_rows = grad_whole.astype(jnp.bfloat16)
        turn_grads.append(jnp.where(leading, grad_whole, sent_rows.astype(jnp.float32)))
        if turn_index < micro_count:
            grad_rows_in, grad_values_in = shifted((sent_rows, send_values), "section", -1)
    grad_gain1, grad_wqkv, grad_wo, grad_gain2, grad_wgu, grad_wd = totals
    grad_wqkv, grad_wo, grad_wgu, grad_wd = (
        lax.psum(grad_wqkv.astype(jnp.bfloat16), "ctx").astype(jnp.float32),
        lax.psum(grad_wo.astype(jnp.bfloat16), "ctx").astype(jnp.float32),
        lax.psum(grad_wgu.astype(jnp.bfloat16), "ctx").astype(jnp.float32),
        lax.psum(grad_wd.astype(jnp.bfloat16), "ctx").astype(jnp.float32),
    )
    grad_gain1, grad_gain2 = lax.psum((grad_gain1, grad_gain2), ("ctx", "tp"))
    acts = jnp.stack(
        [
            jnp.where(leading, outputs[batch_index], outputs[batch_index + 1])
            for batch_index in range(micro_count)
        ]
    )[None]
    input_grads = jnp.stack(
        [
            jnp.where(
                leading,
                turn_grads[micro_count - batch_index],
                turn_grads[micro_count - 1 - batch_index],
            )
            for batch_index in range(micro_count)
        ]
    )[None]
    return (
        acts,
        input_grads,
        grad_gain1[None],
        grad_wqkv[None],
        grad_wo[None],
        grad_gain2[None],
        grad_wgu[None],
        grad_wd[None],
    )


def device_groups(mesh_sizes, key, order):
    sections, contexts, parts = mesh_sizes
    groups = {}
    for section in range(sections):
        for ctx in range(contexts):
            for tp in range(parts):
                place = (section, ctx, tp)
                number = (section * contexts + ctx) * parts + tp
                groups.setdefault(key(*place), []).append((order(*place), number))
    return [[number for _, number in sorted(members)] for _, members in sorted(groups.items())]


def exchange(value, groups):
    return lax.all_to_all(
        value, ALL_AXES, split_axis=0, concat_axis=0, tiled=True, axis_index_groups=groups
    )


def document_bounds(ends_ref, index):
    start = jnp.zeros_like(index)
    for entry in range(ends_ref.shape[0]):
        end = ends_ref[entry]
        start = jnp.where(index >= end, end, start)
    return start


def scalar_start(ends_ref, index):
    start = jnp.int32(0)
    for entry in range(ends_ref.shape[0]):
        start = jnp.where(index >= ends_ref[entry], ends_ref[entry], start)
    return start


def scalar_end(ends_ref, index):
    end = ends_ref[ends_ref.shape[0] - 1]
    for entry in range(ends_ref.shape[0] - 2, -1, -1):
        end = jnp.where(index < ends_ref[entry], ends_ref[entry], end)
    return end


def dot(left, right, left_dim, right_dim):
    return lax.dot_general(
        left, right, (((left_dim,), (right_dim,)), ((), ())), preferred_element_type=jnp.float32
    )


def fold_rows(value, combine):
    rows, width = value.shape
    return combine(value.reshape(rows // 8, 8, width), axis=0)


def block_place(block, parts, width):
    entry = (block // (2 * parts)) * parts + block % parts
    return entry, pl.ds(pl.multiple_of((block // parts % 2) * width, width), width)


def attention_forward_kernel(parts, ends_ref, qkv_ref, out_ref, lse_ref, keys_ref, values_ref):
    program = pl.program_id(0)
    blocks, block_width = 2 * qkv_ref.shape[0], qkv_ref.shape[2] // 2
    width = CHUNK * block_width

    @pl.when(program == 0)
    def _():
        def turn(j, carry):
            entry, columns = block_place(j, parts, block_width)
            keys_ref[j] = qkv_ref[entry, HD : 2 * HD, columns].T
            values_ref[j, 0:HD, :] = qkv_ref[entry, 2 * HD : 3 * HD, columns]
            values_ref[j, HD : HD + ONES, :] = jnp.ones((ONES, block_width), jnp.bfloat16)
            return carry

        lax.fori_loop(0, blocks, turn, 0)

    query = []
    for block in range(CHUNK):
        entry, columns = block_place(program * CHUNK + block, parts, block_width)
        query.append(qkv_ref[entry, 0:HD, columns])
    query = jnp.concatenate(query, axis=1)
    first = program * width
    query_index = first + lax.broadcasted_iota(jnp.int32, (1, width), 1)
    start = document_bounds(ends_ref, query_index)
    low_chunk = scalar_start(ends_ref, first) // width
    high_start = scalar_start(ends_ref, first + width - 1)
    middle = jnp.clip((high_start + width - 1) // width, low_chunk, program)

    def step(chunk, carry, masked):
        top, acc = carry
        parts = []
        for entry in range(CHUNK):
            j = chunk * CHUNK + entry
            scores = dot(keys_ref[j], query, 1, 0)
            if masked:
                key_index = j * block_width + lax.broadcasted_iota(jnp.int32, (block_width, 1), 0)
                allowed = (key_index >= start) & (key_index <= query_index)
                scores = jnp.where(allowed, scores, MASKED)
            parts.append(scores)
        part_top = functools.reduce(jnp.maximum, [fold_rows(part, jnp.max) for part in parts])
        new_top = jnp.maximum(top, jnp.max(part_top, axis=0, keepdims=True))
        acc = acc * jnp.exp2(top - new_top)
        for entry in range(CHUNK):
            weights = jnp.exp2(parts[entry] - new_top).astype(jnp.bfloat16)
            acc = acc + dot(values_ref[chunk * CHUNK + entry], weights, 1, 0)
        return new_top, acc

    def on_diagonal(carry):
        top, acc = carry
        parts_of, tops = [], []
        for block in range(CHUNK):
            columns = slice(block * block_width, width)
            j = program * CHUNK + block
            scores = dot(keys_ref[j], query[:, columns], 1, 0)
            key_index = j * block_width + lax.broadcasted_iota(jnp.int32, (block_width, 1), 0)
            allowed = (key_index >= start[:, columns]) & (key_index <= query_index[:, columns])
            scores = jnp.where(allowed, scores, MASKED)
            parts_of.append(scores)
            part_top = fold_rows(scores, jnp.max)
            if block > 0:
                before = jnp.full((8, block * block_width), MASKED, jnp.float32)
                part_top = jnp.concatenate([before, part_top], axis=1)
            tops.append(part_top)
        chunk_top = jnp.max(functools.reduce(jnp.maximum, tops), axis=0, keepdims=True)
        new_top = jnp.maximum(top, chunk_top)
        acc = acc * jnp.exp2(top - new_top)
        for block, scores in enumerate(parts_of):
            weights = jnp.exp2(scores - new_top[:, block * block_width :]).astype(jnp.bfloat16)
            added = dot(values_ref[program * CHUNK + block], weights, 1, 0)
            if block > 0:
                before = jnp.zeros((HD + ONES, block * block_width), jnp.float32)
                added = jnp.concatenate([before, added], axis=1)
            acc = acc + added
        return new_top, acc

    carry = (
        jnp.full((1, width), MASKED, jnp.float32),
        jnp.zeros((HD + ONES, width), jnp.float32),
    )
    carry = lax.fori_loop(low_chunk, middle, functools.partial(step, masked=True), carry)
    carry = lax.fori_loop(middle, program, functools.partial(step, masked=False), carry)
    top, acc = on_diagonal(carry)
    total = acc[HD : HD + 1]
    out = (acc[:HD] / total).astype(jnp.bfloat16)
    lse = top + jnp.log2(total)
    for entry in range(CHUNK):
        columns = slice(entry * block_width, (entry + 1) * block_width)
        out_ref[entry] = out[:, columns]
        lse_ref[entry] = lse[:, columns]


def attention_forward(ends, qkv, parts):
    blocks, width = 2 * qkv.shape[0], qkv.shape[2] // 2
    return pl.pallas_call(
        functools.partial(attention_forward_kernel, parts),
        grid_spec=pltpu.PrefetchScalarGridSpec(
            num_scalar_prefetch=1,
            grid=(blocks // CHUNK,),
            in_specs=[pl.BlockSpec(qkv.shape, lambda i, ends_ref: (0, 0, 0))],
            out_specs=[
                pl.BlockSpec((CHUNK, HD, width), lambda i, ends_ref: (i, 0, 0)),
                pl.BlockSpec((CHUNK, 1, width), lambda i, ends_ref: (i, 0, 0)),
            ],
            scratch_shapes=[
                pltpu.VMEM((blocks, width, HD), jnp.bfloat16),
                pltpu.VMEM((blocks, HD + ONES, width), jnp.bfloat16),
            ],
        ),
        out_shape=[
            jax.ShapeDtypeStruct((blocks, HD, width), jnp.bfloat16),
            jax.ShapeDtypeStruct((blocks, 1, width), jnp.float32),
        ],
        compiler_params=pltpu.CompilerParams(vmem_limit_bytes=VMEM_LIMIT),
        cost_estimate=LIGHT,
        name="attention_forward",
    )(ends, qkv)


def attention_backward_kernel(
    parts, ends_ref, qkv_ref, out_ref, grad_ref, lse_ref, result_ref,
    query_grad_ref, delta_ref, queries_ref, grads_ref, lses_ref,
):
    program = pl.program_id(0)
    blocks, block_width = 2 * qkv_ref.shape[0], qkv_ref.shape[2] // 2
    width = CHUNK * block_width

    @pl.when(program == 0)
    def _():
        def turn(i, carry):
            for entry in range(CHUNK):
                block = i * CHUNK + entry
                columns = slice(entry * block_width, (entry + 1) * block_width)
                grad = grad_ref[block]
                place, tokens = block_place(block, parts, block_width)
                queries_ref[i, :, columns] = qkv_ref[place, 0:HD, tokens]
                grads_ref[i, :, columns] = grad
                lses_ref[i, :, columns] = lse_ref[block]
                delta_ref[i, :, columns] = jnp.sum(
                    grad.astype(jnp.float32) * out_ref[block].astype(jnp.float32),
                    axis=0,
                    keepdims=True,
                )
            query_grad_ref[i] = jnp.zeros((HD, width), jnp.float32)
            return carry

        lax.fori_loop(0, blocks // CHUNK, turn, 0)

    own_places = [
        block_place(program * CHUNK + block, parts, block_width) for block in range(CHUNK)
    ]

    def joined(low_row, high_row):
        return jnp.concatenate(
            [qkv_ref[place, low_row:high_row, tokens] for place, tokens in own_places], axis=1
        )

    first = program * width
    keys_t = joined(HD, 2 * HD)
    keys = keys_t.T
    values = joined(2 * HD, 3 * HD).T
    key_index = first + lax.broadcasted_iota(jnp.int32, (width, 1), 0)
    near_end = scalar_end(ends_ref, first)
    far_end = scalar_end(ends_ref, first + width - 1)
    stop = (far_end - 1) // width + 1
    middle = jnp.clip(near_end // width, program + 1, stop)

    def step(i, carry, masked):
        key_grad, value_grad = carry
        query = queries_ref[i]
        grad = grads_ref[i]
        weights = jnp.exp2(dot(keys, query, 1, 0) - lses_ref[i])
        if masked:
            query_index = i * width + lax.broadcasted_iota(jnp.int32, (1, width), 1)
            start = document_bounds(ends_ref, query_index)
            allowed = (key_index >= start) & (key_index <= query_index)
            weights = jnp.where(allowed, weights, 0.0)
        grad_weights = dot(values, grad, 1, 0)
        grad_scores = (weights * (grad_weights - delta_ref[i])).astype(jnp.bfloat16)
        query_grad_ref[i] += dot(keys_t, grad_scores, 1, 0)
        value_grad = value_grad + dot(grad, weights.astype(jnp.bfloat16), 1, 1)
        key_grad = key_grad + dot(query, grad_scores, 1, 1)
        return key_grad, value_grad

    key_grad = jnp.zeros((HD, width), jnp.float32)
    value_grad = jnp.zeros((HD, width), jnp.float32)
    own_query_grads = []
    for block in range(CHUNK):
        columns = slice(block * block_width, (block + 1) * block_width)
        height = (block + 1) * block_width
        query = queries_ref[program, :, columns]
        grad = grads_ref[program, :, columns]
        query_index = (
            first + block * block_width + lax.broadcasted_iota(jnp.int32, (1, block_width), 1)
        )
        start = document_bounds(ends_ref, query_index)
        rows_index = key_index[:height]
        allowed = (rows_index >= start) & (rows_index <= query_index)
        scores = dot(keys[:height], query, 1, 0)
        weights = jnp.where(allowed, jnp.exp2(scores - lses_ref[program, :, columns]), 0.0)
        grad_weights = dot(values[:height], grad, 1, 0)
        grad_scores = (weights * (grad_weights - delta_ref[program, :, columns])).astype(
            jnp.bfloat16
        )
        own_query_grads.append(dot(keys_t[:, :height], grad_scores, 1, 0))
        added = (
            dot(query, grad_scores, 1, 1),
            dot(grad, weights.astype(jnp.bfloat16), 1, 1),
        )
        if height < width:
            behind = jnp.zeros((HD, width - height), jnp.float32)
            added = [jnp.concatenate([value, behind], axis=1) for value in added]
        key_grad = key_grad + added[0]
        value_grad = value_grad + added[1]
    query_grad_ref[program] += jnp.concatenate(own_query_grads, axis=1)
    carry = (key_grad, value_grad)
    carry = lax.fori_loop(program + 1, middle, functools.partial(step, masked=False), carry)
    key_grad, value_grad = lax.fori_loop(middle, stop, functools.partial(step, masked=True), carry)
    query_grad = query_grad_ref[program] * HD ** (-0.5)
    key_grad = key_grad * LOG_2
    for block, (place, tokens) in enumerate(own_places):
        columns = slice(block * block_width, (block + 1) * block_width)
        result_ref[place, 0:HD, tokens] = query_grad[:, columns].astype(jnp.bfloat16)
        result_ref[place, HD : 2 * HD, tokens] = key_grad[:, columns].astype(jnp.bfloat16)
        result_ref[place, 2 * HD : 3 * HD, tokens] = value_grad[:, columns].astype(jnp.bfloat16)


def attention_backward(ends, qkv, out, grad, lse, parts):
    blocks, block_width = 2 * qkv.shape[0], qkv.shape[2] // 2
    chunks, width = blocks // CHUNK, CHUNK * block_width

    def whole(value):
        return pl.BlockSpec(value.shape, lambda i, ends_ref: (0, 0, 0))

    return pl.pallas_call(
        functools.partial(attention_backward_kernel, parts),
        grid_spec=pltpu.PrefetchScalarGridSpec(
            num_scalar_prefetch=1,
            grid=(chunks,),
            in_specs=[whole(qkv), whole(out), whole(grad), whole(lse)],
            out_specs=whole(qkv),
            scratch_shapes=[
                pltpu.VMEM((chunks, HD, width), jnp.float32),
                pltpu.VMEM((chunks, 1, width), jnp.float32),
                pltpu.VMEM((chunks, HD, width), jnp.bfloat16),
                pltpu.VMEM((chunks, HD, width), jnp.bfloat16),
                pltpu.VMEM((chunks, 1, width), jnp.float32),
            ],
        ),
        out_shape=jax.ShapeDtypeStruct(qkv.shape, jnp.bfloat16),
        compiler_params=pltpu.CompilerParams(vmem_limit_bytes=VMEM_LIMIT),
        cost_estimate=LIGHT,
        name="attention_backward",
    )(ends, qkv, out, grad, lse)


def rope_pair(leading_half, trailing_half, cosine, sine_part):
    return (
        leading_half * cosine - trailing_half * sine_part,
        trailing_half * cosine + leading_half * sine_part,
    )


def low(value):
    return value.astype(jnp.bfloat16)


def wide(value):
    return value.astype(jnp.float32)


def whole_block(value):
    zeros = (0,) * value.ndim
    return pl.BlockSpec(value.shape, lambda *_: zeros)


def feed_forward_kernel(rows_ref, gate_w_ref, up_w_ref, down_w_ref, gate_ref, up_ref, act_ref, sum_ref):
    rows = rows_ref[...]
    gate = dot(gate_w_ref[...], rows, 1, 1)
    up = dot(up_w_ref[...], rows, 1, 1)
    active = (gate * jax.nn.sigmoid(gate) * up).astype(jnp.bfloat16)
    gate_ref[...] = gate.astype(jnp.bfloat16)
    up_ref[...] = up.astype(jnp.bfloat16)
    act_ref[...] = active

    @pl.when(pl.program_id(0) == 0)
    def _():
        sum_ref[...] = jnp.zeros_like(sum_ref)

    sum_ref[...] += dot(active, down_w_ref[...], 0, 0)


def feed_forward(rows, w_gate, w_up, w_down, tile):
    units, width = w_gate.shape
    count = rows.shape[0]
    weight = pl.BlockSpec((tile, width), lambda i: (i, 0))
    column = pl.BlockSpec((tile, count), lambda i: (i, 0))
    hidden = jax.ShapeDtypeStruct((units, count), jnp.bfloat16)
    return pl.pallas_call(
        feed_forward_kernel,
        grid=(units // tile,),
        in_specs=[whole_block(rows), weight, weight, weight],
        out_specs=[column, column, column, pl.BlockSpec((count, width), lambda i: (0, 0))],
        out_shape=[hidden, hidden, hidden, jax.ShapeDtypeStruct((count, width), jnp.float32)],
        compiler_params=pltpu.CompilerParams(vmem_limit_bytes=VMEM_LIMIT),
        cost_estimate=LIGHT,
        name="feed_forward",
    )(rows, w_gate, w_up, w_down)


def feed_forward_back_kernel(
    grad_ref, gate_ref, up_ref, gate_w_ref, up_w_ref, down_w_ref, grad_gate_ref, grad_up_ref, sum_ref
):
    grad_act = dot(down_w_ref[...], grad_ref[...], 1, 1)
    gate = gate_ref[...].astype(jnp.float32)
    up = up_ref[...].astype(jnp.float32)
    sigmoid_gate = jax.nn.sigmoid(gate)
    grad_gate = (grad_act * up * sigmoid_gate * (1.0 + gate * (1.0 - sigmoid_gate))).astype(
        jnp.bfloat16
    )
    grad_up = (grad_act * gate * sigmoid_gate).astype(jnp.bfloat16)
    grad_gate_ref[...] = grad_gate
    grad_up_ref[...] = grad_up

    @pl.when(pl.program_id(0) == 0)
    def _():
        sum_ref[...] = jnp.zeros_like(sum_ref)

    sum_ref[...] += dot(grad_gate, gate_w_ref[...], 0, 0) + dot(grad_up, up_w_ref[...], 0, 0)


def feed_forward_back(grad, gate, up, w_gate, w_up, w_down, tile):
    units, width = w_gate.shape
    count = grad.shape[0]
    weight = pl.BlockSpec((tile, width), lambda i: (i, 0))
    column = pl.BlockSpec((tile, count), lambda i: (i, 0))
    hidden = jax.ShapeDtypeStruct((units, count), jnp.bfloat16)
    return pl.pallas_call(
        feed_forward_back_kernel,
        grid=(units // tile,),
        in_specs=[whole_block(grad), column, column, weight, weight, weight],
        out_specs=[column, column, pl.BlockSpec((count, width), lambda i: (0, 0))],
        out_shape=[hidden, hidden, jax.ShapeDtypeStruct((count, width), jnp.float32)],
        compiler_params=pltpu.CompilerParams(vmem_limit_bytes=VMEM_LIMIT),
        cost_estimate=LIGHT,
        name="feed_forward_back",
    )(grad, gate, up, w_gate, w_up, w_down)


def half_products_kernel(layout, sizes, has_addend, which_ref, *refs):
    refs = list(refs)
    out_ref = refs.pop()
    addend_ref = refs.pop() if has_addend else None
    totals = [
        sum(dot(refs[left][...], refs[right][...], 1, 0) for left, right in pairs)
        for pairs in layout
    ]
    for piece in range(out_ref.shape[0]):
        parts = [
            total[piece * size : (piece + 1) * size] for total, size in zip(totals, sizes)
        ]
        value = jnp.concatenate(parts, axis=0) if len(parts) > 1 else parts[0]
        if has_addend:
            value = value + addend_ref[piece].astype(jnp.float32)
        out_ref[piece] = value.astype(jnp.bfloat16)


def half_products(which, groups, pieces, per_step, addend=None):
    lefts, rights, layout = [], [], []
    for group in groups:
        for left, right in group:
            if not any(left is known for known in lefts):
                lefts.append(left)
            if not any(right is known for known in rights):
                rights.append(right)
    find = lambda known, value: next(i for i, entry in enumerate(known) if entry is value)
    for group in groups:
        layout.append(
            tuple((find(lefts, left), len(lefts) + find(rights, right)) for left, right in group)
        )
    sizes = tuple(group[0][0].shape[0] // (2 * pieces) for group in groups)
    width = rights[0].shape[1]
    steps = pieces // per_step
    out_spec = pl.BlockSpec((per_step, sum(sizes), width), lambda i, which_ref: (i, 0, 0))
    left_specs = [
        pl.BlockSpec(
            (left.shape[0] // (2 * steps), left.shape[1]),
            lambda i, which_ref: (which_ref[0] * steps + i, 0),
        )
        for left in lefts
    ]
    extra = [] if addend is None else [addend]
    work = sum(left.size // 2 for left, _ in sum(groups, ()))
    return pl.pallas_call(
        functools.partial(half_products_kernel, tuple(layout), sizes, addend is not None),
        grid_spec=pltpu.PrefetchScalarGridSpec(
            num_scalar_prefetch=1,
            grid=(steps,),
            in_specs=left_specs + [whole_block(right) for right in rights] + [out_spec] * len(extra),
            out_specs=out_spec,
        ),
        out_shape=jax.ShapeDtypeStruct((pieces, sum(sizes), width), jnp.bfloat16),
        compiler_params=pltpu.CompilerParams(vmem_limit_bytes=VMEM_LIMIT),
        cost_estimate=LIGHT,
        name="half_products",
    )(which.reshape(1).astype(jnp.int32), *lefts, *rights, *extra)


def together(*values):
    return lax.optimization_barrier(values)


def after(value, *others):
    return lax.optimization_barrier((value, *others))[0]


def split_body(mesh_sizes, inputs, cotangent, lengths, gain1, wqkv, wo, gain2, wgu, wd):
    sections, contexts, parts = mesh_sizes
    half_parts = parts // 2
    section = lax.axis_index("section")
    ctx = lax.axis_index("ctx")
    tp = lax.axis_index("tp")
    row_side, column_side = ctx // 2, ctx % 2
    leading = section == 0
    batch = tp // half_parts
    model_width = inputs.shape[2]
    rows = inputs.shape[1]
    heads = wqkv.shape[2] * parts
    side_heads = heads // 2
    unit_rows = wd.shape[1] // contexts // 2
    head_rows = 3 * HD // 2
    out_rows = HD // 2
    half_width = HD // 2
    tile = 4 * unit_rows
    number = lambda s, c, t: (s * contexts + c) * parts + t
    places = [
        (s, c, t) for s in range(sections) for c in range(contexts) for t in range(parts)
    ]
    everyone = [[number(*place) for place in places]]
    token_of = lambda s, c, t: c * parts + t % half_parts + half_parts * s
    batch_groups = device_groups(mesh_sizes, lambda s, c, t: t // half_parts, token_of)
    head_groups = device_groups(
        mesh_sizes,
        lambda s, c, t: (c % 2, t // half_parts),
        lambda s, c, t: (c // 2, t % half_parts + half_parts * s),
    )
    side_groups = device_groups(mesh_sizes, lambda s, c, t: c % 2, lambda s, c, t: (s, c, t))
    crossing = [
        (number(s, c, t), number(s, c, (t + half_parts) % parts))
        for s, c, t in places
        if t // half_parts == s
    ]

    def to_batch(value):
        mine = lax.dynamic_index_in_dim(value, batch, 0, keepdims=False)
        other = lax.dynamic_index_in_dim(value, 1 - batch, 0, keepdims=False)
        moved = lax.ppermute(other, ALL_AXES, crossing)
        return jnp.where(section == batch, mine, moved)

    def to_home(value, layer):
        stay = [
            (number(s, c, t), number(layer, c, t)) for s, c, t in places if t // half_parts == s
        ]
        cross = [
            (number(s, c, t), number(layer, c, (t + half_parts) % parts))
            for s, c, t in places
            if t // half_parts != s
        ]
        return (lax.ppermute(value, ALL_AXES, stay), lax.ppermute(value, ALL_AXES, cross))

    def at_home(first_pair, second_pair):
        near = jnp.where(leading, first_pair[0], second_pair[0])
        far = jnp.where(leading, first_pair[1], second_pair[1])
        upper = batch == 0
        return jnp.stack([jnp.where(upper, near, far), jnp.where(upper, far, near)])[None]

    def swap_side(value):
        return lax.ppermute(value, "ctx", [(c, c ^ 1) for c in range(contexts)])

    def swap_far(value):
        return lax.ppermute(value, "ctx", [(c, c ^ 2) for c in range(contexts)])

    def swap_near(value):
        return lax.ppermute(value, "tp", [(t, t ^ 1) for t in range(parts)])

    def swap_half(value):
        return lax.ppermute(value, "tp", [(t, (t + half_parts) % parts) for t in range(parts)])

    def swap_section(value):
        return lax.ppermute(value, "section", [(0, 1), (1, 0)])

    def all_to_all(value, axis):
        return lax.all_to_all(value, axis, split_axis=0, concat_axis=0, tiled=True)

    def copies(value, count):
        return jnp.broadcast_to(value[None], (count, *value.shape))

    def gather(value, groups):
        return lax.all_gather(value, ALL_AXES, axis=0, tiled=True, axis_index_groups=groups)

    def ordered(index, own, other):
        return jnp.where(index == 0, own, other), jnp.where(index == 0, other, own)

    def by_core(value, which):
        return lax.dynamic_index_in_dim(value, which, 0, keepdims=False)

    def spread_half(piece):
        return piece, swap_half(piece)

    def spread_near(pieces_pair):
        pair = jnp.stack(ordered(batch, *pieces_pair))
        return pair, swap_near(pair)

    def spread_line(pairs):
        line = jnp.stack(ordered(tp % 2, *pairs), axis=1)
        return line.reshape(parts, *line.shape[2:])

    def spread_far(line):
        return line, swap_far(line)

    def spread_heads(pair):
        pair = jnp.stack(ordered(row_side, *pair))
        own_heads = pair[:, :, :head_rows].reshape(-1, model_width)
        own_outs = pair[:, :, head_rows:]
        return (own_heads, swap_section(own_heads)), (own_outs, swap_side(own_outs))

    def spread_outs(pair):
        own_outs = jnp.stack(ordered(column_side, *pair), axis=1).reshape(-1, model_width)
        return own_outs, swap_section(own_outs)

    def join_outs(pair):
        return jnp.concatenate(ordered(section, *pair), axis=0)

    def own_halves(value, axis, size):
        part = lax.dynamic_slice_in_dim(value, ctx * size, size, axis)
        return part.reshape(2, -1, model_width)

    packed = jnp.concatenate(
        [
            own_halves(wqkv[0], 1, heads // (parts * contexts)),
            own_halves(wo[0], 0, HD),
            own_halves(wgu[0, 0], 0, 2 * unit_rows),
            own_halves(wgu[0, 1], 0, 2 * unit_rows),
            own_halves(wd[0], 0, 2 * unit_rows),
        ],
        axis=1,
    )
    kept = by_core(packed, section)
    passed = swap_section(by_core(packed, 1 - section))
    pieces = ordered(section, kept, passed)
    attention_rows = head_rows + out_rows

    def feed_forward_weights(piece):
        whole = gather(piece[attention_rows:], side_groups)
        whole = whole.reshape(2 * 2 * parts, 3, unit_rows, model_width)
        return [whole[:, entry].reshape(-1, model_width) for entry in range(3)]

    rows_in = to_batch(inputs)
    line = spread_near(spread_half(pieces[0][:attention_rows]))
    line, rows_in = together(spread_line(line), rows_in)
    w_ffn = [feed_forward_weights(after(pieces[0], line)), None]
    w_heads, w_outs = [None, None], [None, None]
    first_pair = spread_far(line)

    gains = wide(jnp.concatenate([gain1, gain2], axis=0))
    gain_sets = ordered(section, gains, swap_section(gains))

    seq_lengths = lax.dynamic_index_in_dim(lengths, batch, 0, keepdims=False)
    ends = jnp.cumsum(seq_lengths).astype(jnp.int32)
    token_index = jnp.concatenate(
        [
            token_of(section, 2 * row_side + side, tp) * rows + jnp.arange(rows, dtype=jnp.int32)
            for side in range(2)
        ]
    )
    before = (ends[None, :] <= token_index[:, None]).astype(jnp.int32)
    position = token_index - jnp.sum(before * seq_lengths[None, :], axis=1)
    frequency = jnp.exp(
        -jnp.log(10000.0) * jnp.arange(half_width, dtype=jnp.float32) / half_width
    )
    angles = position.astype(jnp.float32)[None, :] * frequency[:, None]
    cosine, sine_part = jnp.cos(angles), jnp.sin(angles)

    def head_halves(value):
        size = value.shape[1] // 2
        return value.reshape(heads, 2, size, rows).transpose(1, 0, 2, 3).reshape(2, -1, rows)

    def whole_heads(value):
        value = value.reshape(2, heads, -1, rows)
        return value.transpose(1, 0, 2, 3).reshape(heads, -1, rows)

    def nothing(value):
        return value

    def layer_forward(whole_rows, first_values, layer, in_zero, in_first, in_second, in_middle, in_third, in_fourth):
        gain_first, gain_second = gain_sets[layer][0], gain_sets[layer][1]
        scale_first = lax.rsqrt(jnp.mean(whole_rows * whole_rows, axis=-1, keepdims=True) + EPSILON)
        normed = low(whole_rows * scale_first * gain_first)
        far_normed = in_zero(swap_side(normed))
        side_rows = jnp.concatenate(ordered(column_side, normed, far_normed), axis=0)
        halves = ordered(section, *[dot(weight, side_rows, 1, 1) for weight in w_heads[layer]])
        upper, lower = [half.reshape(side_heads, head_rows, 2 * rows) for half in halves]
        query = rope_pair(upper[:, :half_width], upper[:, half_width:HD], cosine, sine_part)
        key = rope_pair(upper[:, HD:], lower[:, :half_width], cosine, sine_part)
        value = lower[:, half_width:]
        if first_values is not None:
            value = 0.5 * value + 0.5 * wide(first_values)
        mixed = low(value)
        shrunk = [low(half * (HD ** (-0.5) / LOG_2)) for half in query]
        qkv = exchange(
            jnp.concatenate([*shrunk, low(key[0]), low(key[1]), mixed], axis=1), head_groups
        )
        qkv = in_first(qkv)
        out, lse = attention_forward(ends, qkv, parts)
        out = in_second(out)
        attended = head_halves(in_middle(exchange(out, batch_groups)))
        hidden = whole_rows + dot(attended.reshape(-1, rows), w_outs[layer], 0, 0)
        scale_second = lax.rsqrt(jnp.mean(hidden * hidden, axis=-1, keepdims=True) + EPSILON)
        normed_second = low(hidden * scale_second * gain_second)
        far_rows = swap_side(normed_second)
        near = feed_forward(normed_second, *w_ffn[layer], tile)
        far_rows = in_third(after(far_rows, near[3]))
        far = feed_forward(far_rows, *w_ffn[layer], tile)
        sent_down = low(far[3])

        def layer_out(*others):
            far_down = in_fourth(swap_side(after(sent_down, *others)))
            return low(hidden + (near[3] + wide(far_down)))

        saved = (
            whole_rows, scale_first, side_rows, qkv, out, lse, attended, hidden, scale_second,
            (normed_second, far_rows), near[:3], far[:3],
        )
        return layer_out, mixed, saved

    def norm_back(whole_rows, scale_rows, gain, grad_normed, grad_rest):
        unit = whole_rows * scale_rows
        scaled = grad_normed * gain
        grad_gain = jnp.sum(grad_normed * unit, axis=0)
        grad_whole = grad_rest + scale_rows * (
            scaled - unit * jnp.mean(scaled * unit, axis=-1, keepdims=True)
        )
        return grad_gain, grad_whole

    def pick(value, index, axis):
        return lax.dynamic_index_in_dim(value, index, axis, keepdims=False)

    def parted(value, index, axis):
        return pick(value, index, axis), pick(value, 1 - index, axis)

    def moved_pair(pair, swap):
        return pair[0], swap(pair[1])

    def halve(value, index, swap, axis):
        return moved_pair(parted(value, index, axis), swap)

    def add(pair):
        return low(wide(pair[0]) + wide(pair[1]))

    def near_parts(value):
        return parted(value.reshape(2, half_parts, *value.shape[1:]), tp % 2, 1)

    def near_sum(value):
        return moved_pair(near_parts(value), swap_near)

    def far_sum(pair):
        return halve(add(pair), batch, swap_half, 0)

    def layer_backward(grad_rows, extra_values, saved, layer, in_first, in_second, in_third, in_fourth, in_fifth):
        (
            whole_rows, scale_first, _, qkv, out, lse, attended, hidden, scale_second,
            ffn_rows, near, far,
        ) = saved
        gain_first, gain_second = gain_sets[layer][0], gain_sets[layer][1]
        grad_down = low(grad_rows)
        far_down = swap_side(grad_down)
        grad_gate, grad_up, near_back = feed_forward_back(grad_down, *near[:2], *w_ffn[layer], tile)
        far_down = in_first(after(far_down, near_back))
        far_gate, far_up, far_back = feed_forward_back(far_down, *far[:2], *w_ffn[layer], tile)
        far_back = swap_side(low(far_back))
        groups = (
            ((grad_gate, ffn_rows[0]), (far_gate, ffn_rows[1])),
            ((grad_up, ffn_rows[0]), (far_up, ffn_rows[1])),
            ((near[2], grad_down), (far[2], far_down)),
        )
        products = functools.partial(
            half_products, groups=groups, pieces=2 * parts, per_step=2
        )
        sent = products(1 - section)
        moved = swap_section(sent)
        far_back = in_second(after(far_back, sent))
        grad_gain2, grad_hidden = norm_back(
            hidden, scale_second, gain_second, near_back + wide(far_back), wide(grad_rows)
        )
        grad_branch = low(grad_hidden)
        grad_heads = whole_heads(low(dot(w_outs[layer], grad_branch, 1, 1)))
        grad_heads = exchange(grad_heads, batch_groups)
        rest = products(section, addend=moved)
        out_pair = (attended.reshape(-1, rows), grad_branch)
        grad_heads, rest = in_third(grad_heads, rest, out_pair)
        grad_qkv = attention_backward(ends, qkv, out, grad_heads, lse, parts)
        grad_qkv = in_fourth(grad_qkv)
        grad_qkv = in_fifth(exchange(grad_qkv, head_groups))
        grad_qkv = wide(grad_qkv)
        quarter = lambda entry: grad_qkv[:, entry * half_width : (entry + 1) * half_width]
        grad_query = rope_pair(quarter(0), quarter(1), cosine, -sine_part)
        grad_key = rope_pair(quarter(2), quarter(3), cosine, -sine_part)
        grad_value = grad_qkv[:, 2 * HD :]
        send_values = None
        if extra_values is None:
            grad_value = 0.5 * grad_value
            send_values = low(grad_value)
        else:
            grad_value = grad_value + wide(extra_values)
        upper = low(jnp.concatenate([*grad_query, grad_key[0]], axis=1))
        lower = low(jnp.concatenate([grad_key[1], grad_value], axis=1))
        grad_halves = jnp.stack([upper, lower]).reshape(2, -1, 2 * rows)
        return grad_halves, send_values, grad_hidden, out_pair, grad_gain2

    def input_grads_of(grad_halves, grad_hidden, saved, layer, beside):
        whole_rows, scale_first = saved[:2]
        places_of = (section, 1 - section)
        grad_side = sum(
            dot(by_core(grad_halves, place), weight, 0, 0)
            for place, weight in zip(places_of, w_heads[layer])
        ).reshape(2, rows, model_width)
        grad_far = swap_side(low(by_core(grad_side, 1 - column_side)))
        grad_normed = by_core(grad_side, column_side) + wide(beside(grad_far))
        return norm_back(whole_rows, scale_first, gain_sets[layer][0], grad_normed, grad_hidden)

    def piece_sum(value, groups):
        return lax.psum_scatter(
            value, ALL_AXES, scatter_dimension=0, tiled=True, axis_index_groups=groups
        )

    line_groups = device_groups(
        mesh_sizes, lambda s, c, t: (s, c % 2), lambda s, c, t: (c, t)
    )
    plane_shape = (2, 2, parts)
    pending = {}

    def weights_zero(value):
        value, pair = together(value, first_pair)
        w_heads[0], pending["outs"] = spread_heads(pair)
        return value

    def weights_line(value):
        value, piece = together(value, pieces[1][:attention_rows])
        pending["weights"] = spread_half(piece)
        return value

    def weights_outs_first(value):
        value, pending["outs"], w_ffn[0], weights = together(
            value, pending["outs"], w_ffn[0], pending["weights"]
        )
        pending["weights"] = spread_near(weights)
        w_outs[0] = join_outs(spread_outs(pending["outs"]))
        return value

    def weights_far(value):
        value, line = together(value, pending["weights"])
        pending["weights"] = spread_far(spread_line(line))
        w_ffn[1] = feed_forward_weights(after(pieces[1], value))
        return value

    def weights_heads(value):
        value, pairs = together(value, pending["weights"])
        w_heads[1], pending["outs"] = spread_heads(pairs)
        return value

    first_result, first_values, first_saved = layer_forward(
        wide(rows_in), None, 0,
        weights_zero, weights_line, nothing, weights_outs_first, weights_far, weights_heads,
    )

    first_out = first_result()

    def start_outs(value):
        value, grads = together(value, cotangent)
        pending["grad_in"] = to_batch(grads)
        return value

    def end_outs(value):
        value, outs, w_ffn[1], pending["grad_in"] = together(
            value, pending["outs"], w_ffn[1], pending["grad_in"]
        )
        w_outs[1] = join_outs(spread_outs(outs))
        pending["first_home"] = to_home(after(first_out, value), 0)
        return value

    second_result, _, second_saved = layer_forward(
        wide(first_out), first_values, 1,
        nothing, start_outs, end_outs, nothing, nothing, nothing,
    )
    grad_in = pending["grad_in"]

    def out_sides(out_pair):
        products = functools.partial(half_products, groups=((out_pair,),), pieces=heads, per_step=8)
        out_sum = products(section, addend=swap_section(products(1 - section)))
        return parted(out_sum.reshape(*plane_shape, out_rows, model_width), column_side, 1)

    def second_third(value, rest, out_pair):
        value, rest = together(value, rest)
        rest = rest.reshape(-1, model_width)
        pending["second_rest"] = piece_sum(rest, line_groups)
        pending["second_out_rows"] = second_result(value)
        pending["out"] = out_sides(out_pair)
        value = after(value, pending["out"])
        pending["out"] = moved_pair(pending["out"], swap_side)
        return value, rest

    def second_fourth(value):
        value, pending["first_home"], second_out, out_sum = together(
            value, pending["first_home"], pending["second_out_rows"], pending["out"]
        )
        pending["second_home"] = to_home(second_out, 1)
        pending["second_out"] = add(out_sum).reshape(2 * parts, out_rows, model_width)
        return value

    grad_halves, send_values, grad_hidden, _, second_gain2 = layer_backward(
        grad_in, None, second_saved, 1, nothing, nothing, second_third, second_fourth, nothing
    )
    head_products = functools.partial(
        half_products,
        groups=(((grad_halves.reshape(-1, 2 * rows), second_saved[2]),),),
        pieces=side_heads,
        per_step=4,
    )

    def head_start(value):
        value, sent = together(value, head_products(1 - section))
        pending["moved"] = swap_section(sent)
        return value

    second_gain1, second_grad = input_grads_of(
        grad_halves, grad_hidden, second_saved, 1, head_start
    )
    second_grad = low(second_grad)

    def first_first(value):
        head = head_products(section, addend=pending["moved"])
        head = jnp.concatenate([head, pending["second_out"]], axis=1)
        head = parted(head.reshape(2, parts, -1, model_width), row_side, 0)
        value, head = together(value, head)
        pending["head"] = moved_pair(head, swap_far)
        return value

    def first_second(value):
        return value

    def first_third(value, rest, out_pair):
        out_sum = out_sides(out_pair)
        rest = rest.reshape(2, parts, -1, model_width)
        rest_a = parted(rest[:, :, : 2 * unit_rows], row_side, 0)
        rest_b = parted(rest[:, :, 2 * unit_rows :], row_side, 0)
        (
            value, rest_a, rest_b, out_sum, head, pending["second_rest"], pending["second_home"]
        ) = together(
            value, rest_a, rest_b, out_sum, pending["head"], pending["second_rest"],
            pending["second_home"],
        )
        pending["rest_a"] = moved_pair(rest_a, swap_far)
        pending["rest_b"] = rest_b
        pending["out"] = moved_pair(out_sum, swap_side)
        pending["head"] = near_sum(add(head))
        return value, rest

    def first_fourth(value):
        value, rest_a, rest_b, out_sum, head = together(
            value, pending["rest_a"], pending["rest_b"], pending["out"], pending["head"]
        )
        pending["head"] = far_sum(head)
        pending["second_rest"] = lax.all_gather(
            after(pending["second_rest"], value), "ctx", axis=0, tiled=False
        )
        pending["rest_b"] = moved_pair(rest_b, swap_far)
        pending["rest_a"] = near_sum(add(rest_a))
        pending["out"] = halve(add(out_sum), row_side, swap_far, 0)
        return value

    first_halves, _, first_hidden, _, first_gain2 = layer_backward(
        second_grad, send_values, first_saved, 0,
        first_first, first_second, first_third, first_fourth, nothing,
    )
    head_products = functools.partial(
        half_products,
        groups=(((first_halves.reshape(-1, 2 * rows), first_saved[2]),),),
        pieces=side_heads,
        per_step=4,
    )
    sent = head_products(1 - section)
    moved = swap_section(sent)
    def head_end(value):
        head = head_products(section, addend=moved).reshape(2, parts, head_rows, model_width)
        head = parted(head, row_side, 0)
        head, rest_a, rest_b, out_sum, second_head = together(
            head, pending["rest_a"], pending["rest_b"], pending["out"], pending["head"]
        )
        pending["head"] = moved_pair(head, swap_far)
        pending["rest_b"] = near_sum(add(rest_b))
        pending["rest_a"] = far_sum(rest_a)
        pending["out"] = add(out_sum)
        pending["second_head"] = add(second_head)
        return after(value, head)

    first_gain1, first_grad = input_grads_of(
        after(first_halves, sent), first_hidden, first_saved, 0, head_end
    )
    def summed(value, swap):
        return value + swap(value)

    gain_rows = jnp.stack([first_gain1, first_gain2, second_gain1, second_gain2])
    gain_rows = summed(gain_rows, swap_section)
    head, rest_a, rest_b, gain_rows, first_grad = together(
        pending["head"], pending["rest_a"], pending["rest_b"], gain_rows, low(first_grad)
    )
    head = near_sum(jnp.concatenate([add(head), pending["out"]], axis=1))
    rest_b = far_sum(rest_b)
    gain_rows = summed(summed(gain_rows, swap_side), swap_far)
    head, rest_b, gain_rows, first_grad, second_rest = together(
        head, rest_b, gain_rows, first_grad, pending["second_rest"]
    )
    head = far_sum(head)
    rest = jnp.concatenate([add(rest_a), add(rest_b)], axis=0)
    rest = lax.all_gather(rest, "ctx", axis=0, tiled=False)
    gain_rows = summed(gain_rows, swap_near)
    head, first_grad, home = together(head, first_grad, second_grad)
    first_grad_home = to_home(first_grad, 0)
    second_grad_home = to_home(home, 1)
    head = jnp.concatenate([add(head), pending["second_head"]], axis=0)
    head = all_to_all(copies(head, contexts), "ctx")
    head, gain_rows, first_grad_home, second_grad_home = together(
        head, gain_rows, first_grad_home, second_grad_home
    )
    gain_total = summed(gain_rows, swap_half)
    rest, head = together(rest, head)
    first_grads = (rest, head[:, :attention_rows])
    second_grads = (second_rest, head[:, attention_rows:])
    first_home, second_home = pending["first_home"], pending["second_home"]
    gain_total = jnp.where(leading, gain_total[:2], gain_total[2:])

    def finish(first, second):
        mine = jnp.where(leading, first, second)
        moved = swap_section(jnp.where(leading, second, first))
        return ordered(section, mine, moved)

    def joined(halves, first, count):
        both = jnp.stack([half[:, first : first + count] for half in halves], axis=1)
        return wide(both).reshape(-1, model_width)

    rest_grads = finish(first_grads[0], second_grads[0])
    grad_wgate, grad_wup, grad_wd = [
        joined(rest_grads, entry * unit_rows, unit_rows) for entry in range(3)
    ]
    head, grad_wgate, grad_wup, grad_wd = together(first_grads[1], grad_wgate, grad_wup, grad_wd)
    head_grads = finish(head, second_grads[1])
    grad_wqkv = joined(head_grads, 0, head_rows).reshape(contexts, 3, HD, model_width)
    grad_wo = joined(head_grads, head_rows, out_rows)
    return (
        at_home(first_home, second_home),
        wide(at_home(first_grad_home, second_grad_home)),
        gain_total[0:1],
        grad_wqkv.transpose(1, 0, 2, 3)[None],
        grad_wo[None],
        gain_total[1:2],
        jnp.stack([grad_wgate, grad_wup])[None],
        grad_wd[None],
    )


def body(mesh_sizes, *arguments):
    inputs, _, _, _, wqkv = arguments[:5]
    sections, contexts, parts = mesh_sizes
    own_heads, own_units = wqkv.shape[2], arguments[7].shape[2]
    fits = (
        sections == 2
        and inputs.shape[0] == 2
        and contexts == 4
        and parts % 2 == 0
        and own_heads == contexts
        and own_units % (16 * contexts) == 0
        and inputs.shape[1] % 128 == 0
    )
    if fits:
        return split_body(mesh_sizes, *arguments)
    return general_body(*arguments)


def solution(mesh):
    placed = (
        P(None, ("ctx", "tp"), None),
        P(None, ("ctx", "tp"), None),
        P(),
        P("section", None),
        P("section", None, "tp", None, None),
        P("section", "tp", None),
        P("section", None),
        P("section", None, "tp", None),
        P("section", "tp", None),
    )
    mesh_sizes = tuple(mesh.shape[axis] for axis in ALL_AXES)
    return jax.shard_map(
        functools.partial(body, mesh_sizes),
        mesh=mesh,
        in_specs=placed,
        out_specs=(
            P("section", None, ("ctx", "tp"), None),
            P("section", None, ("ctx", "tp"), None),
            P("section", None),
            P("section", None, "tp", None, None),
            P("section", "tp", None),
            P("section", None),
            P("section", None, "tp", None),
            P("section", "tp", None),
        ),
        check_vma=False,
    )
```

```python
import functools

import jax
import jax.numpy as jnp
from jax import lax
from jax.experimental import pallas as pl
from jax.experimental.pallas import tpu as pltpu
from jax.sharding import PartitionSpec as P

HD = 64
EPSILON = 1e-06
MASKED = -1e30
ALL_AXES = ("section", "ctx", "tp")
CHUNK = 2
ONES = 16
LOG_2 = 0.6931471805599453
LIGHT = pl.CostEstimate(flops=1, bytes_accessed=1, transcendentals=0)
VMEM_LIMIT = 40 * 1024 * 1024


def shifted(block, axis, distance):
    devices = range(lax.axis_size(axis))
    route = [(i - distance, i) for i in devices if i - distance in devices]
    return lax.ppermute(block, axis, route)


def rope_parts(position):
    half_width = HD // 2
    frequency = jnp.exp(-jnp.log(10000.0) * jnp.arange(half_width, dtype=jnp.float32) / half_width)
    angles = position.astype(jnp.float32)[:, None] * frequency[None, :]
    return (jnp.cos(angles), jnp.sin(angles))


def rotate(vectors, cosine, sine_part):
    half_width = HD // 2
    leading_half = vectors[..., :half_width]
    trailing_half = vectors[..., half_width:]
    cosine = cosine[:, None, :]
    sine_part = sine_part[:, None, :]
    return jnp.concatenate(
        [
            leading_half * cosine - trailing_half * sine_part,
            trailing_half * cosine + leading_half * sine_part,
        ],
        axis=-1,
    )


def rotate_back(vectors, cosine, sine_part):
    half_width = HD // 2
    leading_half = vectors[..., :half_width]
    trailing_half = vectors[..., half_width:]
    cosine = cosine[:, None, :]
    sine_part = sine_part[:, None, :]
    return jnp.concatenate(
        [
            leading_half * cosine + trailing_half * sine_part,
            trailing_half * cosine - leading_half * sine_part,
        ],
        axis=-1,
    )


def inner_rows(left, right):
    return lax.dot_general(
        left, right, (((0,), (0,)), ((), ())), preferred_element_type=jnp.float32
    )


def outer_cols(left, right):
    return lax.dot_general(
        left, right, (((1,), (1,)), ((), ())), preferred_element_type=jnp.float32
    )


def spread(row_block):
    return lax.all_gather(row_block, "tp", axis=0, tiled=True)


def collect(partial_value):
    return lax.psum_scatter(
        partial_value.astype(jnp.bfloat16), "tp", scatter_dimension=0, tiled=True
    ).astype(jnp.float32)


def fetch_keys(key_value):
    return lax.all_gather(key_value, "ctx", axis=0, tiled=True)


def query_bounds(seq_lengths, block_first, row_count):
    token_index = block_first + jnp.arange(row_count, dtype=jnp.int32)
    doc_ends = jnp.cumsum(seq_lengths)
    before = (doc_ends[None, :] <= token_index[:, None]).astype(jnp.int32)
    doc_start = jnp.sum(before * seq_lengths[None, :], axis=1)
    return (token_index, doc_start)


def block_scores(query_heads, pair_block, block_first, token_index, doc_start, head_width):
    row_count = pair_block.shape[0]
    key_heads = pair_block[:, :head_width].reshape(row_count, head_width // HD, HD)
    value_heads = pair_block[:, head_width:].reshape(row_count, head_width // HD, HD)
    scores = jnp.einsum(
        "qhd,khd->hqk", query_heads, key_heads, preferred_element_type=jnp.float32
    ) * HD ** (-0.5)
    key_index = block_first + jnp.arange(row_count, dtype=jnp.int32)
    allowed = (key_index[None, :] >= doc_start[:, None]) & (
        key_index[None, :] <= token_index[:, None]
    )
    return (scores, allowed[None], key_heads, value_heads)


def split_blocks(pairs_all, row_count):
    blocks = pairs_all.reshape(-1, row_count, pairs_all.shape[1])
    block_starts = jnp.arange(blocks.shape[0], dtype=jnp.int32) * row_count
    return (blocks, block_starts)


def attend(query_heads, pairs_all, token_index, doc_start, head_width):
    row_count = query_heads.shape[0]
    head_count = head_width // HD
    blocks, block_starts = split_blocks(pairs_all, row_count)
    last_query = token_index[row_count - 1]
    first_query = doc_start[0]

    def rowmax_live(carried, block_parts):
        running_top, running_sum = carried
        scores, allowed, unused_keys, unused_values = block_scores(
            query_heads, block_parts[0], block_parts[1], token_index, doc_start, head_width
        )
        masked = jnp.where(allowed, scores, -1e30)
        new_top = jnp.maximum(running_top, jnp.max(masked, axis=-1))
        running_sum = running_sum * jnp.exp(running_top - new_top) + jnp.sum(
            jnp.where(allowed, jnp.exp(masked - new_top[..., None]), 0.0), axis=-1
        )
        return (new_top, running_sum)

    def rowmax_step(carried, block_parts):
        live = (block_parts[1] <= last_query) & (block_parts[1] + row_count > first_query)
        return (
            lax.cond(live, lambda held: rowmax_live(held, block_parts), lambda held: held, carried),
            None,
        )

    initial = (
        jnp.full((head_count, row_count), -1e30, jnp.float32),
        jnp.zeros((head_count, row_count), jnp.float32),
    )
    (running_top, running_sum), unused = lax.scan(rowmax_step, initial, (blocks, block_starts))
    log_total = running_top + jnp.log(running_sum)

    def output_live(accumulated, block_parts):
        scores, allowed, unused_keys, value_heads = block_scores(
            query_heads, block_parts[0], block_parts[1], token_index, doc_start, head_width
        )
        soft_weights = jnp.where(allowed, jnp.exp(scores - log_total[..., None]), 0.0).astype(
            jnp.bfloat16
        )
        return accumulated + jnp.einsum(
            "hqk,khd->qhd", soft_weights, value_heads, preferred_element_type=jnp.float32
        )

    def output_step(accumulated, block_parts):
        live = (block_parts[1] <= last_query) & (block_parts[1] + row_count > first_query)
        return (
            lax.cond(
                live, lambda held: output_live(held, block_parts), lambda held: held, accumulated
            ),
            None,
        )

    accumulated, unused = lax.scan(
        output_step, jnp.zeros((row_count, head_count, HD), jnp.float32), (blocks, block_starts)
    )
    return (accumulated, log_total)


def attend_back(
    query_heads, pairs_all, token_index, doc_start, head_width, log_total, accumulated, grad_heads
):
    row_count = query_heads.shape[0]
    head_count = head_width // HD
    blocks, block_starts = split_blocks(pairs_all, row_count)
    last_query = token_index[row_count - 1]
    first_query = doc_start[0]
    rowdot = jnp.sum(grad_heads.astype(jnp.float32) * accumulated, axis=-1).T

    def grad_live(grad_acc, block_parts):
        scores, allowed, key_heads, value_heads = block_scores(
            query_heads, block_parts[0], block_parts[1], token_index, doc_start, head_width
        )
        soft_weights = jnp.where(allowed, jnp.exp(scores - log_total[..., None]), 0.0)
        grad_soft = jnp.einsum(
            "qhd,khd->hqk", grad_heads, value_heads, preferred_element_type=jnp.float32
        )
        grad_scores = (soft_weights * (grad_soft - rowdot[..., None])).astype(jnp.bfloat16)
        grad_acc = grad_acc + jnp.einsum(
            "hqk,khd->qhd", grad_scores, key_heads, preferred_element_type=jnp.float32
        )
        grad_keys = jnp.einsum(
            "hqk,qhd->khd", grad_scores, query_heads, preferred_element_type=jnp.float32
        ) * HD ** (-0.5)
        grad_values = jnp.einsum(
            "hqk,qhd->khd",
            soft_weights.astype(jnp.bfloat16),
            grad_heads,
            preferred_element_type=jnp.float32,
        )
        return (grad_acc, (grad_keys, grad_values))

    def grad_skip(grad_acc):
        empty = jnp.zeros((row_count, head_count, HD), jnp.float32)
        return (grad_acc, (empty, empty))

    def grad_step(grad_acc, block_parts):
        live = (block_parts[1] <= last_query) & (block_parts[1] + row_count > first_query)
        return lax.cond(live, lambda held: grad_live(held, block_parts), grad_skip, grad_acc)

    grad_query, (grad_keys, grad_values) = lax.scan(
        grad_step, jnp.zeros((row_count, head_count, HD), jnp.float32), (blocks, block_starts)
    )
    grad_query = grad_query * HD ** (-0.5)
    grad_pairs = jnp.concatenate(
        [grad_keys.reshape(-1, head_width), grad_values.reshape(-1, head_width)], axis=1
    )
    return (grad_query, grad_pairs)


def norm_back(whole_rows, scale_rows, gain, grad_normed, grad_rest):
    unit_rows = whole_rows * scale_rows
    scaled = grad_normed * gain.astype(jnp.float32)
    grad_gain = jnp.sum(grad_normed * unit_rows, axis=0)
    grad_whole = grad_rest + scale_rows * (
        scaled - unit_rows * jnp.mean(scaled * unit_rows, axis=-1, keepdims=True)
    )
    return (grad_gain, grad_whole)


def layer_forward(row_block, first_values, value_mix, weights, seq_lengths):
    gain_first, w_qkv, w_out, gain_second, w_gateup, w_down = weights
    head_count = w_qkv.shape[1]
    head_width = head_count * HD
    model_width = row_block.shape[1]
    whole_rows = row_block.astype(jnp.float32)
    scale_first = lax.rsqrt(jnp.mean(whole_rows * whole_rows, axis=-1, keepdims=True) + EPSILON)
    normed = (whole_rows * scale_first * gain_first.astype(jnp.float32)).astype(jnp.bfloat16)
    normed_all = spread(normed)
    row_count = normed_all.shape[0]
    projected = outer_cols(normed_all, w_qkv.reshape(3 * head_width, model_width))
    token_index, doc_start = query_bounds(seq_lengths, lax.axis_index("ctx") * row_count, row_count)
    cosine, sine_part = rope_parts(token_index - doc_start)
    query_heads = rotate(
        projected[:, :head_width].reshape(row_count, head_count, HD), cosine, sine_part
    ).astype(jnp.bfloat16)
    key_heads = rotate(
        projected[:, head_width : 2 * head_width].reshape(row_count, head_count, HD),
        cosine,
        sine_part,
    ).astype(jnp.bfloat16)
    mixed = (
        (1.0 - value_mix) * projected[:, 2 * head_width :]
        + value_mix * first_values.astype(jnp.float32)
    ).astype(jnp.bfloat16)
    key_value = jnp.concatenate([key_heads.reshape(row_count, head_width), mixed], axis=1)
    pairs_all = fetch_keys(key_value)
    accumulated, log_total = attend(query_heads, pairs_all, token_index, doc_start, head_width)
    attended = accumulated.reshape(row_count, head_width).astype(jnp.bfloat16)
    hidden = whole_rows + collect(jnp.dot(attended, w_out, preferred_element_type=jnp.float32))
    scale_second = lax.rsqrt(jnp.mean(hidden * hidden, axis=-1, keepdims=True) + EPSILON)
    normed_second = (hidden * scale_second * gain_second.astype(jnp.float32)).astype(jnp.bfloat16)
    ffn_rows = spread(normed_second)
    gate_up = outer_cols(ffn_rows, w_gateup.reshape(-1, model_width))
    unit_count = gate_up.shape[1] // 2
    gate_part = gate_up[:, :unit_count]
    up_part = gate_up[:, unit_count:]
    activated = (jax.nn.silu(gate_part) * up_part).astype(jnp.bfloat16)
    down_part = jnp.dot(activated, w_down, preferred_element_type=jnp.float32)
    branch_out = collect(down_part)
    layer_out = (hidden + branch_out).astype(jnp.bfloat16)
    saved = (
        whole_rows,
        scale_first,
        normed_all,
        query_heads,
        pairs_all,
        token_index,
        doc_start,
        cosine,
        sine_part,
        log_total,
        accumulated,
        attended,
        hidden,
        scale_second,
        ffn_rows,
        gate_part,
        up_part,
        activated,
    )
    return (layer_out, mixed, pairs_all, saved)


def layer_backward(grad_rows, extra_values, value_mix, weights, saved):
    gain_first, w_qkv, w_out, gain_second, w_gateup, w_down = weights
    (
        whole_rows,
        scale_first,
        normed_all,
        query_heads,
        pairs_all,
        token_index,
        doc_start,
        cosine,
        sine_part,
        log_total,
        accumulated,
        attended,
        hidden,
        scale_second,
        ffn_rows,
        gate_part,
        up_part,
        activated,
    ) = saved
    model_width = whole_rows.shape[1]
    head_count = w_qkv.shape[1]
    head_width = head_count * HD
    row_count = normed_all.shape[0]
    grad_hidden = grad_rows.astype(jnp.float32)
    grad_down = spread(grad_rows)
    grad_wd = inner_rows(activated, grad_down)
    grad_act = outer_cols(grad_down, w_down)
    sigmoid_gate = jax.nn.sigmoid(gate_part)
    grad_gate = grad_act * up_part * sigmoid_gate * (1.0 + gate_part * (1.0 - sigmoid_gate))
    grad_up = grad_act * gate_part * sigmoid_gate
    grad_gate_up = jnp.concatenate([grad_gate, grad_up], axis=1).astype(jnp.bfloat16)
    grad_wgu = inner_rows(grad_gate_up, ffn_rows).reshape(w_gateup.shape)
    back_second = jnp.dot(
        grad_gate_up, w_gateup.reshape(-1, model_width), preferred_element_type=jnp.float32
    )
    grad_normed_second = collect(back_second)
    grad_gain2, grad_hidden = norm_back(
        hidden, scale_second, gain_second, grad_normed_second, grad_hidden
    )
    grad_branch_all = spread(grad_hidden.astype(jnp.bfloat16))
    grad_wo = inner_rows(attended, grad_branch_all)
    grad_heads = (
        outer_cols(grad_branch_all, w_out).astype(jnp.bfloat16).reshape(row_count, head_count, HD)
    )
    grad_query, grad_pairs_all = attend_back(
        query_heads,
        pairs_all,
        token_index,
        doc_start,
        head_width,
        log_total,
        accumulated,
        grad_heads,
    )
    grad_pairs = lax.psum_scatter(
        grad_pairs_all.astype(jnp.bfloat16), "ctx", scatter_dimension=0, tiled=True
    ).astype(jnp.float32)
    grad_mixed = grad_pairs[:, head_width:] + extra_values.astype(jnp.float32)
    grad_keys = rotate_back(
        grad_pairs[:, :head_width].reshape(row_count, head_count, HD), cosine, sine_part
    )
    grad_query = rotate_back(grad_query, cosine, sine_part)
    grad_projected = jnp.concatenate(
        [
            grad_query.reshape(row_count, head_width),
            grad_keys.reshape(row_count, head_width),
            (1.0 - value_mix) * grad_mixed,
        ],
        axis=1,
    ).astype(jnp.bfloat16)
    send_values = (value_mix * grad_mixed).astype(jnp.bfloat16)
    grad_wqkv = inner_rows(grad_projected, normed_all).reshape(w_qkv.shape)
    grad_normed = collect(
        jnp.dot(
            grad_projected,
            w_qkv.reshape(3 * head_width, model_width),
            preferred_element_type=jnp.float32,
        )
    )
    grad_gain1, grad_whole = norm_back(
        whole_rows, scale_first, gain_first, grad_normed, grad_hidden
    )
    return (
        grad_whole,
        send_values,
        (grad_gain1, grad_wqkv, grad_wo, grad_gain2, grad_wgu, grad_wd),
    )


def general_body(inputs, cotangent, lengths, gain1, wqkv, wo, gain2, wgu, wd):
    section_index = lax.axis_index("section")
    leading = section_index == 0
    value_mix = jnp.where(leading, 0.0, 0.5).astype(jnp.float32)
    micro_count = inputs.shape[0]
    local_rows = inputs.shape[1]
    model_width = inputs.shape[2]
    head_width = wqkv.shape[2] * HD
    row_count = local_rows * lax.axis_size("tp")
    gateup_use, down_use = (wgu[0], wd[0])
    weights = (gain1[0], wqkv[0], wo[0], gain2[0], gateup_use, down_use)
    recv_rows = jnp.zeros((local_rows, model_width), jnp.bfloat16)
    recv_values = jnp.zeros((row_count, head_width), jnp.bfloat16)
    states = []
    outputs = []
    for turn_index in range(micro_count + 1):
        own_rows = inputs[min(turn_index, micro_count - 1)]
        row_block = jnp.where(leading, own_rows, recv_rows)
        seq_lengths = jnp.where(
            leading, lengths[min(turn_index, micro_count - 1)], lengths[max(turn_index - 1, 0)]
        )
        layer_out, mixed, pairs_all, unused = layer_forward(
            row_block, recv_values, value_mix, weights, seq_lengths
        )
        kept_pairs = None
        states.append((row_block, recv_values, seq_lengths, kept_pairs))
        outputs.append(layer_out)
        if turn_index < micro_count:
            recv_rows, recv_values = shifted((layer_out, mixed), "section", 1)
    grad_rows_in = jnp.zeros((local_rows, model_width), jnp.bfloat16)
    grad_values_in = jnp.zeros((row_count, head_width), jnp.bfloat16)
    totals = None
    turn_grads = []
    for turn_index in range(micro_count + 1):
        row_block, first_values, seq_lengths, kept_pairs = states[micro_count - turn_index]
        if turn_index < micro_count:
            fed_grad = cotangent[micro_count - 1 - turn_index]
        else:
            fed_grad = jnp.zeros_like(cotangent[0])
        grad_out = jnp.where(leading, grad_rows_in, fed_grad)
        unused_out, unused_mixed, unused_pairs, saved = layer_forward(
            row_block, first_values, value_mix, weights, seq_lengths
        )
        grad_whole, send_values, grads = layer_backward(
            grad_out, grad_values_in, value_mix, weights, saved
        )
        totals = grads if totals is None else jax.tree.map(jnp.add, totals, grads)
        sent_rows = grad_whole.astype(jnp.bfloat16)
        turn_grads.append(jnp.where(leading, grad_whole, sent_rows.astype(jnp.float32)))
        if turn_index < micro_count:
            grad_rows_in, grad_values_in = shifted((sent_rows, send_values), "section", -1)
    grad_gain1, grad_wqkv, grad_wo, grad_gain2, grad_wgu, grad_wd = totals
    grad_wqkv, grad_wo, grad_wgu, grad_wd = (
        lax.psum(grad_wqkv.astype(jnp.bfloat16), "ctx").astype(jnp.float32),
        lax.psum(grad_wo.astype(jnp.bfloat16), "ctx").astype(jnp.float32),
        lax.psum(grad_wgu.astype(jnp.bfloat16), "ctx").astype(jnp.float32),
        lax.psum(grad_wd.astype(jnp.bfloat16), "ctx").astype(jnp.float32),
    )
    grad_gain1, grad_gain2 = lax.psum((grad_gain1, grad_gain2), ("ctx", "tp"))
    acts = jnp.stack(
        [
            jnp.where(leading, outputs[batch_index], outputs[batch_index + 1])
            for batch_index in range(micro_count)
        ]
    )[None]
    input_grads = jnp.stack(
        [
            jnp.where(
                leading,
                turn_grads[micro_count - batch_index],
                turn_grads[micro_count - 1 - batch_index],
            )
            for batch_index in range(micro_count)
        ]
    )[None]
    return (
        acts,
        input_grads,
        grad_gain1[None],
        grad_wqkv[None],
        grad_wo[None],
        grad_gain2[None],
        grad_wgu[None],
        grad_wd[None],
    )


def device_groups(mesh_sizes, key, order):
    sections, contexts, parts = mesh_sizes
    groups = {}
    for section in range(sections):
        for ctx in range(contexts):
            for tp in range(parts):
                place = (section, ctx, tp)
                number = (section * contexts + ctx) * parts + tp
                groups.setdefault(key(*place), []).append((order(*place), number))
    return [[number for _, number in sorted(members)] for _, members in sorted(groups.items())]


def exchange(value, groups):
    return lax.all_to_all(
        value, ALL_AXES, split_axis=0, concat_axis=0, tiled=True, axis_index_groups=groups
    )


def document_bounds(ends_ref, index):
    start = jnp.zeros_like(index)
    for entry in range(ends_ref.shape[0]):
        end = ends_ref[entry]
        start = jnp.where(index >= end, end, start)
    return start


def scalar_start(ends_ref, index):
    start = jnp.int32(0)
    for entry in range(ends_ref.shape[0]):
        start = jnp.where(index >= ends_ref[entry], ends_ref[entry], start)
    return start


def scalar_end(ends_ref, index):
    end = ends_ref[ends_ref.shape[0] - 1]
    for entry in range(ends_ref.shape[0] - 2, -1, -1):
        end = jnp.where(index < ends_ref[entry], ends_ref[entry], end)
    return end


def dot(left, right, left_dim, right_dim):
    return lax.dot_general(
        left, right, (((left_dim,), (right_dim,)), ((), ())), preferred_element_type=jnp.float32
    )


def fold_rows(value, combine):
    rows, width = value.shape
    return combine(value.reshape(rows // 8, 8, width), axis=0)


def block_place(block, parts, width):
    entry = (block // (2 * parts)) * parts + block % parts
    return entry, pl.ds(pl.multiple_of((block // parts % 2) * width, width), width)


def attention_forward_kernel(parts, ends_ref, qkv_ref, out_ref, lse_ref, keys_ref, values_ref):
    program = pl.program_id(0)
    blocks, block_width = 2 * qkv_ref.shape[0], qkv_ref.shape[2] // 2
    width = CHUNK * block_width

    @pl.when(program == 0)
    def _():
        def turn(j, carry):
            entry, columns = block_place(j, parts, block_width)
            keys_ref[j] = qkv_ref[entry, HD : 2 * HD, columns].T
            values_ref[j, 0:HD, :] = qkv_ref[entry, 2 * HD : 3 * HD, columns]
            values_ref[j, HD : HD + ONES, :] = jnp.ones((ONES, block_width), jnp.bfloat16)
            return carry

        lax.fori_loop(0, blocks, turn, 0)

    query = []
    for block in range(CHUNK):
        entry, columns = block_place(program * CHUNK + block, parts, block_width)
        query.append(qkv_ref[entry, 0:HD, columns])
    query = jnp.concatenate(query, axis=1)
    first = program * width
    query_index = first + lax.broadcasted_iota(jnp.int32, (1, width), 1)
    start = document_bounds(ends_ref, query_index)
    low_chunk = scalar_start(ends_ref, first) // width
    high_start = scalar_start(ends_ref, first + width - 1)
    middle = jnp.clip((high_start + width - 1) // width, low_chunk, program)

    def step(chunk, carry, masked):
        top, acc = carry
        parts = []
        for entry in range(CHUNK):
            j = chunk * CHUNK + entry
            scores = dot(keys_ref[j], query, 1, 0)
            if masked:
                key_index = j * block_width + lax.broadcasted_iota(jnp.int32, (block_width, 1), 0)
                allowed = (key_index >= start) & (key_index <= query_index)
                scores = jnp.where(allowed, scores, MASKED)
            parts.append(scores)
        part_top = functools.reduce(jnp.maximum, [fold_rows(part, jnp.max) for part in parts])
        new_top = jnp.maximum(top, jnp.max(part_top, axis=0, keepdims=True))
        acc = acc * jnp.exp2(top - new_top)
        for entry in range(CHUNK):
            weights = jnp.exp2(parts[entry] - new_top).astype(jnp.bfloat16)
            acc = acc + dot(values_ref[chunk * CHUNK + entry], weights, 1, 0)
        return new_top, acc

    def on_diagonal(carry):
        top, acc = carry
        parts_of, tops = [], []
        for block in range(CHUNK):
            columns = slice(block * block_width, width)
            j = program * CHUNK + block
            scores = dot(keys_ref[j], query[:, columns], 1, 0)
            key_index = j * block_width + lax.broadcasted_iota(jnp.int32, (block_width, 1), 0)
            allowed = (key_index >= start[:, columns]) & (key_index <= query_index[:, columns])
            scores = jnp.where(allowed, scores, MASKED)
            parts_of.append(scores)
            part_top = fold_rows(scores, jnp.max)
            if block > 0:
                before = jnp.full((8, block * block_width), MASKED, jnp.float32)
                part_top = jnp.concatenate([before, part_top], axis=1)
            tops.append(part_top)
        chunk_top = jnp.max(functools.reduce(jnp.maximum, tops), axis=0, keepdims=True)
        new_top = jnp.maximum(top, chunk_top)
        acc = acc * jnp.exp2(top - new_top)
        for block, scores in enumerate(parts_of):
            weights = jnp.exp2(scores - new_top[:, block * block_width :]).astype(jnp.bfloat16)
            added = dot(values_ref[program * CHUNK + block], weights, 1, 0)
            if block > 0:
                before = jnp.zeros((HD + ONES, block * block_width), jnp.float32)
                added = jnp.concatenate([before, added], axis=1)
            acc = acc + added
        return new_top, acc

    carry = (
        jnp.full((1, width), MASKED, jnp.float32),
        jnp.zeros((HD + ONES, width), jnp.float32),
    )
    carry = lax.fori_loop(low_chunk, middle, functools.partial(step, masked=True), carry)
    carry = lax.fori_loop(middle, program, functools.partial(step, masked=False), carry)
    top, acc = on_diagonal(carry)
    total = acc[HD : HD + 1]
    out = (acc[:HD] / total).astype(jnp.bfloat16)
    lse = top + jnp.log2(total)
    for entry in range(CHUNK):
        columns = slice(entry * block_width, (entry + 1) * block_width)
        out_ref[entry] = out[:, columns]
        lse_ref[entry] = lse[:, columns]


def attention_forward(ends, qkv, parts):
    blocks, width = 2 * qkv.shape[0], qkv.shape[2] // 2
    return pl.pallas_call(
        functools.partial(attention_forward_kernel, parts),
        grid_spec=pltpu.PrefetchScalarGridSpec(
            num_scalar_prefetch=1,
            grid=(blocks // CHUNK,),
            in_specs=[pl.BlockSpec(qkv.shape, lambda i, ends_ref: (0, 0, 0))],
            out_specs=[
                pl.BlockSpec((CHUNK, HD, width), lambda i, ends_ref: (i, 0, 0)),
                pl.BlockSpec((CHUNK, 1, width), lambda i, ends_ref: (i, 0, 0)),
            ],
            scratch_shapes=[
                pltpu.VMEM((blocks, width, HD), jnp.bfloat16),
                pltpu.VMEM((blocks, HD + ONES, width), jnp.bfloat16),
            ],
        ),
        out_shape=[
            jax.ShapeDtypeStruct((blocks, HD, width), jnp.bfloat16),
            jax.ShapeDtypeStruct((blocks, 1, width), jnp.float32),
        ],
        compiler_params=pltpu.CompilerParams(vmem_limit_bytes=VMEM_LIMIT),
        cost_estimate=LIGHT,
        name="attention_forward",
    )(ends, qkv)


def attention_backward_kernel(
    parts, ends_ref, qkv_ref, out_ref, grad_ref, lse_ref, result_ref,
    query_grad_ref, delta_ref, queries_ref, grads_ref, lses_ref,
):
    program = pl.program_id(0)
    blocks, block_width = 2 * qkv_ref.shape[0], qkv_ref.shape[2] // 2
    width = CHUNK * block_width

    @pl.when(program == 0)
    def _():
        def turn(i, carry):
            for entry in range(CHUNK):
                block = i * CHUNK + entry
                columns = slice(entry * block_width, (entry + 1) * block_width)
                grad = grad_ref[block]
                place, tokens = block_place(block, parts, block_width)
                queries_ref[i, :, columns] = qkv_ref[place, 0:HD, tokens]
                grads_ref[i, :, columns] = grad
                lses_ref[i, :, columns] = lse_ref[block]
                delta_ref[i, :, columns] = jnp.sum(
                    grad.astype(jnp.float32) * out_ref[block].astype(jnp.float32),
                    axis=0,
                    keepdims=True,
                )
            query_grad_ref[i] = jnp.zeros((HD, width), jnp.float32)
            return carry

        lax.fori_loop(0, blocks // CHUNK, turn, 0)

    own_places = [
        block_place(program * CHUNK + block, parts, block_width) for block in range(CHUNK)
    ]

    def joined(low_row, high_row):
        return jnp.concatenate(
            [qkv_ref[place, low_row:high_row, tokens] for place, tokens in own_places], axis=1
        )

    first = program * width
    keys_t = joined(HD, 2 * HD)
    keys = keys_t.T
    values = joined(2 * HD, 3 * HD).T
    key_index = first + lax.broadcasted_iota(jnp.int32, (width, 1), 0)
    near_end = scalar_end(ends_ref, first)
    far_end = scalar_end(ends_ref, first + width - 1)
    stop = (far_end - 1) // width + 1
    middle = jnp.clip(near_end // width, program + 1, stop)

    def step(i, carry, masked):
        key_grad, value_grad = carry
        query = queries_ref[i]
        grad = grads_ref[i]
        weights = jnp.exp2(dot(keys, query, 1, 0) - lses_ref[i])
        if masked:
            query_index = i * width + lax.broadcasted_iota(jnp.int32, (1, width), 1)
            start = document_bounds(ends_ref, query_index)
            allowed = (key_index >= start) & (key_index <= query_index)
            weights = jnp.where(allowed, weights, 0.0)
        grad_weights = dot(values, grad, 1, 0)
        grad_scores = (weights * (grad_weights - delta_ref[i])).astype(jnp.bfloat16)
        query_grad_ref[i] += dot(keys_t, grad_scores, 1, 0)
        value_grad = value_grad + dot(grad, weights.astype(jnp.bfloat16), 1, 1)
        key_grad = key_grad + dot(query, grad_scores, 1, 1)
        return key_grad, value_grad

    key_grad = jnp.zeros((HD, width), jnp.float32)
    value_grad = jnp.zeros((HD, width), jnp.float32)
    own_query_grads = []
    for block in range(CHUNK):
        columns = slice(block * block_width, (block + 1) * block_width)
        height = (block + 1) * block_width
        query = queries_ref[program, :, columns]
        grad = grads_ref[program, :, columns]
        query_index = (
            first + block * block_width + lax.broadcasted_iota(jnp.int32, (1, block_width), 1)
        )
        start = document_bounds(ends_ref, query_index)
        rows_index = key_index[:height]
        allowed = (rows_index >= start) & (rows_index <= query_index)
        scores = dot(keys[:height], query, 1, 0)
        weights = jnp.where(allowed, jnp.exp2(scores - lses_ref[program, :, columns]), 0.0)
        grad_weights = dot(values[:height], grad, 1, 0)
        grad_scores = (weights * (grad_weights - delta_ref[program, :, columns])).astype(
            jnp.bfloat16
        )
        own_query_grads.append(dot(keys_t[:, :height], grad_scores, 1, 0))
        added = (
            dot(query, grad_scores, 1, 1),
            dot(grad, weights.astype(jnp.bfloat16), 1, 1),
        )
        if height < width:
            behind = jnp.zeros((HD, width - height), jnp.float32)
            added = [jnp.concatenate([value, behind], axis=1) for value in added]
        key_grad = key_grad + added[0]
        value_grad = value_grad + added[1]
    query_grad_ref[program] += jnp.concatenate(own_query_grads, axis=1)
    carry = (key_grad, value_grad)
    carry = lax.fori_loop(program + 1, middle, functools.partial(step, masked=False), carry)
    key_grad, value_grad = lax.fori_loop(middle, stop, functools.partial(step, masked=True), carry)
    query_grad = query_grad_ref[program] * HD ** (-0.5)
    key_grad = key_grad * LOG_2
    for block, (place, tokens) in enumerate(own_places):
        columns = slice(block * block_width, (block + 1) * block_width)
        result_ref[place, 0:HD, tokens] = query_grad[:, columns].astype(jnp.bfloat16)
        result_ref[place, HD : 2 * HD, tokens] = key_grad[:, columns].astype(jnp.bfloat16)
        result_ref[place, 2 * HD : 3 * HD, tokens] = value_grad[:, columns].astype(jnp.bfloat16)


def attention_backward(ends, qkv, out, grad, lse, parts):
    blocks, block_width = 2 * qkv.shape[0], qkv.shape[2] // 2
    chunks, width = blocks // CHUNK, CHUNK * block_width

    def whole(value):
        return pl.BlockSpec(value.shape, lambda i, ends_ref: (0, 0, 0))

    return pl.pallas_call(
        functools.partial(attention_backward_kernel, parts),
        grid_spec=pltpu.PrefetchScalarGridSpec(
            num_scalar_prefetch=1,
            grid=(chunks,),
            in_specs=[whole(qkv), whole(out), whole(grad), whole(lse)],
            out_specs=whole(qkv),
            scratch_shapes=[
                pltpu.VMEM((chunks, HD, width), jnp.float32),
                pltpu.VMEM((chunks, 1, width), jnp.float32),
                pltpu.VMEM((chunks, HD, width), jnp.bfloat16),
                pltpu.VMEM((chunks, HD, width), jnp.bfloat16),
                pltpu.VMEM((chunks, 1, width), jnp.float32),
            ],
        ),
        out_shape=jax.ShapeDtypeStruct(qkv.shape, jnp.bfloat16),
        compiler_params=pltpu.CompilerParams(vmem_limit_bytes=VMEM_LIMIT),
        cost_estimate=LIGHT,
        name="attention_backward",
    )(ends, qkv, out, grad, lse)


def rope_pair(leading_half, trailing_half, cosine, sine_part):
    return (
        leading_half * cosine - trailing_half * sine_part,
        trailing_half * cosine + leading_half * sine_part,
    )


def low(value):
    return value.astype(jnp.bfloat16)


def wide(value):
    return value.astype(jnp.float32)


def whole_block(value):
    zeros = (0,) * value.ndim
    return pl.BlockSpec(value.shape, lambda *_: zeros)


def feed_forward_kernel(rows_ref, gate_w_ref, up_w_ref, down_w_ref, gate_ref, up_ref, act_ref, sum_ref):
    rows = rows_ref[...]
    gate = dot(gate_w_ref[...], rows, 1, 1)
    up = dot(up_w_ref[...], rows, 1, 1)
    active = (gate * jax.nn.sigmoid(gate) * up).astype(jnp.bfloat16)
    gate_ref[...] = gate.astype(jnp.bfloat16)
    up_ref[...] = up.astype(jnp.bfloat16)
    act_ref[...] = active

    @pl.when(pl.program_id(0) == 0)
    def _():
        sum_ref[...] = jnp.zeros_like(sum_ref)

    sum_ref[...] += dot(active, down_w_ref[...], 0, 0)


def feed_forward(rows, w_gate, w_up, w_down, tile):
    units, width = w_gate.shape
    count = rows.shape[0]
    weight = pl.BlockSpec((tile, width), lambda i: (i, 0))
    column = pl.BlockSpec((tile, count), lambda i: (i, 0))
    hidden = jax.ShapeDtypeStruct((units, count), jnp.bfloat16)
    return pl.pallas_call(
        feed_forward_kernel,
        grid=(units // tile,),
        in_specs=[whole_block(rows), weight, weight, weight],
        out_specs=[column, column, column, pl.BlockSpec((count, width), lambda i: (0, 0))],
        out_shape=[hidden, hidden, hidden, jax.ShapeDtypeStruct((count, width), jnp.float32)],
        compiler_params=pltpu.CompilerParams(vmem_limit_bytes=VMEM_LIMIT),
        cost_estimate=LIGHT,
        name="feed_forward",
    )(rows, w_gate, w_up, w_down)


def feed_forward_back_kernel(
    grad_ref, gate_ref, up_ref, gate_w_ref, up_w_ref, down_w_ref, grad_gate_ref, grad_up_ref, sum_ref
):
    grad_act = dot(down_w_ref[...], grad_ref[...], 1, 1)
    gate = gate_ref[...].astype(jnp.float32)
    up = up_ref[...].astype(jnp.float32)
    sigmoid_gate = jax.nn.sigmoid(gate)
    grad_gate = (grad_act * up * sigmoid_gate * (1.0 + gate * (1.0 - sigmoid_gate))).astype(
        jnp.bfloat16
    )
    grad_up = (grad_act * gate * sigmoid_gate).astype(jnp.bfloat16)
    grad_gate_ref[...] = grad_gate
    grad_up_ref[...] = grad_up

    @pl.when(pl.program_id(0) == 0)
    def _():
        sum_ref[...] = jnp.zeros_like(sum_ref)

    sum_ref[...] += dot(grad_gate, gate_w_ref[...], 0, 0) + dot(grad_up, up_w_ref[...], 0, 0)


def feed_forward_back(grad, gate, up, w_gate, w_up, w_down, tile):
    units, width = w_gate.shape
    count = grad.shape[0]
    weight = pl.BlockSpec((tile, width), lambda i: (i, 0))
    column = pl.BlockSpec((tile, count), lambda i: (i, 0))
    hidden = jax.ShapeDtypeStruct((units, count), jnp.bfloat16)
    return pl.pallas_call(
        feed_forward_back_kernel,
        grid=(units // tile,),
        in_specs=[whole_block(grad), column, column, weight, weight, weight],
        out_specs=[column, column, pl.BlockSpec((count, width), lambda i: (0, 0))],
        out_shape=[hidden, hidden, jax.ShapeDtypeStruct((count, width), jnp.float32)],
        compiler_params=pltpu.CompilerParams(vmem_limit_bytes=VMEM_LIMIT),
        cost_estimate=LIGHT,
        name="feed_forward_back",
    )(grad, gate, up, w_gate, w_up, w_down)


def half_products_kernel(layout, sizes, has_addend, which_ref, *refs):
    refs = list(refs)
    out_ref = refs.pop()
    addend_ref = refs.pop() if has_addend else None
    totals = [
        sum(dot(refs[left][...], refs[right][...], 1, 0) for left, right in pairs)
        for pairs in layout
    ]
    for piece in range(out_ref.shape[0]):
        parts = [
            total[piece * size : (piece + 1) * size] for total, size in zip(totals, sizes)
        ]
        value = jnp.concatenate(parts, axis=0) if len(parts) > 1 else parts[0]
        if has_addend:
            value = value + addend_ref[piece].astype(jnp.float32)
        out_ref[piece] = value.astype(jnp.bfloat16)


def half_products(which, groups, pieces, per_step, addend=None):
    lefts, rights, layout = [], [], []
    for group in groups:
        for left, right in group:
            if not any(left is known for known in lefts):
                lefts.append(left)
            if not any(right is known for known in rights):
                rights.append(right)
    find = lambda known, value: next(i for i, entry in enumerate(known) if entry is value)
    for group in groups:
        layout.append(
            tuple((find(lefts, left), len(lefts) + find(rights, right)) for left, right in group)
        )
    sizes = tuple(group[0][0].shape[0] // (2 * pieces) for group in groups)
    width = rights[0].shape[1]
    steps = pieces // per_step
    out_spec = pl.BlockSpec((per_step, sum(sizes), width), lambda i, which_ref: (i, 0, 0))
    left_specs = [
        pl.BlockSpec(
            (left.shape[0] // (2 * steps), left.shape[1]),
            lambda i, which_ref: (which_ref[0] * steps + i, 0),
        )
        for left in lefts
    ]
    extra = [] if addend is None else [addend]
    work = sum(left.size // 2 for left, _ in sum(groups, ()))
    return pl.pallas_call(
        functools.partial(half_products_kernel, tuple(layout), sizes, addend is not None),
        grid_spec=pltpu.PrefetchScalarGridSpec(
            num_scalar_prefetch=1,
            grid=(steps,),
            in_specs=left_specs + [whole_block(right) for right in rights] + [out_spec] * len(extra),
            out_specs=out_spec,
        ),
        out_shape=jax.ShapeDtypeStruct((pieces, sum(sizes), width), jnp.bfloat16),
        compiler_params=pltpu.CompilerParams(vmem_limit_bytes=VMEM_LIMIT),
        cost_estimate=LIGHT,
        name="half_products",
    )(which.reshape(1).astype(jnp.int32), *lefts, *rights, *extra)


def together(*values):
    return lax.optimization_barrier(values)


def after(value, *others):
    return lax.optimization_barrier((value, *others))[0]


def split_body(mesh_sizes, inputs, cotangent, lengths, gain1, wqkv, wo, gain2, wgu, wd):
    sections, contexts, parts = mesh_sizes
    half_parts = parts // 2
    section = lax.axis_index("section")
    ctx = lax.axis_index("ctx")
    tp = lax.axis_index("tp")
    row_side, column_side = ctx // 2, ctx % 2
    leading = section == 0
    batch = tp // half_parts
    model_width = inputs.shape[2]
    rows = inputs.shape[1]
    heads = wqkv.shape[2] * parts
    side_heads = heads // 2
    unit_rows = wd.shape[1] // contexts // 2
    head_rows = 3 * HD // 2
    out_rows = HD // 2
    half_width = HD // 2
    tile = 8 * unit_rows
    number = lambda s, c, t: (s * contexts + c) * parts + t
    places = [
        (s, c, t) for s in range(sections) for c in range(contexts) for t in range(parts)
    ]
    everyone = [[number(*place) for place in places]]
    token_of = lambda s, c, t: c * parts + t % half_parts + half_parts * s
    batch_groups = device_groups(mesh_sizes, lambda s, c, t: t // half_parts, token_of)
    head_groups = device_groups(
        mesh_sizes,
        lambda s, c, t: (c % 2, t // half_parts),
        lambda s, c, t: (c // 2, t % half_parts + half_parts * s),
    )
    side_groups = device_groups(mesh_sizes, lambda s, c, t: c % 2, lambda s, c, t: (s, c, t))
    crossing = [
        (number(s, c, t), number(s, c, (t + half_parts) % parts))
        for s, c, t in places
        if t // half_parts == s
    ]

    def to_batch(value):
        mine = lax.dynamic_index_in_dim(value, batch, 0, keepdims=False)
        other = lax.dynamic_index_in_dim(value, 1 - batch, 0, keepdims=False)
        moved = lax.ppermute(other, ALL_AXES, crossing)
        return jnp.where(section == batch, mine, moved)

    def to_home(value, layer):
        stay = [
            (number(s, c, t), number(layer, c, t)) for s, c, t in places if t // half_parts == s
        ]
        cross = [
            (number(s, c, t), number(layer, c, (t + half_parts) % parts))
            for s, c, t in places
            if t // half_parts != s
        ]
        return (lax.ppermute(value, ALL_AXES, stay), lax.ppermute(value, ALL_AXES, cross))

    def at_home(first_pair, second_pair):
        near = jnp.where(leading, first_pair[0], second_pair[0])
        far = jnp.where(leading, first_pair[1], second_pair[1])
        upper = batch == 0
        return jnp.stack([jnp.where(upper, near, far), jnp.where(upper, far, near)])[None]

    def swap_side(value):
        return lax.ppermute(value, "ctx", [(c, c ^ 1) for c in range(contexts)])

    def swap_far(value):
        return lax.ppermute(value, "ctx", [(c, c ^ 2) for c in range(contexts)])

    def swap_near(value):
        return lax.ppermute(value, "tp", [(t, t ^ 1) for t in range(parts)])

    def swap_half(value):
        return lax.ppermute(value, "tp", [(t, (t + half_parts) % parts) for t in range(parts)])

    def swap_section(value):
        return lax.ppermute(value, "section", [(0, 1), (1, 0)])

    def all_to_all(value, axis):
        return lax.all_to_all(value, axis, split_axis=0, concat_axis=0, tiled=True)

    def copies(value, count):
        return jnp.broadcast_to(value[None], (count, *value.shape))

    def gather(value, groups):
        return lax.all_gather(value, ALL_AXES, axis=0, tiled=True, axis_index_groups=groups)

    def ordered(index, own, other):
        return jnp.where(index == 0, own, other), jnp.where(index == 0, other, own)

    def by_core(value, which):
        return lax.dynamic_index_in_dim(value, which, 0, keepdims=False)

    def spread_half(piece):
        return piece, swap_half(piece)

    def spread_near(pieces_pair):
        pair = jnp.stack(ordered(batch, *pieces_pair))
        return pair, swap_near(pair)

    def spread_line(pairs):
        line = jnp.stack(ordered(tp % 2, *pairs), axis=1)
        return line.reshape(parts, *line.shape[2:])

    def spread_far(line):
        return line, swap_far(line)

    def spread_heads(pair):
        pair = jnp.stack(ordered(row_side, *pair))
        own_heads = pair[:, :, :head_rows].reshape(-1, model_width)
        own_outs = pair[:, :, head_rows:]
        return (own_heads, swap_section(own_heads)), (own_outs, swap_side(own_outs))

    def spread_outs(pair):
        own_outs = jnp.stack(ordered(column_side, *pair), axis=1).reshape(-1, model_width)
        return own_outs, swap_section(own_outs)

    def join_outs(pair):
        return jnp.concatenate(ordered(section, *pair), axis=0)

    def own_halves(value, axis, size):
        part = lax.dynamic_slice_in_dim(value, ctx * size, size, axis)
        return part.reshape(2, -1, model_width)

    packed = jnp.concatenate(
        [
            own_halves(wqkv[0], 1, heads // (parts * contexts)),
            own_halves(wo[0], 0, HD),
            own_halves(wgu[0, 0], 0, 2 * unit_rows),
            own_halves(wgu[0, 1], 0, 2 * unit_rows),
            own_halves(wd[0], 0, 2 * unit_rows),
        ],
        axis=1,
    )
    kept = by_core(packed, section)
    passed = swap_section(by_core(packed, 1 - section))
    pieces = ordered(section, kept, passed)
    attention_rows = head_rows + out_rows

    def feed_forward_weights(piece):
        whole = gather(piece[attention_rows:], side_groups)
        whole = whole.reshape(2 * 2 * parts, 3, unit_rows, model_width)
        return [whole[:, entry].reshape(-1, model_width) for entry in range(3)]

    rows_in = to_batch(inputs)
    line = spread_near(spread_half(pieces[0][:attention_rows]))
    line, rows_in = together(spread_line(line), rows_in)
    w_ffn = [feed_forward_weights(after(pieces[0], line)), None]
    w_heads, w_outs = [None, None], [None, None]
    first_pair = spread_far(line)

    gains = wide(jnp.concatenate([gain1, gain2], axis=0))
    gain_sets = ordered(section, gains, swap_section(gains))

    seq_lengths = lax.dynamic_index_in_dim(lengths, batch, 0, keepdims=False)
    ends = jnp.cumsum(seq_lengths).astype(jnp.int32)
    token_index = jnp.concatenate(
        [
            token_of(section, 2 * row_side + side, tp) * rows + jnp.arange(rows, dtype=jnp.int32)
            for side in range(2)
        ]
    )
    before = (ends[None, :] <= token_index[:, None]).astype(jnp.int32)
    position = token_index - jnp.sum(before * seq_lengths[None, :], axis=1)
    frequency = jnp.exp(
        -jnp.log(10000.0) * jnp.arange(half_width, dtype=jnp.float32) / half_width
    )
    angles = position.astype(jnp.float32)[None, :] * frequency[:, None]
    cosine, sine_part = jnp.cos(angles), jnp.sin(angles)

    def head_halves(value):
        size = value.shape[1] // 2
        return value.reshape(heads, 2, size, rows).transpose(1, 0, 2, 3).reshape(2, -1, rows)

    def whole_heads(value):
        value = value.reshape(2, heads, -1, rows)
        return value.transpose(1, 0, 2, 3).reshape(heads, -1, rows)

    def nothing(value):
        return value

    def layer_forward(whole_rows, first_values, layer, in_zero, in_first, in_second, in_middle, in_third, in_fourth):
        gain_first, gain_second = gain_sets[layer][0], gain_sets[layer][1]
        scale_first = lax.rsqrt(jnp.mean(whole_rows * whole_rows, axis=-1, keepdims=True) + EPSILON)
        normed = low(whole_rows * scale_first * gain_first)
        far_normed = in_zero(swap_side(normed))
        side_rows = jnp.concatenate(ordered(column_side, normed, far_normed), axis=0)
        halves = ordered(section, *[dot(weight, side_rows, 1, 1) for weight in w_heads[layer]])
        upper, lower = [half.reshape(side_heads, head_rows, 2 * rows) for half in halves]
        query = rope_pair(upper[:, :half_width], upper[:, half_width:HD], cosine, sine_part)
        key = rope_pair(upper[:, HD:], lower[:, :half_width], cosine, sine_part)
        value = lower[:, half_width:]
        if first_values is not None:
            value = 0.5 * value + 0.5 * wide(first_values)
        mixed = low(value)
        shrunk = [low(half * (HD ** (-0.5) / LOG_2)) for half in query]
        qkv = exchange(
            jnp.concatenate([*shrunk, low(key[0]), low(key[1]), mixed], axis=1), head_groups
        )
        qkv = in_first(qkv)
        out, lse = attention_forward(ends, qkv, parts)
        out = in_second(out)
        attended = head_halves(in_middle(exchange(out, batch_groups)))
        hidden = whole_rows + dot(attended.reshape(-1, rows), w_outs[layer], 0, 0)
        scale_second = lax.rsqrt(jnp.mean(hidden * hidden, axis=-1, keepdims=True) + EPSILON)
        normed_second = low(hidden * scale_second * gain_second)
        far_rows = swap_side(normed_second)
        near = feed_forward(normed_second, *w_ffn[layer], tile)
        far_rows = in_third(after(far_rows, near[3]))
        far = feed_forward(far_rows, *w_ffn[layer], tile)
        sent_down = low(far[3])

        def layer_out(*others):
            far_down = in_fourth(swap_side(after(sent_down, *others)))
            return low(hidden + (near[3] + wide(far_down)))

        saved = (
            whole_rows, scale_first, side_rows, qkv, out, lse, attended, hidden, scale_second,
            (normed_second, far_rows), near[:3], far[:3],
        )
        return layer_out, mixed, saved

    def norm_back(whole_rows, scale_rows, gain, grad_normed, grad_rest):
        unit = whole_rows * scale_rows
        scaled = grad_normed * gain
        grad_gain = jnp.sum(grad_normed * unit, axis=0)
        grad_whole = grad_rest + scale_rows * (
            scaled - unit * jnp.mean(scaled * unit, axis=-1, keepdims=True)
        )
        return grad_gain, grad_whole

    def pick(value, index, axis):
        return lax.dynamic_index_in_dim(value, index, axis, keepdims=False)

    def parted(value, index, axis):
        return pick(value, index, axis), pick(value, 1 - index, axis)

    def moved_pair(pair, swap):
        return pair[0], swap(pair[1])

    def halve(value, index, swap, axis):
        return moved_pair(parted(value, index, axis), swap)

    def add(pair):
        return low(wide(pair[0]) + wide(pair[1]))

    def near_parts(value):
        return parted(value.reshape(2, half_parts, *value.shape[1:]), tp % 2, 1)

    def near_sum(value):
        return moved_pair(near_parts(value), swap_near)

    def far_sum(pair):
        return halve(add(pair), batch, swap_half, 0)

    def layer_backward(grad_rows, extra_values, saved, layer, in_first, in_second, in_third, in_fourth, in_fifth):
        (
            whole_rows, scale_first, _, qkv, out, lse, attended, hidden, scale_second,
            ffn_rows, near, far,
        ) = saved
        gain_first, gain_second = gain_sets[layer][0], gain_sets[layer][1]
        grad_down = low(grad_rows)
        far_down = swap_side(grad_down)
        grad_gate, grad_up, near_back = feed_forward_back(grad_down, *near[:2], *w_ffn[layer], tile)
        far_down = in_first(after(far_down, near_back))
        far_gate, far_up, far_back = feed_forward_back(far_down, *far[:2], *w_ffn[layer], tile)
        far_back = swap_side(low(far_back))
        groups = (
            ((grad_gate, ffn_rows[0]), (far_gate, ffn_rows[1])),
            ((grad_up, ffn_rows[0]), (far_up, ffn_rows[1])),
            ((near[2], grad_down), (far[2], far_down)),
        )
        products = functools.partial(
            half_products, groups=groups, pieces=2 * parts, per_step=2
        )
        sent = products(1 - section)
        moved = swap_section(sent)
        far_back = in_second(after(far_back, sent))
        grad_gain2, grad_hidden = norm_back(
            hidden, scale_second, gain_second, near_back + wide(far_back), wide(grad_rows)
        )
        grad_branch = low(grad_hidden)
        grad_heads = whole_heads(low(dot(w_outs[layer], grad_branch, 1, 1)))
        grad_heads = exchange(grad_heads, batch_groups)
        rest = products(section, addend=moved)
        out_pair = (attended.reshape(-1, rows), grad_branch)
        grad_heads, rest = in_third(grad_heads, rest, out_pair)
        grad_qkv = attention_backward(ends, qkv, out, grad_heads, lse, parts)
        grad_qkv = in_fourth(grad_qkv)
        grad_qkv = in_fifth(exchange(grad_qkv, head_groups))
        grad_qkv = wide(grad_qkv)
        quarter = lambda entry: grad_qkv[:, entry * half_width : (entry + 1) * half_width]
        grad_query = rope_pair(quarter(0), quarter(1), cosine, -sine_part)
        grad_key = rope_pair(quarter(2), quarter(3), cosine, -sine_part)
        grad_value = grad_qkv[:, 2 * HD :]
        send_values = None
        if extra_values is None:
            grad_value = 0.5 * grad_value
            send_values = low(grad_value)
        else:
            grad_value = grad_value + wide(extra_values)
        upper = low(jnp.concatenate([*grad_query, grad_key[0]], axis=1))
        lower = low(jnp.concatenate([grad_key[1], grad_value], axis=1))
        grad_halves = jnp.stack([upper, lower]).reshape(2, -1, 2 * rows)
        return grad_halves, send_values, grad_hidden, out_pair, grad_gain2

    def input_grads_of(grad_halves, grad_hidden, saved, layer, beside):
        whole_rows, scale_first = saved[:2]
        places_of = (section, 1 - section)
        grad_side = sum(
            dot(by_core(grad_halves, place), weight, 0, 0)
            for place, weight in zip(places_of, w_heads[layer])
        ).reshape(2, rows, model_width)
        grad_far = swap_side(low(by_core(grad_side, 1 - column_side)))
        grad_normed = by_core(grad_side, column_side) + wide(beside(grad_far))
        return norm_back(whole_rows, scale_first, gain_sets[layer][0], grad_normed, grad_hidden)

    def piece_sum(value, groups):
        return lax.psum_scatter(
            value, ALL_AXES, scatter_dimension=0, tiled=True, axis_index_groups=groups
        )

    line_groups = device_groups(
        mesh_sizes, lambda s, c, t: (s, c % 2), lambda s, c, t: (c, t)
    )
    plane_shape = (2, 2, parts)
    pending = {}

    def weights_zero(value):
        value, pair = together(value, first_pair)
        w_heads[0], pending["outs"] = spread_heads(pair)
        return value

    def weights_line(value):
        value, piece = together(value, pieces[1][:attention_rows])
        pending["weights"] = spread_half(piece)
        return value

    def weights_outs_first(value):
        value, pending["outs"], w_ffn[0], weights = together(
            value, pending["outs"], w_ffn[0], pending["weights"]
        )
        pending["weights"] = spread_near(weights)
        w_outs[0] = join_outs(spread_outs(pending["outs"]))
        return value

    def weights_far(value):
        value, line = together(value, pending["weights"])
        pending["weights"] = spread_far(spread_line(line))
        w_ffn[1] = feed_forward_weights(after(pieces[1], value))
        return value

    def weights_heads(value):
        value, pairs = together(value, pending["weights"])
        w_heads[1], pending["outs"] = spread_heads(pairs)
        return value

    first_result, first_values, first_saved = layer_forward(
        wide(rows_in), None, 0,
        weights_zero, weights_line, nothing, weights_outs_first, weights_far, weights_heads,
    )

    first_out = first_result()

    def start_outs(value):
        value, grads = together(value, cotangent)
        pending["grad_in"] = to_batch(grads)
        return value

    def end_outs(value):
        value, outs, w_ffn[1], pending["grad_in"] = together(
            value, pending["outs"], w_ffn[1], pending["grad_in"]
        )
        w_outs[1] = join_outs(spread_outs(outs))
        pending["first_home"] = to_home(after(first_out, value), 0)
        return value

    second_result, _, second_saved = layer_forward(
        wide(first_out), first_values, 1,
        nothing, start_outs, end_outs, nothing, nothing, nothing,
    )
    grad_in = pending["grad_in"]

    def out_sides(out_pair):
        products = functools.partial(half_products, groups=((out_pair,),), pieces=heads, per_step=8)
        out_sum = products(section, addend=swap_section(products(1 - section)))
        return parted(out_sum.reshape(*plane_shape, out_rows, model_width), column_side, 1)

    def second_third(value, rest, out_pair):
        value, rest = together(value, rest)
        rest = rest.reshape(-1, model_width)
        pending["second_rest"] = piece_sum(rest, line_groups)
        pending["second_out_rows"] = second_result(value)
        pending["out"] = out_sides(out_pair)
        value = after(value, pending["out"])
        pending["out"] = moved_pair(pending["out"], swap_side)
        return value, rest

    def second_fourth(value):
        value, pending["first_home"], second_out, out_sum = together(
            value, pending["first_home"], pending["second_out_rows"], pending["out"]
        )
        pending["second_home"] = to_home(second_out, 1)
        pending["second_out"] = add(out_sum).reshape(2 * parts, out_rows, model_width)
        return value

    grad_halves, send_values, grad_hidden, _, second_gain2 = layer_backward(
        grad_in, None, second_saved, 1, nothing, nothing, second_third, second_fourth, nothing
    )
    head_products = functools.partial(
        half_products,
        groups=(((grad_halves.reshape(-1, 2 * rows), second_saved[2]),),),
        pieces=side_heads,
        per_step=4,
    )

    def head_start(value):
        value, sent = together(value, head_products(1 - section))
        pending["moved"] = swap_section(sent)
        return value

    second_gain1, second_grad = input_grads_of(
        grad_halves, grad_hidden, second_saved, 1, head_start
    )
    second_grad = low(second_grad)

    def first_first(value):
        head = head_products(section, addend=pending["moved"])
        head = jnp.concatenate([head, pending["second_out"]], axis=1)
        head = parted(head.reshape(2, parts, -1, model_width), row_side, 0)
        value, head = together(value, head)
        pending["head"] = moved_pair(head, swap_far)
        return value

    def first_second(value):
        return value

    def first_third(value, rest, out_pair):
        out_sum = out_sides(out_pair)
        rest = rest.reshape(2, parts, -1, model_width)
        rest_a = parted(rest[:, :, : 2 * unit_rows], row_side, 0)
        rest_b = parted(rest[:, :, 2 * unit_rows :], row_side, 0)
        (
            value, rest_a, rest_b, out_sum, head, pending["second_rest"], pending["second_home"]
        ) = together(
            value, rest_a, rest_b, out_sum, pending["head"], pending["second_rest"],
            pending["second_home"],
        )
        pending["rest_a"] = moved_pair(rest_a, swap_far)
        pending["rest_b"] = rest_b
        pending["out"] = moved_pair(out_sum, swap_side)
        pending["head"] = near_sum(add(head))
        return value, rest

    def first_fourth(value):
        value, rest_a, rest_b, out_sum, head = together(
            value, pending["rest_a"], pending["rest_b"], pending["out"], pending["head"]
        )
        pending["head"] = far_sum(head)
        pending["second_rest"] = lax.all_gather(
            after(pending["second_rest"], value), "ctx", axis=0, tiled=False
        )
        pending["rest_b"] = moved_pair(rest_b, swap_far)
        pending["rest_a"] = near_sum(add(rest_a))
        pending["out"] = halve(add(out_sum), row_side, swap_far, 0)
        return value

    first_halves, _, first_hidden, _, first_gain2 = layer_backward(
        second_grad, send_values, first_saved, 0,
        first_first, first_second, first_third, first_fourth, nothing,
    )
    head_products = functools.partial(
        half_products,
        groups=(((first_halves.reshape(-1, 2 * rows), first_saved[2]),),),
        pieces=side_heads,
        per_step=4,
    )
    sent = head_products(1 - section)
    moved = swap_section(sent)
    def head_end(value):
        head = head_products(section, addend=moved).reshape(2, parts, head_rows, model_width)
        head = parted(head, row_side, 0)
        head, rest_a, rest_b, out_sum, second_head = together(
            head, pending["rest_a"], pending["rest_b"], pending["out"], pending["head"]
        )
        pending["head"] = moved_pair(head, swap_far)
        pending["rest_b"] = near_sum(add(rest_b))
        pending["rest_a"] = far_sum(rest_a)
        pending["out"] = add(out_sum)
        pending["second_head"] = add(second_head)
        return after(value, head)

    first_gain1, first_grad = input_grads_of(
        after(first_halves, sent), first_hidden, first_saved, 0, head_end
    )
    def summed(value, swap):
        return value + swap(value)

    gain_rows = jnp.stack([first_gain1, first_gain2, second_gain1, second_gain2])
    gain_rows = summed(gain_rows, swap_section)
    head, rest_a, rest_b, gain_rows, first_grad = together(
        pending["head"], pending["rest_a"], pending["rest_b"], gain_rows, low(first_grad)
    )
    head = near_sum(jnp.concatenate([add(head), pending["out"]], axis=1))
    rest_b = far_sum(rest_b)
    gain_rows = summed(summed(gain_rows, swap_side), swap_far)
    head, rest_b, gain_rows, first_grad, second_rest = together(
        head, rest_b, gain_rows, first_grad, pending["second_rest"]
    )
    head = far_sum(head)
    rest = jnp.concatenate([add(rest_a), add(rest_b)], axis=0)
    rest = lax.all_gather(rest, "ctx", axis=0, tiled=False)
    gain_rows = summed(gain_rows, swap_near)
    head, first_grad, home = together(head, first_grad, second_grad)
    first_grad_home = to_home(first_grad, 0)
    second_grad_home = to_home(home, 1)
    head = jnp.concatenate([add(head), pending["second_head"]], axis=0)
    head = all_to_all(copies(head, contexts), "ctx")
    head, gain_rows, first_grad_home, second_grad_home = together(
        head, gain_rows, first_grad_home, second_grad_home
    )
    gain_total = summed(gain_rows, swap_half)
    rest, head = together(rest, head)
    first_grads = (rest, head[:, :attention_rows])
    second_grads = (second_rest, head[:, attention_rows:])
    first_home, second_home = pending["first_home"], pending["second_home"]
    gain_total = jnp.where(leading, gain_total[:2], gain_total[2:])

    def finish(first, second):
        mine = jnp.where(leading, first, second)
        moved = swap_section(jnp.where(leading, second, first))
        return ordered(section, mine, moved)

    def joined(halves, first, count):
        both = jnp.stack([half[:, first : first + count] for half in halves], axis=1)
        return wide(both).reshape(-1, model_width)

    rest_grads = finish(first_grads[0], second_grads[0])
    grad_wgate, grad_wup, grad_wd = [
        joined(rest_grads, entry * unit_rows, unit_rows) for entry in range(3)
    ]
    head, grad_wgate, grad_wup, grad_wd = together(first_grads[1], grad_wgate, grad_wup, grad_wd)
    head_grads = finish(head, second_grads[1])
    grad_wqkv = joined(head_grads, 0, head_rows).reshape(contexts, 3, HD, model_width)
    grad_wo = joined(head_grads, head_rows, out_rows)
    return (
        at_home(first_home, second_home),
        wide(at_home(first_grad_home, second_grad_home)),
        gain_total[0:1],
        grad_wqkv.transpose(1, 0, 2, 3)[None],
        grad_wo[None],
        gain_total[1:2],
        jnp.stack([grad_wgate, grad_wup])[None],
        grad_wd[None],
    )


def body(mesh_sizes, *arguments):
    inputs, _, _, _, wqkv = arguments[:5]
    sections, contexts, parts = mesh_sizes
    own_heads, own_units = wqkv.shape[2], arguments[7].shape[2]
    fits = (
        sections == 2
        and inputs.shape[0] == 2
        and contexts == 4
        and parts % 2 == 0
        and own_heads == contexts
        and own_units % (16 * contexts) == 0
        and inputs.shape[1] % 128 == 0
    )
    if fits:
        return split_body(mesh_sizes, *arguments)
    return general_body(*arguments)


def solution(mesh):
    placed = (
        P(None, ("ctx", "tp"), None),
        P(None, ("ctx", "tp"), None),
        P(),
        P("section", None),
        P("section", None, "tp", None, None),
        P("section", "tp", None),
        P("section", None),
        P("section", None, "tp", None),
        P("section", "tp", None),
    )
    mesh_sizes = tuple(mesh.shape[axis] for axis in ALL_AXES)
    return jax.shard_map(
        functools.partial(body, mesh_sizes),
        mesh=mesh,
        in_specs=placed,
        out_specs=(
            P("section", None, ("ctx", "tp"), None),
            P("section", None, ("ctx", "tp"), None),
            P("section", None),
            P("section", None, "tp", None, None),
            P("section", "tp", None),
            P("section", None),
            P("section", None, "tp", None),
            P("section", "tp", None),
        ),
        check_vma=False,
    )
```

```python
import functools

import jax
import jax.numpy as jnp
from jax import lax
from jax.experimental import pallas as pl
from jax.experimental.pallas import tpu as pltpu
from jax.sharding import PartitionSpec as P

HD = 64
EPSILON = 1e-06
MASKED = -1e30
ALL_AXES = ("section", "ctx", "tp")
CHUNK = 2
ONES = 16
LOG_2 = 0.6931471805599453
LIGHT = pl.CostEstimate(flops=1, bytes_accessed=1, transcendentals=0)
VMEM_LIMIT = 40 * 1024 * 1024


def shifted(block, axis, distance):
    devices = range(lax.axis_size(axis))
    route = [(i - distance, i) for i in devices if i - distance in devices]
    return lax.ppermute(block, axis, route)


def rope_parts(position):
    half_width = HD // 2
    frequency = jnp.exp(-jnp.log(10000.0) * jnp.arange(half_width, dtype=jnp.float32) / half_width)
    angles = position.astype(jnp.float32)[:, None] * frequency[None, :]
    return (jnp.cos(angles), jnp.sin(angles))


def rotate(vectors, cosine, sine_part):
    half_width = HD // 2
    leading_half = vectors[..., :half_width]
    trailing_half = vectors[..., half_width:]
    cosine = cosine[:, None, :]
    sine_part = sine_part[:, None, :]
    return jnp.concatenate(
        [
            leading_half * cosine - trailing_half * sine_part,
            trailing_half * cosine + leading_half * sine_part,
        ],
        axis=-1,
    )


def rotate_back(vectors, cosine, sine_part):
    half_width = HD // 2
    leading_half = vectors[..., :half_width]
    trailing_half = vectors[..., half_width:]
    cosine = cosine[:, None, :]
    sine_part = sine_part[:, None, :]
    return jnp.concatenate(
        [
            leading_half * cosine + trailing_half * sine_part,
            trailing_half * cosine - leading_half * sine_part,
        ],
        axis=-1,
    )


def inner_rows(left, right):
    return lax.dot_general(
        left, right, (((0,), (0,)), ((), ())), preferred_element_type=jnp.float32
    )


def outer_cols(left, right):
    return lax.dot_general(
        left, right, (((1,), (1,)), ((), ())), preferred_element_type=jnp.float32
    )


def spread(row_block):
    return lax.all_gather(row_block, "tp", axis=0, tiled=True)


def collect(partial_value):
    return lax.psum_scatter(
        partial_value.astype(jnp.bfloat16), "tp", scatter_dimension=0, tiled=True
    ).astype(jnp.float32)


def fetch_keys(key_value):
    return lax.all_gather(key_value, "ctx", axis=0, tiled=True)


def query_bounds(seq_lengths, block_first, row_count):
    token_index = block_first + jnp.arange(row_count, dtype=jnp.int32)
    doc_ends = jnp.cumsum(seq_lengths)
    before = (doc_ends[None, :] <= token_index[:, None]).astype(jnp.int32)
    doc_start = jnp.sum(before * seq_lengths[None, :], axis=1)
    return (token_index, doc_start)


def block_scores(query_heads, pair_block, block_first, token_index, doc_start, head_width):
    row_count = pair_block.shape[0]
    key_heads = pair_block[:, :head_width].reshape(row_count, head_width // HD, HD)
    value_heads = pair_block[:, head_width:].reshape(row_count, head_width // HD, HD)
    scores = jnp.einsum(
        "qhd,khd->hqk", query_heads, key_heads, preferred_element_type=jnp.float32
    ) * HD ** (-0.5)
    key_index = block_first + jnp.arange(row_count, dtype=jnp.int32)
    allowed = (key_index[None, :] >= doc_start[:, None]) & (
        key_index[None, :] <= token_index[:, None]
    )
    return (scores, allowed[None], key_heads, value_heads)


def split_blocks(pairs_all, row_count):
    blocks = pairs_all.reshape(-1, row_count, pairs_all.shape[1])
    block_starts = jnp.arange(blocks.shape[0], dtype=jnp.int32) * row_count
    return (blocks, block_starts)


def attend(query_heads, pairs_all, token_index, doc_start, head_width):
    row_count = query_heads.shape[0]
    head_count = head_width // HD
    blocks, block_starts = split_blocks(pairs_all, row_count)
    last_query = token_index[row_count - 1]
    first_query = doc_start[0]

    def rowmax_live(carried, block_parts):
        running_top, running_sum = carried
        scores, allowed, unused_keys, unused_values = block_scores(
            query_heads, block_parts[0], block_parts[1], token_index, doc_start, head_width
        )
        masked = jnp.where(allowed, scores, -1e30)
        new_top = jnp.maximum(running_top, jnp.max(masked, axis=-1))
        running_sum = running_sum * jnp.exp(running_top - new_top) + jnp.sum(
            jnp.where(allowed, jnp.exp(masked - new_top[..., None]), 0.0), axis=-1
        )
        return (new_top, running_sum)

    def rowmax_step(carried, block_parts):
        live = (block_parts[1] <= last_query) & (block_parts[1] + row_count > first_query)
        return (
            lax.cond(live, lambda held: rowmax_live(held, block_parts), lambda held: held, carried),
            None,
        )

    initial = (
        jnp.full((head_count, row_count), -1e30, jnp.float32),
        jnp.zeros((head_count, row_count), jnp.float32),
    )
    (running_top, running_sum), unused = lax.scan(rowmax_step, initial, (blocks, block_starts))
    log_total = running_top + jnp.log(running_sum)

    def output_live(accumulated, block_parts):
        scores, allowed, unused_keys, value_heads = block_scores(
            query_heads, block_parts[0], block_parts[1], token_index, doc_start, head_width
        )
        soft_weights = jnp.where(allowed, jnp.exp(scores - log_total[..., None]), 0.0).astype(
            jnp.bfloat16
        )
        return accumulated + jnp.einsum(
            "hqk,khd->qhd", soft_weights, value_heads, preferred_element_type=jnp.float32
        )

    def output_step(accumulated, block_parts):
        live = (block_parts[1] <= last_query) & (block_parts[1] + row_count > first_query)
        return (
            lax.cond(
                live, lambda held: output_live(held, block_parts), lambda held: held, accumulated
            ),
            None,
        )

    accumulated, unused = lax.scan(
        output_step, jnp.zeros((row_count, head_count, HD), jnp.float32), (blocks, block_starts)
    )
    return (accumulated, log_total)


def attend_back(
    query_heads, pairs_all, token_index, doc_start, head_width, log_total, accumulated, grad_heads
):
    row_count = query_heads.shape[0]
    head_count = head_width // HD
    blocks, block_starts = split_blocks(pairs_all, row_count)
    last_query = token_index[row_count - 1]
    first_query = doc_start[0]
    rowdot = jnp.sum(grad_heads.astype(jnp.float32) * accumulated, axis=-1).T

    def grad_live(grad_acc, block_parts):
        scores, allowed, key_heads, value_heads = block_scores(
            query_heads, block_parts[0], block_parts[1], token_index, doc_start, head_width
        )
        soft_weights = jnp.where(allowed, jnp.exp(scores - log_total[..., None]), 0.0)
        grad_soft = jnp.einsum(
            "qhd,khd->hqk", grad_heads, value_heads, preferred_element_type=jnp.float32
        )
        grad_scores = (soft_weights * (grad_soft - rowdot[..., None])).astype(jnp.bfloat16)
        grad_acc = grad_acc + jnp.einsum(
            "hqk,khd->qhd", grad_scores, key_heads, preferred_element_type=jnp.float32
        )
        grad_keys = jnp.einsum(
            "hqk,qhd->khd", grad_scores, query_heads, preferred_element_type=jnp.float32
        ) * HD ** (-0.5)
        grad_values = jnp.einsum(
            "hqk,qhd->khd",
            soft_weights.astype(jnp.bfloat16),
            grad_heads,
            preferred_element_type=jnp.float32,
        )
        return (grad_acc, (grad_keys, grad_values))

    def grad_skip(grad_acc):
        empty = jnp.zeros((row_count, head_count, HD), jnp.float32)
        return (grad_acc, (empty, empty))

    def grad_step(grad_acc, block_parts):
        live = (block_parts[1] <= last_query) & (block_parts[1] + row_count > first_query)
        return lax.cond(live, lambda held: grad_live(held, block_parts), grad_skip, grad_acc)

    grad_query, (grad_keys, grad_values) = lax.scan(
        grad_step, jnp.zeros((row_count, head_count, HD), jnp.float32), (blocks, block_starts)
    )
    grad_query = grad_query * HD ** (-0.5)
    grad_pairs = jnp.concatenate(
        [grad_keys.reshape(-1, head_width), grad_values.reshape(-1, head_width)], axis=1
    )
    return (grad_query, grad_pairs)


def norm_back(whole_rows, scale_rows, gain, grad_normed, grad_rest):
    unit_rows = whole_rows * scale_rows
    scaled = grad_normed * gain.astype(jnp.float32)
    grad_gain = jnp.sum(grad_normed * unit_rows, axis=0)
    grad_whole = grad_rest + scale_rows * (
        scaled - unit_rows * jnp.mean(scaled * unit_rows, axis=-1, keepdims=True)
    )
    return (grad_gain, grad_whole)


def layer_forward(row_block, first_values, value_mix, weights, seq_lengths):
    gain_first, w_qkv, w_out, gain_second, w_gateup, w_down = weights
    head_count = w_qkv.shape[1]
    head_width = head_count * HD
    model_width = row_block.shape[1]
    whole_rows = row_block.astype(jnp.float32)
    scale_first = lax.rsqrt(jnp.mean(whole_rows * whole_rows, axis=-1, keepdims=True) + EPSILON)
    normed = (whole_rows * scale_first * gain_first.astype(jnp.float32)).astype(jnp.bfloat16)
    normed_all = spread(normed)
    row_count = normed_all.shape[0]
    projected = outer_cols(normed_all, w_qkv.reshape(3 * head_width, model_width))
    token_index, doc_start = query_bounds(seq_lengths, lax.axis_index("ctx") * row_count, row_count)
    cosine, sine_part = rope_parts(token_index - doc_start)
    query_heads = rotate(
        projected[:, :head_width].reshape(row_count, head_count, HD), cosine, sine_part
    ).astype(jnp.bfloat16)
    key_heads = rotate(
        projected[:, head_width : 2 * head_width].reshape(row_count, head_count, HD),
        cosine,
        sine_part,
    ).astype(jnp.bfloat16)
    mixed = (
        (1.0 - value_mix) * projected[:, 2 * head_width :]
        + value_mix * first_values.astype(jnp.float32)
    ).astype(jnp.bfloat16)
    key_value = jnp.concatenate([key_heads.reshape(row_count, head_width), mixed], axis=1)
    pairs_all = fetch_keys(key_value)
    accumulated, log_total = attend(query_heads, pairs_all, token_index, doc_start, head_width)
    attended = accumulated.reshape(row_count, head_width).astype(jnp.bfloat16)
    hidden = whole_rows + collect(jnp.dot(attended, w_out, preferred_element_type=jnp.float32))
    scale_second = lax.rsqrt(jnp.mean(hidden * hidden, axis=-1, keepdims=True) + EPSILON)
    normed_second = (hidden * scale_second * gain_second.astype(jnp.float32)).astype(jnp.bfloat16)
    ffn_rows = spread(normed_second)
    gate_up = outer_cols(ffn_rows, w_gateup.reshape(-1, model_width))
    unit_count = gate_up.shape[1] // 2
    gate_part = gate_up[:, :unit_count]
    up_part = gate_up[:, unit_count:]
    activated = (jax.nn.silu(gate_part) * up_part).astype(jnp.bfloat16)
    down_part = jnp.dot(activated, w_down, preferred_element_type=jnp.float32)
    branch_out = collect(down_part)
    layer_out = (hidden + branch_out).astype(jnp.bfloat16)
    saved = (
        whole_rows,
        scale_first,
        normed_all,
        query_heads,
        pairs_all,
        token_index,
        doc_start,
        cosine,
        sine_part,
        log_total,
        accumulated,
        attended,
        hidden,
        scale_second,
        ffn_rows,
        gate_part,
        up_part,
        activated,
    )
    return (layer_out, mixed, pairs_all, saved)


def layer_backward(grad_rows, extra_values, value_mix, weights, saved):
    gain_first, w_qkv, w_out, gain_second, w_gateup, w_down = weights
    (
        whole_rows,
        scale_first,
        normed_all,
        query_heads,
        pairs_all,
        token_index,
        doc_start,
        cosine,
        sine_part,
        log_total,
        accumulated,
        attended,
        hidden,
        scale_second,
        ffn_rows,
        gate_part,
        up_part,
        activated,
    ) = saved
    model_width = whole_rows.shape[1]
    head_count = w_qkv.shape[1]
    head_width = head_count * HD
    row_count = normed_all.shape[0]
    grad_hidden = grad_rows.astype(jnp.float32)
    grad_down = spread(grad_rows)
    grad_wd = inner_rows(activated, grad_down)
    grad_act = outer_cols(grad_down, w_down)
    sigmoid_gate = jax.nn.sigmoid(gate_part)
    grad_gate = grad_act * up_part * sigmoid_gate * (1.0 + gate_part * (1.0 - sigmoid_gate))
    grad_up = grad_act * gate_part * sigmoid_gate
    grad_gate_up = jnp.concatenate([grad_gate, grad_up], axis=1).astype(jnp.bfloat16)
    grad_wgu = inner_rows(grad_gate_up, ffn_rows).reshape(w_gateup.shape)
    back_second = jnp.dot(
        grad_gate_up, w_gateup.reshape(-1, model_width), preferred_element_type=jnp.float32
    )
    grad_normed_second = collect(back_second)
    grad_gain2, grad_hidden = norm_back(
        hidden, scale_second, gain_second, grad_normed_second, grad_hidden
    )
    grad_branch_all = spread(grad_hidden.astype(jnp.bfloat16))
    grad_wo = inner_rows(attended, grad_branch_all)
    grad_heads = (
        outer_cols(grad_branch_all, w_out).astype(jnp.bfloat16).reshape(row_count, head_count, HD)
    )
    grad_query, grad_pairs_all = attend_back(
        query_heads,
        pairs_all,
        token_index,
        doc_start,
        head_width,
        log_total,
        accumulated,
        grad_heads,
    )
    grad_pairs = lax.psum_scatter(
        grad_pairs_all.astype(jnp.bfloat16), "ctx", scatter_dimension=0, tiled=True
    ).astype(jnp.float32)
    grad_mixed = grad_pairs[:, head_width:] + extra_values.astype(jnp.float32)
    grad_keys = rotate_back(
        grad_pairs[:, :head_width].reshape(row_count, head_count, HD), cosine, sine_part
    )
    grad_query = rotate_back(grad_query, cosine, sine_part)
    grad_projected = jnp.concatenate(
        [
            grad_query.reshape(row_count, head_width),
            grad_keys.reshape(row_count, head_width),
            (1.0 - value_mix) * grad_mixed,
        ],
        axis=1,
    ).astype(jnp.bfloat16)
    send_values = (value_mix * grad_mixed).astype(jnp.bfloat16)
    grad_wqkv = inner_rows(grad_projected, normed_all).reshape(w_qkv.shape)
    grad_normed = collect(
        jnp.dot(
            grad_projected,
            w_qkv.reshape(3 * head_width, model_width),
            preferred_element_type=jnp.float32,
        )
    )
    grad_gain1, grad_whole = norm_back(
        whole_rows, scale_first, gain_first, grad_normed, grad_hidden
    )
    return (
        grad_whole,
        send_values,
        (grad_gain1, grad_wqkv, grad_wo, grad_gain2, grad_wgu, grad_wd),
    )


def general_body(inputs, cotangent, lengths, gain1, wqkv, wo, gain2, wgu, wd):
    section_index = lax.axis_index("section")
    leading = section_index == 0
    value_mix = jnp.where(leading, 0.0, 0.5).astype(jnp.float32)
    micro_count = inputs.shape[0]
    local_rows = inputs.shape[1]
    model_width = inputs.shape[2]
    head_width = wqkv.shape[2] * HD
    row_count = local_rows * lax.axis_size("tp")
    gateup_use, down_use = (wgu[0], wd[0])
    weights = (gain1[0], wqkv[0], wo[0], gain2[0], gateup_use, down_use)
    recv_rows = jnp.zeros((local_rows, model_width), jnp.bfloat16)
    recv_values = jnp.zeros((row_count, head_width), jnp.bfloat16)
    states = []
    outputs = []
    for turn_index in range(micro_count + 1):
        own_rows = inputs[min(turn_index, micro_count - 1)]
        row_block = jnp.where(leading, own_rows, recv_rows)
        seq_lengths = jnp.where(
            leading, lengths[min(turn_index, micro_count - 1)], lengths[max(turn_index - 1, 0)]
        )
        layer_out, mixed, pairs_all, unused = layer_forward(
            row_block, recv_values, value_mix, weights, seq_lengths
        )
        kept_pairs = None
        states.append((row_block, recv_values, seq_lengths, kept_pairs))
        outputs.append(layer_out)
        if turn_index < micro_count:
            recv_rows, recv_values = shifted((layer_out, mixed), "section", 1)
    grad_rows_in = jnp.zeros((local_rows, model_width), jnp.bfloat16)
    grad_values_in = jnp.zeros((row_count, head_width), jnp.bfloat16)
    totals = None
    turn_grads = []
    for turn_index in range(micro_count + 1):
        row_block, first_values, seq_lengths, kept_pairs = states[micro_count - turn_index]
        if turn_index < micro_count:
            fed_grad = cotangent[micro_count - 1 - turn_index]
        else:
            fed_grad = jnp.zeros_like(cotangent[0])
        grad_out = jnp.where(leading, grad_rows_in, fed_grad)
        unused_out, unused_mixed, unused_pairs, saved = layer_forward(
            row_block, first_values, value_mix, weights, seq_lengths
        )
        grad_whole, send_values, grads = layer_backward(
            grad_out, grad_values_in, value_mix, weights, saved
        )
        totals = grads if totals is None else jax.tree.map(jnp.add, totals, grads)
        sent_rows = grad_whole.astype(jnp.bfloat16)
        turn_grads.append(jnp.where(leading, grad_whole, sent_rows.astype(jnp.float32)))
        if turn_index < micro_count:
            grad_rows_in, grad_values_in = shifted((sent_rows, send_values), "section", -1)
    grad_gain1, grad_wqkv, grad_wo, grad_gain2, grad_wgu, grad_wd = totals
    grad_wqkv, grad_wo, grad_wgu, grad_wd = (
        lax.psum(grad_wqkv.astype(jnp.bfloat16), "ctx").astype(jnp.float32),
        lax.psum(grad_wo.astype(jnp.bfloat16), "ctx").astype(jnp.float32),
        lax.psum(grad_wgu.astype(jnp.bfloat16), "ctx").astype(jnp.float32),
        lax.psum(grad_wd.astype(jnp.bfloat16), "ctx").astype(jnp.float32),
    )
    grad_gain1, grad_gain2 = lax.psum((grad_gain1, grad_gain2), ("ctx", "tp"))
    acts = jnp.stack(
        [
            jnp.where(leading, outputs[batch_index], outputs[batch_index + 1])
            for batch_index in range(micro_count)
        ]
    )[None]
    input_grads = jnp.stack(
        [
            jnp.where(
                leading,
                turn_grads[micro_count - batch_index],
                turn_grads[micro_count - 1 - batch_index],
            )
            for batch_index in range(micro_count)
        ]
    )[None]
    return (
        acts,
        input_grads,
        grad_gain1[None],
        grad_wqkv[None],
        grad_wo[None],
        grad_gain2[None],
        grad_wgu[None],
        grad_wd[None],
    )


def device_groups(mesh_sizes, key, order):
    sections, contexts, parts = mesh_sizes
    groups = {}
    for section in range(sections):
        for ctx in range(contexts):
            for tp in range(parts):
                place = (section, ctx, tp)
                number = (section * contexts + ctx) * parts + tp
                groups.setdefault(key(*place), []).append((order(*place), number))
    return [[number for _, number in sorted(members)] for _, members in sorted(groups.items())]


def exchange(value, groups):
    return lax.all_to_all(
        value, ALL_AXES, split_axis=0, concat_axis=0, tiled=True, axis_index_groups=groups
    )


def document_bounds(ends_ref, index):
    start = jnp.zeros_like(index)
    for entry in range(ends_ref.shape[0]):
        end = ends_ref[entry]
        start = jnp.where(index >= end, end, start)
    return start


def scalar_start(ends_ref, index):
    start = jnp.int32(0)
    for entry in range(ends_ref.shape[0]):
        start = jnp.where(index >= ends_ref[entry], ends_ref[entry], start)
    return start


def scalar_end(ends_ref, index):
    end = ends_ref[ends_ref.shape[0] - 1]
    for entry in range(ends_ref.shape[0] - 2, -1, -1):
        end = jnp.where(index < ends_ref[entry], ends_ref[entry], end)
    return end


def dot(left, right, left_dim, right_dim):
    return lax.dot_general(
        left, right, (((left_dim,), (right_dim,)), ((), ())), preferred_element_type=jnp.float32
    )


def fold_rows(value, combine):
    rows, width = value.shape
    return combine(value.reshape(rows // 8, 8, width), axis=0)


def block_place(block, parts, width):
    entry = (block // (2 * parts)) * parts + block % parts
    return entry, pl.ds(pl.multiple_of((block // parts % 2) * width, width), width)


def attention_forward_kernel(parts, ends_ref, qkv_ref, out_ref, lse_ref, keys_ref, values_ref):
    program = pl.program_id(0)
    blocks, block_width = 2 * qkv_ref.shape[0], qkv_ref.shape[2] // 2
    width = CHUNK * block_width

    @pl.when(program == 0)
    def _():
        def turn(j, carry):
            entry, columns = block_place(j, parts, block_width)
            keys_ref[j] = qkv_ref[entry, HD : 2 * HD, columns].T
            values_ref[j, 0:HD, :] = qkv_ref[entry, 2 * HD : 3 * HD, columns]
            values_ref[j, HD : HD + ONES, :] = jnp.ones((ONES, block_width), jnp.bfloat16)
            return carry

        lax.fori_loop(0, blocks, turn, 0)

    query = []
    for block in range(CHUNK):
        entry, columns = block_place(program * CHUNK + block, parts, block_width)
        query.append(qkv_ref[entry, 0:HD, columns])
    query = jnp.concatenate(query, axis=1)
    first = program * width
    query_index = first + lax.broadcasted_iota(jnp.int32, (1, width), 1)
    start = document_bounds(ends_ref, query_index)
    low_chunk = scalar_start(ends_ref, first) // width
    high_start = scalar_start(ends_ref, first + width - 1)
    middle = jnp.clip((high_start + width - 1) // width, low_chunk, program)

    def step(chunk, carry, masked):
        top, acc = carry
        parts = []
        for entry in range(CHUNK):
            j = chunk * CHUNK + entry
            scores = dot(keys_ref[j], query, 1, 0)
            if masked:
                key_index = j * block_width + lax.broadcasted_iota(jnp.int32, (block_width, 1), 0)
                allowed = (key_index >= start) & (key_index <= query_index)
                scores = jnp.where(allowed, scores, MASKED)
            parts.append(scores)
        part_top = functools.reduce(jnp.maximum, [fold_rows(part, jnp.max) for part in parts])
        new_top = jnp.maximum(top, jnp.max(part_top, axis=0, keepdims=True))
        acc = acc * jnp.exp2(top - new_top)
        for entry in range(CHUNK):
            weights = jnp.exp2(parts[entry] - new_top).astype(jnp.bfloat16)
            acc = acc + dot(values_ref[chunk * CHUNK + entry], weights, 1, 0)
        return new_top, acc

    def on_diagonal(carry):
        top, acc = carry
        parts_of, tops = [], []
        for block in range(CHUNK):
            columns = slice(block * block_width, width)
            j = program * CHUNK + block
            scores = dot(keys_ref[j], query[:, columns], 1, 0)
            key_index = j * block_width + lax.broadcasted_iota(jnp.int32, (block_width, 1), 0)
            allowed = (key_index >= start[:, columns]) & (key_index <= query_index[:, columns])
            scores = jnp.where(allowed, scores, MASKED)
            parts_of.append(scores)
            part_top = fold_rows(scores, jnp.max)
            if block > 0:
                before = jnp.full((8, block * block_width), MASKED, jnp.float32)
                part_top = jnp.concatenate([before, part_top], axis=1)
            tops.append(part_top)
        chunk_top = jnp.max(functools.reduce(jnp.maximum, tops), axis=0, keepdims=True)
        new_top = jnp.maximum(top, chunk_top)
        acc = acc * jnp.exp2(top - new_top)
        for block, scores in enumerate(parts_of):
            weights = jnp.exp2(scores - new_top[:, block * block_width :]).astype(jnp.bfloat16)
            added = dot(values_ref[program * CHUNK + block], weights, 1, 0)
            if block > 0:
                before = jnp.zeros((HD + ONES, block * block_width), jnp.float32)
                added = jnp.concatenate([before, added], axis=1)
            acc = acc + added
        return new_top, acc

    carry = (
        jnp.full((1, width), MASKED, jnp.float32),
        jnp.zeros((HD + ONES, width), jnp.float32),
    )
    carry = lax.fori_loop(low_chunk, middle, functools.partial(step, masked=True), carry)
    carry = lax.fori_loop(middle, program, functools.partial(step, masked=False), carry)
    top, acc = on_diagonal(carry)
    total = acc[HD : HD + 1]
    out = (acc[:HD] / total).astype(jnp.bfloat16)
    lse = top + jnp.log2(total)
    for entry in range(CHUNK):
        columns = slice(entry * block_width, (entry + 1) * block_width)
        out_ref[entry] = out[:, columns]
        lse_ref[entry] = lse[:, columns]


def attention_forward(ends, qkv, parts):
    blocks, width = 2 * qkv.shape[0], qkv.shape[2] // 2
    return pl.pallas_call(
        functools.partial(attention_forward_kernel, parts),
        grid_spec=pltpu.PrefetchScalarGridSpec(
            num_scalar_prefetch=1,
            grid=(blocks // CHUNK,),
            in_specs=[pl.BlockSpec(qkv.shape, lambda i, ends_ref: (0, 0, 0))],
            out_specs=[
                pl.BlockSpec((CHUNK, HD, width), lambda i, ends_ref: (i, 0, 0)),
                pl.BlockSpec((CHUNK, 1, width), lambda i, ends_ref: (i, 0, 0)),
            ],
            scratch_shapes=[
                pltpu.VMEM((blocks, width, HD), jnp.bfloat16),
                pltpu.VMEM((blocks, HD + ONES, width), jnp.bfloat16),
            ],
        ),
        out_shape=[
            jax.ShapeDtypeStruct((blocks, HD, width), jnp.bfloat16),
            jax.ShapeDtypeStruct((blocks, 1, width), jnp.float32),
        ],
        compiler_params=pltpu.CompilerParams(vmem_limit_bytes=VMEM_LIMIT),
        cost_estimate=LIGHT,
        name="attention_forward",
    )(ends, qkv)


def attention_backward_kernel(
    parts, ends_ref, qkv_ref, out_ref, grad_ref, lse_ref, result_ref,
    query_grad_ref, delta_ref, queries_ref, grads_ref, lses_ref,
):
    program = pl.program_id(0)
    blocks, block_width = 2 * qkv_ref.shape[0], qkv_ref.shape[2] // 2
    width = CHUNK * block_width

    @pl.when(program == 0)
    def _():
        def turn(i, carry):
            for entry in range(CHUNK):
                block = i * CHUNK + entry
                columns = slice(entry * block_width, (entry + 1) * block_width)
                grad = grad_ref[block]
                place, tokens = block_place(block, parts, block_width)
                queries_ref[i, :, columns] = qkv_ref[place, 0:HD, tokens]
                grads_ref[i, :, columns] = grad
                lses_ref[i, :, columns] = lse_ref[block]
                delta_ref[i, :, columns] = jnp.sum(
                    grad.astype(jnp.float32) * out_ref[block].astype(jnp.float32),
                    axis=0,
                    keepdims=True,
                )
            query_grad_ref[i] = jnp.zeros((HD, width), jnp.float32)
            return carry

        lax.fori_loop(0, blocks // CHUNK, turn, 0)

    own_places = [
        block_place(program * CHUNK + block, parts, block_width) for block in range(CHUNK)
    ]

    def joined(low_row, high_row):
        return jnp.concatenate(
            [qkv_ref[place, low_row:high_row, tokens] for place, tokens in own_places], axis=1
        )

    first = program * width
    keys_t = joined(HD, 2 * HD)
    keys = keys_t.T
    values = joined(2 * HD, 3 * HD).T
    key_index = first + lax.broadcasted_iota(jnp.int32, (width, 1), 0)
    near_end = scalar_end(ends_ref, first)
    far_end = scalar_end(ends_ref, first + width - 1)
    stop = (far_end - 1) // width + 1
    middle = jnp.clip(near_end // width, program + 1, stop)

    def step(i, carry, masked):
        key_grad, value_grad = carry
        query = queries_ref[i]
        grad = grads_ref[i]
        weights = jnp.exp2(dot(keys, query, 1, 0) - lses_ref[i])
        if masked:
            query_index = i * width + lax.broadcasted_iota(jnp.int32, (1, width), 1)
            start = document_bounds(ends_ref, query_index)
            allowed = (key_index >= start) & (key_index <= query_index)
            weights = jnp.where(allowed, weights, 0.0)
        grad_weights = dot(values, grad, 1, 0)
        grad_scores = (weights * (grad_weights - delta_ref[i])).astype(jnp.bfloat16)
        query_grad_ref[i] += dot(keys_t, grad_scores, 1, 0)
        value_grad = value_grad + dot(grad, weights.astype(jnp.bfloat16), 1, 1)
        key_grad = key_grad + dot(query, grad_scores, 1, 1)
        return key_grad, value_grad

    key_grad = jnp.zeros((HD, width), jnp.float32)
    value_grad = jnp.zeros((HD, width), jnp.float32)
    own_query_grads = []
    for block in range(CHUNK):
        columns = slice(block * block_width, (block + 1) * block_width)
        height = (block + 1) * block_width
        query = queries_ref[program, :, columns]
        grad = grads_ref[program, :, columns]
        query_index = (
            first + block * block_width + lax.broadcasted_iota(jnp.int32, (1, block_width), 1)
        )
        start = document_bounds(ends_ref, query_index)
        rows_index = key_index[:height]
        allowed = (rows_index >= start) & (rows_index <= query_index)
        scores = dot(keys[:height], query, 1, 0)
        weights = jnp.where(allowed, jnp.exp2(scores - lses_ref[program, :, columns]), 0.0)
        grad_weights = dot(values[:height], grad, 1, 0)
        grad_scores = (weights * (grad_weights - delta_ref[program, :, columns])).astype(
            jnp.bfloat16
        )
        own_query_grads.append(dot(keys_t[:, :height], grad_scores, 1, 0))
        added = (
            dot(query, grad_scores, 1, 1),
            dot(grad, weights.astype(jnp.bfloat16), 1, 1),
        )
        if height < width:
            behind = jnp.zeros((HD, width - height), jnp.float32)
            added = [jnp.concatenate([value, behind], axis=1) for value in added]
        key_grad = key_grad + added[0]
        value_grad = value_grad + added[1]
    query_grad_ref[program] += jnp.concatenate(own_query_grads, axis=1)
    carry = (key_grad, value_grad)
    carry = lax.fori_loop(program + 1, middle, functools.partial(step, masked=False), carry)
    key_grad, value_grad = lax.fori_loop(middle, stop, functools.partial(step, masked=True), carry)
    query_grad = query_grad_ref[program] * HD ** (-0.5)
    key_grad = key_grad * LOG_2
    for block, (place, tokens) in enumerate(own_places):
        columns = slice(block * block_width, (block + 1) * block_width)
        result_ref[place, 0:HD, tokens] = query_grad[:, columns].astype(jnp.bfloat16)
        result_ref[place, HD : 2 * HD, tokens] = key_grad[:, columns].astype(jnp.bfloat16)
        result_ref[place, 2 * HD : 3 * HD, tokens] = value_grad[:, columns].astype(jnp.bfloat16)


def attention_backward(ends, qkv, out, grad, lse, parts):
    blocks, block_width = 2 * qkv.shape[0], qkv.shape[2] // 2
    chunks, width = blocks // CHUNK, CHUNK * block_width

    def whole(value):
        return pl.BlockSpec(value.shape, lambda i, ends_ref: (0, 0, 0))

    return pl.pallas_call(
        functools.partial(attention_backward_kernel, parts),
        grid_spec=pltpu.PrefetchScalarGridSpec(
            num_scalar_prefetch=1,
            grid=(chunks,),
            in_specs=[whole(qkv), whole(out), whole(grad), whole(lse)],
            out_specs=whole(qkv),
            scratch_shapes=[
                pltpu.VMEM((chunks, HD, width), jnp.float32),
                pltpu.VMEM((chunks, 1, width), jnp.float32),
                pltpu.VMEM((chunks, HD, width), jnp.bfloat16),
                pltpu.VMEM((chunks, HD, width), jnp.bfloat16),
                pltpu.VMEM((chunks, 1, width), jnp.float32),
            ],
        ),
        out_shape=jax.ShapeDtypeStruct(qkv.shape, jnp.bfloat16),
        compiler_params=pltpu.CompilerParams(vmem_limit_bytes=VMEM_LIMIT),
        cost_estimate=LIGHT,
        name="attention_backward",
    )(ends, qkv, out, grad, lse)


def rope_pair(leading_half, trailing_half, cosine, sine_part):
    return (
        leading_half * cosine - trailing_half * sine_part,
        trailing_half * cosine + leading_half * sine_part,
    )


def low(value):
    return value.astype(jnp.bfloat16)


def wide(value):
    return value.astype(jnp.float32)


def whole_block(value):
    zeros = (0,) * value.ndim
    return pl.BlockSpec(value.shape, lambda *_: zeros)


def feed_forward_kernel(rows_ref, gate_w_ref, up_w_ref, down_w_ref, gate_ref, up_ref, act_ref, sum_ref):
    rows = rows_ref[...]
    gate = dot(gate_w_ref[...], rows, 1, 1)
    up = dot(up_w_ref[...], rows, 1, 1)
    active = (gate * jax.nn.sigmoid(gate) * up).astype(jnp.bfloat16)
    gate_ref[...] = gate.astype(jnp.bfloat16)
    up_ref[...] = up.astype(jnp.bfloat16)
    act_ref[...] = active

    @pl.when(pl.program_id(0) == 0)
    def _():
        sum_ref[...] = jnp.zeros_like(sum_ref)

    sum_ref[...] += dot(active, down_w_ref[...], 0, 0)


def feed_forward(rows, w_gate, w_up, w_down, tile):
    units, width = w_gate.shape
    count = rows.shape[0]
    weight = pl.BlockSpec((tile, width), lambda i: (i, 0))
    column = pl.BlockSpec((tile, count), lambda i: (i, 0))
    hidden = jax.ShapeDtypeStruct((units, count), jnp.bfloat16)
    return pl.pallas_call(
        feed_forward_kernel,
        grid=(units // tile,),
        in_specs=[whole_block(rows), weight, weight, weight],
        out_specs=[column, column, column, pl.BlockSpec((count, width), lambda i: (0, 0))],
        out_shape=[hidden, hidden, hidden, jax.ShapeDtypeStruct((count, width), jnp.float32)],
        compiler_params=pltpu.CompilerParams(vmem_limit_bytes=VMEM_LIMIT),
        cost_estimate=LIGHT,
        name="feed_forward",
    )(rows, w_gate, w_up, w_down)


def feed_forward_back_kernel(
    grad_ref, gate_ref, up_ref, gate_w_ref, up_w_ref, down_w_ref, grad_gate_ref, grad_up_ref, sum_ref
):
    grad_act = dot(down_w_ref[...], grad_ref[...], 1, 1)
    gate = gate_ref[...].astype(jnp.float32)
    up = up_ref[...].astype(jnp.float32)
    sigmoid_gate = jax.nn.sigmoid(gate)
    grad_gate = (grad_act * up * sigmoid_gate * (1.0 + gate * (1.0 - sigmoid_gate))).astype(
        jnp.bfloat16
    )
    grad_up = (grad_act * gate * sigmoid_gate).astype(jnp.bfloat16)
    grad_gate_ref[...] = grad_gate
    grad_up_ref[...] = grad_up

    @pl.when(pl.program_id(0) == 0)
    def _():
        sum_ref[...] = jnp.zeros_like(sum_ref)

    sum_ref[...] += dot(grad_gate, gate_w_ref[...], 0, 0) + dot(grad_up, up_w_ref[...], 0, 0)


def feed_forward_back(grad, gate, up, w_gate, w_up, w_down, tile):
    units, width = w_gate.shape
    count = grad.shape[0]
    weight = pl.BlockSpec((tile, width), lambda i: (i, 0))
    column = pl.BlockSpec((tile, count), lambda i: (i, 0))
    hidden = jax.ShapeDtypeStruct((units, count), jnp.bfloat16)
    return pl.pallas_call(
        feed_forward_back_kernel,
        grid=(units // tile,),
        in_specs=[whole_block(grad), column, column, weight, weight, weight],
        out_specs=[column, column, pl.BlockSpec((count, width), lambda i: (0, 0))],
        out_shape=[hidden, hidden, jax.ShapeDtypeStruct((count, width), jnp.float32)],
        compiler_params=pltpu.CompilerParams(vmem_limit_bytes=VMEM_LIMIT),
        cost_estimate=LIGHT,
        name="feed_forward_back",
    )(grad, gate, up, w_gate, w_up, w_down)


def half_products_kernel(layout, sizes, has_addend, which_ref, *refs):
    refs = list(refs)
    out_ref = refs.pop()
    addend_ref = refs.pop() if has_addend else None
    totals = [
        sum(dot(refs[left][...], refs[right][...], 1, 0) for left, right in pairs)
        for pairs in layout
    ]
    for piece in range(out_ref.shape[0]):
        parts = [
            total[piece * size : (piece + 1) * size] for total, size in zip(totals, sizes)
        ]
        value = jnp.concatenate(parts, axis=0) if len(parts) > 1 else parts[0]
        if has_addend:
            value = value + addend_ref[piece].astype(jnp.float32)
        out_ref[piece] = value.astype(jnp.bfloat16)


def half_products(which, groups, pieces, per_step, addend=None):
    lefts, rights, layout = [], [], []
    for group in groups:
        for left, right in group:
            if not any(left is known for known in lefts):
                lefts.append(left)
            if not any(right is known for known in rights):
                rights.append(right)
    find = lambda known, value: next(i for i, entry in enumerate(known) if entry is value)
    for group in groups:
        layout.append(
            tuple((find(lefts, left), len(lefts) + find(rights, right)) for left, right in group)
        )
    sizes = tuple(group[0][0].shape[0] // (2 * pieces) for group in groups)
    width = rights[0].shape[1]
    steps = pieces // per_step
    out_spec = pl.BlockSpec((per_step, sum(sizes), width), lambda i, which_ref: (i, 0, 0))
    left_specs = [
        pl.BlockSpec(
            (left.shape[0] // (2 * steps), left.shape[1]),
            lambda i, which_ref: (which_ref[0] * steps + i, 0),
        )
        for left in lefts
    ]
    extra = [] if addend is None else [addend]
    work = sum(left.size // 2 for left, _ in sum(groups, ()))
    return pl.pallas_call(
        functools.partial(half_products_kernel, tuple(layout), sizes, addend is not None),
        grid_spec=pltpu.PrefetchScalarGridSpec(
            num_scalar_prefetch=1,
            grid=(steps,),
            in_specs=left_specs + [whole_block(right) for right in rights] + [out_spec] * len(extra),
            out_specs=out_spec,
        ),
        out_shape=jax.ShapeDtypeStruct((pieces, sum(sizes), width), jnp.bfloat16),
        compiler_params=pltpu.CompilerParams(vmem_limit_bytes=VMEM_LIMIT),
        cost_estimate=LIGHT,
        name="half_products",
    )(which.reshape(1).astype(jnp.int32), *lefts, *rights, *extra)


def together(*values):
    return lax.optimization_barrier(values)


def after(value, *others):
    return lax.optimization_barrier((value, *others))[0]


def split_body(mesh_sizes, inputs, cotangent, lengths, gain1, wqkv, wo, gain2, wgu, wd):
    sections, contexts, parts = mesh_sizes
    half_parts = parts // 2
    section = lax.axis_index("section")
    ctx = lax.axis_index("ctx")
    tp = lax.axis_index("tp")
    row_side, column_side = ctx // 2, ctx % 2
    leading = section == 0
    batch = tp // half_parts
    model_width = inputs.shape[2]
    rows = inputs.shape[1]
    heads = wqkv.shape[2] * parts
    side_heads = heads // 2
    unit_rows = wd.shape[1] // contexts // 2
    head_rows = 3 * HD // 2
    out_rows = HD // 2
    half_width = HD // 2
    tile = 8 * unit_rows
    number = lambda s, c, t: (s * contexts + c) * parts + t
    places = [
        (s, c, t) for s in range(sections) for c in range(contexts) for t in range(parts)
    ]
    everyone = [[number(*place) for place in places]]
    token_of = lambda s, c, t: c * parts + t % half_parts + half_parts * s
    batch_groups = device_groups(mesh_sizes, lambda s, c, t: t // half_parts, token_of)
    head_groups = device_groups(
        mesh_sizes,
        lambda s, c, t: (c % 2, t // half_parts),
        lambda s, c, t: (c // 2, t % half_parts + half_parts * s),
    )
    side_groups = device_groups(mesh_sizes, lambda s, c, t: c % 2, lambda s, c, t: (s, c, t))
    crossing = [
        (number(s, c, t), number(s, c, (t + half_parts) % parts))
        for s, c, t in places
        if t // half_parts == s
    ]

    def to_batch(value):
        mine = lax.dynamic_index_in_dim(value, batch, 0, keepdims=False)
        other = lax.dynamic_index_in_dim(value, 1 - batch, 0, keepdims=False)
        moved = lax.ppermute(other, ALL_AXES, crossing)
        return jnp.where(section == batch, mine, moved)

    def to_home(value, layer):
        stay = [
            (number(s, c, t), number(layer, c, t)) for s, c, t in places if t // half_parts == s
        ]
        cross = [
            (number(s, c, t), number(layer, c, (t + half_parts) % parts))
            for s, c, t in places
            if t // half_parts != s
        ]
        return (lax.ppermute(value, ALL_AXES, stay), lax.ppermute(value, ALL_AXES, cross))

    def at_home(first_pair, second_pair):
        near = jnp.where(leading, first_pair[0], second_pair[0])
        far = jnp.where(leading, first_pair[1], second_pair[1])
        upper = batch == 0
        return jnp.stack([jnp.where(upper, near, far), jnp.where(upper, far, near)])[None]

    def swap_side(value):
        return lax.ppermute(value, "ctx", [(c, c ^ 1) for c in range(contexts)])

    def swap_far(value):
        return lax.ppermute(value, "ctx", [(c, c ^ 2) for c in range(contexts)])

    def swap_near(value):
        return lax.ppermute(value, "tp", [(t, t ^ 1) for t in range(parts)])

    def swap_half(value):
        return lax.ppermute(value, "tp", [(t, (t + half_parts) % parts) for t in range(parts)])

    def swap_section(value):
        return lax.ppermute(value, "section", [(0, 1), (1, 0)])

    def all_to_all(value, axis):
        return lax.all_to_all(value, axis, split_axis=0, concat_axis=0, tiled=True)

    def copies(value, count):
        return jnp.broadcast_to(value[None], (count, *value.shape))

    def gather(value, groups):
        return lax.all_gather(value, ALL_AXES, axis=0, tiled=True, axis_index_groups=groups)

    def ordered(index, own, other):
        return jnp.where(index == 0, own, other), jnp.where(index == 0, other, own)

    def by_core(value, which):
        return lax.dynamic_index_in_dim(value, which, 0, keepdims=False)

    def spread_half(piece):
        return piece, swap_half(piece)

    def spread_near(pieces_pair):
        pair = jnp.stack(ordered(batch, *pieces_pair))
        return pair, swap_near(pair)

    def spread_line(pairs):
        line = jnp.stack(ordered(tp % 2, *pairs), axis=1)
        return line.reshape(parts, *line.shape[2:])

    def spread_far(line):
        return line, swap_far(line)

    def spread_heads(pair):
        pair = jnp.stack(ordered(row_side, *pair))
        own_heads = pair[:, :, :head_rows].reshape(-1, model_width)
        own_outs = pair[:, :, head_rows:]
        return (own_heads, swap_section(own_heads)), (own_outs, swap_side(own_outs))

    def spread_outs(pair):
        own_outs = jnp.stack(ordered(column_side, *pair), axis=1).reshape(-1, model_width)
        return own_outs, swap_section(own_outs)

    def join_outs(pair):
        return jnp.concatenate(ordered(section, *pair), axis=0)

    def own_halves(value, axis, size):
        part = lax.dynamic_slice_in_dim(value, ctx * size, size, axis)
        return part.reshape(2, -1, model_width)

    packed = jnp.concatenate(
        [
            own_halves(wqkv[0], 1, heads // (parts * contexts)),
            own_halves(wo[0], 0, HD),
            own_halves(wgu[0, 0], 0, 2 * unit_rows),
            own_halves(wgu[0, 1], 0, 2 * unit_rows),
            own_halves(wd[0], 0, 2 * unit_rows),
        ],
        axis=1,
    )
    kept = by_core(packed, section)
    passed = swap_section(by_core(packed, 1 - section))
    pieces = ordered(section, kept, passed)
    attention_rows = head_rows + out_rows

    def feed_forward_weights(piece):
        whole = gather(piece[attention_rows:], side_groups)
        whole = whole.reshape(2 * 2 * parts, 3, unit_rows, model_width)
        return [whole[:, entry].reshape(-1, model_width) for entry in range(3)]

    rows_in = to_batch(inputs)
    line = spread_near(spread_half(pieces[0][:attention_rows]))
    line, rows_in = together(spread_line(line), rows_in)
    w_ffn = [feed_forward_weights(after(pieces[0], line)), None]
    w_heads, w_outs = [None, None], [None, None]
    first_pair = spread_far(line)

    gains = wide(jnp.concatenate([gain1, gain2], axis=0))
    gain_sets = ordered(section, gains, swap_section(gains))

    seq_lengths = lax.dynamic_index_in_dim(lengths, batch, 0, keepdims=False)
    ends = jnp.cumsum(seq_lengths).astype(jnp.int32)
    token_index = jnp.concatenate(
        [
            token_of(section, 2 * row_side + side, tp) * rows + jnp.arange(rows, dtype=jnp.int32)
            for side in range(2)
        ]
    )
    before = (ends[None, :] <= token_index[:, None]).astype(jnp.int32)
    position = token_index - jnp.sum(before * seq_lengths[None, :], axis=1)
    frequency = jnp.exp(
        -jnp.log(10000.0) * jnp.arange(half_width, dtype=jnp.float32) / half_width
    )
    angles = position.astype(jnp.float32)[None, :] * frequency[:, None]
    cosine, sine_part = jnp.cos(angles), jnp.sin(angles)

    def head_halves(value):
        size = value.shape[1] // 2
        return value.reshape(heads, 2, size, rows).transpose(1, 0, 2, 3).reshape(2, -1, rows)

    def whole_heads(value):
        value = value.reshape(2, heads, -1, rows)
        return value.transpose(1, 0, 2, 3).reshape(heads, -1, rows)

    def nothing(value):
        return value

    def layer_forward(whole_rows, first_values, layer, in_zero, in_first, in_second, in_middle, in_third, in_fourth):
        gain_first, gain_second = gain_sets[layer][0], gain_sets[layer][1]
        scale_first = lax.rsqrt(jnp.mean(whole_rows * whole_rows, axis=-1, keepdims=True) + EPSILON)
        normed = low(whole_rows * scale_first * gain_first)
        far_normed = in_zero(swap_side(normed))
        side_rows = jnp.concatenate(ordered(column_side, normed, far_normed), axis=0)
        halves = ordered(section, *[dot(weight, side_rows, 1, 1) for weight in w_heads[layer]])
        upper, lower = [half.reshape(side_heads, head_rows, 2 * rows) for half in halves]
        query = rope_pair(upper[:, :half_width], upper[:, half_width:HD], cosine, sine_part)
        key = rope_pair(upper[:, HD:], lower[:, :half_width], cosine, sine_part)
        value = lower[:, half_width:]
        if first_values is not None:
            value = 0.5 * value + 0.5 * wide(first_values)
        mixed = low(value)
        shrunk = [low(half * (HD ** (-0.5) / LOG_2)) for half in query]
        qkv = exchange(
            jnp.concatenate([*shrunk, low(key[0]), low(key[1]), mixed], axis=1), head_groups
        )
        qkv = in_first(qkv)
        out, lse = attention_forward(ends, qkv, parts)
        out = in_second(out)
        attended = head_halves(in_middle(exchange(out, batch_groups)))
        hidden = whole_rows + dot(attended.reshape(-1, rows), w_outs[layer], 0, 0)
        scale_second = lax.rsqrt(jnp.mean(hidden * hidden, axis=-1, keepdims=True) + EPSILON)
        normed_second = low(hidden * scale_second * gain_second)
        far_rows = swap_side(normed_second)
        near = feed_forward(normed_second, *w_ffn[layer], tile)
        far_rows = in_third(after(far_rows, near[3]))
        far = feed_forward(far_rows, *w_ffn[layer], tile)
        sent_down = low(far[3])

        def layer_out(*others):
            far_down = in_fourth(swap_side(after(sent_down, *others)))
            return low(hidden + (near[3] + wide(far_down)))

        saved = (
            whole_rows, scale_first, side_rows, qkv, out, lse, attended, hidden, scale_second,
            (normed_second, far_rows), near[:3], far[:3],
        )
        return layer_out, mixed, saved

    def norm_back(whole_rows, scale_rows, gain, grad_normed, grad_rest):
        unit = whole_rows * scale_rows
        scaled = grad_normed * gain
        grad_gain = jnp.sum(grad_normed * unit, axis=0)
        grad_whole = grad_rest + scale_rows * (
            scaled - unit * jnp.mean(scaled * unit, axis=-1, keepdims=True)
        )
        return grad_gain, grad_whole

    def pick(value, index, axis):
        return lax.dynamic_index_in_dim(value, index, axis, keepdims=False)

    def parted(value, index, axis):
        return pick(value, index, axis), pick(value, 1 - index, axis)

    def moved_pair(pair, swap):
        return pair[0], swap(pair[1])

    def halve(value, index, swap, axis):
        return moved_pair(parted(value, index, axis), swap)

    def add(pair):
        return low(wide(pair[0]) + wide(pair[1]))

    def near_parts(value):
        return parted(value.reshape(2, half_parts, *value.shape[1:]), tp % 2, 1)

    def near_sum(value):
        return moved_pair(near_parts(value), swap_near)

    def far_sum(pair):
        return halve(add(pair), batch, swap_half, 0)

    def layer_backward(grad_rows, extra_values, saved, layer, in_first, in_second, in_third, in_fourth, in_fifth):
        (
            whole_rows, scale_first, _, qkv, out, lse, attended, hidden, scale_second,
            ffn_rows, near, far,
        ) = saved
        gain_first, gain_second = gain_sets[layer][0], gain_sets[layer][1]
        grad_down = low(grad_rows)
        far_down = swap_side(grad_down)
        grad_gate, grad_up, near_back = feed_forward_back(grad_down, *near[:2], *w_ffn[layer], tile)
        far_down = in_first(after(far_down, near_back))
        far_gate, far_up, far_back = feed_forward_back(far_down, *far[:2], *w_ffn[layer], tile)
        far_back = swap_side(low(far_back))
        groups = (
            ((grad_gate, ffn_rows[0]), (far_gate, ffn_rows[1])),
            ((grad_up, ffn_rows[0]), (far_up, ffn_rows[1])),
            ((near[2], grad_down), (far[2], far_down)),
        )
        products = functools.partial(
            half_products, groups=groups, pieces=2 * parts, per_step=4
        )
        sent = products(1 - section)
        moved = swap_section(sent)
        far_back = in_second(after(far_back, sent))
        grad_gain2, grad_hidden = norm_back(
            hidden, scale_second, gain_second, near_back + wide(far_back), wide(grad_rows)
        )
        grad_branch = low(grad_hidden)
        grad_heads = whole_heads(low(dot(w_outs[layer], grad_branch, 1, 1)))
        grad_heads = exchange(grad_heads, batch_groups)
        rest = products(section, addend=moved)
        out_pair = (attended.reshape(-1, rows), grad_branch)
        grad_heads, rest = in_third(grad_heads, rest, out_pair)
        grad_qkv = attention_backward(ends, qkv, out, grad_heads, lse, parts)
        grad_qkv = in_fourth(grad_qkv)
        grad_qkv = in_fifth(exchange(grad_qkv, head_groups))
        grad_qkv = wide(grad_qkv)
        quarter = lambda entry: grad_qkv[:, entry * half_width : (entry + 1) * half_width]
        grad_query = rope_pair(quarter(0), quarter(1), cosine, -sine_part)
        grad_key = rope_pair(quarter(2), quarter(3), cosine, -sine_part)
        grad_value = grad_qkv[:, 2 * HD :]
        send_values = None
        if extra_values is None:
            grad_value = 0.5 * grad_value
            send_values = low(grad_value)
        else:
            grad_value = grad_value + wide(extra_values)
        upper = low(jnp.concatenate([*grad_query, grad_key[0]], axis=1))
        lower = low(jnp.concatenate([grad_key[1], grad_value], axis=1))
        grad_halves = jnp.stack([upper, lower]).reshape(2, -1, 2 * rows)
        return grad_halves, send_values, grad_hidden, out_pair, grad_gain2

    def input_grads_of(grad_halves, grad_hidden, saved, layer, beside):
        whole_rows, scale_first = saved[:2]
        places_of = (section, 1 - section)
        grad_side = sum(
            dot(by_core(grad_halves, place), weight, 0, 0)
            for place, weight in zip(places_of, w_heads[layer])
        ).reshape(2, rows, model_width)
        grad_far = swap_side(low(by_core(grad_side, 1 - column_side)))
        grad_normed = by_core(grad_side, column_side) + wide(beside(grad_far))
        return norm_back(whole_rows, scale_first, gain_sets[layer][0], grad_normed, grad_hidden)

    def piece_sum(value, groups):
        return lax.psum_scatter(
            value, ALL_AXES, scatter_dimension=0, tiled=True, axis_index_groups=groups
        )

    line_groups = device_groups(
        mesh_sizes, lambda s, c, t: (s, c % 2), lambda s, c, t: (c, t)
    )
    plane_shape = (2, 2, parts)
    pending = {}

    def weights_zero(value):
        value, pair = together(value, first_pair)
        w_heads[0], pending["outs"] = spread_heads(pair)
        return value

    def weights_line(value):
        value, piece = together(value, pieces[1][:attention_rows])
        pending["weights"] = spread_half(piece)
        return value

    def weights_outs_first(value):
        value, pending["outs"], w_ffn[0], weights = together(
            value, pending["outs"], w_ffn[0], pending["weights"]
        )
        pending["weights"] = spread_near(weights)
        w_outs[0] = join_outs(spread_outs(pending["outs"]))
        return value

    def weights_far(value):
        value, line = together(value, pending["weights"])
        pending["weights"] = spread_far(spread_line(line))
        w_ffn[1] = feed_forward_weights(after(pieces[1], value))
        return value

    def weights_heads(value):
        value, pairs = together(value, pending["weights"])
        w_heads[1], pending["outs"] = spread_heads(pairs)
        return value

    first_result, first_values, first_saved = layer_forward(
        wide(rows_in), None, 0,
        weights_zero, weights_line, nothing, weights_outs_first, weights_far, weights_heads,
    )

    first_out = first_result()

    def start_outs(value):
        value, grads = together(value, cotangent)
        pending["grad_in"] = to_batch(grads)
        return value

    def end_outs(value):
        value, outs, w_ffn[1], pending["grad_in"] = together(
            value, pending["outs"], w_ffn[1], pending["grad_in"]
        )
        w_outs[1] = join_outs(spread_outs(outs))
        pending["first_home"] = to_home(after(first_out, value), 0)
        return value

    second_result, _, second_saved = layer_forward(
        wide(first_out), first_values, 1,
        nothing, start_outs, end_outs, nothing, nothing, nothing,
    )
    grad_in = pending["grad_in"]

    def out_sides(out_pair):
        products = functools.partial(half_products, groups=((out_pair,),), pieces=heads, per_step=8)
        out_sum = products(section, addend=swap_section(products(1 - section)))
        return parted(out_sum.reshape(*plane_shape, out_rows, model_width), column_side, 1)

    def second_third(value, rest, out_pair):
        value, rest = together(value, rest)
        rest = rest.reshape(-1, model_width)
        pending["second_rest"] = piece_sum(rest, line_groups)
        pending["second_out_rows"] = second_result(value)
        pending["out"] = out_sides(out_pair)
        value = after(value, pending["out"])
        pending["out"] = moved_pair(pending["out"], swap_side)
        return value, rest

    def second_fourth(value):
        value, pending["first_home"], second_out, out_sum = together(
            value, pending["first_home"], pending["second_out_rows"], pending["out"]
        )
        pending["second_home"] = to_home(second_out, 1)
        pending["second_out"] = add(out_sum).reshape(2 * parts, out_rows, model_width)
        return value

    grad_halves, send_values, grad_hidden, _, second_gain2 = layer_backward(
        grad_in, None, second_saved, 1, nothing, nothing, second_third, second_fourth, nothing
    )
    head_products = functools.partial(
        half_products,
        groups=(((grad_halves.reshape(-1, 2 * rows), second_saved[2]),),),
        pieces=side_heads,
        per_step=4,
    )

    def head_start(value):
        value, sent = together(value, head_products(1 - section))
        pending["moved"] = swap_section(sent)
        return value

    second_gain1, second_grad = input_grads_of(
        grad_halves, grad_hidden, second_saved, 1, head_start
    )
    second_grad = low(second_grad)

    def first_first(value):
        head = head_products(section, addend=pending["moved"])
        head = jnp.concatenate([head, pending["second_out"]], axis=1)
        head = parted(head.reshape(2, parts, -1, model_width), row_side, 0)
        value, head = together(value, head)
        pending["head"] = moved_pair(head, swap_far)
        return value

    def first_second(value):
        return value

    def first_third(value, rest, out_pair):
        out_sum = out_sides(out_pair)
        rest = rest.reshape(2, parts, -1, model_width)
        rest_a = parted(rest[:, :, : 2 * unit_rows], row_side, 0)
        rest_b = parted(rest[:, :, 2 * unit_rows :], row_side, 0)
        (
            value, rest_a, rest_b, out_sum, head, pending["second_rest"], pending["second_home"]
        ) = together(
            value, rest_a, rest_b, out_sum, pending["head"], pending["second_rest"],
            pending["second_home"],
        )
        pending["rest_a"] = moved_pair(rest_a, swap_far)
        pending["rest_b"] = rest_b
        pending["out"] = moved_pair(out_sum, swap_side)
        pending["head"] = near_sum(add(head))
        return value, rest

    def first_fourth(value):
        value, rest_a, rest_b, out_sum, head = together(
            value, pending["rest_a"], pending["rest_b"], pending["out"], pending["head"]
        )
        pending["head"] = far_sum(head)
        pending["second_rest"] = lax.all_gather(
            after(pending["second_rest"], value), "ctx", axis=0, tiled=False
        )
        pending["rest_b"] = moved_pair(rest_b, swap_far)
        pending["rest_a"] = near_sum(add(rest_a))
        pending["out"] = halve(add(out_sum), row_side, swap_far, 0)
        return value

    first_halves, _, first_hidden, _, first_gain2 = layer_backward(
        second_grad, send_values, first_saved, 0,
        first_first, first_second, first_third, first_fourth, nothing,
    )
    head_products = functools.partial(
        half_products,
        groups=(((first_halves.reshape(-1, 2 * rows), first_saved[2]),),),
        pieces=side_heads,
        per_step=4,
    )
    sent = head_products(1 - section)
    moved = swap_section(sent)
    def head_end(value):
        head = head_products(section, addend=moved).reshape(2, parts, head_rows, model_width)
        head = parted(head, row_side, 0)
        head, rest_a, rest_b, out_sum, second_head = together(
            head, pending["rest_a"], pending["rest_b"], pending["out"], pending["head"]
        )
        pending["head"] = moved_pair(head, swap_far)
        pending["rest_b"] = near_sum(add(rest_b))
        pending["rest_a"] = far_sum(rest_a)
        pending["out"] = add(out_sum)
        pending["second_head"] = add(second_head)
        return after(value, head)

    first_gain1, first_grad = input_grads_of(
        after(first_halves, sent), first_hidden, first_saved, 0, head_end
    )
    def summed(value, swap):
        return value + swap(value)

    gain_rows = jnp.stack([first_gain1, first_gain2, second_gain1, second_gain2])
    gain_rows = summed(gain_rows, swap_section)
    head, rest_a, rest_b, gain_rows, first_grad = together(
        pending["head"], pending["rest_a"], pending["rest_b"], gain_rows, low(first_grad)
    )
    head = near_sum(jnp.concatenate([add(head), pending["out"]], axis=1))
    rest_b = far_sum(rest_b)
    gain_rows = summed(summed(gain_rows, swap_side), swap_far)
    head, rest_b, gain_rows, first_grad, second_rest = together(
        head, rest_b, gain_rows, first_grad, pending["second_rest"]
    )
    head = far_sum(head)
    rest = jnp.concatenate([add(rest_a), add(rest_b)], axis=0)
    rest = lax.all_gather(rest, "ctx", axis=0, tiled=False)
    gain_rows = summed(gain_rows, swap_near)
    head, first_grad, home = together(head, first_grad, second_grad)
    first_grad_home = to_home(first_grad, 0)
    second_grad_home = to_home(home, 1)
    head = jnp.concatenate([add(head), pending["second_head"]], axis=0)
    head = all_to_all(copies(head, contexts), "ctx")
    head, gain_rows, first_grad_home, second_grad_home = together(
        head, gain_rows, first_grad_home, second_grad_home
    )
    gain_total = summed(gain_rows, swap_half)
    rest, head = together(rest, head)
    first_grads = (rest, head[:, :attention_rows])
    second_grads = (second_rest, head[:, attention_rows:])
    first_home, second_home = pending["first_home"], pending["second_home"]
    gain_total = jnp.where(leading, gain_total[:2], gain_total[2:])

    def finish(first, second):
        mine = jnp.where(leading, first, second)
        moved = swap_section(jnp.where(leading, second, first))
        return ordered(section, mine, moved)

    def joined(halves, first, count):
        both = jnp.stack([half[:, first : first + count] for half in halves], axis=1)
        return wide(both).reshape(-1, model_width)

    rest_grads = finish(first_grads[0], second_grads[0])
    grad_wgate, grad_wup, grad_wd = [
        joined(rest_grads, entry * unit_rows, unit_rows) for entry in range(3)
    ]
    head, grad_wgate, grad_wup, grad_wd = together(first_grads[1], grad_wgate, grad_wup, grad_wd)
    head_grads = finish(head, second_grads[1])
    grad_wqkv = joined(head_grads, 0, head_rows).reshape(contexts, 3, HD, model_width)
    grad_wo = joined(head_grads, head_rows, out_rows)
    return (
        at_home(first_home, second_home),
        wide(at_home(first_grad_home, second_grad_home)),
        gain_total[0:1],
        grad_wqkv.transpose(1, 0, 2, 3)[None],
        grad_wo[None],
        gain_total[1:2],
        jnp.stack([grad_wgate, grad_wup])[None],
        grad_wd[None],
    )


def body(mesh_sizes, *arguments):
    inputs, _, _, _, wqkv = arguments[:5]
    sections, contexts, parts = mesh_sizes
    own_heads, own_units = wqkv.shape[2], arguments[7].shape[2]
    fits = (
        sections == 2
        and inputs.shape[0] == 2
        and contexts == 4
        and parts % 2 == 0
        and own_heads == contexts
        and own_units % (16 * contexts) == 0
        and inputs.shape[1] % 128 == 0
    )
    if fits:
        return split_body(mesh_sizes, *arguments)
    return general_body(*arguments)


def solution(mesh):
    placed = (
        P(None, ("ctx", "tp"), None),
        P(None, ("ctx", "tp"), None),
        P(),
        P("section", None),
        P("section", None, "tp", None, None),
        P("section", "tp", None),
        P("section", None),
        P("section", None, "tp", None),
        P("section", "tp", None),
    )
    mesh_sizes = tuple(mesh.shape[axis] for axis in ALL_AXES)
    return jax.shard_map(
        functools.partial(body, mesh_sizes),
        mesh=mesh,
        in_specs=placed,
        out_specs=(
            P("section", None, ("ctx", "tp"), None),
            P("section", None, ("ctx", "tp"), None),
            P("section", None),
            P("section", None, "tp", None, None),
            P("section", "tp", None),
            P("section", None),
            P("section", None, "tp", None),
            P("section", "tp", None),
        ),
        check_vma=False,
    )
```
